32 devices in a mesh: pas: 16 (over z, y, x), mdl: 2 (over core).
Axes of the slice: x: 2, y: 2, z: 4, core: 2. Of those that a mesh axis runs over, the one named last changes fastest.
Arguments:
- target_states: bfloat16 [4096, 768], P('pas'), may hold values from -6 to 6
- passage_states: bfloat16 [640, 64, 768], P('pas', None, 'mdl'), may hold values from -6 to 6
- slot_query: int32 [640], P('pas'), may hold values from 0 to 15, as said below
- slot_live: int32 [640], P('pas'), may hold values from 0 to 1, as said below
- norm_gains: float32 [3, 768], replicated, may hold values from 0.5 to 1.5
- self_query: bfloat16 [768, 768], P('pas', 'mdl'), may hold values from -0.078125 to 0.078125
- self_key: bfloat16 [768, 768], P('pas', 'mdl'), may hold values from -0.21875 to 0.21875
- self_value: bfloat16 [768, 768], P('pas', 'mdl'), may hold values from -0.21875 to 0.21875
- self_output: bfloat16 [768, 768], P('mdl', 'pas'), may hold values from -0.625 to 0.625
- position_bias: float32 [32, 12], P(None, 'mdl'), may hold values from -4 to 4
- cross_query: bfloat16 [768, 768], P('pas', 'mdl'), may hold values from -0.078125 to 0.078125
- cross_key: bfloat16 [768, 768], P('pas', 'mdl'), may hold values from -0.21875 to 0.21875
- cross_value: bfloat16 [768, 768], P('pas', 'mdl'), may hold values from -0.21875 to 0.21875
- cross_output: bfloat16 [768, 768], P('mdl', 'pas'), may hold values from -1.25 to 1.25
- expand_weight: bfloat16 [768, 3072], P('pas', 'mdl'), may hold values from -0.21875 to 0.21875
- reduce_weight: bfloat16 [3072, 768], P('mdl', 'pas'), may hold values from -0.109375 to 0.109375
- output_cotangent: bfloat16 [4096, 768], P('pas'), may hold values from -6 to 6
Outputs:
- block_out: bfloat16 [4096, 768], P('pas')
- target_grad: bfloat16 [4096, 768], P('pas')
- passage_grad: bfloat16 [640, 64, 768], P('pas', None, 'mdl')
- norm_gains_grad: float32 [3, 768], replicated
- self_query_grad: float32 [768, 768], P('pas', 'mdl')
- self_key_grad: float32 [768, 768], P('pas', 'mdl')
- self_value_grad: float32 [768, 768], P('pas', 'mdl')
- self_output_grad: float32 [768, 768], P('mdl', 'pas')
- position_bias_grad: float32 [32, 12], P(None, 'mdl')
- cross_query_grad: float32 [768, 768], P('pas', 'mdl')
- cross_key_grad: float32 [768, 768], P('pas', 'mdl')
- cross_value_grad: float32 [768, 768], P('pas', 'mdl')
- cross_output_grad: float32 [768, 768], P('mdl', 'pas')
- expand_weight_grad: float32 [768, 3072], P('pas', 'mdl')
- reduce_weight_grad: float32 [3072, 768], P('mdl', 'pas')
The draws below stay inside these ranges and needn't reach their ends.
Inputs may be any that keep to these rules, and one draw needn't show every extreme that they name: `slot_query`: each query id names exactly 40 slots; query q's target tokens are rows q * 256 to (q + 1) * 256 - 1. The 40 slots of one index of pas hold at most 3 slots of the 1 queries of any one index of pas, and in every draw some pair reaches 3. `slot_live`: of each query's 40 slots, 5 or more are live, and some query has all 40 live.
All inputs are finite; a program needn't handle non-finite values.
Results may differ from the reference program's by a relative error of at most 0.025.
The reference program's roundings to bfloat16 on the way count: a program that leaves them out, or rounds other values in their place, can miss the bound.
Values may be sent and summed in bfloat16 or wider, within the bound.
A program may use at most 192 MiB of HBM per device.

```python
import math
import jax
import jax.numpy as jnp
import numpy as np
from jax import lax

D = 768
HEADS = 12
HEAD_DIM = 64
FF = 3072
NBUCKET = 32
MAXDIST = 128
TLEN = 256
PQ = 40
MINP = 5
Q_DEV = 1
PLEN = 64
SLOT_DEV = 40
SLOTS = 640
QUERIES = 16
TOKENS = 4096


def shuffle_one(subkey):
    return jax.random.permutation(subkey, SLOT_DEV)


def slot_layout(key):
    devices = SLOTS // SLOT_DEV
    incoming = SLOT_DEV
    sender_order = jax.random.permutation(jax.random.fold_in(key, 101), devices)
    receiver_order = jax.random.permutation(jax.random.fold_in(key, 102), devices)
    offsets = jax.random.permutation(jax.random.fold_in(key, 103), devices)[jnp.arange(incoming) % devices]
    local_orders = jax.vmap(shuffle_one)(jax.random.split(jax.random.fold_in(key, 104), devices))
    receivers = jnp.arange(devices)[:, None]
    places = jnp.arange(incoming)[None, :]
    senders = sender_order[(receiver_order[receivers] + offsets[places]) % devices]
    local_slot = local_orders[senders, places]
    flat_slot = (senders * incoming + local_slot).reshape(-1)
    owners = receivers * Q_DEV + places // PQ
    counts = jax.random.randint(jax.random.fold_in(key, 105), (QUERIES,), MINP, PQ + 1)
    counts = counts.at[jax.random.randint(jax.random.fold_in(key, 106), (), 0, QUERIES)].set(PQ)
    alive = (places % PQ < counts[owners]).astype(jnp.int32)
    owners_full = jnp.broadcast_to(owners, (devices, incoming)).reshape(-1).astype(jnp.int32)
    slot_query = jnp.zeros((SLOTS,), jnp.int32).at[flat_slot].set(owners_full)
    slot_live = jnp.zeros((SLOTS,), jnp.int32).at[flat_slot].set(alive.reshape(-1))
    return (slot_query, slot_live)


def draw_slot_query(key, part):
    return slot_layout(key)[0]


def draw_slot_live(key, part):
    return slot_layout(key)[1]


def spiked(values, stream_key, source, target, shards_of, factor):
    owner, partner = [(jnp.arange(values.shape[dim]) // (values.shape[dim] // shards_of)).reshape([-1 if axis == dim else 1 for axis in range(values.ndim)]) for dim in (source, target)]
    chosen = jax.random.permutation(stream_key, shards_of)[partner]
    strong = (owner == chosen) | (owner == (partner + shards_of // 2) % shards_of)
    return jnp.where(strong, factor * values, values)


def steps_of(stream_key, shape, cuts, least, top_value):
    loudness, own = 1.0, jax.random.fold_in(stream_key, 6)
    for axis_at, shards_of in cuts:
        steps = jnp.exp(jax.random.uniform(jax.random.fold_in(own, axis_at), (shards_of,), jnp.float32, least / len(cuts), top_value / len(cuts)))
        loudness = loudness * jnp.repeat(steps, shape[axis_at] // shards_of).reshape([-1 if axis == axis_at else 1 for axis in range(len(shape))])
    return loudness


def centred(stream_key, dims, scale, reach, pieces=(), kind=jnp.bfloat16):
    drawn = jax.random.normal(stream_key, dims, jnp.float32) * scale
    if len(pieces) > 0:
        drawn = steps_of(stream_key, dims, pieces, -0.22, 0.18) * drawn
    return jnp.clip(drawn, min=-reach, max=reach).astype(kind)


def heavy_noise(own_key, dims, deviation, reach, pieces, heavy, held_as=jnp.bfloat16):
    values = deviation * jax.random.normal(own_key, dims, jnp.float32)
    if pieces:
        values = values * steps_of(own_key, dims, pieces, -0.22, 0.18)
    return jnp.clip(spiked(values, jax.random.fold_in(own_key, 3), *heavy), -reach, reach).astype(held_as)


def setup_inputs(seed: int = 0) -> dict:
    key_of = jax.random.split(jax.random.key(seed), 18)
    return {
        "target_states": centred(key_of[0], (TOKENS, D), 1.0, 6.0, ((0, 16),)),
        "passage_states": centred(key_of[1], (SLOTS, PLEN, D), 1.0, 6.0, ((0, 16), (2, 2))),
        "slot_query": draw_slot_query(jax.random.fold_in(key_of[17], 71), 0),
        "slot_live": draw_slot_live(jax.random.fold_in(key_of[17], 71), 0),
        "norm_gains": jnp.clip(1.0 + 0.1 * jax.random.normal(key_of[4], (3, D), jnp.float32), 0.5, 1.5),
        "self_query": centred(key_of[5], (D, D), (8 * D) ** -0.5, 0.078125, ((0, 16), (1, 2))),
        "self_key": centred(key_of[6], (D, D), D ** -0.5, 0.21875, ((0, 16), (1, 2))),
        "self_value": centred(key_of[7], (D, D), D ** -0.5, 0.21875, ((0, 16), (1, 2))),
        "self_output": centred(key_of[8], (D, D), (D // 8) ** -0.5, 0.625, ((0, 2), (1, 16))),
        "position_bias": centred(key_of[9], (NBUCKET, HEADS), 1.0, 4.0, ((1, 2),), jnp.float32),
        "cross_query": centred(key_of[10], (D, D), (8 * D) ** -0.5, 0.078125, ((0, 16), (1, 2))),
        "cross_key": centred(key_of[11], (D, D), D ** -0.5, 0.21875, ((0, 16), (1, 2))),
        "cross_value": centred(key_of[12], (D, D), D ** -0.5, 0.21875, ((0, 16), (1, 2))),
        "cross_output": centred(key_of[13], (D, D), (D // 32) ** -0.5, 1.25, ((0, 2), (1, 16))),
        "expand_weight": centred(key_of[14], (D, FF), D ** -0.5, 0.21875, ((0, 16), (1, 2))),
        "reduce_weight": centred(key_of[15], (FF, D), FF ** -0.5, 0.109375, ((0, 2), (1, 16))),
        "output_cotangent": heavy_noise(key_of[16], (TOKENS, D), 1.0, 6.0, ((0, 16),), (0, 1, 16, 2.0)),
    }


EPSILON = 1e-06
MASKED = -1e+30
PRECISE = lax.Precision.HIGHEST

@jax.custom_vjp
def low(v):
    return lax.optimization_barrier(v.astype(jnp.bfloat16)).astype(jnp.float32)

@jax.custom_vjp
def low_back(v):
    return v

def low_keep(v):
    return (low(v), None)

def low_pass(kept, grad):
    return (grad,)

def back_keep(v):
    return (v, None)

def back_low(kept, grad):
    return (low(grad),)
low.defvjp(low_keep, low_pass)
low_back.defvjp(back_keep, back_low)

def bucket_table(length, buckets, distance):
    later = np.arange(length)[:, None]
    earlier = np.arange(length)[None, :]
    behind = np.maximum(later - earlier, 0)
    exact = buckets // 2
    spread = np.log(np.maximum(behind, 1) / exact) / math.log(distance / exact) * (buckets - exact)
    far_bucket = np.minimum(exact + np.floor(spread).astype(np.int32), buckets - 1)
    return np.where(behind < exact, behind, far_bucket).astype(np.int32)

def rms_norm(values, gain):
    return values * lax.rsqrt(lax.optimization_barrier(jnp.mean(values * values, axis=-1, keepdims=True)) + EPSILON) * gain

def matmul(left, right):
    return jnp.dot(left, right, precision=PRECISE, preferred_element_type=jnp.float32)

def attention(queries, key_rows, values, allowed, bias):
    scores = jnp.einsum('sihe,sjhe->shij', queries, key_rows, precision=PRECISE)
    if bias is not None:
        scores = scores + bias
    scores = low_back(scores)
    scores = jnp.where(allowed, scores, MASKED)
    highest = lax.optimization_barrier(jnp.max(scores, axis=-1, keepdims=True))
    exponent = jnp.exp(scores - highest)
    probability = low(exponent / lax.optimization_barrier(jnp.sum(exponent, axis=-1, keepdims=True)))
    mixed = jnp.einsum('shij,sjhe->sihe', probability, values, precision=PRECISE)
    return low_back(low(mixed))

def layer(weights, residual, passages, live):
    norm_gains, self_query, self_key, self_value, self_output, position_bias, cross_query, cross_key, cross_value, cross_output, expand_weight, reduce_weight = weights
    sequences = residual.shape[0] // TLEN
    normed = low(rms_norm(residual, norm_gains[0]))
    queries = low_back(low(matmul(normed, self_query))).reshape(sequences, TLEN, HEADS, HEAD_DIM)
    key_rows = low_back(low(matmul(normed, self_key))).reshape(sequences, TLEN, HEADS, HEAD_DIM)
    values = low_back(low(matmul(normed, self_value))).reshape(sequences, TLEN, HEADS, HEAD_DIM)
    buckets = jnp.asarray(bucket_table(TLEN, NBUCKET, MAXDIST))
    bias = jnp.transpose(position_bias[buckets], (2, 0, 1))[None]
    causal = jnp.asarray(np.tril(np.ones((TLEN, TLEN), dtype=bool)))
    mixed = attention(queries, key_rows, values, causal, bias).reshape(sequences * TLEN, D)
    residual = residual + low_back(matmul(mixed, self_output))
    normed = low(rms_norm(residual, norm_gains[1]))
    cross_queries = low_back(low(matmul(normed, cross_query))).reshape(sequences, TLEN, HEADS, HEAD_DIM)
    flat_states = passages.reshape(sequences * PQ * PLEN, D)
    cross_keys = low_back(low(matmul(flat_states, cross_key))).reshape(sequences, PQ * PLEN, HEADS, HEAD_DIM)
    cross_values = low_back(low(matmul(flat_states, cross_value))).reshape(sequences, PQ * PLEN, HEADS, HEAD_DIM)
    allowed = jnp.repeat(live > 0, PLEN, axis=1)[:, None, None, :]
    mixed = attention(cross_queries, cross_keys, cross_values, allowed, None).reshape(sequences * TLEN, D)
    residual = residual + low_back(matmul(mixed, cross_output))
    normed = low(rms_norm(residual, norm_gains[2]))
    before = low_back(matmul(normed, expand_weight))
    hidden = low(jax.nn.gelu(before, approximate=True))
    return residual + low_back(matmul(hidden, reduce_weight))

def reference(target_states, passage_states, slot_query, slot_live, norm_gains, self_query, self_key, self_value, self_output, position_bias, cross_query, cross_key, cross_value, cross_output, expand_weight, reduce_weight, output_cotangent):
    order = jnp.argsort(slot_query, stable=True).astype(jnp.int32)
    groups = QUERIES // Q_DEV
    live_sorted = slot_live[order].reshape(groups, Q_DEV, PQ)
    weights = tuple((weight.astype(jnp.float32) for weight in (norm_gains, self_query, self_key, self_value, self_output, position_bias, cross_query, cross_key, cross_value, cross_output, expand_weight, reduce_weight)))

    def forward(target, passages, params):
        arranged = passages[order].reshape(groups, Q_DEV, PQ, PLEN, D)
        rows = target.reshape(groups, Q_DEV * TLEN, D)

        def one_group(member):
            return layer(params, member[0], member[1], member[2])
        outputs = lax.map(jax.checkpoint(one_group), (rows, arranged, live_sorted))
        return outputs.reshape(TOKENS, D)
    result, pullback = jax.vjp(forward, target_states.astype(jnp.float32), passage_states.astype(jnp.float32), weights)
    target_grad, passage_grad, weight_grads = pullback(output_cotangent.astype(jnp.float32))
    return (result.astype(jnp.bfloat16), target_grad.astype(jnp.bfloat16), passage_grad.astype(jnp.bfloat16), weight_grads[0], weight_grads[1], weight_grads[2], weight_grads[3], weight_grads[4], weight_grads[5], weight_grads[6], weight_grads[7], weight_grads[8], weight_grads[9], weight_grads[10], weight_grads[11])
```

```python
from functools import partial
import math

import jax
import jax.numpy as jnp
import numpy as np
from jax import lax
from jax.experimental import pallas as pl
from jax.experimental.pallas import tpu as pltpu
from jax.sharding import PartitionSpec as P

HEAD_DIM = 64
MAXDIST = 128
TLEN = 256
PQ = 40


EPSILON = 1e-06
MASKED = -1e30


def bucket_table(length, buckets, distance):
    later = np.arange(length)[:, None]
    earlier = np.arange(length)[None, :]
    behind = np.maximum(later - earlier, 0)
    exact = buckets // 2
    spread = np.log(np.maximum(behind, 1) / exact) / math.log(distance / exact) * (buckets - exact)
    far_bucket = np.minimum(exact + np.floor(spread).astype(np.int32), buckets - 1)
    return np.where(behind < exact, behind, far_bucket).astype(np.int32)


def rms_forward(values, gain):
    factor = lax.rsqrt(jnp.mean(values * values, axis=-1, keepdims=True) + EPSILON)
    unit_rows = values * factor
    return (unit_rows, factor, (unit_rows * gain).astype(jnp.bfloat16))


def rms_backward(normed_grad, unit_rows, factor, gain):
    scaled_grad = normed_grad * gain
    input_grad = factor * (
        scaled_grad - unit_rows * jnp.mean(scaled_grad * unit_rows, axis=-1, keepdims=True)
    )
    return (input_grad, jnp.sum(normed_grad * unit_rows, axis=0))


def over_heads(partial_rows):
    return lax.psum(partial_rows, "mdl")


def score_block(queries, key_rows, allowed, bias):
    scores = jnp.einsum("sihe,sjhe->shij", queries, key_rows, preferred_element_type=jnp.float32)
    if bias is not None:
        scores = scores + bias
    return jnp.where(allowed, scores, MASKED)


def attend(queries, key_rows, values, allowed, bias):
    scores = score_block(queries, key_rows, allowed, bias)
    highest = jnp.max(scores, axis=-1, keepdims=True)
    totals = highest + jnp.log(jnp.sum(jnp.exp(scores - highest), axis=-1, keepdims=True))
    probability = jnp.exp(scores - totals)
    mixed = jnp.einsum(
        "shij,sjhe->sihe",
        probability.astype(jnp.bfloat16),
        values,
        preferred_element_type=jnp.float32,
    )
    return (mixed.astype(jnp.bfloat16), totals)


def attend_back(queries, key_rows, values, allowed, bias, totals, out_grad):
    scores = score_block(queries, key_rows, allowed, bias)
    probability = jnp.exp(scores - totals)
    prob_grad = jnp.einsum("sihe,sjhe->shij", out_grad, values, preferred_element_type=jnp.float32)
    centered = jnp.sum(probability * prob_grad, axis=-1, keepdims=True)
    score_grad = (probability * (prob_grad - centered)).astype(jnp.bfloat16)
    query_grad = jnp.einsum(
        "shij,sjhe->sihe", score_grad, key_rows, preferred_element_type=jnp.float32
    )
    key_grad = jnp.einsum(
        "shij,sihe->sjhe", score_grad, queries, preferred_element_type=jnp.float32
    )
    value_grad = jnp.einsum(
        "shij,sihe->sjhe",
        probability.astype(jnp.bfloat16),
        out_grad,
        preferred_element_type=jnp.float32,
    )
    return (query_grad, key_grad, value_grad, score_grad)


def send_plan(slot_query, slot_live, per_device, capacity):
    target_device = slot_query // per_device
    matching = target_device[:, None] == target_device[None, :]
    lower_part = jnp.tril(jnp.ones(matching.shape, jnp.bool_), -1)
    ranking = jnp.sum(jnp.logical_and(matching, lower_part), axis=1)
    position = target_device * capacity + ranking
    codes = jnp.where(slot_live > 0, slot_query % per_device + 1, 0).astype(jnp.bfloat16)
    return (position, codes)


def arrange_plan(got_codes, per_device, slots_each):
    local_query = got_codes.astype(jnp.int32) - 1
    matches = (local_query[:, None] == jnp.arange(per_device, dtype=jnp.int32)[None, :]).astype(
        jnp.int32
    )
    ranking = jnp.sum((jnp.cumsum(matches, axis=0) - 1) * matches, axis=1)
    spare_place = per_device * slots_each
    places = jnp.where(local_query >= 0, local_query * slots_each + ranking, spare_place)
    arrivals = got_codes.shape[0]
    gather_index = (
        jnp.zeros((spare_place + 1,), jnp.int32)
        .at[places]
        .set(jnp.arange(arrivals, dtype=jnp.int32))
    )
    valid_slot = jnp.zeros((spare_place + 1,), jnp.int32).at[places].set(1)
    return (gather_index[:spare_place], valid_slot[:spare_place] > 0)


def place_rows(rows, position, total_rows):
    return jnp.zeros((total_rows,) + rows.shape[1:], rows.dtype).at[position].set(rows)


def return_rows(rows, gather_index, total_rows):
    return jnp.zeros((total_rows,) + rows.shape[1:], rows.dtype).at[gather_index].add(rows)


def body_any(
    target_states,
    passage_states,
    slot_query,
    slot_live,
    norm_gains,
    self_query,
    self_key,
    self_value,
    self_output,
    position_bias,
    cross_query,
    cross_key,
    cross_value,
    cross_output,
    expand_weight,
    reduce_weight,
    output_cotangent,
):
    (
        query_full,
        key_full,
        value_full,
        cross_query_full,
        cross_key_full,
        cross_value_full,
        expand_full,
    ) = (
        lax.all_gather(self_query, "pas", axis=0, tiled=True),
        lax.all_gather(self_key, "pas", axis=0, tiled=True),
        lax.all_gather(self_value, "pas", axis=0, tiled=True),
        lax.all_gather(cross_query, "pas", axis=0, tiled=True),
        lax.all_gather(cross_key, "pas", axis=0, tiled=True),
        lax.all_gather(cross_value, "pas", axis=0, tiled=True),
        lax.all_gather(expand_weight, "pas", axis=0, tiled=True),
    )
    output_full, cross_output_full, reduce_full = (
        lax.all_gather(self_output, "pas", axis=1, tiled=True),
        lax.all_gather(cross_output, "pas", axis=1, tiled=True),
        lax.all_gather(reduce_weight, "pas", axis=1, tiled=True),
    )
    width_here = query_full.shape[1]
    heads_here = width_here // HEAD_DIM
    sequences = target_states.shape[0] // TLEN
    passage_len = passage_states.shape[1]
    bucket_count = position_bias.shape[0]
    devices = lax.axis_size("pas")
    slots_here = slot_query.shape[0]
    capacity = -(-slots_here // devices)
    buffer_rows = devices * capacity
    residual = target_states.astype(jnp.float32)
    unit_one, factor_one, normed_one = rms_forward(residual, norm_gains[0])
    self_weights = jnp.concatenate([query_full, key_full, value_full], axis=1)
    projected = jnp.dot(normed_one, self_weights, preferred_element_type=jnp.float32).astype(
        jnp.bfloat16
    )
    projected = projected.reshape(sequences, TLEN, 3, heads_here, HEAD_DIM)
    queries_self = projected[:, :, 0]
    keys_self = projected[:, :, 1]
    values_self = projected[:, :, 2]
    buckets = jnp.asarray(bucket_table(TLEN, bucket_count, MAXDIST))
    one_hot = (jnp.arange(bucket_count, dtype=jnp.int32)[:, None, None] == buckets[None]).astype(
        jnp.float32
    )
    bias_full = jnp.einsum("bij,bh->hij", one_hot, position_bias, precision=lax.Precision.HIGHEST)[
        None
    ]
    causal = jnp.asarray(np.tril(np.ones((TLEN, TLEN), dtype=bool)))
    attended_self, total_self = attend(queries_self, keys_self, values_self, causal, bias_full)
    merged_self = attended_self.reshape(sequences * TLEN, width_here)
    residual_two = residual + over_heads(
        jnp.dot(merged_self, output_full, preferred_element_type=jnp.float32)
    )
    unit_two, factor_two, normed_two = rms_forward(residual_two, norm_gains[1])
    cross_queries = jnp.dot(
        normed_two, cross_query_full, preferred_element_type=jnp.float32
    ).astype(jnp.bfloat16)
    cross_queries = cross_queries.reshape(sequences, TLEN, heads_here, HEAD_DIM)
    kv_weights = jnp.concatenate([cross_key_full, cross_value_full], axis=1)
    position, codes = send_plan(slot_query, slot_live, sequences, capacity)
    sent_codes = place_rows(codes, position, buffer_rows)
    states_full = lax.all_gather(passage_states, "mdl", axis=2, tiled=True)
    key_values = jnp.einsum(
        "tpd,dc->tpc", states_full, kv_weights, preferred_element_type=jnp.float32
    ).astype(jnp.bfloat16)
    received, got_codes = (
        lax.all_to_all(
            place_rows(key_values, position, buffer_rows),
            "pas",
            split_axis=0,
            concat_axis=0,
            tiled=True,
        ),
        lax.all_to_all(sent_codes, "pas", split_axis=0, concat_axis=0, tiled=True),
    )
    gather_index, valid_slot = arrange_plan(got_codes, sequences, PQ)
    arranged = jnp.take(received, gather_index, axis=0)
    arranged = arranged.reshape(sequences, PQ * passage_len, 2, heads_here, HEAD_DIM)
    key_rows = arranged[:, :, 0]
    value_rows = arranged[:, :, 1]
    allowed = jnp.repeat(valid_slot.reshape(sequences, PQ), passage_len, axis=1)[:, None, None, :]
    head_block = 2
    head_ranges = [
        slice(start_head, start_head + head_block)
        for start_head in range(0, heads_here, head_block)
    ]
    cross_parts = []
    cross_totals = []
    for head_range in head_ranges:
        mixed_part, total_part = attend(
            cross_queries[:, :, head_range],
            key_rows[:, :, head_range],
            value_rows[:, :, head_range],
            allowed,
            None,
        )
        cross_parts.append(mixed_part)
        cross_totals.append(total_part)
    merged_cross = jnp.concatenate(cross_parts, axis=2).reshape(sequences * TLEN, width_here)
    residual_three = residual_two + over_heads(
        jnp.dot(merged_cross, cross_output_full, preferred_element_type=jnp.float32)
    )
    unit_three, factor_three, normed_three = rms_forward(residual_three, norm_gains[2])
    before = jnp.dot(normed_three, expand_full, preferred_element_type=jnp.float32)
    hidden = jax.nn.gelu(before, approximate=True).astype(jnp.bfloat16)
    block_out = residual_three + over_heads(
        jnp.dot(hidden, reduce_full, preferred_element_type=jnp.float32)
    )
    grad_out = output_cotangent.astype(jnp.float32)
    reduce_grad = jnp.dot(hidden.T, output_cotangent, preferred_element_type=jnp.float32)
    hidden_grad = jnp.dot(output_cotangent, reduce_full.T, preferred_element_type=jnp.float32)
    unused_value, gelu_pullback = jax.vjp(partial(jax.nn.gelu, approximate=True), before)
    before_grad = gelu_pullback(hidden_grad)[0].astype(jnp.bfloat16)
    expand_grad = jnp.dot(normed_three.T, before_grad, preferred_element_type=jnp.float32)
    normed_grad = over_heads(
        jnp.dot(before_grad, expand_full.T, preferred_element_type=jnp.float32)
    )
    back_three, gain_three = rms_backward(normed_grad, unit_three, factor_three, norm_gains[2])
    grad_three = grad_out + back_three
    grad_low = grad_three.astype(jnp.bfloat16)
    cross_output_grad = jnp.dot(merged_cross.T, grad_low, preferred_element_type=jnp.float32)
    mixed_grad = jnp.dot(grad_low, cross_output_full.T, preferred_element_type=jnp.float32).astype(
        jnp.bfloat16
    )
    mixed_grad = mixed_grad.reshape(sequences, TLEN, heads_here, HEAD_DIM)
    query_parts = []
    key_parts = []
    value_parts = []
    for number, head_range in enumerate(head_ranges):
        query_part, key_part, value_part, unused_scores = attend_back(
            cross_queries[:, :, head_range],
            key_rows[:, :, head_range],
            value_rows[:, :, head_range],
            allowed,
            None,
            cross_totals[number],
            mixed_grad[:, :, head_range],
        )
        query_parts.append(query_part)
        key_parts.append(key_part)
        value_parts.append(value_part)
    cross_query_rows = (
        jnp.concatenate(query_parts, axis=2)
        .astype(jnp.bfloat16)
        .reshape(sequences * TLEN, width_here)
    )
    kv_grad = jnp.stack(
        [jnp.concatenate(key_parts, axis=2), jnp.concatenate(value_parts, axis=2)], axis=2
    )
    kv_grad = kv_grad.astype(jnp.bfloat16).reshape(sequences * PQ, passage_len, 2 * width_here)
    returned = lax.all_to_all(
        return_rows(kv_grad, gather_index, buffer_rows),
        "pas",
        split_axis=0,
        concat_axis=0,
        tiled=True,
    )
    kv_grad_here = jnp.take(returned, position, axis=0)
    kv_weight_grad = jnp.einsum(
        "tpd,tpc->dc", states_full, kv_grad_here, preferred_element_type=jnp.float32
    )
    states_grad = jnp.einsum(
        "tpc,dc->tpd", kv_grad_here, kv_weights, preferred_element_type=jnp.float32
    )
    passage_grad = lax.psum_scatter(
        states_grad.astype(jnp.bfloat16), "mdl", scatter_dimension=2, tiled=True
    )
    cross_query_grad = jnp.dot(normed_two.T, cross_query_rows, preferred_element_type=jnp.float32)
    normed_grad = over_heads(
        jnp.dot(cross_query_rows, cross_query_full.T, preferred_element_type=jnp.float32)
    )
    back_two, gain_two = rms_backward(normed_grad, unit_two, factor_two, norm_gains[1])
    grad_two = grad_three + back_two
    grad_low = grad_two.astype(jnp.bfloat16)
    self_output_grad = jnp.dot(merged_self.T, grad_low, preferred_element_type=jnp.float32)
    attended_grad = jnp.dot(grad_low, output_full.T, preferred_element_type=jnp.float32).astype(
        jnp.bfloat16
    )
    attended_grad = attended_grad.reshape(sequences, TLEN, heads_here, HEAD_DIM)
    query_grad, key_grad, value_grad, score_grad = attend_back(
        queries_self, keys_self, values_self, causal, bias_full, total_self, attended_grad
    )
    bias_grad = jnp.einsum(
        "hij,bij->bh",
        jnp.sum(score_grad.astype(jnp.float32), axis=0),
        one_hot,
        precision=lax.Precision.HIGHEST,
    )
    projected_grad = jnp.stack([query_grad, key_grad, value_grad], axis=2).astype(jnp.bfloat16)
    projected_grad = projected_grad.reshape(sequences * TLEN, 3 * width_here)
    self_weight_grad = jnp.dot(normed_one.T, projected_grad, preferred_element_type=jnp.float32)
    normed_grad = over_heads(
        jnp.dot(projected_grad, self_weights.T, preferred_element_type=jnp.float32)
    )
    back_one, gain_one = rms_backward(normed_grad, unit_one, factor_one, norm_gains[0])
    target_grad = (grad_two + back_one).astype(jnp.bfloat16)
    row_grads = (
        lax.psum_scatter(self_weight_grad[:, :width_here], "pas", scatter_dimension=0, tiled=True),
        lax.psum_scatter(
            self_weight_grad[:, width_here : 2 * width_here], "pas", scatter_dimension=0, tiled=True
        ),
        lax.psum_scatter(
            self_weight_grad[:, 2 * width_here :], "pas", scatter_dimension=0, tiled=True
        ),
        lax.psum_scatter(cross_query_grad, "pas", scatter_dimension=0, tiled=True),
        lax.psum_scatter(kv_weight_grad[:, :width_here], "pas", scatter_dimension=0, tiled=True),
        lax.psum_scatter(kv_weight_grad[:, width_here:], "pas", scatter_dimension=0, tiled=True),
        lax.psum_scatter(expand_grad, "pas", scatter_dimension=0, tiled=True),
    )
    col_grads = (
        lax.psum_scatter(self_output_grad, "pas", scatter_dimension=1, tiled=True),
        lax.psum_scatter(cross_output_grad, "pas", scatter_dimension=1, tiled=True),
        lax.psum_scatter(reduce_grad, "pas", scatter_dimension=1, tiled=True),
    )
    gains_total, bias_total = lax.psum(
        (jnp.stack([gain_one, gain_two, gain_three]), bias_grad), "pas"
    )
    return (
        block_out.astype(jnp.bfloat16),
        target_grad,
        passage_grad,
        gains_total,
        row_grads[0],
        row_grads[1],
        row_grads[2],
        col_grads[0],
        bias_total,
        row_grads[3],
        row_grads[4],
        row_grads[5],
        col_grads[1],
        row_grads[6],
        col_grads[2],
    )


CHIPS = 16
RANKS = 3
FLAG_ROWS = 16
MESH_ID = pl.DeviceIdType.MESH
VMEM_LIMIT = 56 * 2**20


def fits(mesh):
    return mesh.shape["pas"] == CHIPS and mesh.shape["mdl"] == 2


def places():
    me, core = lax.axis_index("pas"), lax.axis_index("mdl")
    x, y, z = me % 2, (me // 2) % 2, me // 4
    across_x, across_y = me + 1 - 2 * x, me + 2 - 4 * y
    near = across_y + (across_x - across_y) * core
    far = across_x + (across_y - across_x) * core
    return me, core, x, y, z, near, far


def remote(src, dst, send_sem, recv_sem, device):
    return pltpu.make_async_remote_copy(
        src_ref=src,
        dst_ref=dst,
        send_sem=send_sem,
        recv_sem=recv_sem,
        device_id=device,
        device_id_type=MESH_ID,
    )


def greet_all(me, core):
    barrier = pltpu.get_barrier_semaphore()
    for k in range(1, CHIPS):
        pl.semaphore_signal(
            barrier, inc=1, device_id=((me + k) % CHIPS, core), device_id_type=MESH_ID
        )
    pl.semaphore_signal(barrier, inc=1, device_id=(me, 1 - core), device_id_type=MESH_ID)
    pl.semaphore_wait(barrier, CHIPS)


def gather_kernel(
    index_ref,
    shard_ref,
    passage_ref,
    flag_ref,
    full_ref,
    states_ref,
    outgoing,
    own_sem,
    z_send,
    z_recv,
    near_send,
    near_recv,
    far_send,
    far_recv,
    slot_send,
    slot_recv,
    core_send,
    core_recv,
    slot_own,
):
    me, core, x, y, z, near, far = places()
    groups = shard_ref.shape[0]
    greet_all(me, core)

    def z_copy(g, k):
        return remote(
            shard_ref.at[g],
            full_ref.at[g, z, y, x],
            z_send.at[g, k - 1],
            z_recv.at[g, k - 1],
            ((me + 4 * k) % CHIPS, core),
        )

    def near_copy(g):
        block = full_ref.at[g, :, y, x]
        return remote(block, block, near_send.at[g], near_recv.at[g], (near, core))

    def far_copy(g, across_x):
        block = full_ref.at[g, :, :, x] if across_x else full_ref.at[g, :, y, :]
        return remote(block, block, far_send.at[g], far_recv.at[g], (far, core))

    def own_copy(g):
        return pltpu.make_async_copy(shard_ref.at[g], full_ref.at[g, z, y, x], own_sem.at[g])

    def slot_copy(k):
        to = (me + k) % CHIPS
        return remote(
            outgoing.at[to],
            states_ref.at[core, me],
            slot_send.at[k - 1],
            slot_recv.at[k - 1],
            (to, core),
        )

    def core_copy(k):
        block = states_ref.at[core, (me + CHIPS - k) % CHIPS]
        return remote(block, block, core_send.at[k], core_recv.at[k], (me, 1 - core))

    for g in range(groups):
        own_copy(g).start()
        for k in range(1, 4):
            z_copy(g, k).start()

    def fill(to, carry):
        for rank in range(RANKS):
            rows = passage_ref.shape[1]
            outgoing[to, rank * rows : (rank + 1) * rows, :] = passage_ref[
                index_ref[to * RANKS + rank]
            ]
        outgoing[to, RANKS * passage_ref.shape[1] :, :] = flag_ref[to]
        return carry

    lax.fori_loop(0, CHIPS, fill, 0)
    for k in range(1, CHIPS):
        slot_copy(k).start()
    mine = pltpu.make_async_copy(outgoing.at[me], states_ref.at[core, me], slot_own)
    mine.start()

    def second(g):
        own_copy(g).wait()
        for k in range(1, 4):
            z_copy(g, k).wait_recv()
        near_copy(g).start()

    def third(g):
        near_copy(g).wait_recv()

        @pl.when(core == 0)
        def _():
            far_copy(g, True).start()

        @pl.when(core == 1)
        def _():
            far_copy(g, False).start()

    second(0)
    second(1)
    third(0)
    second(2)
    third(1)
    second(3)
    third(2)
    third(3)
    mine.wait()
    core_copy(0).start()
    for k in range(1, CHIPS):
        slot_copy(k).wait_recv()
        core_copy(k).start()
    for g in range(groups):
        far_copy(g, True).wait_recv()
    for k in range(CHIPS):
        core_copy(k).wait()
    for k in range(1, CHIPS):
        slot_copy(k).wait_send()
    for g in range(groups):
        for k in range(1, 4):
            z_copy(g, k).wait_send()
        near_copy(g).wait_send()
        far_copy(g, True).wait_send()


ANY = pl.BlockSpec(memory_space=pl.ANY)
IN_VMEM = pl.BlockSpec(memory_space=pltpu.VMEM)
IN_SMEM = pl.BlockSpec(memory_space=pltpu.SMEM)
DMA = pltpu.SemaphoreType.DMA


def gather_everything(index, shards, passages, flags):
    groups, rows, columns = shards.shape
    passage_len, half = passages.shape[1:]
    block_rows = RANKS * passage_len + FLAG_ROWS
    return pl.pallas_call(
        gather_kernel,
        out_shape=(
            jax.ShapeDtypeStruct((groups, 4, 2, 2, rows, columns), jnp.bfloat16),
            jax.ShapeDtypeStruct((2, CHIPS, block_rows, half), jnp.bfloat16),
        ),
        in_specs=[IN_SMEM, ANY, IN_VMEM, IN_VMEM],
        out_specs=(ANY, ANY),
        scratch_shapes=[
            pltpu.VMEM((CHIPS, block_rows, half), jnp.bfloat16),
            DMA((groups,)),
            DMA((groups, 3)),
            DMA((groups, 3)),
            DMA((groups,)),
            DMA((groups,)),
            DMA((groups,)),
            DMA((groups,)),
            DMA((CHIPS - 1,)),
            DMA((CHIPS - 1,)),
            DMA((CHIPS,)),
            DMA((CHIPS,)),
            DMA,
        ],
        compiler_params=pltpu.CompilerParams(
            collective_id=0, has_side_effects=True, vmem_limit_bytes=VMEM_LIMIT
        ),
    )(index, shards, passages, flags)


def pair_kernel(mine_ref, sum_ref, other, send_sem, recv_sem):
    partner = (lax.axis_index("pas"), 1 - lax.axis_index("mdl"))
    barrier = pltpu.get_barrier_semaphore()
    pl.semaphore_signal(barrier, inc=1, device_id=partner, device_id_type=MESH_ID)
    pl.semaphore_wait(barrier, 1)
    copy = remote(mine_ref, other, send_sem, recv_sem, partner)
    copy.start()
    copy.wait()
    sum_ref[...] = mine_ref[...] + other[...]


def over_pair(partial_rows):
    return pl.pallas_call(
        pair_kernel,
        out_shape=jax.ShapeDtypeStruct(partial_rows.shape, partial_rows.dtype),
        in_specs=[IN_VMEM],
        out_specs=IN_VMEM,
        scratch_shapes=[pltpu.VMEM(partial_rows.shape, partial_rows.dtype), DMA, DMA],
        compiler_params=pltpu.CompilerParams(
            collective_id=1, has_side_effects=True, vmem_limit_bytes=VMEM_LIMIT
        ),
    )(partial_rows)


def scatter_kernel(
    position_ref,
    grads_ref,
    passage_ref,
    small_ref,
    shard_ref,
    slots_ref,
    total_ref,
    far_got,
    far_sum,
    near_got,
    near_sum,
    z_got,
    pair_got,
    pair_sum,
    slot_got,
    small_got,
    small_sum,
    far_send,
    far_recv,
    near_send,
    near_recv,
    z_send,
    z_recv,
    pair_send,
    pair_recv,
    slot_send,
    slot_recv,
    small_send,
    small_recv,
):
    me, core, x, y, z, near, far = places()
    groups = grads_ref.shape[0]
    across_x, across_y = me + 1 - 2 * x, me + 2 - 4 * y
    kept = (1 - core) * y + core * x
    greet_all(me, core)

    def far_copy(g, over_x):
        block = grads_ref.at[g, :, :, 1 - x] if over_x else grads_ref.at[g, :, 1 - y, :]
        return remote(block, far_got.at[g], far_send.at[g], far_recv.at[g], (far, core))

    def near_copy(g):
        return remote(
            far_sum.at[g, :, 1 - kept], near_got.at[g], near_send.at[g], near_recv.at[g], (near, core)
        )

    def z_copy(g, k):
        return remote(
            near_sum.at[g, (z + k) % 4],
            z_got.at[g, k - 1],
            z_send.at[g, k - 1],
            z_recv.at[g, k - 1],
            ((me + 4 * k) % CHIPS, core),
        )

    def pair_copy(k):
        to = (me + k) % CHIPS
        return remote(
            passage_ref.at[1 - core, to],
            pair_got.at[to],
            pair_send.at[k],
            pair_recv.at[k],
            (me, 1 - core),
        )

    def slot_copy(k):
        to = (me + k) % CHIPS
        return remote(
            pair_sum.at[to],
            slot_got.at[me],
            slot_send.at[k - 1],
            slot_recv.at[k - 1],
            (to, core),
        )

    def small_copy(step):
        if step == 0:
            return remote(
                small_ref, small_got.at[0], small_send.at[0], small_recv.at[0], (across_x, core)
            )
        if step == 1:
            return remote(
                small_sum.at[0],
                small_got.at[1],
                small_send.at[1],
                small_recv.at[1],
                (across_y, core),
            )
        return remote(
            small_sum.at[1],
            small_got.at[2 + z],
            small_send.at[step],
            small_recv.at[step],
            ((me + 4 * (step - 1)) % CHIPS, core),
        )

    for k in range(CHIPS):
        pair_copy(k).start()
    small_copy(0).start()
    for g in range(groups):

        @pl.when(core == 0)
        def _():
            far_copy(g, True).start()

        @pl.when(core == 1)
        def _():
            far_copy(g, False).start()

    for k in list(range(1, CHIPS)) + [0]:
        to = (me + k) % CHIPS
        pair_copy(k).wait_recv()
        pair_sum[to] = (
            passage_ref[core, to].astype(jnp.float32) + pair_got[to].astype(jnp.float32)
        ).astype(jnp.bfloat16)
        if k:
            slot_copy(k).start()
    slot_got[me] = pair_sum[me]
    small_copy(0).wait_recv()
    small_sum[0] = small_ref[...] + small_got[0]
    small_copy(1).start()

    def far_add(g):
        far_copy(g, True).wait_recv()

        def step(i, carry):
            zi, o = i // 2, i % 2
            mine = grads_ref[g, zi, (1 - core) * o + core * y, (1 - core) * x + core * o]
            far_sum[g, zi, o] = (
                mine.astype(jnp.float32) + far_got[g, zi, o].astype(jnp.float32)
            ).astype(jnp.bfloat16)
            return carry

        lax.fori_loop(0, 8, step, 0)
        near_copy(g).start()

    def near_add(g):
        near_copy(g).wait_recv()

        def step(zi, carry):
            near_sum[g, zi] = (
                far_sum[g, zi, kept].astype(jnp.float32) + near_got[g, zi].astype(jnp.float32)
            ).astype(jnp.bfloat16)
            return carry

        lax.fori_loop(0, 4, step, 0)
        for k in range(1, 4):
            z_copy(g, k).start()

    def z_add(g):
        for k in range(1, 4):
            z_copy(g, k).wait_recv()
        total = near_sum[g, z].astype(jnp.float32)
        for k in range(3):
            total = total + z_got[g, k].astype(jnp.float32)
        shard_ref[g] = total

    far_add(0)
    small_copy(1).wait_recv()
    small_sum[1] = small_sum[0] + small_got[1]
    for step in range(2, 5):
        small_copy(step).start()
    small_got[2 + z] = small_sum[1]
    far_add(1)
    near_add(0)
    far_add(2)
    near_add(1)
    z_add(0)
    far_add(3)
    near_add(2)
    z_add(1)
    near_add(3)
    z_add(2)
    z_add(3)
    for step in range(2, 5):
        small_copy(step).wait_recv()
    total_ref[...] = small_got[2] + small_got[3] + small_got[4] + small_got[5]
    for k in range(1, CHIPS):
        slot_copy(k).wait_recv()
    rows = slots_ref.shape[1]

    def pick(slot, carry):
        at = position_ref[slot]
        slots_ref[slot] = slot_got[at // RANKS, pl.ds(at % RANKS * rows, rows), :]
        return carry

    lax.fori_loop(0, slots_ref.shape[0], pick, 0)
    for g in range(groups):
        far_copy(g, True).wait_send()
        near_copy(g).wait_send()
        for k in range(1, 4):
            z_copy(g, k).wait_send()
    for k in range(CHIPS):
        pair_copy(k).wait_send()
    for k in range(1, CHIPS):
        slot_copy(k).wait_send()
    for step in range(5):
        small_copy(step).wait_send()


def scatter_everything(position, grads, passage_parts, small, slots):
    groups, _, _, _, rows, columns = grads.shape
    _, _, block_rows, half = passage_parts.shape
    low = jnp.bfloat16
    return pl.pallas_call(
        scatter_kernel,
        out_shape=(
            jax.ShapeDtypeStruct((groups, rows, columns), jnp.float32),
            jax.ShapeDtypeStruct((slots, block_rows // RANKS, half), low),
            jax.ShapeDtypeStruct(small.shape, jnp.float32),
        ),
        in_specs=[IN_SMEM, IN_VMEM, IN_VMEM, IN_VMEM],
        out_specs=(IN_VMEM, IN_VMEM, IN_VMEM),
        scratch_shapes=[
            pltpu.VMEM((groups, 4, 2, rows, columns), low),
            pltpu.VMEM((groups, 4, 2, rows, columns), low),
            pltpu.VMEM((groups, 4, rows, columns), low),
            pltpu.VMEM((groups, 4, rows, columns), low),
            pltpu.VMEM((groups, 3, rows, columns), low),
            pltpu.VMEM((CHIPS, block_rows, half), low),
            pltpu.VMEM((CHIPS, block_rows, half), low),
            pltpu.VMEM((CHIPS, block_rows, half), low),
            pltpu.VMEM((6,) + small.shape, jnp.float32),
            pltpu.VMEM((2,) + small.shape, jnp.float32),
            DMA((groups,)),
            DMA((groups,)),
            DMA((groups,)),
            DMA((groups,)),
            DMA((groups, 3)),
            DMA((groups, 3)),
            DMA((CHIPS,)),
            DMA((CHIPS,)),
            DMA((CHIPS - 1,)),
            DMA((CHIPS - 1,)),
            DMA((5,)),
            DMA((5,)),
        ],
        compiler_params=pltpu.CompilerParams(
            collective_id=2, has_side_effects=True, vmem_limit_bytes=VMEM_LIMIT
        ),
    )(position, grads, passage_parts, small)


def rows_nt(left, right):
    return lax.dot_general(
        left, right, (((1,), (1,)), ((), ())), preferred_element_type=jnp.float32
    )


def rows_tn(left, right):
    return lax.dot_general(
        left, right, (((0,), (0,)), ((), ())), preferred_element_type=jnp.float32
    )


def route(slot_query, slot_live):
    matching = slot_query[:, None] == slot_query[None, :]
    earlier = jnp.tril(jnp.ones(matching.shape, jnp.bool_), -1)
    position = slot_query * RANKS + jnp.sum(jnp.logical_and(matching, earlier), axis=1).astype(
        jnp.int32
    )
    here = position[None, :] == jnp.arange(CHIPS * RANKS, dtype=jnp.int32)[:, None]
    slots = slot_query.shape[0]
    index = jnp.sum(jnp.where(here, jnp.arange(slots, dtype=jnp.int32)[None, :], 0), axis=1)
    live = jnp.sum(jnp.where(here, slot_live[None, :], 0), axis=1)
    return position, index, live


def body(
    target_states,
    passage_states,
    slot_query,
    slot_live,
    norm_gains,
    self_query,
    self_key,
    self_value,
    self_output,
    position_bias,
    cross_query,
    cross_key,
    cross_value,
    cross_output,
    expand_weight,
    reduce_weight,
    output_cotangent,
):
    low = jnp.bfloat16
    width_here = self_query.shape[1]
    heads_here = width_here // HEAD_DIM
    slots_here, passage_len, half = passage_states.shape
    bucket_count = position_bias.shape[0]
    shards = jnp.stack(
        [
            jnp.concatenate([self_query, self_key, self_value, self_output.T], axis=1),
            jnp.concatenate([cross_query, cross_key, cross_value, cross_output.T], axis=1),
            expand_weight,
            reduce_weight.T,
        ]
    )
    position, index, live = route(slot_query, slot_live)
    flags = jnp.repeat(live.reshape(CHIPS, RANKS), passage_len, axis=1).astype(low)
    flags = jnp.pad(flags, ((0, 0), (0, half - RANKS * passage_len)))
    flags = jnp.broadcast_to(flags[:, None, :], (CHIPS, FLAG_ROWS, half))
    full, states = gather_everything(index, shards, passage_states, flags)
    full = full.reshape(4, -1, full.shape[-1])
    w = width_here
    self_in, output_t = full[0, :, : 3 * w], full[0, :, 3 * w :]
    cross_query_full = full[1, :, :w]
    kv_weights = full[1, :, w : 3 * w]
    cross_output_t = full[1, :, 3 * w :]
    expand_full, reduce_t = full[2], full[3]
    key_rows_n = CHIPS * RANKS * passage_len
    live_keys = states[0, :, RANKS * passage_len, : RANKS * passage_len].reshape(1, key_rows_n)
    allowed = (live_keys > 0)[:, None, None, :]
    states = states[:, :, : RANKS * passage_len].reshape(2, key_rows_n, half)

    residual = target_states.astype(jnp.float32)
    unit_one, factor_one, normed_one = rms_forward(residual, norm_gains[0])
    projected = jnp.dot(normed_one, self_in, preferred_element_type=jnp.float32).astype(low)
    projected = projected.reshape(1, TLEN, 3, heads_here, HEAD_DIM)
    queries_self = projected[:, :, 0]
    keys_self = projected[:, :, 1]
    values_self = projected[:, :, 2]
    buckets = jnp.asarray(bucket_table(TLEN, bucket_count, MAXDIST))
    one_hot = (jnp.arange(bucket_count, dtype=jnp.int32)[:, None, None] == buckets[None]).astype(
        jnp.float32
    )
    bias_full = jnp.einsum("bij,bh->hij", one_hot, position_bias, precision=lax.Precision.HIGHEST)[
        None
    ]
    causal = jnp.asarray(np.tril(np.ones((TLEN, TLEN), dtype=bool)))
    attended_self, total_self = attend(queries_self, keys_self, values_self, causal, bias_full)
    merged_self = attended_self.reshape(TLEN, w)
    residual_two = residual + over_pair(rows_nt(merged_self, output_t))
    unit_two, factor_two, normed_two = rms_forward(residual_two, norm_gains[1])
    cross_queries = jnp.dot(
        normed_two, cross_query_full, preferred_element_type=jnp.float32
    ).astype(low)
    cross_queries = cross_queries.reshape(1, TLEN, heads_here, HEAD_DIM)
    key_values = jnp.dot(states[0], kv_weights[:half], preferred_element_type=jnp.float32) + jnp.dot(
        states[1], kv_weights[half:], preferred_element_type=jnp.float32
    )
    key_values = key_values.astype(low).reshape(1, key_rows_n, 2, heads_here, HEAD_DIM)
    key_rows = key_values[:, :, 0]
    value_rows = key_values[:, :, 1]
    head_block = 2
    head_ranges = [
        slice(start_head, start_head + head_block)
        for start_head in range(0, heads_here, head_block)
    ]
    cross_parts = []
    cross_totals = []
    for head_range in head_ranges:
        mixed_part, total_part = attend(
            cross_queries[:, :, head_range],
            key_rows[:, :, head_range],
            value_rows[:, :, head_range],
            allowed,
            None,
        )
        cross_parts.append(mixed_part)
        cross_totals.append(total_part)
    merged_cross = jnp.concatenate(cross_parts, axis=2).reshape(TLEN, w)
    residual_three = residual_two + over_pair(rows_nt(merged_cross, cross_output_t))
    unit_three, factor_three, normed_three = rms_forward(residual_three, norm_gains[2])
    before = jnp.dot(normed_three, expand_full, preferred_element_type=jnp.float32)
    hidden = jax.nn.gelu(before, approximate=True).astype(low)
    block_out = residual_three + over_pair(rows_nt(hidden, reduce_t))
    grad_out = output_cotangent.astype(jnp.float32)
    reduce_grad_t = rows_tn(output_cotangent, hidden)
    hidden_grad = jnp.dot(output_cotangent, reduce_t, preferred_element_type=jnp.float32)
    unused_value, gelu_pullback = jax.vjp(partial(jax.nn.gelu, approximate=True), before)
    before_grad = gelu_pullback(hidden_grad)[0].astype(low)
    expand_grad = rows_tn(normed_three, before_grad)
    normed_grad = over_pair(rows_nt(before_grad, expand_full))
    back_three, gain_three = rms_backward(normed_grad, unit_three, factor_three, norm_gains[2])
    grad_three = grad_out + back_three
    grad_low = grad_three.astype(low)
    cross_output_grad_t = rows_tn(grad_low, merged_cross)
    mixed_grad = jnp.dot(grad_low, cross_output_t, preferred_element_type=jnp.float32).astype(low)
    mixed_grad = mixed_grad.reshape(1, TLEN, heads_here, HEAD_DIM)
    query_parts = []
    key_parts = []
    value_parts = []
    for number, head_range in enumerate(head_ranges):
        query_part, key_part, value_part, unused_scores = attend_back(
            cross_queries[:, :, head_range],
            key_rows[:, :, head_range],
            value_rows[:, :, head_range],
            allowed,
            None,
            cross_totals[number],
            mixed_grad[:, :, head_range],
        )
        query_parts.append(query_part)
        key_parts.append(key_part)
        value_parts.append(value_part)
    cross_query_rows = jnp.concatenate(query_parts, axis=2).astype(low).reshape(TLEN, w)
    kv_grad = jnp.stack(
        [jnp.concatenate(key_parts, axis=2), jnp.concatenate(value_parts, axis=2)], axis=2
    )
    kv_grad = kv_grad.astype(low).reshape(key_rows_n, 2 * w)
    kv_weight_grad = jnp.concatenate([rows_tn(states[0], kv_grad), rows_tn(states[1], kv_grad)])
    passage_parts = jnp.stack(
        [rows_nt(kv_grad, kv_weights[:half]), rows_nt(kv_grad, kv_weights[half:])]
    ).astype(low)
    passage_parts = passage_parts.reshape(2, CHIPS, RANKS * passage_len, half)
    cross_query_grad = rows_tn(normed_two, cross_query_rows)
    normed_grad = over_pair(rows_nt(cross_query_rows, cross_query_full))
    back_two, gain_two = rms_backward(normed_grad, unit_two, factor_two, norm_gains[1])
    grad_two = grad_three + back_two
    grad_low = grad_two.astype(low)
    self_output_grad_t = rows_tn(grad_low, merged_self)
    attended_grad = jnp.dot(grad_low, output_t, preferred_element_type=jnp.float32).astype(low)
    attended_grad = attended_grad.reshape(1, TLEN, heads_here, HEAD_DIM)
    query_grad, key_grad, value_grad, score_grad = attend_back(
        queries_self, keys_self, values_self, causal, bias_full, total_self, attended_grad
    )
    bias_grad = jnp.einsum(
        "hij,bij->bh",
        jnp.sum(score_grad.astype(jnp.float32), axis=0),
        one_hot,
        precision=lax.Precision.HIGHEST,
    )
    projected_grad = jnp.stack([query_grad, key_grad, value_grad], axis=2).astype(low)
    projected_grad = projected_grad.reshape(TLEN, 3 * w)
    self_weight_grad = rows_tn(normed_one, projected_grad)
    normed_grad = over_pair(rows_nt(projected_grad, self_in))
    back_one, gain_one = rms_backward(normed_grad, unit_one, factor_one, norm_gains[0])
    target_grad = (grad_two + back_one).astype(low)

    grads = jnp.stack(
        [
            jnp.concatenate([self_weight_grad, self_output_grad_t], axis=1),
            jnp.concatenate([cross_query_grad, kv_weight_grad, cross_output_grad_t], axis=1),
            expand_grad,
            reduce_grad_t,
        ]
    ).astype(low)
    grads = grads.reshape((4, 4, 2, 2) + shards.shape[1:])
    bias_row = jnp.pad(bias_grad.reshape(-1), (0, norm_gains.shape[1] - bias_grad.size))
    small = jnp.stack([gain_one, gain_two, gain_three, bias_row])
    small = jnp.pad(small, ((0, 4), (0, 0)))
    shard_grads, passage_grad, small_total = scatter_everything(
        position, grads, passage_parts, small, slots_here
    )
    first, second = shard_grads[0], shard_grads[1]
    return (
        block_out.astype(low),
        target_grad,
        passage_grad,
        small_total[:3],
        first[:, :w],
        first[:, w : 2 * w],
        first[:, 2 * w : 3 * w],
        first[:, 3 * w :].T,
        small_total[3, : bias_grad.size].reshape(bias_grad.shape),
        second[:, :w],
        second[:, w : 2 * w],
        second[:, 2 * w : 3 * w],
        second[:, 3 * w :].T,
        shard_grads[2],
        shard_grads[3].T,
    )


def solution(mesh):
    return jax.shard_map(
        body if fits(mesh) else body_any,
        mesh=mesh,
        in_specs=(
            P("pas", None),
            P("pas", None, "mdl"),
            P("pas"),
            P("pas"),
            P(),
            P("pas", "mdl"),
            P("pas", "mdl"),
            P("pas", "mdl"),
            P("mdl", "pas"),
            P(None, "mdl"),
            P("pas", "mdl"),
            P("pas", "mdl"),
            P("pas", "mdl"),
            P("mdl", "pas"),
            P("pas", "mdl"),
            P("mdl", "pas"),
            P("pas", None),
        ),
        out_specs=(
            P("pas", None),
            P("pas", None),
            P("pas", None, "mdl"),
            P(),
            P("pas", "mdl"),
            P("pas", "mdl"),
            P("pas", "mdl"),
            P("mdl", "pas"),
            P(None, "mdl"),
            P("pas", "mdl"),
            P("pas", "mdl"),
            P("pas", "mdl"),
            P("mdl", "pas"),
            P("pas", "mdl"),
            P("mdl", "pas"),
        ),
        check_vma=False,
    )
```

```python
from functools import partial
import math

import jax
import jax.numpy as jnp
import numpy as np
from jax import lax
from jax.experimental import pallas as pl
from jax.experimental.pallas import tpu as pltpu
from jax.sharding import PartitionSpec as P

HEAD_DIM = 64
MAXDIST = 128
TLEN = 256
PQ = 40


EPSILON = 1e-06
MASKED = -1e30


def bucket_table(length, buckets, distance):
    later = np.arange(length)[:, None]
    earlier = np.arange(length)[None, :]
    behind = np.maximum(later - earlier, 0)
    exact = buckets // 2
    spread = np.log(np.maximum(behind, 1) / exact) / math.log(distance / exact) * (buckets - exact)
    far_bucket = np.minimum(exact + np.floor(spread).astype(np.int32), buckets - 1)
    return np.where(behind < exact, behind, far_bucket).astype(np.int32)


def rms_forward(values, gain):
    factor = lax.rsqrt(jnp.mean(values * values, axis=-1, keepdims=True) + EPSILON)
    unit_rows = values * factor
    return (unit_rows, factor, (unit_rows * gain).astype(jnp.bfloat16))


def rms_backward(normed_grad, unit_rows, factor, gain):
    scaled_grad = normed_grad * gain
    input_grad = factor * (
        scaled_grad - unit_rows * jnp.mean(scaled_grad * unit_rows, axis=-1, keepdims=True)
    )
    return (input_grad, jnp.sum(normed_grad * unit_rows, axis=0))


def over_heads(partial_rows):
    return lax.psum(partial_rows, "mdl")


def score_block(queries, key_rows, allowed, bias):
    scores = jnp.einsum("sihe,sjhe->shij", queries, key_rows, preferred_element_type=jnp.float32)
    if bias is not None:
        scores = scores + bias
    return jnp.where(allowed, scores, MASKED)


def attend(queries, key_rows, values, allowed, bias):
    scores = score_block(queries, key_rows, allowed, bias)
    highest = jnp.max(scores, axis=-1, keepdims=True)
    totals = highest + jnp.log(jnp.sum(jnp.exp(scores - highest), axis=-1, keepdims=True))
    probability = jnp.exp(scores - totals)
    mixed = jnp.einsum(
        "shij,sjhe->sihe",
        probability.astype(jnp.bfloat16),
        values,
        preferred_element_type=jnp.float32,
    )
    return (mixed.astype(jnp.bfloat16), totals)


def attend_back(queries, key_rows, values, allowed, bias, totals, out_grad):
    scores = score_block(queries, key_rows, allowed, bias)
    probability = jnp.exp(scores - totals)
    prob_grad = jnp.einsum("sihe,sjhe->shij", out_grad, values, preferred_element_type=jnp.float32)
    centered = jnp.sum(probability * prob_grad, axis=-1, keepdims=True)
    score_grad = (probability * (prob_grad - centered)).astype(jnp.bfloat16)
    query_grad = jnp.einsum(
        "shij,sjhe->sihe", score_grad, key_rows, preferred_element_type=jnp.float32
    )
    key_grad = jnp.einsum(
        "shij,sihe->sjhe", score_grad, queries, preferred_element_type=jnp.float32
    )
    value_grad = jnp.einsum(
        "shij,sihe->sjhe",
        probability.astype(jnp.bfloat16),
        out_grad,
        preferred_element_type=jnp.float32,
    )
    return (query_grad, key_grad, value_grad, score_grad)


def send_plan(slot_query, slot_live, per_device, capacity):
    target_device = slot_query // per_device
    matching = target_device[:, None] == target_device[None, :]
    lower_part = jnp.tril(jnp.ones(matching.shape, jnp.bool_), -1)
    ranking = jnp.sum(jnp.logical_and(matching, lower_part), axis=1)
    position = target_device * capacity + ranking
    codes = jnp.where(slot_live > 0, slot_query % per_device + 1, 0).astype(jnp.bfloat16)
    return (position, codes)


def arrange_plan(got_codes, per_device, slots_each):
    local_query = got_codes.astype(jnp.int32) - 1
    matches = (local_query[:, None] == jnp.arange(per_device, dtype=jnp.int32)[None, :]).astype(
        jnp.int32
    )
    ranking = jnp.sum((jnp.cumsum(matches, axis=0) - 1) * matches, axis=1)
    spare_place = per_device * slots_each
    places = jnp.where(local_query >= 0, local_query * slots_each + ranking, spare_place)
    arrivals = got_codes.shape[0]
    gather_index = (
        jnp.zeros((spare_place + 1,), jnp.int32)
        .at[places]
        .set(jnp.arange(arrivals, dtype=jnp.int32))
    )
    valid_slot = jnp.zeros((spare_place + 1,), jnp.int32).at[places].set(1)
    return (gather_index[:spare_place], valid_slot[:spare_place] > 0)


def place_rows(rows, position, total_rows):
    return jnp.zeros((total_rows,) + rows.shape[1:], rows.dtype).at[position].set(rows)


def return_rows(rows, gather_index, total_rows):
    return jnp.zeros((total_rows,) + rows.shape[1:], rows.dtype).at[gather_index].add(rows)


def body_any(
    target_states,
    passage_states,
    slot_query,
    slot_live,
    norm_gains,
    self_query,
    self_key,
    self_value,
    self_output,
    position_bias,
    cross_query,
    cross_key,
    cross_value,
    cross_output,
    expand_weight,
    reduce_weight,
    output_cotangent,
):
    (
        query_full,
        key_full,
        value_full,
        cross_query_full,
        cross_key_full,
        cross_value_full,
        expand_full,
    ) = (
        lax.all_gather(self_query, "pas", axis=0, tiled=True),
        lax.all_gather(self_key, "pas", axis=0, tiled=True),
        lax.all_gather(self_value, "pas", axis=0, tiled=True),
        lax.all_gather(cross_query, "pas", axis=0, tiled=True),
        lax.all_gather(cross_key, "pas", axis=0, tiled=True),
        lax.all_gather(cross_value, "pas", axis=0, tiled=True),
        lax.all_gather(expand_weight, "pas", axis=0, tiled=True),
    )
    output_full, cross_output_full, reduce_full = (
        lax.all_gather(self_output, "pas", axis=1, tiled=True),
        lax.all_gather(cross_output, "pas", axis=1, tiled=True),
        lax.all_gather(reduce_weight, "pas", axis=1, tiled=True),
    )
    width_here = query_full.shape[1]
    heads_here = width_here // HEAD_DIM
    sequences = target_states.shape[0] // TLEN
    passage_len = passage_states.shape[1]
    bucket_count = position_bias.shape[0]
    devices = lax.axis_size("pas")
    slots_here = slot_query.shape[0]
    capacity = -(-slots_here // devices)
    buffer_rows = devices * capacity
    residual = target_states.astype(jnp.float32)
    unit_one, factor_one, normed_one = rms_forward(residual, norm_gains[0])
    self_weights = jnp.concatenate([query_full, key_full, value_full], axis=1)
    projected = jnp.dot(normed_one, self_weights, preferred_element_type=jnp.float32).astype(
        jnp.bfloat16
    )
    projected = projected.reshape(sequences, TLEN, 3, heads_here, HEAD_DIM)
    queries_self = projected[:, :, 0]
    keys_self = projected[:, :, 1]
    values_self = projected[:, :, 2]
    buckets = jnp.asarray(bucket_table(TLEN, bucket_count, MAXDIST))
    one_hot = (jnp.arange(bucket_count, dtype=jnp.int32)[:, None, None] == buckets[None]).astype(
        jnp.float32
    )
    bias_full = jnp.einsum("bij,bh->hij", one_hot, position_bias, precision=lax.Precision.HIGHEST)[
        None
    ]
    causal = jnp.asarray(np.tril(np.ones((TLEN, TLEN), dtype=bool)))
    attended_self, total_self = attend(queries_self, keys_self, values_self, causal, bias_full)
    merged_self = attended_self.reshape(sequences * TLEN, width_here)
    residual_two = residual + over_heads(
        jnp.dot(merged_self, output_full, preferred_element_type=jnp.float32)
    )
    unit_two, factor_two, normed_two = rms_forward(residual_two, norm_gains[1])
    cross_queries = jnp.dot(
        normed_two, cross_query_full, preferred_element_type=jnp.float32
    ).astype(jnp.bfloat16)
    cross_queries = cross_queries.reshape(sequences, TLEN, heads_here, HEAD_DIM)
    kv_weights = jnp.concatenate([cross_key_full, cross_value_full], axis=1)
    position, codes = send_plan(slot_query, slot_live, sequences, capacity)
    sent_codes = place_rows(codes, position, buffer_rows)
    states_full = lax.all_gather(passage_states, "mdl", axis=2, tiled=True)
    key_values = jnp.einsum(
        "tpd,dc->tpc", states_full, kv_weights, preferred_element_type=jnp.float32
    ).astype(jnp.bfloat16)
    received, got_codes = (
        lax.all_to_all(
            place_rows(key_values, position, buffer_rows),
            "pas",
            split_axis=0,
            concat_axis=0,
            tiled=True,
        ),
        lax.all_to_all(sent_codes, "pas", split_axis=0, concat_axis=0, tiled=True),
    )
    gather_index, valid_slot = arrange_plan(got_codes, sequences, PQ)
    arranged = jnp.take(received, gather_index, axis=0)
    arranged = arranged.reshape(sequences, PQ * passage_len, 2, heads_here, HEAD_DIM)
    key_rows = arranged[:, :, 0]
    value_rows = arranged[:, :, 1]
    allowed = jnp.repeat(valid_slot.reshape(sequences, PQ), passage_len, axis=1)[:, None, None, :]
    head_block = 2
    head_ranges = [
        slice(start_head, start_head + head_block)
        for start_head in range(0, heads_here, head_block)
    ]
    cross_parts = []
    cross_totals = []
    for head_range in head_ranges:
        mixed_part, total_part = attend(
            cross_queries[:, :, head_range],
            key_rows[:, :, head_range],
            value_rows[:, :, head_range],
            allowed,
            None,
        )
        cross_parts.append(mixed_part)
        cross_totals.append(total_part)
    merged_cross = jnp.concatenate(cross_parts, axis=2).reshape(sequences * TLEN, width_here)
    residual_three = residual_two + over_heads(
        jnp.dot(merged_cross, cross_output_full, preferred_element_type=jnp.float32)
    )
    unit_three, factor_three, normed_three = rms_forward(residual_three, norm_gains[2])
    before = jnp.dot(normed_three, expand_full, preferred_element_type=jnp.float32)
    hidden = jax.nn.gelu(before, approximate=True).astype(jnp.bfloat16)
    block_out = residual_three + over_heads(
        jnp.dot(hidden, reduce_full, preferred_element_type=jnp.float32)
    )
    grad_out = output_cotangent.astype(jnp.float32)
    reduce_grad = jnp.dot(hidden.T, output_cotangent, preferred_element_type=jnp.float32)
    hidden_grad = jnp.dot(output_cotangent, reduce_full.T, preferred_element_type=jnp.float32)
    unused_value, gelu_pullback = jax.vjp(partial(jax.nn.gelu, approximate=True), before)
    before_grad = gelu_pullback(hidden_grad)[0].astype(jnp.bfloat16)
    expand_grad = jnp.dot(normed_three.T, before_grad, preferred_element_type=jnp.float32)
    normed_grad = over_heads(
        jnp.dot(before_grad, expand_full.T, preferred_element_type=jnp.float32)
    )
    back_three, gain_three = rms_backward(normed_grad, unit_three, factor_three, norm_gains[2])
    grad_three = grad_out + back_three
    grad_low = grad_three.astype(jnp.bfloat16)
    cross_output_grad = jnp.dot(merged_cross.T, grad_low, preferred_element_type=jnp.float32)
    mixed_grad = jnp.dot(grad_low, cross_output_full.T, preferred_element_type=jnp.float32).astype(
        jnp.bfloat16
    )
    mixed_grad = mixed_grad.reshape(sequences, TLEN, heads_here, HEAD_DIM)
    query_parts = []
    key_parts = []
    value_parts = []
    for number, head_range in enumerate(head_ranges):
        query_part, key_part, value_part, unused_scores = attend_back(
            cross_queries[:, :, head_range],
            key_rows[:, :, head_range],
            value_rows[:, :, head_range],
            allowed,
            None,
            cross_totals[number],
            mixed_grad[:, :, head_range],
        )
        query_parts.append(query_part)
        key_parts.append(key_part)
        value_parts.append(value_part)
    cross_query_rows = (
        jnp.concatenate(query_parts, axis=2)
        .astype(jnp.bfloat16)
        .reshape(sequences * TLEN, width_here)
    )
    kv_grad = jnp.stack(
        [jnp.concatenate(key_parts, axis=2), jnp.concatenate(value_parts, axis=2)], axis=2
    )
    kv_grad = kv_grad.astype(jnp.bfloat16).reshape(sequences * PQ, passage_len, 2 * width_here)
    returned = lax.all_to_all(
        return_rows(kv_grad, gather_index, buffer_rows),
        "pas",
        split_axis=0,
        concat_axis=0,
        tiled=True,
    )
    kv_grad_here = jnp.take(returned, position, axis=0)
    kv_weight_grad = jnp.einsum(
        "tpd,tpc->dc", states_full, kv_grad_here, preferred_element_type=jnp.float32
    )
    states_grad = jnp.einsum(
        "tpc,dc->tpd", kv_grad_here, kv_weights, preferred_element_type=jnp.float32
    )
    passage_grad = lax.psum_scatter(
        states_grad.astype(jnp.bfloat16), "mdl", scatter_dimension=2, tiled=True
    )
    cross_query_grad = jnp.dot(normed_two.T, cross_query_rows, preferred_element_type=jnp.float32)
    normed_grad = over_heads(
        jnp.dot(cross_query_rows, cross_query_full.T, preferred_element_type=jnp.float32)
    )
    back_two, gain_two = rms_backward(normed_grad, unit_two, factor_two, norm_gains[1])
    grad_two = grad_three + back_two
    grad_low = grad_two.astype(jnp.bfloat16)
    self_output_grad = jnp.dot(merged_self.T, grad_low, preferred_element_type=jnp.float32)
    attended_grad = jnp.dot(grad_low, output_full.T, preferred_element_type=jnp.float32).astype(
        jnp.bfloat16
    )
    attended_grad = attended_grad.reshape(sequences, TLEN, heads_here, HEAD_DIM)
    query_grad, key_grad, value_grad, score_grad = attend_back(
        queries_self, keys_self, values_self, causal, bias_full, total_self, attended_grad
    )
    bias_grad = jnp.einsum(
        "hij,bij->bh",
        jnp.sum(score_grad.astype(jnp.float32), axis=0),
        one_hot,
        precision=lax.Precision.HIGHEST,
    )
    projected_grad = jnp.stack([query_grad, key_grad, value_grad], axis=2).astype(jnp.bfloat16)
    projected_grad = projected_grad.reshape(sequences * TLEN, 3 * width_here)
    self_weight_grad = jnp.dot(normed_one.T, projected_grad, preferred_element_type=jnp.float32)
    normed_grad = over_heads(
        jnp.dot(projected_grad, self_weights.T, preferred_element_type=jnp.float32)
    )
    back_one, gain_one = rms_backward(normed_grad, unit_one, factor_one, norm_gains[0])
    target_grad = (grad_two + back_one).astype(jnp.bfloat16)
    row_grads = (
        lax.psum_scatter(self_weight_grad[:, :width_here], "pas", scatter_dimension=0, tiled=True),
        lax.psum_scatter(
            self_weight_grad[:, width_here : 2 * width_here], "pas", scatter_dimension=0, tiled=True
        ),
        lax.psum_scatter(
            self_weight_grad[:, 2 * width_here :], "pas", scatter_dimension=0, tiled=True
        ),
        lax.psum_scatter(cross_query_grad, "pas", scatter_dimension=0, tiled=True),
        lax.psum_scatter(kv_weight_grad[:, :width_here], "pas", scatter_dimension=0, tiled=True),
        lax.psum_scatter(kv_weight_grad[:, width_here:], "pas", scatter_dimension=0, tiled=True),
        lax.psum_scatter(expand_grad, "pas", scatter_dimension=0, tiled=True),
    )
    col_grads = (
        lax.psum_scatter(self_output_grad, "pas", scatter_dimension=1, tiled=True),
        lax.psum_scatter(cross_output_grad, "pas", scatter_dimension=1, tiled=True),
        lax.psum_scatter(reduce_grad, "pas", scatter_dimension=1, tiled=True),
    )
    gains_total, bias_total = lax.psum(
        (jnp.stack([gain_one, gain_two, gain_three]), bias_grad), "pas"
    )
    return (
        block_out.astype(jnp.bfloat16),
        target_grad,
        passage_grad,
        gains_total,
        row_grads[0],
        row_grads[1],
        row_grads[2],
        col_grads[0],
        bias_total,
        row_grads[3],
        row_grads[4],
        row_grads[5],
        col_grads[1],
        row_grads[6],
        col_grads[2],
    )


CHIPS = 16
RANKS = 3
FLAG_ROWS = 16
MESH_ID = pl.DeviceIdType.MESH
VMEM_LIMIT = 56 * 2**20


def fits(mesh):
    return mesh.shape["pas"] == CHIPS and mesh.shape["mdl"] == 2


def places():
    me, core = lax.axis_index("pas"), lax.axis_index("mdl")
    x, y, z = me % 2, (me // 2) % 2, me // 4
    across_x, across_y = me + 1 - 2 * x, me + 2 - 4 * y
    near = across_y + (across_x - across_y) * core
    far = across_x + (across_y - across_x) * core
    return me, core, x, y, z, near, far


def remote(src, dst, send_sem, recv_sem, device):
    return pltpu.make_async_remote_copy(
        src_ref=src,
        dst_ref=dst,
        send_sem=send_sem,
        recv_sem=recv_sem,
        device_id=device,
        device_id_type=MESH_ID,
    )


def greet_all(me, core):
    barrier = pltpu.get_barrier_semaphore()
    for k in range(1, CHIPS):
        pl.semaphore_signal(
            barrier, inc=1, device_id=((me + k) % CHIPS, core), device_id_type=MESH_ID
        )
    pl.semaphore_signal(barrier, inc=1, device_id=(me, 1 - core), device_id_type=MESH_ID)
    pl.semaphore_wait(barrier, CHIPS)


def gather_kernel(
    index_ref,
    shard_ref,
    passage_ref,
    flag_ref,
    full_ref,
    states_ref,
    outgoing,
    own_sem,
    z_send,
    z_recv,
    near_send,
    near_recv,
    far_send,
    far_recv,
    slot_send,
    slot_recv,
    core_send,
    core_recv,
    slot_own,
):
    me, core, x, y, z, near, far = places()
    groups = shard_ref.shape[0]
    greet_all(me, core)

    def z_copy(g, k):
        return remote(
            shard_ref.at[g],
            full_ref.at[g, z, y, x],
            z_send.at[g, k - 1],
            z_recv.at[g, k - 1],
            ((me + 4 * k) % CHIPS, core),
        )

    def near_copy(g):
        block = full_ref.at[g, :, y, x]
        return remote(block, block, near_send.at[g], near_recv.at[g], (near, core))

    def far_copy(g, across_x):
        block = full_ref.at[g, :, :, x] if across_x else full_ref.at[g, :, y, :]
        return remote(block, block, far_send.at[g], far_recv.at[g], (far, core))

    def own_copy(g):
        return pltpu.make_async_copy(shard_ref.at[g], full_ref.at[g, z, y, x], own_sem.at[g])

    def slot_copy(k):
        to = (me + k) % CHIPS
        return remote(
            outgoing.at[to],
            states_ref.at[core, me],
            slot_send.at[k - 1],
            slot_recv.at[k - 1],
            (to, core),
        )

    def core_copy(k):
        block = states_ref.at[core, (me + CHIPS - k) % CHIPS]
        return remote(block, block, core_send.at[k], core_recv.at[k], (me, 1 - core))

    for g in range(groups):
        own_copy(g).start()
        for k in range(1, 4):
            z_copy(g, k).start()

    def fill(to, carry):
        for rank in range(RANKS):
            rows = passage_ref.shape[1]
            outgoing[to, rank * rows : (rank + 1) * rows, :] = passage_ref[
                index_ref[to * RANKS + rank]
            ]
        outgoing[to, RANKS * passage_ref.shape[1] :, :] = flag_ref[to]
        return carry

    lax.fori_loop(0, CHIPS, fill, 0)
    for k in range(1, CHIPS):
        slot_copy(k).start()
    mine = pltpu.make_async_copy(outgoing.at[me], states_ref.at[core, me], slot_own)
    mine.start()

    def second(g):
        own_copy(g).wait()
        for k in range(1, 4):
            z_copy(g, k).wait_recv()
        near_copy(g).start()

    def third(g):
        near_copy(g).wait_recv()

        @pl.when(core == 0)
        def _():
            far_copy(g, True).start()

        @pl.when(core == 1)
        def _():
            far_copy(g, False).start()

    second(0)
    second(1)
    third(0)
    second(2)
    third(1)
    second(3)
    third(2)
    third(3)
    mine.wait()
    core_copy(0).start()
    for k in range(1, CHIPS):
        slot_copy(k).wait_recv()
        core_copy(k).start()
    for g in range(groups):
        far_copy(g, True).wait_recv()
    for k in range(CHIPS):
        core_copy(k).wait()
    for k in range(1, CHIPS):
        slot_copy(k).wait_send()
    for g in range(groups):
        for k in range(1, 4):
            z_copy(g, k).wait_send()
        near_copy(g).wait_send()
        far_copy(g, True).wait_send()


ANY = pl.BlockSpec(memory_space=pl.ANY)
IN_VMEM = pl.BlockSpec(memory_space=pltpu.VMEM)
IN_SMEM = pl.BlockSpec(memory_space=pltpu.SMEM)
DMA = pltpu.SemaphoreType.DMA


def gather_everything(index, shards, passages, flags):
    groups, rows, columns = shards.shape
    passage_len, half = passages.shape[1:]
    block_rows = RANKS * passage_len + FLAG_ROWS
    return pl.pallas_call(
        gather_kernel,
        out_shape=(
            jax.ShapeDtypeStruct((groups, 4, 2, 2, rows, columns), jnp.bfloat16),
            jax.ShapeDtypeStruct((2, CHIPS, block_rows, half), jnp.bfloat16),
        ),
        in_specs=[IN_SMEM, ANY, IN_VMEM, IN_VMEM],
        out_specs=(ANY, ANY),
        scratch_shapes=[
            pltpu.VMEM((CHIPS, block_rows, half), jnp.bfloat16),
            DMA((groups,)),
            DMA((groups, 3)),
            DMA((groups, 3)),
            DMA((groups,)),
            DMA((groups,)),
            DMA((groups,)),
            DMA((groups,)),
            DMA((CHIPS - 1,)),
            DMA((CHIPS - 1,)),
            DMA((CHIPS,)),
            DMA((CHIPS,)),
            DMA,
        ],
        compiler_params=pltpu.CompilerParams(
            collective_id=0, has_side_effects=True, vmem_limit_bytes=VMEM_LIMIT
        ),
    )(index, shards, passages, flags)


def pair_kernel(mine_ref, sum_ref, other, send_sem, recv_sem):
    partner = (lax.axis_index("pas"), 1 - lax.axis_index("mdl"))
    barrier = pltpu.get_barrier_semaphore()
    pl.semaphore_signal(barrier, inc=1, device_id=partner, device_id_type=MESH_ID)
    pl.semaphore_wait(barrier, 1)
    copy = remote(mine_ref, other, send_sem, recv_sem, partner)
    copy.start()
    copy.wait()
    sum_ref[...] = mine_ref[...] + other[...]


def over_pair(partial_rows):
    return pl.pallas_call(
        pair_kernel,
        out_shape=jax.ShapeDtypeStruct(partial_rows.shape, partial_rows.dtype),
        in_specs=[IN_VMEM],
        out_specs=IN_VMEM,
        scratch_shapes=[pltpu.VMEM(partial_rows.shape, partial_rows.dtype), DMA, DMA],
        compiler_params=pltpu.CompilerParams(
            collective_id=1, has_side_effects=True, vmem_limit_bytes=VMEM_LIMIT
        ),
    )(partial_rows)


def rows_nt(left, right):
    return lax.dot_general(
        left, right, (((1,), (1,)), ((), ())), preferred_element_type=jnp.float32
    )


def rows_tn(left, right):
    return lax.dot_general(
        left, right, (((0,), (0,)), ((), ())), preferred_element_type=jnp.float32
    )


TILE = 2


def mm(left, right):
    return jnp.dot(left, right, preferred_element_type=jnp.float32)


def halves_of_pair(rows, head):
    lane = lax.broadcasted_iota(jnp.int32, (rows.shape[0], 2 * HEAD_DIM), 1)
    at = head // 2 * 2 * HEAD_DIM
    return jnp.where(lane // HEAD_DIM == head % 2, rows[:, at : at + 2 * HEAD_DIM], 0.0).astype(
        jnp.bfloat16
    )


def halves_of_rows(rows, head):
    row = lax.broadcasted_iota(jnp.int32, (2 * HEAD_DIM, rows.shape[1]), 0)
    at = head // 2 * 2 * HEAD_DIM
    return jnp.where(row // HEAD_DIM == head % 2, rows[at : at + 2 * HEAD_DIM], 0.0).astype(
        jnp.bfloat16
    )


def unit_of(values):
    factor = lax.rsqrt(jnp.mean(values * values, axis=-1, keepdims=True) + EPSILON)
    return values * factor, factor


def prepare_heads(heads, query_ref, grad, mixed, q_pair, o_pair, o_rows, centre):
    grad = grad.astype(jnp.float32)
    grad_t = grad.T
    product = (grad * mixed.astype(jnp.float32)).T
    queries = query_ref[...].astype(jnp.float32)
    for h in range(heads):
        q_pair[h] = halves_of_pair(queries, h)
        o_pair[h] = halves_of_pair(grad, h)
        o_rows[h] = halves_of_rows(grad_t, h)
        centre[h : h + 1, :] = jnp.sum(
            product[h * HEAD_DIM : (h + 1) * HEAD_DIM], axis=0, keepdims=True
        )


def head_pair_back(p, keys, values, prob, q_pair, o_pair, o_rows, centre, keep_scores):
    low = jnp.bfloat16
    keys_t = keys.T
    query_parts = []
    for a in range(2):
        h = 2 * p + a
        prob_grad = mm(values, o_rows[h])
        weights = prob(h)
        score_grad = (weights * (prob_grad - centre[h : h + 1, :])).astype(low)
        if keep_scores is not None:
            keep_scores(h, score_grad)
        key_part = mm(score_grad, q_pair[h])
        value_part = mm(weights.astype(low), o_pair[h])
        key_grad = key_part if a == 0 else key_grad + key_part
        value_grad = value_part if a == 0 else value_grad + value_part
        query_parts.append(mm(keys_t[a * HEAD_DIM : (a + 1) * HEAD_DIM], score_grad))
    return key_grad.astype(low), value_grad.astype(low), query_parts


def backward_kernel(
    position_ref,
    exps_ref,
    scale_ref,
    kv_ref,
    states_ref,
    query_ref,
    mixed_ref,
    self_w_ref,
    cross_w_ref,
    ff_ref,
    grad_ref,
    residual_ref,
    target_ref,
    gains_ref,
    qkv_ref,
    self_mixed_ref,
    self_exps_ref,
    self_scale_ref,
    bucket_ref,
    gain_ref,
    shard_ref,
    slots_ref,
    small_ref,
    target_grad_ref,
    exps,
    keys,
    grads,
    far_got,
    near_got,
    z_got,
    dkv,
    outgoing,
    kept_sum,
    pair_got,
    slot_got,
    small,
    small_got,
    q_pair,
    o_pair,
    o_rows,
    centre,
    dq_t,
    row_sent,
    row_got,
    upper_grad,
    self_scores,
    exps_sem,
    keys_sem,
    far_send,
    far_recv,
    near_send,
    near_recv,
    z_send,
    z_recv,
    pair_send,
    pair_recv,
    slot_send,
    slot_recv,
    small_send,
    small_recv,
    row_send,
    row_recv,
):
    low, wide = jnp.bfloat16, jnp.float32
    me, core, x, y, z, near, far = places()
    groups = shard_ref.shape[0]
    across_x, across_y = me + 1 - 2 * x, me + 2 - 4 * y
    kept = (1 - core) * y + core * x
    partner = (me, 1 - core)
    width = query_ref.shape[1]
    pairs = width // (2 * HEAD_DIM)
    heads = 2 * pairs
    block_rows = states_ref.shape[1] // CHIPS
    tile_rows = TILE * block_rows
    tiles = CHIPS // TILE
    half = states_ref.shape[2]

    def tile_at(t):
        return (t + me // TILE) % tiles

    def exps_copy(t):
        rows = pl.ds(tile_at(t) * tile_rows, tile_rows)
        return pltpu.make_async_copy(exps_ref.at[:, rows], exps.at[t % 2], exps_sem.at[t % 2])

    def keys_copy(t):
        rows = pl.ds(tile_at(t) * tile_rows, tile_rows)
        return pltpu.make_async_copy(kv_ref.at[rows], keys.at[t % 2], keys_sem.at[t % 2])

    exps_copy(0).start()
    keys_copy(0).start()
    greet_all(me, core)

    def source(g):
        return ff_ref.at[g - 2] if g >= 2 else grads.at[g]

    def far_copy(g, over_x):
        block = source(g).at[:, :, 1 - x] if over_x else source(g).at[:, 1 - y, :]
        return remote(block, far_got.at[g], far_send.at[g], far_recv.at[g], (far, core))

    def far_start(g):
        @pl.when(core == 0)
        def _():
            far_copy(g, True).start()

        @pl.when(core == 1)
        def _():
            far_copy(g, False).start()

    def near_copy(g):
        return remote(
            far_got.at[g, :, 1 - kept], near_got.at[g], near_send.at[g], near_recv.at[g], (near, core)
        )

    def z_copy(g, k):
        return remote(
            near_got.at[g, (z + k) % 4],
            z_got.at[g, k - 1],
            z_send.at[g, k - 1],
            z_recv.at[g, k - 1],
            ((me + 4 * k) % CHIPS, core),
        )

    def far_add(g):
        far_copy(g, True).wait_recv()

        def step(i, carry):
            zi, o = i // 2, i % 2
            mine = source(g)[zi, (1 - core) * o + core * y, (1 - core) * x + core * o]
            far_got[g, zi, o] = (mine.astype(wide) + far_got[g, zi, o].astype(wide)).astype(low)
            return carry

        lax.fori_loop(0, 8, step, 0)
        near_copy(g).start()

    def near_add(g):
        near_copy(g).wait_recv()

        def step(zi, carry):
            near_got[g, zi] = (
                far_got[g, zi, kept].astype(wide) + near_got[g, zi].astype(wide)
            ).astype(low)
            return carry

        lax.fori_loop(0, 4, step, 0)
        for k in range(1, 4):
            z_copy(g, k).start()

    def z_add(g):
        for k in range(1, 4):
            z_copy(g, k).wait_recv()
        total = near_got[g, z].astype(wide)
        for k in range(3):
            total = total + z_got[g, k].astype(wide)
        shard_ref[g] = total

    def pair_copy(t):
        return remote(
            outgoing.at[t % 2],
            pair_got.at[tile_at(t)],
            pair_send.at[t % 2],
            pair_recv.at[t],
            partner,
        )

    def slot_copy(to):
        return remote(
            kept_sum.at[to], slot_got.at[me], slot_send.at[to], slot_recv.at[me], (to, core)
        )

    def slot_arrival(k):
        came = (me + k) % CHIPS
        return remote(
            kept_sum.at[came], slot_got.at[came], slot_send.at[came], slot_recv.at[came], (came, core)
        )

    def finish_tile(t):
        tile = tile_at(t)
        pair_copy(t).wait_recv()
        for j in range(TILE):
            to = tile * TILE + j
            rows = slice(j * block_rows, (j + 1) * block_rows)
            kept_sum[to] = (
                kept_sum[to].astype(wide) + pair_got[tile, rows].astype(wide)
            ).astype(low)

            @pl.when(to != me)
            def _():
                slot_copy(to).start()

            @pl.when(to == me)
            def _():
                slot_got[me] = kept_sum[me]

    def row_copy(i):
        return remote(row_sent.at[i], row_got.at[i], row_send.at[i], row_recv.at[i], partner)

    def store_grad(g, first, value):
        blocks = value.astype(low).reshape(grads.shape[1:5] + (value.shape[1],))
        grads[g, :, :, :, :, first : first + value.shape[1]] = blocks

    far_start(2)
    far_start(3)

    upper_grad[...] = grad_ref[...]
    grad_low = upper_grad[...].astype(low)
    store_grad(1, 3 * width, rows_tn(grad_low, mixed_ref[...]))
    mixed_grad = mm(grad_low, cross_w_ref[:, 3 * width :]).astype(low)
    prepare_heads(heads, query_ref, mixed_grad, mixed_ref[...], q_pair, o_pair, o_rows, centre)
    dq_t[...] = jnp.zeros_like(dq_t)

    def tile_step(t, carry):
        tile = tile_at(t)
        rows = pl.ds(pl.multiple_of(tile * tile_rows, tile_rows), tile_rows)

        @pl.when(t + 1 < tiles)
        def _():
            exps_copy(t + 1).start()
            keys_copy(t + 1).start()

        exps_copy(t).wait()
        keys_copy(t).wait()

        def prob(h):
            return exps[t % 2, h].astype(wide) * scale_ref[tile, h : h + 1, :]

        for p in range(pairs):
            at = 2 * HEAD_DIM * p
            key_grad, value_grad, query_parts = head_pair_back(
                p,
                keys[t % 2, :, at : at + 2 * HEAD_DIM],
                keys[t % 2, :, width + at : width + at + 2 * HEAD_DIM],
                prob,
                q_pair,
                o_pair,
                o_rows,
                centre,
                None,
            )
            dkv[rows, at : at + 2 * HEAD_DIM] = key_grad
            dkv[rows, width + at : width + at + 2 * HEAD_DIM] = value_grad
            for a in range(2):
                first = at + a * HEAD_DIM
                dq_t[first : first + HEAD_DIM, :] += query_parts[a]
        here = dkv[rows, :]

        @pl.when(t >= 2)
        def _():
            pair_copy(t - 2).wait_send()

        weights = cross_w_ref[pl.ds((1 - core) * half, half), width : 3 * width]
        outgoing[t % 2] = rows_nt(here, weights).astype(low)
        pair_copy(t).start()
        weights = cross_w_ref[pl.ds(core * half, half), width : 3 * width]
        mine = rows_nt(here, weights).astype(low)
        for j in range(TILE):
            kept_sum[tile * TILE + j] = mine[j * block_rows : (j + 1) * block_rows]

        @pl.when(t >= 1)
        def _():
            finish_tile(t - 1)

        @pl.when(t == 5)
        def _():
            far_add(2)

        return carry

    lax.fori_loop(0, tiles, tile_step, 0)
    dq = dq_t[...].T.astype(low)
    row_sent[0] = rows_nt(dq, cross_w_ref[:, :width])
    row_copy(0).start()
    finish_tile(tiles - 1)
    far_add(3)
    unit_two, factor_two = unit_of(residual_ref[...])
    normed_two = (unit_two * gains_ref[1:2, :]).astype(low)
    store_grad(1, 0, rows_tn(normed_two, dq))

    for n in range(2 * width // 256):
        columns = slice(n * 256, (n + 1) * 256)
        parts = [rows_tn(states_ref[i], dkv[:, columns]) for i in range(2)]
        store_grad(1, width + n * 256, jnp.concatenate(parts))
    far_start(1)
    near_add(2)

    row_copy(0).wait_recv()
    normed_grad = row_sent[0] + row_got[0]
    back, gain_two = rms_backward(normed_grad, unit_two, factor_two, gains_ref[1:2, :])
    upper_grad[...] += back

    grad_low = upper_grad[...].astype(low)
    store_grad(0, 3 * width, rows_tn(grad_low, self_mixed_ref[...]))
    mixed_grad = mm(grad_low, self_w_ref[:, 3 * width :]).astype(low)
    prepare_heads(
        heads,
        qkv_ref.at[:, :width],
        mixed_grad,
        self_mixed_ref[...],
        q_pair,
        o_pair,
        o_rows,
        centre,
    )

    def self_prob(h):
        return self_exps_ref[h].astype(wide) * self_scale_ref[h : h + 1, :]

    def keep_scores(h, score_grad):
        self_scores[h] = score_grad

    query_rows, key_columns, value_columns = [], [], []
    for p in range(pairs):
        at = 2 * HEAD_DIM * p
        key_grad, value_grad, query_parts = head_pair_back(
            p,
            qkv_ref[:, width + at : width + at + 2 * HEAD_DIM],
            qkv_ref[:, 2 * width + at : 2 * width + at + 2 * HEAD_DIM],
            self_prob,
            q_pair,
            o_pair,
            o_rows,
            centre,
            keep_scores,
        )
        key_columns.append(key_grad)
        value_columns.append(value_grad)
        query_rows.extend(query_parts)
    dq = jnp.concatenate(query_rows, axis=0).T.astype(low)
    dqkv = jnp.concatenate([dq] + key_columns + value_columns, axis=1)
    row_sent[1] = rows_nt(dqkv, self_w_ref[:, : 3 * width])
    row_copy(1).start()
    unit_one, factor_one = unit_of(target_ref[...].astype(wide))
    normed_one = (unit_one * gains_ref[0:1, :]).astype(low)
    store_grad(0, 0, rows_tn(normed_one, dqkv))
    far_start(0)
    near_add(3)

    length = self_scores.shape[1]

    def diagonal_step(i, total):
        rows = self_scores[:, pl.ds(pl.multiple_of(16 * i, 16), 16), :].astype(wide)
        rows = rows.reshape(heads * 16, length)
        return total + pltpu.roll(rows, (length - 16 * i) % length, 1)

    total = lax.fori_loop(
        0, length // 16, diagonal_step, jnp.zeros((heads * 16, length), wide)
    ).reshape(heads, 16, length)
    small[...] = jnp.zeros_like(small)
    for h in range(heads):
        line = total[h, 0:1]
        for s in range(1, 16):
            line = line + pltpu.roll(total[h, s : s + 1], length - s, 1)
        small[8 + h : 9 + h, :length] = line
    by_bucket = jnp.dot(
        small[8:16, :length], bucket_ref[...], precision=lax.Precision.HIGHEST,
        preferred_element_type=wide,
    )
    small[8:16, :length] = jnp.zeros((8, length), wide)
    small[8:16, : bucket_ref.shape[1]] = by_bucket

    row_copy(1).wait_recv()
    normed_grad = row_sent[1] + row_got[1]
    back, gain_one = rms_backward(normed_grad, unit_one, factor_one, gains_ref[0:1, :])
    target_grad_ref[...] = (upper_grad[...] + back).astype(low)
    small[0:1, :] = gain_one[None, :]
    small[1:2, :] = gain_two[None, :]
    small[2:3, :] = gain_ref[...]

    def small_copy(step):
        if step == 0:
            return remote(small, small_got.at[0], small_send.at[0], small_recv.at[0], (across_x, core))
        if step == 1:
            return remote(
                small_got.at[6], small_got.at[1], small_send.at[1], small_recv.at[1], (across_y, core)
            )
        return remote(
            small_got.at[7],
            small_got.at[2 + z],
            small_send.at[step],
            small_recv.at[step],
            ((me + 4 * (step - 1)) % CHIPS, core),
        )

    small_copy(0).start()
    far_add(1)
    small_copy(0).wait_recv()
    small_got[6] = small[...] + small_got[0]
    small_copy(1).start()
    z_add(2)
    near_add(1)
    small_copy(1).wait_recv()
    small_got[7] = small_got[6] + small_got[1]
    for step in range(2, 5):
        small_copy(step).start()
    small_got[2 + z] = small_got[7]
    far_add(0)
    z_add(3)
    z_add(1)
    near_add(0)
    for step in range(2, 5):
        small_copy(step).wait_recv()
    small_ref[...] = small_got[2] + small_got[3] + small_got[4] + small_got[5]
    for k in range(1, CHIPS):
        slot_arrival(k).wait_recv()
    rows = slots_ref.shape[1]

    def pick(slot, carry):
        at = position_ref[slot]
        slots_ref[slot] = slot_got[at // RANKS, pl.ds(at % RANKS * rows, rows), :]
        return carry

    lax.fori_loop(0, slots_ref.shape[0], pick, 0)
    z_add(0)
    for g in range(groups):
        far_copy(g, True).wait_send()
        near_copy(g).wait_send()
        for k in range(1, 4):
            z_copy(g, k).wait_send()
    for t in range(tiles - 2, tiles):
        pair_copy(t).wait_send()
    for k in range(1, CHIPS):
        slot_copy((me + k) % CHIPS).wait_send()
    for step in range(5):
        small_copy(step).wait_send()
    for i in range(2):
        row_copy(i).wait_send()


def run_backward(
    position,
    exps,
    scale,
    key_values,
    states,
    queries,
    mixed,
    self_w,
    cross_w,
    ff_grads,
    grad,
    residual,
    target,
    gains,
    qkv,
    self_mixed,
    self_exps,
    self_scale,
    buckets,
    gain_three,
    slots,
):
    low, wide = jnp.bfloat16, jnp.float32
    groups = 4
    rows, columns = ff_grads.shape[-2:]
    heads = exps.shape[0]
    key_count, half = states.shape[1:]
    tokens, model = grad.shape
    block_rows = key_count // CHIPS
    tile_rows = TILE * block_rows
    width = queries.shape[1]
    small_shape = (16, model)
    vmem = pltpu.VMEM
    return pl.pallas_call(
        backward_kernel,
        out_shape=(
            jax.ShapeDtypeStruct((groups, rows, columns), wide),
            jax.ShapeDtypeStruct((slots, block_rows // RANKS, half), low),
            jax.ShapeDtypeStruct(small_shape, wide),
            jax.ShapeDtypeStruct((tokens, model), low),
        ),
        in_specs=[IN_SMEM, ANY, IN_VMEM, ANY] + [IN_VMEM] * 16,
        out_specs=(IN_VMEM,) * 4,
        scratch_shapes=[
            vmem((2, heads, tile_rows, tokens), low),
            vmem((2, tile_rows, 2 * width), low),
            vmem((2, 4, 2, 2, rows, columns), low),
            vmem((groups, 4, 2, rows, columns), low),
            vmem((groups, 4, rows, columns), low),
            vmem((groups, 3, rows, columns), low),
            vmem((key_count, 2 * width), low),
            vmem((2, tile_rows, half), low),
            vmem((CHIPS, block_rows, half), low),
            vmem((CHIPS // TILE, tile_rows, half), low),
            vmem((CHIPS, block_rows, half), low),
            vmem(small_shape, wide),
            vmem((8,) + small_shape, wide),
            vmem((heads, tokens, 2 * HEAD_DIM), low),
            vmem((heads, tokens, 2 * HEAD_DIM), low),
            vmem((heads, 2 * HEAD_DIM, tokens), low),
            vmem((8, tokens), wide),
            vmem((width, tokens), wide),
            vmem((2, tokens, model), wide),
            vmem((2, tokens, model), wide),
            vmem((tokens, model), wide),
            vmem((heads, tokens, tokens), low),
            DMA((2,)),
            DMA((2,)),
            DMA((groups,)),
            DMA((groups,)),
            DMA((groups,)),
            DMA((groups,)),
            DMA((groups, 3)),
            DMA((groups, 3)),
            DMA((2,)),
            DMA((CHIPS // TILE,)),
            DMA((CHIPS,)),
            DMA((CHIPS,)),
            DMA((5,)),
            DMA((5,)),
            DMA((2,)),
            DMA((2,)),
        ],
        compiler_params=pltpu.CompilerParams(
            collective_id=2, has_side_effects=True, vmem_limit_bytes=62 * 2**20
        ),
    )(
        position,
        exps,
        scale,
        key_values,
        states,
        queries,
        mixed,
        self_w,
        cross_w,
        ff_grads,
        grad,
        residual,
        target,
        gains,
        qkv,
        self_mixed,
        self_exps,
        self_scale,
        buckets,
        gain_three,
    )


def route(slot_query, slot_live):
    matching = slot_query[:, None] == slot_query[None, :]
    earlier = jnp.tril(jnp.ones(matching.shape, jnp.bool_), -1)
    position = slot_query * RANKS + jnp.sum(jnp.logical_and(matching, earlier), axis=1).astype(
        jnp.int32
    )
    here = position[None, :] == jnp.arange(CHIPS * RANKS, dtype=jnp.int32)[:, None]
    slots = slot_query.shape[0]
    index = jnp.sum(jnp.where(here, jnp.arange(slots, dtype=jnp.int32)[None, :], 0), axis=1)
    live = jnp.sum(jnp.where(here, slot_live[None, :], 0), axis=1)
    return position, index, live


def body(
    target_states,
    passage_states,
    slot_query,
    slot_live,
    norm_gains,
    self_query,
    self_key,
    self_value,
    self_output,
    position_bias,
    cross_query,
    cross_key,
    cross_value,
    cross_output,
    expand_weight,
    reduce_weight,
    output_cotangent,
):
    low = jnp.bfloat16
    width_here = self_query.shape[1]
    heads_here = width_here // HEAD_DIM
    slots_here, passage_len, half = passage_states.shape
    bucket_count = position_bias.shape[0]
    shards = jnp.stack(
        [
            jnp.concatenate([self_query, self_key, self_value, self_output.T], axis=1),
            jnp.concatenate([cross_query, cross_key, cross_value, cross_output.T], axis=1),
            expand_weight,
            reduce_weight.T,
        ]
    )
    position, index, live = route(slot_query, slot_live)
    flags = jnp.repeat(live.reshape(CHIPS, RANKS), passage_len, axis=1).astype(low)
    flags = jnp.pad(flags, ((0, 0), (0, half - RANKS * passage_len)))
    flags = jnp.broadcast_to(flags[:, None, :], (CHIPS, FLAG_ROWS, half))
    full, states = gather_everything(index, shards, passage_states, flags)
    full = full.reshape(4, -1, full.shape[-1])
    w = width_here
    self_in, output_t = full[0, :, : 3 * w], full[0, :, 3 * w :]
    cross_query_full = full[1, :, :w]
    kv_weights = full[1, :, w : 3 * w]
    cross_output_t = full[1, :, 3 * w :]
    expand_full, reduce_t = full[2], full[3]
    key_rows_n = CHIPS * RANKS * passage_len
    live_keys = states[0, :, RANKS * passage_len, : RANKS * passage_len].reshape(1, key_rows_n)
    allowed = (live_keys > 0)[:, None, None, :]
    states = states[:, :, : RANKS * passage_len].reshape(2, key_rows_n, half)

    residual = target_states.astype(jnp.float32)
    unit_one, factor_one, normed_one = rms_forward(residual, norm_gains[0])
    projected = jnp.dot(normed_one, self_in, preferred_element_type=jnp.float32).astype(low)
    projected = projected.reshape(1, TLEN, 3, heads_here, HEAD_DIM)
    queries_self = projected[:, :, 0]
    keys_self = projected[:, :, 1]
    values_self = projected[:, :, 2]
    buckets = jnp.asarray(bucket_table(TLEN, bucket_count, MAXDIST))
    one_hot = (jnp.arange(bucket_count, dtype=jnp.int32)[:, None, None] == buckets[None]).astype(
        jnp.float32
    )
    bias_full = jnp.einsum("bij,bh->hij", one_hot, position_bias, precision=lax.Precision.HIGHEST)[
        None
    ]
    causal = jnp.asarray(np.tril(np.ones((TLEN, TLEN), dtype=bool)))
    attended_self, total_self = attend(queries_self, keys_self, values_self, causal, bias_full)
    merged_self = attended_self.reshape(TLEN, w)
    residual_two = residual + over_pair(rows_nt(merged_self, output_t))
    unit_two, factor_two, normed_two = rms_forward(residual_two, norm_gains[1])
    cross_queries = jnp.dot(
        normed_two, cross_query_full, preferred_element_type=jnp.float32
    ).astype(low)
    cross_queries = cross_queries.reshape(1, TLEN, heads_here, HEAD_DIM)
    key_values = jnp.dot(states[0], kv_weights[:half], preferred_element_type=jnp.float32) + jnp.dot(
        states[1], kv_weights[half:], preferred_element_type=jnp.float32
    )
    key_values = key_values.astype(low).reshape(1, key_rows_n, 2, heads_here, HEAD_DIM)
    key_rows = key_values[:, :, 0]
    value_rows = key_values[:, :, 1]
    scores_t = jnp.einsum(
        "jhe,ihe->hji", key_rows[0], cross_queries[0], preferred_element_type=jnp.float32
    )
    head_block = 2
    head_ranges = [
        slice(start_head, start_head + head_block)
        for start_head in range(0, heads_here, head_block)
    ]
    cross_parts = []
    cross_totals = []
    for head_range in head_ranges:
        mixed_part, total_part = attend(
            cross_queries[:, :, head_range],
            key_rows[:, :, head_range],
            value_rows[:, :, head_range],
            allowed,
            None,
        )
        cross_parts.append(mixed_part)
        cross_totals.append(total_part)
    merged_cross = jnp.concatenate(cross_parts, axis=2).reshape(TLEN, w)
    residual_three = residual_two + over_pair(rows_nt(merged_cross, cross_output_t))
    unit_three, factor_three, normed_three = rms_forward(residual_three, norm_gains[2])
    before = jnp.dot(normed_three, expand_full, preferred_element_type=jnp.float32)
    hidden = jax.nn.gelu(before, approximate=True).astype(low)
    block_out = residual_three + over_pair(rows_nt(hidden, reduce_t))
    grad_out = output_cotangent.astype(jnp.float32)
    reduce_grad_t = rows_tn(output_cotangent, hidden)
    hidden_grad = jnp.dot(output_cotangent, reduce_t, preferred_element_type=jnp.float32)
    unused_value, gelu_pullback = jax.vjp(partial(jax.nn.gelu, approximate=True), before)
    before_grad = gelu_pullback(hidden_grad)[0].astype(low)
    expand_grad = rows_tn(normed_three, before_grad)
    normed_grad = over_pair(rows_nt(before_grad, expand_full))
    back_three, gain_three = rms_backward(normed_grad, unit_three, factor_three, norm_gains[2])
    grad_three = grad_out + back_three
    totals_t = jnp.concatenate(cross_totals, axis=1)[0, :, :, 0]
    live_column = (live_keys[0] > 0)[None, :, None]
    exps = jnp.where(live_column, jnp.exp(scores_t - totals_t[:, None, :]), 0.0).astype(low)
    tiles = CHIPS // TILE
    scale = jnp.ones((tiles, 8, TLEN), jnp.float32)
    self_scores_t = jnp.einsum(
        "jhe,ihe->hji", keys_self[0], queries_self[0], preferred_element_type=jnp.float32
    ) + jnp.swapaxes(bias_full[0], 1, 2)
    self_exps = jnp.where(
        causal.T[None], jnp.exp(self_scores_t - total_self[0, :, :, 0][:, None, :]), 0.0
    ).astype(low)
    self_scale = jnp.ones((8, TLEN), jnp.float32)
    ff_grads = jnp.stack([expand_grad, reduce_grad_t]).astype(low)
    ff_grads = ff_grads.reshape((2, 4, 2, 2) + shards.shape[1:])
    distance = np.zeros((TLEN, 128), np.float32)
    distance[np.arange(TLEN), bucket_table(TLEN, bucket_count, MAXDIST)[:, 0]] = 1.0
    shard_grads, passage_grad, small_total, target_grad = run_backward(
        position,
        exps,
        scale,
        key_values.reshape(key_rows_n, 2 * w),
        states,
        cross_queries.reshape(TLEN, w),
        merged_cross,
        full[0],
        full[1],
        ff_grads,
        grad_three,
        residual_two,
        target_states,
        norm_gains,
        projected.reshape(TLEN, 3 * w),
        merged_self,
        self_exps,
        self_scale,
        jnp.asarray(distance),
        gain_three[None, :],
        slots_here,
    )
    first, second = shard_grads[0], shard_grads[1]
    return (
        block_out.astype(low),
        target_grad,
        passage_grad,
        small_total[:3],
        first[:, :w],
        first[:, w : 2 * w],
        first[:, 2 * w : 3 * w],
        first[:, 3 * w :].T,
        small_total[8 : 8 + heads_here, :bucket_count].T,
        second[:, :w],
        second[:, w : 2 * w],
        second[:, 2 * w : 3 * w],
        second[:, 3 * w :].T,
        shard_grads[2],
        shard_grads[3].T,
    )


def solution(mesh):
    return jax.shard_map(
        body if fits(mesh) else body_any,
        mesh=mesh,
        in_specs=(
            P("pas", None),
            P("pas", None, "mdl"),
            P("pas"),
            P("pas"),
            P(),
            P("pas", "mdl"),
            P("pas", "mdl"),
            P("pas", "mdl"),
            P("mdl", "pas"),
            P(None, "mdl"),
            P("pas", "mdl"),
            P("pas", "mdl"),
            P("pas", "mdl"),
            P("mdl", "pas"),
            P("pas", "mdl"),
            P("mdl", "pas"),
            P("pas", None),
        ),
        out_specs=(
            P("pas", None),
            P("pas", None),
            P("pas", None, "mdl"),
            P(),
            P("pas", "mdl"),
            P("pas", "mdl"),
            P("pas", "mdl"),
            P("mdl", "pas"),
            P(None, "mdl"),
            P("pas", "mdl"),
            P("pas", "mdl"),
            P("pas", "mdl"),
            P("mdl", "pas"),
            P("pas", "mdl"),
            P("mdl", "pas"),
        ),
        check_vma=False,
    )
```

```python
from functools import partial
import math

import jax
import jax.numpy as jnp
import numpy as np
from jax import lax
from jax.experimental import pallas as pl
from jax.experimental.pallas import tpu as pltpu
from jax.sharding import PartitionSpec as P

HEAD_DIM = 64
MAXDIST = 128
TLEN = 256
PQ = 40


EPSILON = 1e-06
MASKED = -1e30


def bucket_table(length, buckets, distance):
    later = np.arange(length)[:, None]
    earlier = np.arange(length)[None, :]
    behind = np.maximum(later - earlier, 0)
    exact = buckets // 2
    spread = np.log(np.maximum(behind, 1) / exact) / math.log(distance / exact) * (buckets - exact)
    far_bucket = np.minimum(exact + np.floor(spread).astype(np.int32), buckets - 1)
    return np.where(behind < exact, behind, far_bucket).astype(np.int32)


def rms_forward(values, gain):
    factor = lax.rsqrt(jnp.mean(values * values, axis=-1, keepdims=True) + EPSILON)
    unit_rows = values * factor
    return (unit_rows, factor, (unit_rows * gain).astype(jnp.bfloat16))


def rms_backward(normed_grad, unit_rows, factor, gain):
    scaled_grad = normed_grad * gain
    input_grad = factor * (
        scaled_grad - unit_rows * jnp.mean(scaled_grad * unit_rows, axis=-1, keepdims=True)
    )
    return (input_grad, jnp.sum(normed_grad * unit_rows, axis=0))


def over_heads(partial_rows):
    return lax.psum(partial_rows, "mdl")


def score_block(queries, key_rows, allowed, bias):
    scores = jnp.einsum("sihe,sjhe->shij", queries, key_rows, preferred_element_type=jnp.float32)
    if bias is not None:
        scores = scores + bias
    return jnp.where(allowed, scores, MASKED)


def attend(queries, key_rows, values, allowed, bias):
    scores = score_block(queries, key_rows, allowed, bias)
    highest = jnp.max(scores, axis=-1, keepdims=True)
    totals = highest + jnp.log(jnp.sum(jnp.exp(scores - highest), axis=-1, keepdims=True))
    probability = jnp.exp(scores - totals)
    mixed = jnp.einsum(
        "shij,sjhe->sihe",
        probability.astype(jnp.bfloat16),
        values,
        preferred_element_type=jnp.float32,
    )
    return (mixed.astype(jnp.bfloat16), totals)


def attend_back(queries, key_rows, values, allowed, bias, totals, out_grad):
    scores = score_block(queries, key_rows, allowed, bias)
    probability = jnp.exp(scores - totals)
    prob_grad = jnp.einsum("sihe,sjhe->shij", out_grad, values, preferred_element_type=jnp.float32)
    centered = jnp.sum(probability * prob_grad, axis=-1, keepdims=True)
    score_grad = (probability * (prob_grad - centered)).astype(jnp.bfloat16)
    query_grad = jnp.einsum(
        "shij,sjhe->sihe", score_grad, key_rows, preferred_element_type=jnp.float32
    )
    key_grad = jnp.einsum(
        "shij,sihe->sjhe", score_grad, queries, preferred_element_type=jnp.float32
    )
    value_grad = jnp.einsum(
        "shij,sihe->sjhe",
        probability.astype(jnp.bfloat16),
        out_grad,
        preferred_element_type=jnp.float32,
    )
    return (query_grad, key_grad, value_grad, score_grad)


def send_plan(slot_query, slot_live, per_device, capacity):
    target_device = slot_query // per_device
    matching = target_device[:, None] == target_device[None, :]
    lower_part = jnp.tril(jnp.ones(matching.shape, jnp.bool_), -1)
    ranking = jnp.sum(jnp.logical_and(matching, lower_part), axis=1)
    position = target_device * capacity + ranking
    codes = jnp.where(slot_live > 0, slot_query % per_device + 1, 0).astype(jnp.bfloat16)
    return (position, codes)


def arrange_plan(got_codes, per_device, slots_each):
    local_query = got_codes.astype(jnp.int32) - 1
    matches = (local_query[:, None] == jnp.arange(per_device, dtype=jnp.int32)[None, :]).astype(
        jnp.int32
    )
    ranking = jnp.sum((jnp.cumsum(matches, axis=0) - 1) * matches, axis=1)
    spare_place = per_device * slots_each
    places = jnp.where(local_query >= 0, local_query * slots_each + ranking, spare_place)
    arrivals = got_codes.shape[0]
    gather_index = (
        jnp.zeros((spare_place + 1,), jnp.int32)
        .at[places]
        .set(jnp.arange(arrivals, dtype=jnp.int32))
    )
    valid_slot = jnp.zeros((spare_place + 1,), jnp.int32).at[places].set(1)
    return (gather_index[:spare_place], valid_slot[:spare_place] > 0)


def place_rows(rows, position, total_rows):
    return jnp.zeros((total_rows,) + rows.shape[1:], rows.dtype).at[position].set(rows)


def return_rows(rows, gather_index, total_rows):
    return jnp.zeros((total_rows,) + rows.shape[1:], rows.dtype).at[gather_index].add(rows)


def body_any(
    target_states,
    passage_states,
    slot_query,
    slot_live,
    norm_gains,
    self_query,
    self_key,
    self_value,
    self_output,
    position_bias,
    cross_query,
    cross_key,
    cross_value,
    cross_output,
    expand_weight,
    reduce_weight,
    output_cotangent,
):
    (
        query_full,
        key_full,
        value_full,
        cross_query_full,
        cross_key_full,
        cross_value_full,
        expand_full,
    ) = (
        lax.all_gather(self_query, "pas", axis=0, tiled=True),
        lax.all_gather(self_key, "pas", axis=0, tiled=True),
        lax.all_gather(self_value, "pas", axis=0, tiled=True),
        lax.all_gather(cross_query, "pas", axis=0, tiled=True),
        lax.all_gather(cross_key, "pas", axis=0, tiled=True),
        lax.all_gather(cross_value, "pas", axis=0, tiled=True),
        lax.all_gather(expand_weight, "pas", axis=0, tiled=True),
    )
    output_full, cross_output_full, reduce_full = (
        lax.all_gather(self_output, "pas", axis=1, tiled=True),
        lax.all_gather(cross_output, "pas", axis=1, tiled=True),
        lax.all_gather(reduce_weight, "pas", axis=1, tiled=True),
    )
    width_here = query_full.shape[1]
    heads_here = width_here // HEAD_DIM
    sequences = target_states.shape[0] // TLEN
    passage_len = passage_states.shape[1]
    bucket_count = position_bias.shape[0]
    devices = lax.axis_size("pas")
    slots_here = slot_query.shape[0]
    capacity = -(-slots_here // devices)
    buffer_rows = devices * capacity
    residual = target_states.astype(jnp.float32)
    unit_one, factor_one, normed_one = rms_forward(residual, norm_gains[0])
    self_weights = jnp.concatenate([query_full, key_full, value_full], axis=1)
    projected = jnp.dot(normed_one, self_weights, preferred_element_type=jnp.float32).astype(
        jnp.bfloat16
    )
    projected = projected.reshape(sequences, TLEN, 3, heads_here, HEAD_DIM)
    queries_self = projected[:, :, 0]
    keys_self = projected[:, :, 1]
    values_self = projected[:, :, 2]
    buckets = jnp.asarray(bucket_table(TLEN, bucket_count, MAXDIST))
    one_hot = (jnp.arange(bucket_count, dtype=jnp.int32)[:, None, None] == buckets[None]).astype(
        jnp.float32
    )
    bias_full = jnp.einsum("bij,bh->hij", one_hot, position_bias, precision=lax.Precision.HIGHEST)[
        None
    ]
    causal = jnp.asarray(np.tril(np.ones((TLEN, TLEN), dtype=bool)))
    attended_self, total_self = attend(queries_self, keys_self, values_self, causal, bias_full)
    merged_self = attended_self.reshape(sequences * TLEN, width_here)
    residual_two = residual + over_heads(
        jnp.dot(merged_self, output_full, preferred_element_type=jnp.float32)
    )
    unit_two, factor_two, normed_two = rms_forward(residual_two, norm_gains[1])
    cross_queries = jnp.dot(
        normed_two, cross_query_full, preferred_element_type=jnp.float32
    ).astype(jnp.bfloat16)
    cross_queries = cross_queries.reshape(sequences, TLEN, heads_here, HEAD_DIM)
    kv_weights = jnp.concatenate([cross_key_full, cross_value_full], axis=1)
    position, codes = send_plan(slot_query, slot_live, sequences, capacity)
    sent_codes = place_rows(codes, position, buffer_rows)
    states_full = lax.all_gather(passage_states, "mdl", axis=2, tiled=True)
    key_values = jnp.einsum(
        "tpd,dc->tpc", states_full, kv_weights, preferred_element_type=jnp.float32
    ).astype(jnp.bfloat16)
    received, got_codes = (
        lax.all_to_all(
            place_rows(key_values, position, buffer_rows),
            "pas",
            split_axis=0,
            concat_axis=0,
            tiled=True,
        ),
        lax.all_to_all(sent_codes, "pas", split_axis=0, concat_axis=0, tiled=True),
    )
    gather_index, valid_slot = arrange_plan(got_codes, sequences, PQ)
    arranged = jnp.take(received, gather_index, axis=0)
    arranged = arranged.reshape(sequences, PQ * passage_len, 2, heads_here, HEAD_DIM)
    key_rows = arranged[:, :, 0]
    value_rows = arranged[:, :, 1]
    allowed = jnp.repeat(valid_slot.reshape(sequences, PQ), passage_len, axis=1)[:, None, None, :]
    head_block = 2
    head_ranges = [
        slice(start_head, start_head + head_block)
        for start_head in range(0, heads_here, head_block)
    ]
    cross_parts = []
    cross_totals = []
    for head_range in head_ranges:
        mixed_part, total_part = attend(
            cross_queries[:, :, head_range],
            key_rows[:, :, head_range],
            value_rows[:, :, head_range],
            allowed,
            None,
        )
        cross_parts.append(mixed_part)
        cross_totals.append(total_part)
    merged_cross = jnp.concatenate(cross_parts, axis=2).reshape(sequences * TLEN, width_here)
    residual_three = residual_two + over_heads(
        jnp.dot(merged_cross, cross_output_full, preferred_element_type=jnp.float32)
    )
    unit_three, factor_three, normed_three = rms_forward(residual_three, norm_gains[2])
    before = jnp.dot(normed_three, expand_full, preferred_element_type=jnp.float32)
    hidden = jax.nn.gelu(before, approximate=True).astype(jnp.bfloat16)
    block_out = residual_three + over_heads(
        jnp.dot(hidden, reduce_full, preferred_element_type=jnp.float32)
    )
    grad_out = output_cotangent.astype(jnp.float32)
    reduce_grad = jnp.dot(hidden.T, output_cotangent, preferred_element_type=jnp.float32)
    hidden_grad = jnp.dot(output_cotangent, reduce_full.T, preferred_element_type=jnp.float32)
    unused_value, gelu_pullback = jax.vjp(partial(jax.nn.gelu, approximate=True), before)
    before_grad = gelu_pullback(hidden_grad)[0].astype(jnp.bfloat16)
    expand_grad = jnp.dot(normed_three.T, before_grad, preferred_element_type=jnp.float32)
    normed_grad = over_heads(
        jnp.dot(before_grad, expand_full.T, preferred_element_type=jnp.float32)
    )
    back_three, gain_three = rms_backward(normed_grad, unit_three, factor_three, norm_gains[2])
    grad_three = grad_out + back_three
    grad_low = grad_three.astype(jnp.bfloat16)
    cross_output_grad = jnp.dot(merged_cross.T, grad_low, preferred_element_type=jnp.float32)
    mixed_grad = jnp.dot(grad_low, cross_output_full.T, preferred_element_type=jnp.float32).astype(
        jnp.bfloat16
    )
    mixed_grad = mixed_grad.reshape(sequences, TLEN, heads_here, HEAD_DIM)
    query_parts = []
    key_parts = []
    value_parts = []
    for number, head_range in enumerate(head_ranges):
        query_part, key_part, value_part, unused_scores = attend_back(
            cross_queries[:, :, head_range],
            key_rows[:, :, head_range],
            value_rows[:, :, head_range],
            allowed,
            None,
            cross_totals[number],
            mixed_grad[:, :, head_range],
        )
        query_parts.append(query_part)
        key_parts.append(key_part)
        value_parts.append(value_part)
    cross_query_rows = (
        jnp.concatenate(query_parts, axis=2)
        .astype(jnp.bfloat16)
        .reshape(sequences * TLEN, width_here)
    )
    kv_grad = jnp.stack(
        [jnp.concatenate(key_parts, axis=2), jnp.concatenate(value_parts, axis=2)], axis=2
    )
    kv_grad = kv_grad.astype(jnp.bfloat16).reshape(sequences * PQ, passage_len, 2 * width_here)
    returned = lax.all_to_all(
        return_rows(kv_grad, gather_index, buffer_rows),
        "pas",
        split_axis=0,
        concat_axis=0,
        tiled=True,
    )
    kv_grad_here = jnp.take(returned, position, axis=0)
    kv_weight_grad = jnp.einsum(
        "tpd,tpc->dc", states_full, kv_grad_here, preferred_element_type=jnp.float32
    )
    states_grad = jnp.einsum(
        "tpc,dc->tpd", kv_grad_here, kv_weights, preferred_element_type=jnp.float32
    )
    passage_grad = lax.psum_scatter(
        states_grad.astype(jnp.bfloat16), "mdl", scatter_dimension=2, tiled=True
    )
    cross_query_grad = jnp.dot(normed_two.T, cross_query_rows, preferred_element_type=jnp.float32)
    normed_grad = over_heads(
        jnp.dot(cross_query_rows, cross_query_full.T, preferred_element_type=jnp.float32)
    )
    back_two, gain_two = rms_backward(normed_grad, unit_two, factor_two, norm_gains[1])
    grad_two = grad_three + back_two
    grad_low = grad_two.astype(jnp.bfloat16)
    self_output_grad = jnp.dot(merged_self.T, grad_low, preferred_element_type=jnp.float32)
    attended_grad = jnp.dot(grad_low, output_full.T, preferred_element_type=jnp.float32).astype(
        jnp.bfloat16
    )
    attended_grad = attended_grad.reshape(sequences, TLEN, heads_here, HEAD_DIM)
    query_grad, key_grad, value_grad, score_grad = attend_back(
        queries_self, keys_self, values_self, causal, bias_full, total_self, attended_grad
    )
    bias_grad = jnp.einsum(
        "hij,bij->bh",
        jnp.sum(score_grad.astype(jnp.float32), axis=0),
        one_hot,
        precision=lax.Precision.HIGHEST,
    )
    projected_grad = jnp.stack([query_grad, key_grad, value_grad], axis=2).astype(jnp.bfloat16)
    projected_grad = projected_grad.reshape(sequences * TLEN, 3 * width_here)
    self_weight_grad = jnp.dot(normed_one.T, projected_grad, preferred_element_type=jnp.float32)
    normed_grad = over_heads(
        jnp.dot(projected_grad, self_weights.T, preferred_element_type=jnp.float32)
    )
    back_one, gain_one = rms_backward(normed_grad, unit_one, factor_one, norm_gains[0])
    target_grad = (grad_two + back_one).astype(jnp.bfloat16)
    row_grads = (
        lax.psum_scatter(self_weight_grad[:, :width_here], "pas", scatter_dimension=0, tiled=True),
        lax.psum_scatter(
            self_weight_grad[:, width_here : 2 * width_here], "pas", scatter_dimension=0, tiled=True
        ),
        lax.psum_scatter(
            self_weight_grad[:, 2 * width_here :], "pas", scatter_dimension=0, tiled=True
        ),
        lax.psum_scatter(cross_query_grad, "pas", scatter_dimension=0, tiled=True),
        lax.psum_scatter(kv_weight_grad[:, :width_here], "pas", scatter_dimension=0, tiled=True),
        lax.psum_scatter(kv_weight_grad[:, width_here:], "pas", scatter_dimension=0, tiled=True),
        lax.psum_scatter(expand_grad, "pas", scatter_dimension=0, tiled=True),
    )
    col_grads = (
        lax.psum_scatter(self_output_grad, "pas", scatter_dimension=1, tiled=True),
        lax.psum_scatter(cross_output_grad, "pas", scatter_dimension=1, tiled=True),
        lax.psum_scatter(reduce_grad, "pas", scatter_dimension=1, tiled=True),
    )
    gains_total, bias_total = lax.psum(
        (jnp.stack([gain_one, gain_two, gain_three]), bias_grad), "pas"
    )
    return (
        block_out.astype(jnp.bfloat16),
        target_grad,
        passage_grad,
        gains_total,
        row_grads[0],
        row_grads[1],
        row_grads[2],
        col_grads[0],
        bias_total,
        row_grads[3],
        row_grads[4],
        row_grads[5],
        col_grads[1],
        row_grads[6],
        col_grads[2],
    )


CHIPS = 16
RANKS = 3
FLAG_ROWS = 16
MESH_ID = pl.DeviceIdType.MESH
VMEM_LIMIT = 56 * 2**20


def fits(mesh):
    return mesh.shape["pas"] == CHIPS and mesh.shape["mdl"] == 2


def places():
    me, core = lax.axis_index("pas"), lax.axis_index("mdl")
    x, y, z = me % 2, (me // 2) % 2, me // 4
    across_x, across_y = me + 1 - 2 * x, me + 2 - 4 * y
    near = across_y + (across_x - across_y) * core
    far = across_x + (across_y - across_x) * core
    return me, core, x, y, z, near, far


def remote(src, dst, send_sem, recv_sem, device):
    return pltpu.make_async_remote_copy(
        src_ref=src,
        dst_ref=dst,
        send_sem=send_sem,
        recv_sem=recv_sem,
        device_id=device,
        device_id_type=MESH_ID,
    )


def greet_all(me, core):
    barrier = pltpu.get_barrier_semaphore()
    for k in range(1, CHIPS):
        pl.semaphore_signal(
            barrier, inc=1, device_id=((me + k) % CHIPS, core), device_id_type=MESH_ID
        )
    pl.semaphore_signal(barrier, inc=1, device_id=(me, 1 - core), device_id_type=MESH_ID)
    pl.semaphore_wait(barrier, CHIPS)


ANY = pl.BlockSpec(memory_space=pl.ANY)
IN_VMEM = pl.BlockSpec(memory_space=pltpu.VMEM)
IN_SMEM = pl.BlockSpec(memory_space=pltpu.SMEM)
DMA = pltpu.SemaphoreType.DMA


def rows_nt(left, right):
    return lax.dot_general(
        left, right, (((1,), (1,)), ((), ())), preferred_element_type=jnp.float32
    )


def rows_tn(left, right):
    return lax.dot_general(
        left, right, (((0,), (0,)), ((), ())), preferred_element_type=jnp.float32
    )


TILE = 2


def mm(left, right):
    return jnp.dot(left, right, preferred_element_type=jnp.float32)


def halves_of_pair(rows, head):
    lane = lax.broadcasted_iota(jnp.int32, (rows.shape[0], 2 * HEAD_DIM), 1)
    at = head // 2 * 2 * HEAD_DIM
    return jnp.where(lane // HEAD_DIM == head % 2, rows[:, at : at + 2 * HEAD_DIM], 0.0).astype(
        jnp.bfloat16
    )


def halves_of_rows(rows, head):
    row = lax.broadcasted_iota(jnp.int32, (2 * HEAD_DIM, rows.shape[1]), 0)
    at = head // 2 * 2 * HEAD_DIM
    return jnp.where(row // HEAD_DIM == head % 2, rows[at : at + 2 * HEAD_DIM], 0.0).astype(
        jnp.bfloat16
    )


def unit_of(values):
    factor = lax.rsqrt(jnp.mean(values * values, axis=-1, keepdims=True) + EPSILON)
    return values * factor, factor


def prepare_heads(heads, query_ref, grad, mixed, q_pair, o_pair, o_rows, centre):
    grad = grad.astype(jnp.float32)
    grad_t = grad.T
    product = (grad * mixed.astype(jnp.float32)).T
    queries = query_ref[...].astype(jnp.float32)
    for h in range(heads):
        q_pair[h] = halves_of_pair(queries, h)
        o_pair[h] = halves_of_pair(grad, h)
        o_rows[h] = halves_of_rows(grad_t, h)
        centre[h : h + 1, :] = jnp.sum(
            product[h * HEAD_DIM : (h + 1) * HEAD_DIM], axis=0, keepdims=True
        )


def head_pair_back(p, keys, values, prob, q_pair, o_pair, o_rows, centre, keep_scores):
    low = jnp.bfloat16
    keys_t = keys.T
    query_parts = []
    for a in range(2):
        h = 2 * p + a
        prob_grad = mm(values, o_rows[h])
        weights = prob(h)
        score_grad = (weights * (prob_grad - centre[h : h + 1, :])).astype(low)
        if keep_scores is not None:
            keep_scores(h, score_grad)
        key_part = mm(score_grad, q_pair[h])
        value_part = mm(weights.astype(low), o_pair[h])
        key_grad = key_part if a == 0 else key_grad + key_part
        value_grad = value_part if a == 0 else value_grad + value_part
        query_parts.append(mm(keys_t[a * HEAD_DIM : (a + 1) * HEAD_DIM], score_grad))
    return key_grad.astype(low), value_grad.astype(low), query_parts


def backward_kernel(
    position_ref,
    exps_ref,
    scale_ref,
    kv_ref,
    states_ref,
    query_ref,
    mixed_ref,
    self_w_ref,
    cross_w_ref,
    ff_ref,
    grad_ref,
    residual_ref,
    target_ref,
    gains_ref,
    qkv_ref,
    self_mixed_ref,
    self_exps_ref,
    self_scale_ref,
    bucket_ref,
    gain_ref,
    shard_ref,
    slots_ref,
    small_ref,
    target_grad_ref,
    exps,
    keys,
    grads,
    far_got,
    near_got,
    z_got,
    dkv,
    outgoing,
    kept_sum,
    pair_got,
    slot_got,
    small,
    small_got,
    q_pair,
    o_pair,
    o_rows,
    centre,
    dq_t,
    row_sent,
    row_got,
    upper_grad,
    self_scores,
    exps_sem,
    keys_sem,
    far_send,
    far_recv,
    near_send,
    near_recv,
    z_send,
    z_recv,
    pair_send,
    pair_recv,
    slot_send,
    slot_recv,
    small_send,
    small_recv,
    row_send,
    row_recv,
):
    low, wide = jnp.bfloat16, jnp.float32
    me, core, x, y, z, near, far = places()
    groups = shard_ref.shape[0]
    across_x, across_y = me + 1 - 2 * x, me + 2 - 4 * y
    kept = (1 - core) * y + core * x
    partner = (me, 1 - core)
    width = query_ref.shape[1]
    pairs = width // (2 * HEAD_DIM)
    heads = 2 * pairs
    block_rows = states_ref.shape[1] // CHIPS
    tile_rows = TILE * block_rows
    tiles = CHIPS // TILE
    half = states_ref.shape[2]

    def tile_at(t):
        return (t + me // TILE) % tiles

    def exps_copy(t):
        rows = pl.ds(tile_at(t) * tile_rows, tile_rows)
        return pltpu.make_async_copy(exps_ref.at[:, rows], exps.at[t % 2], exps_sem.at[t % 2])

    def keys_copy(t):
        rows = pl.ds(tile_at(t) * tile_rows, tile_rows)
        return pltpu.make_async_copy(kv_ref.at[rows], keys.at[t % 2], keys_sem.at[t % 2])

    exps_copy(0).start()
    keys_copy(0).start()
    greet_all(me, core)

    def source(g):
        return ff_ref.at[g - 2] if g >= 2 else grads.at[g]

    def far_copy(g, over_x):
        block = source(g).at[:, :, 1 - x] if over_x else source(g).at[:, 1 - y, :]
        return remote(block, far_got.at[g], far_send.at[g], far_recv.at[g], (far, core))

    def far_start(g):
        @pl.when(core == 0)
        def _():
            far_copy(g, True).start()

        @pl.when(core == 1)
        def _():
            far_copy(g, False).start()

    def near_copy(g):
        return remote(
            far_got.at[g, :, 1 - kept], near_got.at[g], near_send.at[g], near_recv.at[g], (near, core)
        )

    def z_copy(g, k):
        return remote(
            near_got.at[g, (z + k) % 4],
            z_got.at[g, k - 1],
            z_send.at[g, k - 1],
            z_recv.at[g, k - 1],
            ((me + 4 * k) % CHIPS, core),
        )

    def far_add(g):
        far_copy(g, True).wait_recv()

        def step(i, carry):
            zi, o = i // 2, i % 2
            mine = source(g)[zi, (1 - core) * o + core * y, (1 - core) * x + core * o]
            far_got[g, zi, o] = (mine.astype(wide) + far_got[g, zi, o].astype(wide)).astype(low)
            return carry

        lax.fori_loop(0, 8, step, 0)
        near_copy(g).start()

    def near_add(g):
        near_copy(g).wait_recv()

        def step(zi, carry):
            near_got[g, zi] = (
                far_got[g, zi, kept].astype(wide) + near_got[g, zi].astype(wide)
            ).astype(low)
            return carry

        lax.fori_loop(0, 4, step, 0)
        for k in range(1, 4):
            z_copy(g, k).start()

    def z_add(g):
        for k in range(1, 4):
            z_copy(g, k).wait_recv()
        total = near_got[g, z].astype(wide)
        for k in range(3):
            total = total + z_got[g, k].astype(wide)
        shard_ref[g] = total

    def pair_copy(t):
        return remote(
            outgoing.at[t % 2],
            pair_got.at[tile_at(t)],
            pair_send.at[t % 2],
            pair_recv.at[t],
            partner,
        )

    def slot_copy(to):
        return remote(
            kept_sum.at[to], slot_got.at[me], slot_send.at[to], slot_recv.at[me], (to, core)
        )

    def slot_arrival(k):
        came = (me + k) % CHIPS
        return remote(
            kept_sum.at[came], slot_got.at[came], slot_send.at[came], slot_recv.at[came], (came, core)
        )

    def finish_tile(t):
        tile = tile_at(t)
        pair_copy(t).wait_recv()
        for j in range(TILE):
            to = tile * TILE + j
            rows = slice(j * block_rows, (j + 1) * block_rows)
            kept_sum[to] = (
                kept_sum[to].astype(wide) + pair_got[tile, rows].astype(wide)
            ).astype(low)

            @pl.when(to != me)
            def _():
                slot_copy(to).start()

            @pl.when(to == me)
            def _():
                slot_got[me] = kept_sum[me]

    def row_copy(i):
        return remote(row_sent.at[i], row_got.at[i], row_send.at[i], row_recv.at[i], partner)

    def store_grad(g, first, value):
        blocks = value.astype(low).reshape(grads.shape[1:5] + (value.shape[1],))
        grads[g, :, :, :, :, first : first + value.shape[1]] = blocks

    far_start(2)
    far_start(3)

    upper_grad[...] = grad_ref[...]
    grad_low = upper_grad[...].astype(low)
    store_grad(1, 3 * width, rows_tn(grad_low, mixed_ref[...]))
    mixed_grad = mm(grad_low, cross_w_ref[:, 3 * width :]).astype(low)
    prepare_heads(heads, query_ref, mixed_grad, mixed_ref[...], q_pair, o_pair, o_rows, centre)
    dq_t[...] = jnp.zeros_like(dq_t)

    def tile_step(t, carry):
        tile = tile_at(t)
        rows = pl.ds(pl.multiple_of(tile * tile_rows, tile_rows), tile_rows)

        @pl.when(t + 1 < tiles)
        def _():
            exps_copy(t + 1).start()
            keys_copy(t + 1).start()

        exps_copy(t).wait()
        keys_copy(t).wait()

        def prob(h):
            return exps[t % 2, h].astype(wide) * scale_ref[tile, h : h + 1, :]

        for p in range(pairs):
            at = 2 * HEAD_DIM * p
            key_grad, value_grad, query_parts = head_pair_back(
                p,
                keys[t % 2, :, at : at + 2 * HEAD_DIM],
                keys[t % 2, :, width + at : width + at + 2 * HEAD_DIM],
                prob,
                q_pair,
                o_pair,
                o_rows,
                centre,
                None,
            )
            dkv[rows, at : at + 2 * HEAD_DIM] = key_grad
            dkv[rows, width + at : width + at + 2 * HEAD_DIM] = value_grad
            for a in range(2):
                first = at + a * HEAD_DIM
                dq_t[first : first + HEAD_DIM, :] += query_parts[a]
        here = dkv[rows, :]

        @pl.when(t >= 2)
        def _():
            pair_copy(t - 2).wait_send()

        weights = cross_w_ref[pl.ds((1 - core) * half, half), width : 3 * width]
        outgoing[t % 2] = rows_nt(here, weights).astype(low)
        pair_copy(t).start()
        weights = cross_w_ref[pl.ds(core * half, half), width : 3 * width]
        mine = rows_nt(here, weights).astype(low)
        for j in range(TILE):
            kept_sum[tile * TILE + j] = mine[j * block_rows : (j + 1) * block_rows]

        @pl.when(t >= 1)
        def _():
            finish_tile(t - 1)

        @pl.when(t == 5)
        def _():
            far_add(2)

        return carry

    lax.fori_loop(0, tiles, tile_step, 0)
    dq = dq_t[...].T.astype(low)
    row_sent[0] = rows_nt(dq, cross_w_ref[:, :width])
    row_copy(0).start()
    finish_tile(tiles - 1)
    far_add(3)
    unit_two, factor_two = unit_of(residual_ref[...])
    normed_two = (unit_two * gains_ref[1:2, :]).astype(low)
    store_grad(1, 0, rows_tn(normed_two, dq))

    for n in range(2 * width // 256):
        columns = slice(n * 256, (n + 1) * 256)
        parts = [rows_tn(states_ref[i], dkv[:, columns]) for i in range(2)]
        store_grad(1, width + n * 256, jnp.concatenate(parts))
    far_start(1)
    near_add(2)

    row_copy(0).wait_recv()
    normed_grad = row_sent[0] + row_got[0]
    back, gain_two = rms_backward(normed_grad, unit_two, factor_two, gains_ref[1:2, :])
    upper_grad[...] += back

    grad_low = upper_grad[...].astype(low)
    store_grad(0, 3 * width, rows_tn(grad_low, self_mixed_ref[...]))
    mixed_grad = mm(grad_low, self_w_ref[:, 3 * width :]).astype(low)
    prepare_heads(
        heads,
        qkv_ref.at[:, :width],
        mixed_grad,
        self_mixed_ref[...],
        q_pair,
        o_pair,
        o_rows,
        centre,
    )

    def self_prob(h):
        return self_exps_ref[h].astype(wide) * self_scale_ref[h : h + 1, :]

    def keep_scores(h, score_grad):
        self_scores[h] = score_grad

    query_rows, key_columns, value_columns = [], [], []
    for p in range(pairs):
        at = 2 * HEAD_DIM * p
        key_grad, value_grad, query_parts = head_pair_back(
            p,
            qkv_ref[:, width + at : width + at + 2 * HEAD_DIM],
            qkv_ref[:, 2 * width + at : 2 * width + at + 2 * HEAD_DIM],
            self_prob,
            q_pair,
            o_pair,
            o_rows,
            centre,
            keep_scores,
        )
        key_columns.append(key_grad)
        value_columns.append(value_grad)
        query_rows.extend(query_parts)
    dq = jnp.concatenate(query_rows, axis=0).T.astype(low)
    dqkv = jnp.concatenate([dq] + key_columns + value_columns, axis=1)
    row_sent[1] = rows_nt(dqkv, self_w_ref[:, : 3 * width])
    row_copy(1).start()
    unit_one, factor_one = unit_of(target_ref[...].astype(wide))
    normed_one = (unit_one * gains_ref[0:1, :]).astype(low)
    store_grad(0, 0, rows_tn(normed_one, dqkv))
    far_start(0)
    near_add(3)

    length = self_scores.shape[1]

    def diagonal_step(i, total):
        rows = self_scores[:, pl.ds(pl.multiple_of(16 * i, 16), 16), :].astype(wide)
        rows = rows.reshape(heads * 16, length)
        return total + pltpu.roll(rows, (length - 16 * i) % length, 1)

    total = lax.fori_loop(
        0, length // 16, diagonal_step, jnp.zeros((heads * 16, length), wide)
    ).reshape(heads, 16, length)
    small[...] = jnp.zeros_like(small)
    for h in range(heads):
        line = total[h, 0:1]
        for s in range(1, 16):
            line = line + pltpu.roll(total[h, s : s + 1], length - s, 1)
        small[8 + h : 9 + h, :length] = line
    by_bucket = jnp.dot(
        small[8:16, :length], bucket_ref[...], precision=lax.Precision.HIGHEST,
        preferred_element_type=wide,
    )
    small[8:16, :length] = jnp.zeros((8, length), wide)
    small[8:16, : bucket_ref.shape[1]] = by_bucket

    row_copy(1).wait_recv()
    normed_grad = row_sent[1] + row_got[1]
    back, gain_one = rms_backward(normed_grad, unit_one, factor_one, gains_ref[0:1, :])
    target_grad_ref[...] = (upper_grad[...] + back).astype(low)
    small[0:1, :] = gain_one[None, :]
    small[1:2, :] = gain_two[None, :]
    small[2:3, :] = gain_ref[...]

    def small_copy(step):
        if step == 0:
            return remote(small, small_got.at[0], small_send.at[0], small_recv.at[0], (across_x, core))
        if step == 1:
            return remote(
                small_got.at[6], small_got.at[1], small_send.at[1], small_recv.at[1], (across_y, core)
            )
        return remote(
            small_got.at[7],
            small_got.at[2 + z],
            small_send.at[step],
            small_recv.at[step],
            ((me + 4 * (step - 1)) % CHIPS, core),
        )

    small_copy(0).start()
    far_add(1)
    small_copy(0).wait_recv()
    small_got[6] = small[...] + small_got[0]
    small_copy(1).start()
    z_add(2)
    near_add(1)
    small_copy(1).wait_recv()
    small_got[7] = small_got[6] + small_got[1]
    for step in range(2, 5):
        small_copy(step).start()
    small_got[2 + z] = small_got[7]
    far_add(0)
    z_add(3)
    z_add(1)
    near_add(0)
    for step in range(2, 5):
        small_copy(step).wait_recv()
    small_ref[...] = small_got[2] + small_got[3] + small_got[4] + small_got[5]
    for k in range(1, CHIPS):
        slot_arrival(k).wait_recv()
    rows = slots_ref.shape[1]

    def pick(slot, carry):
        at = position_ref[slot]
        slots_ref[slot] = slot_got[at // RANKS, pl.ds(at % RANKS * rows, rows), :]
        return carry

    lax.fori_loop(0, slots_ref.shape[0], pick, 0)
    z_add(0)
    for g in range(groups):
        far_copy(g, True).wait_send()
        near_copy(g).wait_send()
        for k in range(1, 4):
            z_copy(g, k).wait_send()
    for t in range(tiles - 2, tiles):
        pair_copy(t).wait_send()
    for k in range(1, CHIPS):
        slot_copy((me + k) % CHIPS).wait_send()
    for step in range(5):
        small_copy(step).wait_send()
    for i in range(2):
        row_copy(i).wait_send()


def run_backward(
    position,
    exps,
    scale,
    key_values,
    states,
    queries,
    mixed,
    self_w,
    cross_w,
    ff_grads,
    grad,
    residual,
    target,
    gains,
    qkv,
    self_mixed,
    self_exps,
    self_scale,
    buckets,
    gain_three,
    slots,
):
    low, wide = jnp.bfloat16, jnp.float32
    groups = 4
    rows, columns = ff_grads.shape[-2:]
    heads = exps.shape[0]
    key_count, half = states.shape[1:]
    tokens, model = grad.shape
    block_rows = key_count // CHIPS
    tile_rows = TILE * block_rows
    width = queries.shape[1]
    small_shape = (16, model)
    vmem = pltpu.VMEM
    return pl.pallas_call(
        backward_kernel,
        out_shape=(
            jax.ShapeDtypeStruct((groups, rows, columns), wide),
            jax.ShapeDtypeStruct((slots, block_rows // RANKS, half), low),
            jax.ShapeDtypeStruct(small_shape, wide),
            jax.ShapeDtypeStruct((tokens, model), low),
        ),
        in_specs=[IN_SMEM, ANY, IN_VMEM, ANY] + [IN_VMEM] * 16,
        out_specs=(IN_VMEM,) * 4,
        scratch_shapes=[
            vmem((2, heads, tile_rows, tokens), low),
            vmem((2, tile_rows, 2 * width), low),
            vmem((2, 4, 2, 2, rows, columns), low),
            vmem((groups, 4, 2, rows, columns), low),
            vmem((groups, 4, rows, columns), low),
            vmem((groups, 3, rows, columns), low),
            vmem((key_count, 2 * width), low),
            vmem((2, tile_rows, half), low),
            vmem((CHIPS, block_rows, half), low),
            vmem((CHIPS // TILE, tile_rows, half), low),
            vmem((CHIPS, block_rows, half), low),
            vmem(small_shape, wide),
            vmem((8,) + small_shape, wide),
            vmem((heads, tokens, 2 * HEAD_DIM), low),
            vmem((heads, tokens, 2 * HEAD_DIM), low),
            vmem((heads, 2 * HEAD_DIM, tokens), low),
            vmem((8, tokens), wide),
            vmem((width, tokens), wide),
            vmem((2, tokens, model), wide),
            vmem((2, tokens, model), wide),
            vmem((tokens, model), wide),
            vmem((heads, tokens, tokens), low),
            DMA((2,)),
            DMA((2,)),
            DMA((groups,)),
            DMA((groups,)),
            DMA((groups,)),
            DMA((groups,)),
            DMA((groups, 3)),
            DMA((groups, 3)),
            DMA((2,)),
            DMA((CHIPS // TILE,)),
            DMA((CHIPS,)),
            DMA((CHIPS,)),
            DMA((5,)),
            DMA((5,)),
            DMA((2,)),
            DMA((2,)),
        ],
        compiler_params=pltpu.CompilerParams(
            collective_id=2, has_side_effects=True, vmem_limit_bytes=62 * 2**20
        ),
    )(
        position,
        exps,
        scale,
        key_values,
        states,
        queries,
        mixed,
        self_w,
        cross_w,
        ff_grads,
        grad,
        residual,
        target,
        gains,
        qkv,
        self_mixed,
        self_exps,
        self_scale,
        buckets,
        gain_three,
    )


def exp_rows(scores):
    highest = jnp.max(scores, axis=0, keepdims=True)
    exps = jnp.exp(scores - highest)
    return exps, highest, jnp.sum(exps, axis=0, keepdims=True)


def gelu_both(values):
    first = math.sqrt(2 / math.pi)
    square = values * values
    curve = jnp.tanh(first * values * (1.0 + 0.044715 * square))
    half = 0.5 * (1.0 + curve)
    slope = half + 0.5 * values * (1.0 - curve * curve) * first * (1.0 + 3 * 0.044715 * square)
    return values * half, slope


def forward_kernel(
    index_ref,
    shard_ref,
    passage_ref,
    flag_ref,
    target_ref,
    cotangent_ref,
    gains_ref,
    table_ref,
    bucket_ref,
    weights_ref,
    states_out,
    exps_out,
    kv_out,
    scale_ref,
    query_ref,
    mixed_ref,
    residual_ref,
    qkv_ref,
    self_mixed_ref,
    self_exps_ref,
    self_scale_ref,
    ff_ref,
    grad_ref,
    gain_ref,
    block_ref,
    full,
    states,
    flags,
    outgoing,
    exps,
    keys,
    bias,
    q_rows,
    out_t,
    highest,
    total,
    tile_highest,
    row_sent,
    row_got,
    z_send,
    z_recv,
    near_send,
    near_recv,
    first_send,
    first_recv,
    second_send,
    second_recv,
    slot_send,
    slot_recv,
    flag_send,
    flag_recv,
    core_send,
    core_recv,
    row_send,
    row_recv,
    own_sem,
    exps_sem,
    keys_sem,
    out_sem,
):
    low, wide = jnp.bfloat16, jnp.float32
    me, core, x, y, z, near, far = places()
    groups = shard_ref.shape[0]
    partner = (me, 1 - core)
    pair = me // TILE
    tiles = CHIPS // TILE
    block_rows = states.shape[2]
    passage_len = block_rows // RANKS
    tile_rows = TILE * block_rows
    tokens = target_ref.shape[0]
    width = query_ref.shape[1]
    pairs = width // (2 * HEAD_DIM)
    heads = 2 * pairs
    half = states.shape[3]
    other_y = y + (1 - core) * (1 - 2 * y)
    other_x = x + core * (1 - 2 * x)

    def own_copy(g):
        return pltpu.make_async_copy(shard_ref.at[g], full.at[g, z, y, x], own_sem.at[g])

    def z_copy(g, k):
        return remote(
            shard_ref.at[g],
            full.at[g, z, y, x],
            z_send.at[g, k - 1],
            z_recv.at[g, k - 1],
            ((me + 4 * k) % CHIPS, core),
        )

    def held(g, k):
        return shard_ref.at[g] if k == 0 else full.at[g, (z + k) % 4, y, x]

    def near_copy(g, k):
        dst = full.at[g, (z + k) % 4, y, x]
        return remote(held(g, k), dst, near_send.at[g, k], near_recv.at[g, k], (near, core))

    def first_copy(g, k):
        dst = full.at[g, (z + k) % 4, y, x]
        return remote(held(g, k), dst, first_send.at[g, k], first_recv.at[g, k], (far, core))

    def second_copy(g, k):
        block = full.at[g, (z + k) % 4, other_y, other_x]
        return remote(block, block, second_send.at[g, k], second_recv.at[g, k], (far, core))

    def slot_copy(to):
        return remote(
            outgoing.at[to], states.at[core, me], slot_send.at[to], slot_recv.at[me], (to, core)
        )

    def slot_arrival(came):
        block = states.at[core, came]
        return remote(block, block, slot_send.at[came], slot_recv.at[came], (came, core))

    def flag_copy(to):
        return remote(flag_ref.at[to], flags.at[me], flag_send.at[to], flag_recv.at[me], (to, core))

    def flag_arrival(came):
        block = flags.at[came]
        return remote(block, block, flag_send.at[came], flag_recv.at[came], (came, core))

    def core_copy(came):
        block = states.at[core, came]
        return remote(block, block, core_send.at[came], core_recv.at[came], partner)

    def row_copy(i):
        return remote(row_sent.at[i], row_got.at[i], row_send.at[i], row_recv.at[i], partner)

    def pair_sum(i):
        row_copy(i).wait_recv()
        return row_sent[i] + row_got[i]

    def launch(g):
        for k in range(1, 4):
            z_copy(g, k).start()
        near_copy(g, 0).start()
        first_copy(g, 0).start()
        own_copy(g).start()

    def relay(g):
        for k in range(1, 4):
            z_copy(g, 4 - k).wait_recv()
            near_copy(g, k).start()
            first_copy(g, k).start()

    def relay_near(g):
        for k in range(4):
            near_copy(g, k).wait_recv()
            second_copy(g, k).start()

    def arrived(g):
        own_copy(g).wait()
        for k in range(4):
            first_copy(g, k).wait_recv()
            second_copy(g, k).wait_recv()

    def weight(g):
        return full[g].reshape(full.shape[1] * 4 * full.shape[4], full.shape[5])

    def weights_copy(g):
        return pltpu.make_async_copy(full.at[g], weights_ref.at[g], out_sem.at[g])

    greet_all(me, core)
    launch(0)
    launch(1)

    def fill(to, carry):
        for rank in range(RANKS):
            outgoing[to, rank * passage_len : (rank + 1) * passage_len, :] = passage_ref[
                index_ref[to * RANKS + rank]
            ]
        return carry

    lax.fori_loop(0, CHIPS, fill, 0)
    mate = me + 1 - 2 * x
    flag_copy(mate).start()
    slot_copy(mate).start()

    def send_pair(j, carry):
        for i in range(TILE):
            to = (pair + j) % tiles * TILE + i
            flag_copy(to).start()
            slot_copy(to).start()
        return carry

    lax.fori_loop(1, tiles, send_pair, 0)
    states[core, me] = outgoing[me]
    flags[me] = flag_ref[me]
    core_copy(me).start()

    line = jnp.dot(
        table_ref[...], bucket_ref[...], precision=lax.Precision.HIGHEST, preferred_element_type=wide
    )
    for h in range(heads):
        for s in range(8):
            row = line[h : h + 1]
            bias[h, s : s + 1, :] = row if s == 0 else pltpu.roll(row, s, 1)
    base = bias[:, 0:8, :].reshape(heads * 8, tokens)

    def bias_step(i, carry):
        rows = pltpu.roll(base, 8 * i, 1).reshape(heads, 8, tokens)
        bias[:, pl.ds(pl.multiple_of(8 * i, 8), 8), :] = rows
        return carry

    lax.fori_loop(1, tokens // 8, bias_step, 0)
    residual = target_ref[...].astype(wide)
    normed = (unit_of(residual)[0] * gains_ref[0:1, :]).astype(low)

    relay(0)
    relay_near(0)
    relay(1)
    arrived(0)

    qkv_ref[...] = mm(normed, weight(0)[:, : 3 * width]).astype(low)
    weights_copy(0).start()
    relay_near(1)
    launch(2)
    launch(3)
    queries_t = qkv_ref[:, :width].astype(wide).T
    for h in range(heads):
        q_rows[h] = halves_of_rows(queries_t, h)
    key_at = lax.broadcasted_iota(jnp.int32, (tokens, tokens), 0)
    query_at = lax.broadcasted_iota(jnp.int32, (tokens, tokens), 1)
    self_scale_ref[...] = jnp.zeros_like(self_scale_ref)
    for p in range(pairs):
        at = 2 * HEAD_DIM * p
        head_keys = qkv_ref[:, width + at : width + at + 2 * HEAD_DIM]
        values_t = qkv_ref[:, 2 * width + at : 2 * width + at + 2 * HEAD_DIM].T
        for a in range(2):
            h = 2 * p + a
            scores = mm(head_keys, q_rows[h]) + bias[h]
            scores = jnp.where(key_at <= query_at, scores, MASKED)
            head_exps, unused, sums = exp_rows(scores)
            head_exps = head_exps.astype(low)
            self_exps_ref[h] = head_exps
            inverse = 1.0 / sums
            self_scale_ref[h : h + 1, :] = inverse
            first = at + a * HEAD_DIM
            out_t[first : first + HEAD_DIM, :] = (
                mm(values_t[a * HEAD_DIM : (a + 1) * HEAD_DIM], head_exps) * inverse
            )
    self_mixed_ref[...] = out_t[...].T.astype(low)
    row_sent[0] = rows_nt(self_mixed_ref[...], weight(0)[:, 3 * width :])
    row_copy(0).start()
    relay(2)
    arrived(1)
    weights_copy(1).start()
    residual_ref[...] = residual + pair_sum(0)

    normed = (unit_of(residual_ref[...])[0] * gains_ref[1:2, :]).astype(low)
    query_ref[...] = mm(normed, weight(1)[:, :width]).astype(low)
    queries_t = query_ref[...].astype(wide).T
    for h in range(heads):
        q_rows[h] = halves_of_rows(queries_t, h)
    out_t[...] = jnp.zeros_like(out_t)
    highest[...] = jnp.full_like(highest, MASKED)
    total[...] = jnp.zeros_like(total)
    tile_highest[...] = jnp.zeros_like(tile_highest)

    def take_in(t):
        for i in range(TILE):
            came = (pair - t + tiles) % tiles * TILE + i

            @pl.when(came != me)
            def _():
                flag_arrival(came).wait_recv()
                slot_arrival(came).wait_recv()
                core_copy(came).start()

    def exps_copy(t):
        rows = pl.ds((pair - t + tiles) % tiles * tile_rows, tile_rows)
        return pltpu.make_async_copy(exps.at[t % 2], exps_out.at[:, rows], exps_sem.at[t % 2])

    def keys_copy(t):
        rows = pl.ds((pair - t + tiles) % tiles * tile_rows, tile_rows)
        return pltpu.make_async_copy(keys.at[t % 2], kv_out.at[rows], keys_sem.at[t % 2])

    take_in(0)

    def tile_step(t, carry):
        tile = (pair - t + tiles) % tiles

        @pl.when(t + 1 < tiles)
        def _():
            take_in(t + 1)

        @pl.when(t >= 2)
        def _():
            exps_copy(t - 2).wait()
            keys_copy(t - 2).wait()

        for i in range(TILE):
            core_copy(tile * TILE + i).wait_recv()
        kv_parts = []
        for c in range(2):
            rows = states[c, pl.ds(tile * TILE, TILE)].reshape(tile_rows, half)
            w = full[1, 2 * c : 2 * c + 2, :, :, :, width : 3 * width]
            kv_parts.append(mm(rows, w.reshape(half, 2 * width)))
        keys[t % 2] = (kv_parts[0] + kv_parts[1]).astype(low)
        keys_copy(t).start()
        masks = []
        for i in range(TILE):
            for rank in range(RANKS):
                masks.append(flags[tile * TILE + i, rank : rank + 1, :].astype(wide)[None])
        masks = jnp.concatenate(masks, axis=0)
        for p in range(pairs):
            at = 2 * HEAD_DIM * p
            head_keys = keys[t % 2, :, at : at + 2 * HEAD_DIM]
            values_t = keys[t % 2, :, width + at : width + at + 2 * HEAD_DIM].T
            for a in range(2):
                h = 2 * p + a
                scores = mm(head_keys, q_rows[h]).reshape(TILE * RANKS, passage_len, tokens) + masks
                head_exps, top, sums = exp_rows(scores.reshape(tile_rows, tokens))
                head_exps = head_exps.astype(low)
                exps[t % 2, h] = head_exps
                before = highest[h : h + 1, :]
                now = jnp.maximum(before, top)
                keep, add = jnp.exp(before - now), jnp.exp(top - now)
                highest[h : h + 1, :] = now
                tile_highest[tile, h : h + 1, :] = top
                total[h : h + 1, :] = total[h : h + 1, :] * keep + sums * add
                first = at + a * HEAD_DIM
                out_t[first : first + HEAD_DIM, :] = (
                    out_t[first : first + HEAD_DIM, :] * keep
                    + mm(values_t[a * HEAD_DIM : (a + 1) * HEAD_DIM], head_exps) * add
                )
        exps_copy(t).start()

        @pl.when(t == 1)
        def _():
            relay_near(2)
            relay(3)

        @pl.when(t == 3)
        def _():
            relay_near(3)

        return carry

    lax.fori_loop(0, tiles, tile_step, 0)
    states_copy = pltpu.make_async_copy(states, states_out, out_sem.at[2])
    states_copy.start()
    for h in range(heads):
        inverse = 1.0 / total[h : h + 1, :]
        out_t[h * HEAD_DIM : (h + 1) * HEAD_DIM, :] *= inverse
        scale_ref[:, h, :] = jnp.exp(tile_highest[:, h, :] - highest[h : h + 1, :]) * inverse
    mixed_ref[...] = out_t[...].T.astype(low)
    row_sent[1] = rows_nt(mixed_ref[...], weight(1)[:, 3 * width :])
    row_copy(1).start()
    residual_three = residual_ref[...] + pair_sum(1)
    unit, factor = unit_of(residual_three)
    normed = (unit * gains_ref[2:3, :]).astype(low)

    def store_grad(i, value):
        ff_ref[i] = value.astype(low).reshape(ff_ref.shape[1:])

    arrived(2)
    hidden, slope = gelu_both(mm(normed, weight(2)))
    hidden = hidden.astype(low)
    arrived(3)
    hidden_grad = mm(cotangent_ref[...], weight(3))
    before_grad = (hidden_grad * slope).astype(low)
    row_sent[2] = rows_nt(before_grad, weight(2))
    row_copy(2).start()
    row_sent[3] = rows_nt(hidden, weight(3))
    row_copy(3).start()
    store_grad(0, rows_tn(normed, before_grad))
    store_grad(1, rows_tn(cotangent_ref[...], hidden))
    back, gain = rms_backward(pair_sum(2), unit, factor, gains_ref[2:3, :])
    grad_ref[...] = cotangent_ref[...].astype(wide) + back
    gain_ref[...] = gain[None, :]
    block_ref[...] = (residual_three + pair_sum(3)).astype(low)

    for g in range(groups):
        for k in range(1, 4):
            z_copy(g, k).wait_send()
        for k in range(4):
            near_copy(g, k).wait_send()
            first_copy(g, k).wait_send()
            second_copy(g, k).wait_send()
    for k in range(1, CHIPS):
        to = (me + k) % CHIPS
        slot_copy(to).wait_send()
        flag_copy(to).wait_send()
    for k in range(CHIPS):
        core_copy(k).wait_send()
    for i in range(4):
        row_copy(i).wait_send()
    for t in range(tiles - 2, tiles):
        exps_copy(t).wait()
        keys_copy(t).wait()
    for g in range(2):
        weights_copy(g).wait()
    states_copy.wait()


def run_forward(index, shards, passages, flags, target, cotangent, gains, table, buckets):
    low, wide = jnp.bfloat16, jnp.float32
    groups, rows, columns = shards.shape
    passage_len, half = passages.shape[1:]
    tokens, model = target.shape
    width = columns // 4
    heads = width // HEAD_DIM
    block_rows = RANKS * passage_len
    key_count = CHIPS * block_rows
    tile_rows = TILE * block_rows
    tiles = CHIPS // TILE
    shape = jax.ShapeDtypeStruct
    vmem = pltpu.VMEM
    return pl.pallas_call(
        forward_kernel,
        out_shape=(
            shape((2, 4, 2, 2, rows, columns), low),
            shape((2, CHIPS, block_rows, half), low),
            shape((heads, key_count, tokens), low),
            shape((key_count, 2 * width), low),
            shape((tiles, 8, tokens), wide),
            shape((tokens, width), low),
            shape((tokens, width), low),
            shape((tokens, model), wide),
            shape((tokens, 3 * width), low),
            shape((tokens, width), low),
            shape((heads, tokens, tokens), low),
            shape((8, tokens), wide),
            shape((2, 4, 2, 2, rows, columns), low),
            shape((tokens, model), wide),
            shape((1, model), wide),
            shape((tokens, model), low),
        ),
        in_specs=[IN_SMEM] + [IN_VMEM] * 8,
        out_specs=(ANY,) * 4 + (IN_VMEM,) * 12,
        scratch_shapes=[
            vmem((groups, 4, 2, 2, rows, columns), low),
            vmem((2, CHIPS, block_rows, half), low),
            vmem((CHIPS, FLAG_ROWS, tokens), low),
            vmem((CHIPS, block_rows, half), low),
            vmem((2, heads, tile_rows, tokens), low),
            vmem((2, tile_rows, 2 * width), low),
            vmem((heads, tokens, tokens), wide),
            vmem((heads, 2 * HEAD_DIM, tokens), low),
            vmem((width, tokens), wide),
            vmem((8, tokens), wide),
            vmem((8, tokens), wide),
            vmem((tiles, 8, tokens), wide),
            vmem((4, tokens, model), wide),
            vmem((4, tokens, model), wide),
            DMA((groups, 3)),
            DMA((groups, 3)),
            DMA((groups, 4)),
            DMA((groups, 4)),
            DMA((groups, 4)),
            DMA((groups, 4)),
            DMA((groups, 4)),
            DMA((groups, 4)),
            DMA((CHIPS,)),
            DMA((CHIPS,)),
            DMA((CHIPS,)),
            DMA((CHIPS,)),
            DMA((CHIPS,)),
            DMA((CHIPS,)),
            DMA((4,)),
            DMA((4,)),
            DMA((groups,)),
            DMA((2,)),
            DMA((2,)),
            DMA((3,)),
        ],
        compiler_params=pltpu.CompilerParams(
            collective_id=0, has_side_effects=True, vmem_limit_bytes=VMEM_LIMIT
        ),
    )(index, shards, passages, flags, target, cotangent, gains, table, buckets)


def route(slot_query, slot_live):
    matching = slot_query[:, None] == slot_query[None, :]
    earlier = jnp.tril(jnp.ones(matching.shape, jnp.bool_), -1)
    position = slot_query * RANKS + jnp.sum(jnp.logical_and(matching, earlier), axis=1).astype(
        jnp.int32
    )
    here = position[None, :] == jnp.arange(CHIPS * RANKS, dtype=jnp.int32)[:, None]
    slots = slot_query.shape[0]
    index = jnp.sum(jnp.where(here, jnp.arange(slots, dtype=jnp.int32)[None, :], 0), axis=1)
    live = jnp.sum(jnp.where(here, slot_live[None, :], 0), axis=1)
    return position, index, live


def body(
    target_states,
    passage_states,
    slot_query,
    slot_live,
    norm_gains,
    self_query,
    self_key,
    self_value,
    self_output,
    position_bias,
    cross_query,
    cross_key,
    cross_value,
    cross_output,
    expand_weight,
    reduce_weight,
    output_cotangent,
):
    low = jnp.bfloat16
    width_here = self_query.shape[1]
    heads_here = width_here // HEAD_DIM
    slots_here, passage_len, half = passage_states.shape
    bucket_count = position_bias.shape[0]
    shards = jnp.stack(
        [
            jnp.concatenate([self_query, self_key, self_value, self_output.T], axis=1),
            jnp.concatenate([cross_query, cross_key, cross_value, cross_output.T], axis=1),
            expand_weight,
            reduce_weight.T,
        ]
    )
    position, index, live = route(slot_query, slot_live)
    flags = jnp.where(live > 0, 0.0, MASKED).astype(low).reshape(CHIPS, RANKS, 1)
    flags = jnp.pad(flags, ((0, 0), (0, FLAG_ROWS - RANKS), (0, 0)))
    flags = jnp.broadcast_to(flags, (CHIPS, FLAG_ROWS, TLEN))
    distance = np.zeros((TLEN, 128), np.float32)
    distance[np.arange(TLEN), bucket_table(TLEN, bucket_count, MAXDIST)[:, 0]] = 1.0
    table = jnp.pad(position_bias.T, ((0, 8 - heads_here), (0, 0)))
    (
        weights,
        states,
        exps,
        key_values,
        scale,
        queries,
        mixed,
        residual,
        qkv,
        self_mixed,
        self_exps,
        self_scale,
        ff_grads,
        grad,
        gain,
        block_out,
    ) = run_forward(
        index,
        shards,
        passage_states,
        flags,
        target_states,
        output_cotangent,
        norm_gains,
        table,
        jnp.asarray(distance[:, :bucket_count].T),
    )
    w = width_here
    weights = weights.reshape(2, -1, weights.shape[-1])
    shard_grads, passage_grad, small_total, target_grad = run_backward(
        position,
        exps,
        scale,
        key_values,
        states.reshape(2, -1, half),
        queries,
        mixed,
        weights[0],
        weights[1],
        ff_grads,
        grad,
        residual,
        target_states,
        norm_gains,
        qkv,
        self_mixed,
        self_exps,
        self_scale,
        jnp.asarray(distance),
        gain,
        slots_here,
    )
    first, second = shard_grads[0], shard_grads[1]
    return (
        block_out,
        target_grad,
        passage_grad,
        small_total[:3],
        first[:, :w],
        first[:, w : 2 * w],
        first[:, 2 * w : 3 * w],
        first[:, 3 * w :].T,
        small_total[8 : 8 + heads_here, :bucket_count].T,
        second[:, :w],
        second[:, w : 2 * w],
        second[:, 2 * w : 3 * w],
        second[:, 3 * w :].T,
        shard_grads[2],
        shard_grads[3].T,
    )


def solution(mesh):
    return jax.shard_map(
        body if fits(mesh) else body_any,
        mesh=mesh,
        in_specs=(
            P("pas", None),
            P("pas", None, "mdl"),
            P("pas"),
            P("pas"),
            P(),
            P("pas", "mdl"),
            P("pas", "mdl"),
            P("pas", "mdl"),
            P("mdl", "pas"),
            P(None, "mdl"),
            P("pas", "mdl"),
            P("pas", "mdl"),
            P("pas", "mdl"),
            P("mdl", "pas"),
            P("pas", "mdl"),
            P("mdl", "pas"),
            P("pas", None),
        ),
        out_specs=(
            P("pas", None),
            P("pas", None),
            P("pas", None, "mdl"),
            P(),
            P("pas", "mdl"),
            P("pas", "mdl"),
            P("pas", "mdl"),
            P("mdl", "pas"),
            P(None, "mdl"),
            P("pas", "mdl"),
            P("pas", "mdl"),
            P("pas", "mdl"),
            P("mdl", "pas"),
            P("pas", "mdl"),
            P("mdl", "pas"),
        ),
        check_vma=False,
    )
```

```python
from functools import partial
import math

import jax
import jax.numpy as jnp
import numpy as np
from jax import lax
from jax.experimental import pallas as pl
from jax.experimental.pallas import tpu as pltpu
from jax.sharding import PartitionSpec as P

HEAD_DIM = 64
MAXDIST = 128
TLEN = 256
PQ = 40


EPSILON = 1e-06
MASKED = -1e30


def bucket_table(length, buckets, distance):
    later = np.arange(length)[:, None]
    earlier = np.arange(length)[None, :]
    behind = np.maximum(later - earlier, 0)
    exact = buckets // 2
    spread = np.log(np.maximum(behind, 1) / exact) / math.log(distance / exact) * (buckets - exact)
    far_bucket = np.minimum(exact + np.floor(spread).astype(np.int32), buckets - 1)
    return np.where(behind < exact, behind, far_bucket).astype(np.int32)


def rms_forward(values, gain):
    factor = lax.rsqrt(jnp.mean(values * values, axis=-1, keepdims=True) + EPSILON)
    unit_rows = values * factor
    return (unit_rows, factor, (unit_rows * gain).astype(jnp.bfloat16))


def rms_backward(normed_grad, unit_rows, factor, gain):
    scaled_grad = normed_grad * gain
    input_grad = factor * (
        scaled_grad - unit_rows * jnp.mean(scaled_grad * unit_rows, axis=-1, keepdims=True)
    )
    return (input_grad, jnp.sum(normed_grad * unit_rows, axis=0))


def over_heads(partial_rows):
    return lax.psum(partial_rows, "mdl")


def score_block(queries, key_rows, allowed, bias):
    scores = jnp.einsum("sihe,sjhe->shij", queries, key_rows, preferred_element_type=jnp.float32)
    if bias is not None:
        scores = scores + bias
    return jnp.where(allowed, scores, MASKED)


def attend(queries, key_rows, values, allowed, bias):
    scores = score_block(queries, key_rows, allowed, bias)
    highest = jnp.max(scores, axis=-1, keepdims=True)
    totals = highest + jnp.log(jnp.sum(jnp.exp(scores - highest), axis=-1, keepdims=True))
    probability = jnp.exp(scores - totals)
    mixed = jnp.einsum(
        "shij,sjhe->sihe",
        probability.astype(jnp.bfloat16),
        values,
        preferred_element_type=jnp.float32,
    )
    return (mixed.astype(jnp.bfloat16), totals)


def attend_back(queries, key_rows, values, allowed, bias, totals, out_grad):
    scores = score_block(queries, key_rows, allowed, bias)
    probability = jnp.exp(scores - totals)
    prob_grad = jnp.einsum("sihe,sjhe->shij", out_grad, values, preferred_element_type=jnp.float32)
    centered = jnp.sum(probability * prob_grad, axis=-1, keepdims=True)
    score_grad = (probability * (prob_grad - centered)).astype(jnp.bfloat16)
    query_grad = jnp.einsum(
        "shij,sjhe->sihe", score_grad, key_rows, preferred_element_type=jnp.float32
    )
    key_grad = jnp.einsum(
        "shij,sihe->sjhe", score_grad, queries, preferred_element_type=jnp.float32
    )
    value_grad = jnp.einsum(
        "shij,sihe->sjhe",
        probability.astype(jnp.bfloat16),
        out_grad,
        preferred_element_type=jnp.float32,
    )
    return (query_grad, key_grad, value_grad, score_grad)


def send_plan(slot_query, slot_live, per_device, capacity):
    target_device = slot_query // per_device
    matching = target_device[:, None] == target_device[None, :]
    lower_part = jnp.tril(jnp.ones(matching.shape, jnp.bool_), -1)
    ranking = jnp.sum(jnp.logical_and(matching, lower_part), axis=1)
    position = target_device * capacity + ranking
    codes = jnp.where(slot_live > 0, slot_query % per_device + 1, 0).astype(jnp.bfloat16)
    return (position, codes)


def arrange_plan(got_codes, per_device, slots_each):
    local_query = got_codes.astype(jnp.int32) - 1
    matches = (local_query[:, None] == jnp.arange(per_device, dtype=jnp.int32)[None, :]).astype(
        jnp.int32
    )
    ranking = jnp.sum((jnp.cumsum(matches, axis=0) - 1) * matches, axis=1)
    spare_place = per_device * slots_each
    places = jnp.where(local_query >= 0, local_query * slots_each + ranking, spare_place)
    arrivals = got_codes.shape[0]
    gather_index = (
        jnp.zeros((spare_place + 1,), jnp.int32)
        .at[places]
        .set(jnp.arange(arrivals, dtype=jnp.int32))
    )
    valid_slot = jnp.zeros((spare_place + 1,), jnp.int32).at[places].set(1)
    return (gather_index[:spare_place], valid_slot[:spare_place] > 0)


def place_rows(rows, position, total_rows):
    return jnp.zeros((total_rows,) + rows.shape[1:], rows.dtype).at[position].set(rows)


def return_rows(rows, gather_index, total_rows):
    return jnp.zeros((total_rows,) + rows.shape[1:], rows.dtype).at[gather_index].add(rows)


def body_any(
    target_states,
    passage_states,
    slot_query,
    slot_live,
    norm_gains,
    self_query,
    self_key,
    self_value,
    self_output,
    position_bias,
    cross_query,
    cross_key,
    cross_value,
    cross_output,
    expand_weight,
    reduce_weight,
    output_cotangent,
):
    (
        query_full,
        key_full,
        value_full,
        cross_query_full,
        cross_key_full,
        cross_value_full,
        expand_full,
    ) = (
        lax.all_gather(self_query, "pas", axis=0, tiled=True),
        lax.all_gather(self_key, "pas", axis=0, tiled=True),
        lax.all_gather(self_value, "pas", axis=0, tiled=True),
        lax.all_gather(cross_query, "pas", axis=0, tiled=True),
        lax.all_gather(cross_key, "pas", axis=0, tiled=True),
        lax.all_gather(cross_value, "pas", axis=0, tiled=True),
        lax.all_gather(expand_weight, "pas", axis=0, tiled=True),
    )
    output_full, cross_output_full, reduce_full = (
        lax.all_gather(self_output, "pas", axis=1, tiled=True),
        lax.all_gather(cross_output, "pas", axis=1, tiled=True),
        lax.all_gather(reduce_weight, "pas", axis=1, tiled=True),
    )
    width_here = query_full.shape[1]
    heads_here = width_here // HEAD_DIM
    sequences = target_states.shape[0] // TLEN
    passage_len = passage_states.shape[1]
    bucket_count = position_bias.shape[0]
    devices = lax.axis_size("pas")
    slots_here = slot_query.shape[0]
    capacity = -(-slots_here // devices)
    buffer_rows = devices * capacity
    residual = target_states.astype(jnp.float32)
    unit_one, factor_one, normed_one = rms_forward(residual, norm_gains[0])
    self_weights = jnp.concatenate([query_full, key_full, value_full], axis=1)
    projected = jnp.dot(normed_one, self_weights, preferred_element_type=jnp.float32).astype(
        jnp.bfloat16
    )
    projected = projected.reshape(sequences, TLEN, 3, heads_here, HEAD_DIM)
    queries_self = projected[:, :, 0]
    keys_self = projected[:, :, 1]
    values_self = projected[:, :, 2]
    buckets = jnp.asarray(bucket_table(TLEN, bucket_count, MAXDIST))
    one_hot = (jnp.arange(bucket_count, dtype=jnp.int32)[:, None, None] == buckets[None]).astype(
        jnp.float32
    )
    bias_full = jnp.einsum("bij,bh->hij", one_hot, position_bias, precision=lax.Precision.HIGHEST)[
        None
    ]
    causal = jnp.asarray(np.tril(np.ones((TLEN, TLEN), dtype=bool)))
    attended_self, total_self = attend(queries_self, keys_self, values_self, causal, bias_full)
    merged_self = attended_self.reshape(sequences * TLEN, width_here)
    residual_two = residual + over_heads(
        jnp.dot(merged_self, output_full, preferred_element_type=jnp.float32)
    )
    unit_two, factor_two, normed_two = rms_forward(residual_two, norm_gains[1])
    cross_queries = jnp.dot(
        normed_two, cross_query_full, preferred_element_type=jnp.float32
    ).astype(jnp.bfloat16)
    cross_queries = cross_queries.reshape(sequences, TLEN, heads_here, HEAD_DIM)
    kv_weights = jnp.concatenate([cross_key_full, cross_value_full], axis=1)
    position, codes = send_plan(slot_query, slot_live, sequences, capacity)
    sent_codes = place_rows(codes, position, buffer_rows)
    states_full = lax.all_gather(passage_states, "mdl", axis=2, tiled=True)
    key_values = jnp.einsum(
        "tpd,dc->tpc", states_full, kv_weights, preferred_element_type=jnp.float32
    ).astype(jnp.bfloat16)
    received, got_codes = (
        lax.all_to_all(
            place_rows(key_values, position, buffer_rows),
            "pas",
            split_axis=0,
            concat_axis=0,
            tiled=True,
        ),
        lax.all_to_all(sent_codes, "pas", split_axis=0, concat_axis=0, tiled=True),
    )
    gather_index, valid_slot = arrange_plan(got_codes, sequences, PQ)
    arranged = jnp.take(received, gather_index, axis=0)
    arranged = arranged.reshape(sequences, PQ * passage_len, 2, heads_here, HEAD_DIM)
    key_rows = arranged[:, :, 0]
    value_rows = arranged[:, :, 1]
    allowed = jnp.repeat(valid_slot.reshape(sequences, PQ), passage_len, axis=1)[:, None, None, :]
    head_block = 2
    head_ranges = [
        slice(start_head, start_head + head_block)
        for start_head in range(0, heads_here, head_block)
    ]
    cross_parts = []
    cross_totals = []
    for head_range in head_ranges:
        mixed_part, total_part = attend(
            cross_queries[:, :, head_range],
            key_rows[:, :, head_range],
            value_rows[:, :, head_range],
            allowed,
            None,
        )
        cross_parts.append(mixed_part)
        cross_totals.append(total_part)
    merged_cross = jnp.concatenate(cross_parts, axis=2).reshape(sequences * TLEN, width_here)
    residual_three = residual_two + over_heads(
        jnp.dot(merged_cross, cross_output_full, preferred_element_type=jnp.float32)
    )
    unit_three, factor_three, normed_three = rms_forward(residual_three, norm_gains[2])
    before = jnp.dot(normed_three, expand_full, preferred_element_type=jnp.float32)
    hidden = jax.nn.gelu(before, approximate=True).astype(jnp.bfloat16)
    block_out = residual_three + over_heads(
        jnp.dot(hidden, reduce_full, preferred_element_type=jnp.float32)
    )
    grad_out = output_cotangent.astype(jnp.float32)
    reduce_grad = jnp.dot(hidden.T, output_cotangent, preferred_element_type=jnp.float32)
    hidden_grad = jnp.dot(output_cotangent, reduce_full.T, preferred_element_type=jnp.float32)
    unused_value, gelu_pullback = jax.vjp(partial(jax.nn.gelu, approximate=True), before)
    before_grad = gelu_pullback(hidden_grad)[0].astype(jnp.bfloat16)
    expand_grad = jnp.dot(normed_three.T, before_grad, preferred_element_type=jnp.float32)
    normed_grad = over_heads(
        jnp.dot(before_grad, expand_full.T, preferred_element_type=jnp.float32)
    )
    back_three, gain_three = rms_backward(normed_grad, unit_three, factor_three, norm_gains[2])
    grad_three = grad_out + back_three
    grad_low = grad_three.astype(jnp.bfloat16)
    cross_output_grad = jnp.dot(merged_cross.T, grad_low, preferred_element_type=jnp.float32)
    mixed_grad = jnp.dot(grad_low, cross_output_full.T, preferred_element_type=jnp.float32).astype(
        jnp.bfloat16
    )
    mixed_grad = mixed_grad.reshape(sequences, TLEN, heads_here, HEAD_DIM)
    query_parts = []
    key_parts = []
    value_parts = []
    for number, head_range in enumerate(head_ranges):
        query_part, key_part, value_part, unused_scores = attend_back(
            cross_queries[:, :, head_range],
            key_rows[:, :, head_range],
            value_rows[:, :, head_range],
            allowed,
            None,
            cross_totals[number],
            mixed_grad[:, :, head_range],
        )
        query_parts.append(query_part)
        key_parts.append(key_part)
        value_parts.append(value_part)
    cross_query_rows = (
        jnp.concatenate(query_parts, axis=2)
        .astype(jnp.bfloat16)
        .reshape(sequences * TLEN, width_here)
    )
    kv_grad = jnp.stack(
        [jnp.concatenate(key_parts, axis=2), jnp.concatenate(value_parts, axis=2)], axis=2
    )
    kv_grad = kv_grad.astype(jnp.bfloat16).reshape(sequences * PQ, passage_len, 2 * width_here)
    returned = lax.all_to_all(
        return_rows(kv_grad, gather_index, buffer_rows),
        "pas",
        split_axis=0,
        concat_axis=0,
        tiled=True,
    )
    kv_grad_here = jnp.take(returned, position, axis=0)
    kv_weight_grad = jnp.einsum(
        "tpd,tpc->dc", states_full, kv_grad_here, preferred_element_type=jnp.float32
    )
    states_grad = jnp.einsum(
        "tpc,dc->tpd", kv_grad_here, kv_weights, preferred_element_type=jnp.float32
    )
    passage_grad = lax.psum_scatter(
        states_grad.astype(jnp.bfloat16), "mdl", scatter_dimension=2, tiled=True
    )
    cross_query_grad = jnp.dot(normed_two.T, cross_query_rows, preferred_element_type=jnp.float32)
    normed_grad = over_heads(
        jnp.dot(cross_query_rows, cross_query_full.T, preferred_element_type=jnp.float32)
    )
    back_two, gain_two = rms_backward(normed_grad, unit_two, factor_two, norm_gains[1])
    grad_two = grad_three + back_two
    grad_low = grad_two.astype(jnp.bfloat16)
    self_output_grad = jnp.dot(merged_self.T, grad_low, preferred_element_type=jnp.float32)
    attended_grad = jnp.dot(grad_low, output_full.T, preferred_element_type=jnp.float32).astype(
        jnp.bfloat16
    )
    attended_grad = attended_grad.reshape(sequences, TLEN, heads_here, HEAD_DIM)
    query_grad, key_grad, value_grad, score_grad = attend_back(
        queries_self, keys_self, values_self, causal, bias_full, total_self, attended_grad
    )
    bias_grad = jnp.einsum(
        "hij,bij->bh",
        jnp.sum(score_grad.astype(jnp.float32), axis=0),
        one_hot,
        precision=lax.Precision.HIGHEST,
    )
    projected_grad = jnp.stack([query_grad, key_grad, value_grad], axis=2).astype(jnp.bfloat16)
    projected_grad = projected_grad.reshape(sequences * TLEN, 3 * width_here)
    self_weight_grad = jnp.dot(normed_one.T, projected_grad, preferred_element_type=jnp.float32)
    normed_grad = over_heads(
        jnp.dot(projected_grad, self_weights.T, preferred_element_type=jnp.float32)
    )
    back_one, gain_one = rms_backward(normed_grad, unit_one, factor_one, norm_gains[0])
    target_grad = (grad_two + back_one).astype(jnp.bfloat16)
    row_grads = (
        lax.psum_scatter(self_weight_grad[:, :width_here], "pas", scatter_dimension=0, tiled=True),
        lax.psum_scatter(
            self_weight_grad[:, width_here : 2 * width_here], "pas", scatter_dimension=0, tiled=True
        ),
        lax.psum_scatter(
            self_weight_grad[:, 2 * width_here :], "pas", scatter_dimension=0, tiled=True
        ),
        lax.psum_scatter(cross_query_grad, "pas", scatter_dimension=0, tiled=True),
        lax.psum_scatter(kv_weight_grad[:, :width_here], "pas", scatter_dimension=0, tiled=True),
        lax.psum_scatter(kv_weight_grad[:, width_here:], "pas", scatter_dimension=0, tiled=True),
        lax.psum_scatter(expand_grad, "pas", scatter_dimension=0, tiled=True),
    )
    col_grads = (
        lax.psum_scatter(self_output_grad, "pas", scatter_dimension=1, tiled=True),
        lax.psum_scatter(cross_output_grad, "pas", scatter_dimension=1, tiled=True),
        lax.psum_scatter(reduce_grad, "pas", scatter_dimension=1, tiled=True),
    )
    gains_total, bias_total = lax.psum(
        (jnp.stack([gain_one, gain_two, gain_three]), bias_grad), "pas"
    )
    return (
        block_out.astype(jnp.bfloat16),
        target_grad,
        passage_grad,
        gains_total,
        row_grads[0],
        row_grads[1],
        row_grads[2],
        col_grads[0],
        bias_total,
        row_grads[3],
        row_grads[4],
        row_grads[5],
        col_grads[1],
        row_grads[6],
        col_grads[2],
    )


CHIPS = 16
RANKS = 3
FLAG_ROWS = 16
MESH_ID = pl.DeviceIdType.MESH
VMEM_LIMIT = 56 * 2**20


def fits(mesh):
    return mesh.shape["pas"] == CHIPS and mesh.shape["mdl"] == 2


def places():
    me, core = lax.axis_index("pas"), lax.axis_index("mdl")
    x, y, z = me % 2, (me // 2) % 2, me // 4
    across_x, across_y = me + 1 - 2 * x, me + 2 - 4 * y
    near = across_y + (across_x - across_y) * core
    far = across_x + (across_y - across_x) * core
    return me, core, x, y, z, near, far


def remote(src, dst, send_sem, recv_sem, device):
    return pltpu.make_async_remote_copy(
        src_ref=src,
        dst_ref=dst,
        send_sem=send_sem,
        recv_sem=recv_sem,
        device_id=device,
        device_id_type=MESH_ID,
    )


def greet_all(me, core):
    barrier = pltpu.get_barrier_semaphore()
    for k in range(1, CHIPS):
        pl.semaphore_signal(
            barrier, inc=1, device_id=((me + k) % CHIPS, core), device_id_type=MESH_ID
        )
    pl.semaphore_signal(barrier, inc=1, device_id=(me, 1 - core), device_id_type=MESH_ID)
    pl.semaphore_wait(barrier, CHIPS)


ANY = pl.BlockSpec(memory_space=pl.ANY)
IN_VMEM = pl.BlockSpec(memory_space=pltpu.VMEM)
IN_SMEM = pl.BlockSpec(memory_space=pltpu.SMEM)
DMA = pltpu.SemaphoreType.DMA


def rows_nt(left, right):
    return lax.dot_general(
        left, right, (((1,), (1,)), ((), ())), preferred_element_type=jnp.float32
    )


def rows_tn(left, right):
    return lax.dot_general(
        left, right, (((0,), (0,)), ((), ())), preferred_element_type=jnp.float32
    )


TILE = 2


def mm(left, right):
    return jnp.dot(left, right, preferred_element_type=jnp.float32)


def halves_of_pair(rows, head):
    lane = lax.broadcasted_iota(jnp.int32, (rows.shape[0], 2 * HEAD_DIM), 1)
    at = head // 2 * 2 * HEAD_DIM
    return jnp.where(lane // HEAD_DIM == head % 2, rows[:, at : at + 2 * HEAD_DIM], 0.0).astype(
        jnp.bfloat16
    )


def halves_of_rows(rows, head):
    row = lax.broadcasted_iota(jnp.int32, (2 * HEAD_DIM, rows.shape[1]), 0)
    at = head // 2 * 2 * HEAD_DIM
    return jnp.where(row // HEAD_DIM == head % 2, rows[at : at + 2 * HEAD_DIM], 0.0).astype(
        jnp.bfloat16
    )


def unit_of(values):
    factor = lax.rsqrt(jnp.mean(values * values, axis=-1, keepdims=True) + EPSILON)
    return values * factor, factor


def prepare_heads(heads, query_ref, grad, mixed, q_pair, o_pair, o_rows, centre):
    grad = grad.astype(jnp.float32)
    grad_t = grad.T
    product = (grad * mixed.astype(jnp.float32)).T
    queries = query_ref[...].astype(jnp.float32)
    for h in range(heads):
        q_pair[h] = halves_of_pair(queries, h)
        o_pair[h] = halves_of_pair(grad, h)
        o_rows[h] = halves_of_rows(grad_t, h)
        centre[h : h + 1, :] = jnp.sum(
            product[h * HEAD_DIM : (h + 1) * HEAD_DIM], axis=0, keepdims=True
        )


def head_pair_back(p, keys, values, prob, q_pair, o_pair, o_rows, centre, keep_scores):
    low = jnp.bfloat16
    keys_t = keys.T
    query_parts = []
    for a in range(2):
        h = 2 * p + a
        prob_grad = mm(values, o_rows[h])
        weights = prob(h)
        score_grad = (weights * (prob_grad - centre[h : h + 1, :])).astype(low)
        if keep_scores is not None:
            keep_scores(h, score_grad)
        key_part = mm(score_grad, q_pair[h])
        value_part = mm(weights.astype(low), o_pair[h])
        key_grad = key_part if a == 0 else key_grad + key_part
        value_grad = value_part if a == 0 else value_grad + value_part
        query_parts.append(mm(keys_t[a * HEAD_DIM : (a + 1) * HEAD_DIM], score_grad))
    return key_grad.astype(low), value_grad.astype(low), query_parts


def backward_kernel(
    position_ref,
    exps_ref,
    scale_ref,
    kv_ref,
    states_ref,
    query_ref,
    mixed_ref,
    weights_ref,
    ff_ref,
    grad_ref,
    residual_ref,
    target_ref,
    gains_ref,
    qkv_ref,
    self_mixed_ref,
    self_exps_ref,
    self_scale_ref,
    bucket_ref,
    gain_ref,
    shard_ref,
    slots_ref,
    small_ref,
    target_grad_ref,
    exps,
    keys,
    grads,
    far_got,
    near_got,
    next_got,
    skip_got,
    dkv,
    outgoing,
    kept_sum,
    pair_got,
    slot_got,
    small,
    small_got,
    q_pair,
    o_pair,
    o_rows,
    centre,
    dq_t,
    row_sent,
    row_got,
    upper_grad,
    self_scores,
    exps_sem,
    keys_sem,
    far_send,
    far_recv,
    near_send,
    near_recv,
    next_send,
    next_recv,
    skip_send,
    skip_recv,
    pair_send,
    pair_recv,
    slot_send,
    slot_recv,
    small_send,
    small_recv,
    row_send,
    row_recv,
):
    low, wide = jnp.bfloat16, jnp.float32
    me, core, x, y, z, near, far = places()
    groups = shard_ref.shape[0]
    across_x, across_y = me + 1 - 2 * x, me + 2 - 4 * y
    kept = (1 - core) * y + core * x
    own_side = (1 - core) * x + core * y
    partner = (me, 1 - core)
    width = query_ref.shape[1]
    pairs = width // (2 * HEAD_DIM)
    heads = 2 * pairs
    block_rows = states_ref.shape[1] // CHIPS
    tile_rows = TILE * block_rows
    tiles = CHIPS // TILE
    half = states_ref.shape[2]

    def tile_at(t):
        return (t + me // TILE) % tiles

    def exps_copy(t):
        rows = pl.ds(tile_at(t) * tile_rows, tile_rows)
        return pltpu.make_async_copy(exps_ref.at[:, rows], exps.at[t % 2], exps_sem.at[t % 2])

    def keys_copy(t):
        rows = pl.ds(tile_at(t) * tile_rows, tile_rows)
        return pltpu.make_async_copy(kv_ref.at[rows], keys.at[t % 2], keys_sem.at[t % 2])

    exps_copy(0).start()
    keys_copy(0).start()
    greet_all(me, core)

    def source(g):
        return ff_ref.at[g - 2] if g >= 2 else grads.at[g]

    def block_at(k, o, side):
        return z_turned(z, k), (1 - core) * o + core * side, (1 - core) * side + core * o

    def far_copy(g, i, k):
        a, b, c = block_at(k, kept + (1 - i) * (1 - 2 * kept), 1 - own_side)
        return remote(
            source(g).at[a, b, c],
            far_got.at[g, i, k],
            far_send.at[g, i, k],
            far_recv.at[g, i, k],
            (far, core),
        )

    def far_start(g):
        for i in range(2):
            for k in range(3, -1, -1):
                far_copy(g, i, k).start()

    def near_copy(g, k):
        return remote(
            far_got.at[g, 0, k], near_got.at[g, k], near_send.at[g, k], near_recv.at[g, k], (near, core)
        )

    def next_copy(g, k):
        to = (me - 4 * z + 4 * z_turned(z, 2), core)
        return remote(
            near_got.at[g, 2 + k], next_got.at[g, k], next_send.at[g, k], next_recv.at[g, k], to
        )

    def skip_copy(g):
        to = (me - 4 * z + 4 * z_turned(z, 1), core)
        return remote(near_got.at[g, 1], skip_got.at[g], skip_send.at[g], skip_recv.at[g], to)

    def far_add(g):
        for k in range(3, -1, -1):
            far_copy(g, 0, k).wait_recv()
            a, b, c = block_at(k, 1 - kept, own_side)
            far_got[g, 0, k] = (
                source(g)[a, b, c].astype(wide) + far_got[g, 0, k].astype(wide)
            ).astype(low)
            near_copy(g, k).start()

    def near_add(g):
        for k in range(3, -1, -1):
            far_copy(g, 1, k).wait_recv()
            near_copy(g, k).wait_recv()
            a, b, c = block_at(k, kept, own_side)
            near_got[g, k] = (
                source(g)[a, b, c].astype(wide)
                + far_got[g, 1, k].astype(wide)
                + near_got[g, k].astype(wide)
            ).astype(low)
            if k >= 2:
                next_copy(g, k - 2).start()

    def next_add(g):
        next_copy(g, 1).wait_recv()
        near_got[g, 1] = (near_got[g, 1].astype(wide) + next_got[g, 1].astype(wide)).astype(low)
        skip_copy(g).start()

    def skip_add(g):
        next_copy(g, 0).wait_recv()
        skip_copy(g).wait_recv()
        shard_ref[g] = (
            near_got[g, 0].astype(wide) + next_got[g, 0].astype(wide) + skip_got[g].astype(wide)
        )

    def pair_copy(t):
        return remote(
            outgoing.at[t % 2],
            pair_got.at[tile_at(t)],
            pair_send.at[t % 2],
            pair_recv.at[t],
            partner,
        )

    def slot_copy(to):
        return remote(
            kept_sum.at[to], slot_got.at[me], slot_send.at[to], slot_recv.at[me], (to, core)
        )

    def slot_arrival(k):
        came = (me + k) % CHIPS
        return remote(
            kept_sum.at[came], slot_got.at[came], slot_send.at[came], slot_recv.at[came], (came, core)
        )

    def finish_tile(t):
        tile = tile_at(t)
        pair_copy(t).wait_recv()
        for j in range(TILE):
            to = tile * TILE + j
            rows = slice(j * block_rows, (j + 1) * block_rows)
            kept_sum[to] = (
                kept_sum[to].astype(wide) + pair_got[tile, rows].astype(wide)
            ).astype(low)

            @pl.when(to != me)
            def _():
                slot_copy(to).start()

            @pl.when(to == me)
            def _():
                slot_got[me] = kept_sum[me]

    def row_copy(i):
        return remote(row_sent.at[i], row_got.at[i], row_send.at[i], row_recv.at[i], partner)

    def store_grad(g, first, value):
        blocks = value.astype(low).reshape(grads.shape[1:5] + (value.shape[1],))
        grads[g, :, :, :, :, first : first + value.shape[1]] = blocks

    far_start(2)
    far_start(3)

    upper_grad[...] = grad_ref[...]
    grad_low = upper_grad[...].astype(low)
    store_grad(1, 3 * width, rows_tn(grad_low, mixed_ref[...]))
    mixed_grad = mm(grad_low, weights_ref[1, :, 3 * width :]).astype(low)
    prepare_heads(heads, query_ref, mixed_grad, mixed_ref[...], q_pair, o_pair, o_rows, centre)
    dq_t[...] = jnp.zeros_like(dq_t)

    def tile_step(t, carry):
        tile = tile_at(t)
        rows = pl.ds(pl.multiple_of(tile * tile_rows, tile_rows), tile_rows)

        @pl.when(t + 1 < tiles)
        def _():
            exps_copy(t + 1).start()
            keys_copy(t + 1).start()

        exps_copy(t).wait()
        keys_copy(t).wait()

        def prob(h):
            return exps[t % 2, h].astype(wide) * scale_ref[tile, h : h + 1, :]

        for p in range(pairs):
            at = 2 * HEAD_DIM * p
            key_grad, value_grad, query_parts = head_pair_back(
                p,
                keys[t % 2, :, at : at + 2 * HEAD_DIM],
                keys[t % 2, :, width + at : width + at + 2 * HEAD_DIM],
                prob,
                q_pair,
                o_pair,
                o_rows,
                centre,
                None,
            )
            dkv[rows, at : at + 2 * HEAD_DIM] = key_grad
            dkv[rows, width + at : width + at + 2 * HEAD_DIM] = value_grad
            for a in range(2):
                first = at + a * HEAD_DIM
                dq_t[first : first + HEAD_DIM, :] += query_parts[a]
        here = dkv[rows, :]

        @pl.when(t >= 2)
        def _():
            pair_copy(t - 2).wait_send()

        weights = weights_ref[1, pl.ds((1 - core) * half, half), width : 3 * width]
        outgoing[t % 2] = rows_nt(here, weights).astype(low)
        pair_copy(t).start()
        weights = weights_ref[1, pl.ds(core * half, half), width : 3 * width]
        mine = rows_nt(here, weights).astype(low)
        for j in range(TILE):
            kept_sum[tile * TILE + j] = mine[j * block_rows : (j + 1) * block_rows]

        @pl.when(t >= 1)
        def _():
            finish_tile(t - 1)

        @pl.when(t == 3)
        def _():
            far_add(2)

        @pl.when(t == 6)
        def _():
            far_add(3)

        return carry

    lax.fori_loop(0, tiles, tile_step, 0)
    dq = dq_t[...].T.astype(low)
    row_sent[0] = rows_nt(dq, weights_ref[1, :, :width])
    row_copy(0).start()
    finish_tile(tiles - 1)
    near_add(2)
    unit_two, factor_two = unit_of(residual_ref[...])
    normed_two = (unit_two * gains_ref[1:2, :]).astype(low)
    store_grad(1, 0, rows_tn(normed_two, dq))

    for n in range(2 * width // 256):
        columns = slice(n * 256, (n + 1) * 256)
        parts = [rows_tn(states_ref[i], dkv[:, columns]) for i in range(2)]
        store_grad(1, width + n * 256, jnp.concatenate(parts))
    far_start(1)
    next_add(2)
    near_add(3)

    row_copy(0).wait_recv()
    normed_grad = row_sent[0] + row_got[0]
    back, gain_two = rms_backward(normed_grad, unit_two, factor_two, gains_ref[1:2, :])
    upper_grad[...] += back

    grad_low = upper_grad[...].astype(low)
    store_grad(0, 3 * width, rows_tn(grad_low, self_mixed_ref[...]))
    mixed_grad = mm(grad_low, weights_ref[0, :, 3 * width :]).astype(low)
    prepare_heads(
        heads,
        qkv_ref.at[:, :width],
        mixed_grad,
        self_mixed_ref[...],
        q_pair,
        o_pair,
        o_rows,
        centre,
    )

    def self_prob(h):
        return self_exps_ref[h].astype(wide) * self_scale_ref[h : h + 1, :]

    def keep_scores(h, score_grad):
        self_scores[h] = score_grad

    query_rows, key_columns, value_columns = [], [], []
    for p in range(pairs):
        at = 2 * HEAD_DIM * p
        key_grad, value_grad, query_parts = head_pair_back(
            p,
            qkv_ref[:, width + at : width + at + 2 * HEAD_DIM],
            qkv_ref[:, 2 * width + at : 2 * width + at + 2 * HEAD_DIM],
            self_prob,
            q_pair,
            o_pair,
            o_rows,
            centre,
            keep_scores,
        )
        key_columns.append(key_grad)
        value_columns.append(value_grad)
        query_rows.extend(query_parts)
    dq = jnp.concatenate(query_rows, axis=0).T.astype(low)
    dqkv = jnp.concatenate([dq] + key_columns + value_columns, axis=1)
    row_sent[1] = rows_nt(dqkv, weights_ref[0, :, : 3 * width])
    row_copy(1).start()
    unit_one, factor_one = unit_of(target_ref[...].astype(wide))
    normed_one = (unit_one * gains_ref[0:1, :]).astype(low)
    store_grad(0, 0, rows_tn(normed_one, dqkv))
    far_start(0)
    far_add(1)
    next_add(3)

    length = self_scores.shape[1]

    def diagonal_step(i, total):
        rows = self_scores[:, pl.ds(pl.multiple_of(16 * i, 16), 16), :].astype(wide)
        rows = rows.reshape(heads * 16, length)
        return total + pltpu.roll(rows, (length - 16 * i) % length, 1)

    total = lax.fori_loop(
        0, length // 16, diagonal_step, jnp.zeros((heads * 16, length), wide)
    ).reshape(heads, 16, length)
    small[...] = jnp.zeros_like(small)
    for h in range(heads):
        line = total[h, 0:1]
        for s in range(1, 16):
            line = line + pltpu.roll(total[h, s : s + 1], length - s, 1)
        small[8 + h : 9 + h, :length] = line
    by_bucket = jnp.dot(
        small[8:16, :length], bucket_ref[...], precision=lax.Precision.HIGHEST,
        preferred_element_type=wide,
    )
    small[8:16, :length] = jnp.zeros((8, length), wide)
    small[8:16, : bucket_ref.shape[1]] = by_bucket

    row_copy(1).wait_recv()
    normed_grad = row_sent[1] + row_got[1]
    back, gain_one = rms_backward(normed_grad, unit_one, factor_one, gains_ref[0:1, :])
    target_grad_ref[...] = (upper_grad[...] + back).astype(low)
    small[0:1, :] = gain_one[None, :]
    small[1:2, :] = gain_two[None, :]
    small[2:3, :] = gain_ref[...]

    def small_copy(step):
        if step == 0:
            return remote(small, small_got.at[0], small_send.at[0], small_recv.at[0], (across_x, core))
        if step == 1:
            return remote(
                small_got.at[6], small_got.at[1], small_send.at[1], small_recv.at[1], (across_y, core)
            )
        return remote(
            small_got.at[7],
            small_got.at[2 + z],
            small_send.at[step],
            small_recv.at[step],
            ((me + 4 * (step - 1)) % CHIPS, core),
        )

    small_copy(0).start()
    skip_add(2)
    near_add(1)
    small_copy(0).wait_recv()
    small_got[6] = small[...] + small_got[0]
    small_copy(1).start()
    far_add(0)
    skip_add(3)
    next_add(1)
    small_copy(1).wait_recv()
    small_got[7] = small_got[6] + small_got[1]
    for step in range(2, 5):
        small_copy(step).start()
    small_got[2 + z] = small_got[7]
    near_add(0)
    skip_add(1)
    next_add(0)
    for step in range(2, 5):
        small_copy(step).wait_recv()
    small_ref[...] = small_got[2] + small_got[3] + small_got[4] + small_got[5]
    for k in range(1, CHIPS):
        slot_arrival(k).wait_recv()
    rows = slots_ref.shape[1]

    def pick(slot, carry):
        at = position_ref[slot]
        slots_ref[slot] = slot_got[at // RANKS, pl.ds(at % RANKS * rows, rows), :]
        return carry

    lax.fori_loop(0, slots_ref.shape[0], pick, 0)
    skip_add(0)
    for g in range(groups):
        for k in range(4):
            far_copy(g, 0, k).wait_send()
            far_copy(g, 1, k).wait_send()
            near_copy(g, k).wait_send()
        for k in range(2):
            next_copy(g, k).wait_send()
        skip_copy(g).wait_send()
    for t in range(tiles - 2, tiles):
        pair_copy(t).wait_send()
    for k in range(1, CHIPS):
        slot_copy((me + k) % CHIPS).wait_send()
    for step in range(5):
        small_copy(step).wait_send()
    for i in range(2):
        row_copy(i).wait_send()


def run_backward(
    position,
    exps,
    scale,
    key_values,
    states,
    queries,
    mixed,
    weights,
    ff_grads,
    grad,
    residual,
    target,
    gains,
    qkv,
    self_mixed,
    self_exps,
    self_scale,
    buckets,
    gain_three,
    slots,
):
    low, wide = jnp.bfloat16, jnp.float32
    groups = 4
    rows, columns = ff_grads.shape[-2:]
    heads = exps.shape[0]
    key_count, half = states.shape[1:]
    tokens, model = grad.shape
    block_rows = key_count // CHIPS
    tile_rows = TILE * block_rows
    width = queries.shape[1]
    small_shape = (16, model)
    vmem = pltpu.VMEM
    return pl.pallas_call(
        backward_kernel,
        out_shape=(
            jax.ShapeDtypeStruct((groups, rows, columns), wide),
            jax.ShapeDtypeStruct((slots, block_rows // RANKS, half), low),
            jax.ShapeDtypeStruct(small_shape, wide),
            jax.ShapeDtypeStruct((tokens, model), low),
        ),
        in_specs=[IN_SMEM, ANY, IN_VMEM, ANY] + [IN_VMEM] * 15,
        out_specs=(IN_VMEM,) * 4,
        scratch_shapes=[
            vmem((2, heads, tile_rows, tokens), low),
            vmem((2, tile_rows, 2 * width), low),
            vmem((2, 4, 2, 2, rows, columns), low),
            vmem((groups, 2, 4, rows, columns), low),
            vmem((groups, 4, rows, columns), low),
            vmem((groups, 2, rows, columns), low),
            vmem((groups, rows, columns), low),
            vmem((key_count, 2 * width), low),
            vmem((2, tile_rows, half), low),
            vmem((CHIPS, block_rows, half), low),
            vmem((CHIPS // TILE, tile_rows, half), low),
            vmem((CHIPS, block_rows, half), low),
            vmem(small_shape, wide),
            vmem((8,) + small_shape, wide),
            vmem((heads, tokens, 2 * HEAD_DIM), low),
            vmem((heads, tokens, 2 * HEAD_DIM), low),
            vmem((heads, 2 * HEAD_DIM, tokens), low),
            vmem((8, tokens), wide),
            vmem((width, tokens), wide),
            vmem((2, tokens, model), wide),
            vmem((2, tokens, model), wide),
            vmem((tokens, model), wide),
            vmem((heads, tokens, tokens), low),
            DMA((2,)),
            DMA((2,)),
            DMA((groups, 2, 4)),
            DMA((groups, 2, 4)),
            DMA((groups, 4)),
            DMA((groups, 4)),
            DMA((groups, 2)),
            DMA((groups, 2)),
            DMA((groups,)),
            DMA((groups,)),
            DMA((2,)),
            DMA((CHIPS // TILE,)),
            DMA((CHIPS,)),
            DMA((CHIPS,)),
            DMA((5,)),
            DMA((5,)),
            DMA((2,)),
            DMA((2,)),
        ],
        compiler_params=pltpu.CompilerParams(
            collective_id=2, has_side_effects=True, vmem_limit_bytes=62 * 2**20
        ),
    )(
        position,
        exps,
        scale,
        key_values,
        states,
        queries,
        mixed,
        weights,
        ff_grads,
        grad,
        residual,
        target,
        gains,
        qkv,
        self_mixed,
        self_exps,
        self_scale,
        buckets,
        gain_three,
    )


def z_turned(z, k):
    high, low = z // 2, z % 2
    if k % 2:
        high = 1 - high
    if k // 2:
        low = 1 - low
    return 2 * high + low


def exp_rows(scores):
    highest = jnp.max(scores, axis=0, keepdims=True)
    exps = jnp.exp(scores - highest)
    return exps, highest, jnp.sum(exps, axis=0, keepdims=True)


def gelu_both(values):
    first = math.sqrt(2 / math.pi)
    square = values * values
    curve = jnp.tanh(first * values * (1.0 + 0.044715 * square))
    half = 0.5 * (1.0 + curve)
    slope = half + 0.5 * values * (1.0 - curve * curve) * first * (1.0 + 3 * 0.044715 * square)
    return values * half, slope


def forward_kernel(
    index_ref,
    shard_ref,
    passage_ref,
    flag_ref,
    target_ref,
    cotangent_ref,
    gains_ref,
    table_ref,
    bucket_ref,
    weights_ref,
    states_out,
    exps_out,
    kv_out,
    scale_ref,
    query_ref,
    mixed_ref,
    residual_ref,
    qkv_ref,
    self_mixed_ref,
    self_exps_ref,
    self_scale_ref,
    ff_ref,
    grad_ref,
    gain_ref,
    block_ref,
    full,
    states,
    flags,
    outgoing,
    exps,
    keys,
    bias,
    q_rows,
    out_t,
    highest,
    total,
    tile_highest,
    row_sent,
    row_got,
    skip_send,
    skip_recv,
    next_send,
    next_recv,
    near_send,
    near_recv,
    first_send,
    first_recv,
    second_send,
    second_recv,
    slot_send,
    slot_recv,
    flag_send,
    flag_recv,
    core_send,
    core_recv,
    row_send,
    row_recv,
    own_sem,
    exps_sem,
    keys_sem,
    out_sem,
):
    low, wide = jnp.bfloat16, jnp.float32
    me, core, x, y, z, near, far = places()
    groups = shard_ref.shape[0]
    partner = (me, 1 - core)
    pair = me // TILE
    tiles = CHIPS // TILE
    block_rows = states.shape[2]
    passage_len = block_rows // RANKS
    tile_rows = TILE * block_rows
    tokens = target_ref.shape[0]
    width = query_ref.shape[1]
    pairs = width // (2 * HEAD_DIM)
    heads = 2 * pairs
    half = states.shape[3]
    other_y = y + (1 - core) * (1 - 2 * y)
    other_x = x + core * (1 - 2 * x)

    def own_copy(g):
        return pltpu.make_async_copy(shard_ref.at[g], full.at[g, z, y, x], own_sem.at[g])

    def z_at(k):
        return z_turned(z, k)

    def skip_copy(g):
        dst = full.at[g, z, y, x]
        return remote(
            shard_ref.at[g], dst, skip_send.at[g], skip_recv.at[g], (me - 4 * z + 4 * z_at(1), core)
        )

    def next_copy(g, k):
        dst = full.at[g, z_at(k), y, x]
        to = (me - 4 * z + 4 * z_at(2), core)
        return remote(held(g, k), dst, next_send.at[g, k], next_recv.at[g, k], to)

    def held(g, k):
        return shard_ref.at[g] if k == 0 else full.at[g, z_at(k), y, x]

    def near_copy(g, k):
        dst = full.at[g, z_at(k), y, x]
        return remote(held(g, k), dst, near_send.at[g, k], near_recv.at[g, k], (near, core))

    def first_copy(g, k):
        dst = full.at[g, z_at(k), y, x]
        return remote(held(g, k), dst, first_send.at[g, k], first_recv.at[g, k], (far, core))

    def second_copy(g, k):
        block = full.at[g, z_at(k), other_y, other_x]
        return remote(block, block, second_send.at[g, k], second_recv.at[g, k], (far, core))

    def slot_copy(to):
        return remote(
            outgoing.at[to], states.at[core, me], slot_send.at[to], slot_recv.at[me], (to, core)
        )

    def slot_arrival(came):
        block = states.at[core, came]
        return remote(block, block, slot_send.at[came], slot_recv.at[came], (came, core))

    def flag_copy(to):
        return remote(flag_ref.at[to], flags.at[me], flag_send.at[to], flag_recv.at[me], (to, core))

    def flag_arrival(came):
        block = flags.at[came]
        return remote(block, block, flag_send.at[came], flag_recv.at[came], (came, core))

    def core_copy(came):
        block = states.at[core, came]
        return remote(block, block, core_send.at[came], core_recv.at[came], partner)

    def row_copy(i):
        return remote(row_sent.at[i], row_got.at[i], row_send.at[i], row_recv.at[i], partner)

    def pair_sum(i):
        row_copy(i).wait_recv()
        return row_sent[i] + row_got[i]

    def launch(g):
        skip_copy(g).start()
        next_copy(g, 0).start()
        near_copy(g, 0).start()
        first_copy(g, 0).start()
        own_copy(g).start()

    def relay_skip(g):
        skip_copy(g).wait_recv()
        next_copy(g, 1).start()
        near_copy(g, 1).start()
        first_copy(g, 1).start()

    def relay_next(g):
        for k in range(2):
            next_copy(g, k).wait_recv()
            near_copy(g, k + 2).start()
            first_copy(g, k + 2).start()

    def relay_near(g):
        for k in range(4):
            near_copy(g, k).wait_recv()
            second_copy(g, k).start()

    def arrived(g):
        own_copy(g).wait()
        for k in range(4):
            first_copy(g, k).wait_recv()
            second_copy(g, k).wait_recv()

    def weight(g):
        return full[g].reshape(full.shape[1] * 4 * full.shape[4], full.shape[5])

    def weights_copy(g):
        return pltpu.make_async_copy(full.at[g], weights_ref.at[g], out_sem.at[g])

    greet_all(me, core)
    def send_pair(j):
        for i in range(TILE):
            to = (pair + j) % tiles * TILE + i

            @pl.when(to != me)
            def _():
                flag_copy(to).start()
                slot_copy(to).start()

    launch(0)

    def fill(to, carry):
        for rank in range(RANKS):
            outgoing[to, rank * passage_len : (rank + 1) * passage_len, :] = passage_ref[
                index_ref[to * RANKS + rank]
            ]
        return carry

    lax.fori_loop(0, CHIPS, fill, 0)
    send_pair(0)
    launch(1)
    send_pair(1)
    send_pair(2)
    states[core, me] = outgoing[me]
    flags[me] = flag_ref[me]
    core_copy(me).start()

    line = jnp.dot(
        table_ref[...], bucket_ref[...], precision=lax.Precision.HIGHEST, preferred_element_type=wide
    )
    for h in range(heads):
        for s in range(8):
            row = line[h : h + 1]
            bias[h, s : s + 1, :] = row if s == 0 else pltpu.roll(row, s, 1)
    base = bias[:, 0:8, :].reshape(heads * 8, tokens)

    def bias_step(i, carry):
        rows = pltpu.roll(base, 8 * i, 1).reshape(heads, 8, tokens)
        bias[:, pl.ds(pl.multiple_of(8 * i, 8), 8), :] = rows
        return carry

    lax.fori_loop(1, tokens // 8, bias_step, 0)
    residual = target_ref[...].astype(wide)
    normed = (unit_of(residual)[0] * gains_ref[0:1, :]).astype(low)

    relay_skip(0)
    send_pair(3)
    launch(2)
    relay_next(0)
    relay_near(0)
    relay_skip(1)
    send_pair(4)
    relay_next(1)
    arrived(0)

    qkv_ref[...] = mm(normed, weight(0)[:, : 3 * width]).astype(low)
    weights_copy(0).start()
    relay_near(1)
    relay_skip(2)
    queries_t = qkv_ref[:, :width].astype(wide).T
    for h in range(heads):
        q_rows[h] = halves_of_rows(queries_t, h)
    key_at = lax.broadcasted_iota(jnp.int32, (tokens, tokens), 0)
    query_at = lax.broadcasted_iota(jnp.int32, (tokens, tokens), 1)
    self_scale_ref[...] = jnp.zeros_like(self_scale_ref)
    for p in range(pairs):
        at = 2 * HEAD_DIM * p
        head_keys = qkv_ref[:, width + at : width + at + 2 * HEAD_DIM]
        values_t = qkv_ref[:, 2 * width + at : 2 * width + at + 2 * HEAD_DIM].T
        for a in range(2):
            h = 2 * p + a
            scores = mm(head_keys, q_rows[h]) + bias[h]
            scores = jnp.where(key_at <= query_at, scores, MASKED)
            head_exps, unused, sums = exp_rows(scores)
            head_exps = head_exps.astype(low)
            self_exps_ref[h] = head_exps
            inverse = 1.0 / sums
            self_scale_ref[h : h + 1, :] = inverse
            first = at + a * HEAD_DIM
            out_t[first : first + HEAD_DIM, :] = (
                mm(values_t[a * HEAD_DIM : (a + 1) * HEAD_DIM], head_exps) * inverse
            )
    self_mixed_ref[...] = out_t[...].T.astype(low)
    row_sent[0] = rows_nt(self_mixed_ref[...], weight(0)[:, 3 * width :])
    row_copy(0).start()
    launch(3)
    send_pair(5)
    arrived(1)
    weights_copy(1).start()
    residual_ref[...] = residual + pair_sum(0)

    normed = (unit_of(residual_ref[...])[0] * gains_ref[1:2, :]).astype(low)
    query_ref[...] = mm(normed, weight(1)[:, :width]).astype(low)
    queries_t = query_ref[...].astype(wide).T
    for h in range(heads):
        q_rows[h] = halves_of_rows(queries_t, h)
    out_t[...] = jnp.zeros_like(out_t)
    highest[...] = jnp.full_like(highest, MASKED)
    total[...] = jnp.zeros_like(total)
    tile_highest[...] = jnp.zeros_like(tile_highest)

    def take_in(t):
        for i in range(TILE):
            came = (pair - t + tiles) % tiles * TILE + i

            @pl.when(came != me)
            def _():
                flag_arrival(came).wait_recv()
                slot_arrival(came).wait_recv()
                core_copy(came).start()

    def exps_copy(t):
        rows = pl.ds((pair - t + tiles) % tiles * tile_rows, tile_rows)
        return pltpu.make_async_copy(exps.at[t % 2], exps_out.at[:, rows], exps_sem.at[t % 2])

    def keys_copy(t):
        rows = pl.ds((pair - t + tiles) % tiles * tile_rows, tile_rows)
        return pltpu.make_async_copy(keys.at[t % 2], kv_out.at[rows], keys_sem.at[t % 2])

    send_pair(6)
    send_pair(7)
    take_in(0)

    def tile_step(t, carry):
        tile = (pair - t + tiles) % tiles

        @pl.when(t == 5)
        def _():
            relay_skip(3)

        @pl.when(t == 6)
        def _():
            relay_next(3)

        @pl.when(t + 1 < tiles)
        def _():
            take_in(t + 1)

        @pl.when(t == 2)
        def _():
            relay_next(2)

        @pl.when(t == 3)
        def _():
            relay_near(2)

        @pl.when(t >= 2)
        def _():
            exps_copy(t - 2).wait()
            keys_copy(t - 2).wait()

        for i in range(TILE):
            core_copy(tile * TILE + i).wait_recv()
        kv_parts = []
        for c in range(2):
            rows = states[c, pl.ds(tile * TILE, TILE)].reshape(tile_rows, half)
            w = full[1, 2 * c : 2 * c + 2, :, :, :, width : 3 * width]
            kv_parts.append(mm(rows, w.reshape(half, 2 * width)))
        keys[t % 2] = (kv_parts[0] + kv_parts[1]).astype(low)
        keys_copy(t).start()
        masks = []
        for i in range(TILE):
            for rank in range(RANKS):
                masks.append(flags[tile * TILE + i, rank : rank + 1, :].astype(wide)[None])
        masks = jnp.concatenate(masks, axis=0)
        for p in range(pairs):
            at = 2 * HEAD_DIM * p
            head_keys = keys[t % 2, :, at : at + 2 * HEAD_DIM]
            values_t = keys[t % 2, :, width + at : width + at + 2 * HEAD_DIM].T
            for a in range(2):
                h = 2 * p + a
                scores = mm(head_keys, q_rows[h]).reshape(TILE * RANKS, passage_len, tokens) + masks
                head_exps, top, sums = exp_rows(scores.reshape(tile_rows, tokens))
                head_exps = head_exps.astype(low)
                exps[t % 2, h] = head_exps
                before = highest[h : h + 1, :]
                now = jnp.maximum(before, top)
                keep, add = jnp.exp(before - now), jnp.exp(top - now)
                highest[h : h + 1, :] = now
                tile_highest[tile, h : h + 1, :] = top
                total[h : h + 1, :] = total[h : h + 1, :] * keep + sums * add
                first = at + a * HEAD_DIM
                out_t[first : first + HEAD_DIM, :] = (
                    out_t[first : first + HEAD_DIM, :] * keep
                    + mm(values_t[a * HEAD_DIM : (a + 1) * HEAD_DIM], head_exps) * add
                )
        exps_copy(t).start()

        return carry

    lax.fori_loop(0, tiles, tile_step, 0)
    relay_near(3)
    states_copy = pltpu.make_async_copy(states, states_out, out_sem.at[2])
    states_copy.start()
    for h in range(heads):
        inverse = 1.0 / total[h : h + 1, :]
        out_t[h * HEAD_DIM : (h + 1) * HEAD_DIM, :] *= inverse
        scale_ref[:, h, :] = jnp.exp(tile_highest[:, h, :] - highest[h : h + 1, :]) * inverse
    mixed_ref[...] = out_t[...].T.astype(low)
    row_sent[1] = rows_nt(mixed_ref[...], weight(1)[:, 3 * width :])
    row_copy(1).start()
    residual_three = residual_ref[...] + pair_sum(1)
    unit, factor = unit_of(residual_three)
    normed = (unit * gains_ref[2:3, :]).astype(low)

    def store_grad(i, value):
        ff_ref[i] = value.astype(low).reshape(ff_ref.shape[1:])

    arrived(2)
    hidden, slope = gelu_both(mm(normed, weight(2)))
    hidden = hidden.astype(low)
    arrived(3)
    hidden_grad = mm(cotangent_ref[...], weight(3))
    before_grad = (hidden_grad * slope).astype(low)
    row_sent[2] = rows_nt(before_grad, weight(2))
    row_copy(2).start()
    row_sent[3] = rows_nt(hidden, weight(3))
    row_copy(3).start()
    store_grad(0, rows_tn(normed, before_grad))
    store_grad(1, rows_tn(cotangent_ref[...], hidden))
    back, gain = rms_backward(pair_sum(2), unit, factor, gains_ref[2:3, :])
    grad_ref[...] = cotangent_ref[...].astype(wide) + back
    gain_ref[...] = gain[None, :]
    block_ref[...] = (residual_three + pair_sum(3)).astype(low)

    for g in range(groups):
        skip_copy(g).wait_send()
        for k in range(2):
            next_copy(g, k).wait_send()
        for k in range(4):
            near_copy(g, k).wait_send()
            first_copy(g, k).wait_send()
            second_copy(g, k).wait_send()
    for k in range(1, CHIPS):
        to = (me + k) % CHIPS
        slot_copy(to).wait_send()
        flag_copy(to).wait_send()
    for k in range(CHIPS):
        core_copy(k).wait_send()
    for i in range(4):
        row_copy(i).wait_send()
    for t in range(tiles - 2, tiles):
        exps_copy(t).wait()
        keys_copy(t).wait()
    for g in range(2):
        weights_copy(g).wait()
    states_copy.wait()


def run_forward(index, shards, passages, flags, target, cotangent, gains, table, buckets):
    low, wide = jnp.bfloat16, jnp.float32
    groups, rows, columns = shards.shape
    passage_len, half = passages.shape[1:]
    tokens, model = target.shape
    width = columns // 4
    heads = width // HEAD_DIM
    block_rows = RANKS * passage_len
    key_count = CHIPS * block_rows
    tile_rows = TILE * block_rows
    tiles = CHIPS // TILE
    shape = jax.ShapeDtypeStruct
    vmem = pltpu.VMEM
    return pl.pallas_call(
        forward_kernel,
        out_shape=(
            shape((2, 4, 2, 2, rows, columns), low),
            shape((2, CHIPS, block_rows, half), low),
            shape((heads, key_count, tokens), low),
            shape((key_count, 2 * width), low),
            shape((tiles, 8, tokens), wide),
            shape((tokens, width), low),
            shape((tokens, width), low),
            shape((tokens, model), wide),
            shape((tokens, 3 * width), low),
            shape((tokens, width), low),
            shape((heads, tokens, tokens), low),
            shape((8, tokens), wide),
            shape((2, 4, 2, 2, rows, columns), low),
            shape((tokens, model), wide),
            shape((1, model), wide),
            shape((tokens, model), low),
        ),
        in_specs=[IN_SMEM] + [IN_VMEM] * 8,
        out_specs=(ANY,) * 4 + (IN_VMEM,) * 12,
        scratch_shapes=[
            vmem((groups, 4, 2, 2, rows, columns), low),
            vmem((2, CHIPS, block_rows, half), low),
            vmem((CHIPS, FLAG_ROWS, tokens), low),
            vmem((CHIPS, block_rows, half), low),
            vmem((2, heads, tile_rows, tokens), low),
            vmem((2, tile_rows, 2 * width), low),
            vmem((heads, tokens, tokens), wide),
            vmem((heads, 2 * HEAD_DIM, tokens), low),
            vmem((width, tokens), wide),
            vmem((8, tokens), wide),
            vmem((8, tokens), wide),
            vmem((tiles, 8, tokens), wide),
            vmem((4, tokens, model), wide),
            vmem((4, tokens, model), wide),
            DMA((groups,)),
            DMA((groups,)),
            DMA((groups, 2)),
            DMA((groups, 2)),
            DMA((groups, 4)),
            DMA((groups, 4)),
            DMA((groups, 4)),
            DMA((groups, 4)),
            DMA((groups, 4)),
            DMA((groups, 4)),
            DMA((CHIPS,)),
            DMA((CHIPS,)),
            DMA((CHIPS,)),
            DMA((CHIPS,)),
            DMA((CHIPS,)),
            DMA((CHIPS,)),
            DMA((4,)),
            DMA((4,)),
            DMA((groups,)),
            DMA((2,)),
            DMA((2,)),
            DMA((3,)),
        ],
        compiler_params=pltpu.CompilerParams(
            collective_id=0, has_side_effects=True, vmem_limit_bytes=VMEM_LIMIT
        ),
    )(index, shards, passages, flags, target, cotangent, gains, table, buckets)


def route(slot_query, slot_live):
    matching = slot_query[:, None] == slot_query[None, :]
    earlier = jnp.tril(jnp.ones(matching.shape, jnp.bool_), -1)
    position = slot_query * RANKS + jnp.sum(jnp.logical_and(matching, earlier), axis=1).astype(
        jnp.int32
    )
    here = position[None, :] == jnp.arange(CHIPS * RANKS, dtype=jnp.int32)[:, None]
    slots = slot_query.shape[0]
    index = jnp.sum(jnp.where(here, jnp.arange(slots, dtype=jnp.int32)[None, :], 0), axis=1)
    live = jnp.sum(jnp.where(here, slot_live[None, :], 0), axis=1)
    return position, index, live


def body(
    target_states,
    passage_states,
    slot_query,
    slot_live,
    norm_gains,
    self_query,
    self_key,
    self_value,
    self_output,
    position_bias,
    cross_query,
    cross_key,
    cross_value,
    cross_output,
    expand_weight,
    reduce_weight,
    output_cotangent,
):
    low = jnp.bfloat16
    width_here = self_query.shape[1]
    heads_here = width_here // HEAD_DIM
    slots_here, passage_len, half = passage_states.shape
    bucket_count = position_bias.shape[0]
    shards = jnp.stack(
        [
            jnp.concatenate([self_query, self_key, self_value, self_output.T], axis=1),
            jnp.concatenate([cross_query, cross_key, cross_value, cross_output.T], axis=1),
            expand_weight,
            reduce_weight.T,
        ]
    )
    position, index, live = route(slot_query, slot_live)
    flags = jnp.where(live > 0, 0.0, MASKED).astype(low).reshape(CHIPS, RANKS, 1)
    flags = jnp.pad(flags, ((0, 0), (0, FLAG_ROWS - RANKS), (0, 0)))
    flags = jnp.broadcast_to(flags, (CHIPS, FLAG_ROWS, TLEN))
    distance = np.zeros((TLEN, 128), np.float32)
    distance[np.arange(TLEN), bucket_table(TLEN, bucket_count, MAXDIST)[:, 0]] = 1.0
    table = jnp.pad(position_bias.T, ((0, 8 - heads_here), (0, 0)))
    (
        weights,
        states,
        exps,
        key_values,
        scale,
        queries,
        mixed,
        residual,
        qkv,
        self_mixed,
        self_exps,
        self_scale,
        ff_grads,
        grad,
        gain,
        block_out,
    ) = run_forward(
        index,
        shards,
        passage_states,
        flags,
        target_states,
        output_cotangent,
        norm_gains,
        table,
        jnp.asarray(distance[:, :bucket_count].T),
    )
    w = width_here
    weights = weights.reshape(2, -1, weights.shape[-1])
    shard_grads, passage_grad, small_total, target_grad = run_backward(
        position,
        exps,
        scale,
        key_values,
        states.reshape(2, -1, half),
        queries,
        mixed,
        weights,
        ff_grads,
        grad,
        residual,
        target_states,
        norm_gains,
        qkv,
        self_mixed,
        self_exps,
        self_scale,
        jnp.asarray(distance),
        gain,
        slots_here,
    )
    first, second = shard_grads[0], shard_grads[1]
    return (
        block_out,
        target_grad,
        passage_grad,
        small_total[:3],
        first[:, :w],
        first[:, w : 2 * w],
        first[:, 2 * w : 3 * w],
        first[:, 3 * w :].T,
        small_total[8 : 8 + heads_here, :bucket_count].T,
        second[:, :w],
        second[:, w : 2 * w],
        second[:, 2 * w : 3 * w],
        second[:, 3 * w :].T,
        shard_grads[2],
        shard_grads[3].T,
    )


def solution(mesh):
    return jax.shard_map(
        body if fits(mesh) else body_any,
        mesh=mesh,
        in_specs=(
            P("pas", None),
            P("pas", None, "mdl"),
            P("pas"),
            P("pas"),
            P(),
            P("pas", "mdl"),
            P("pas", "mdl"),
            P("pas", "mdl"),
            P("mdl", "pas"),
            P(None, "mdl"),
            P("pas", "mdl"),
            P("pas", "mdl"),
            P("pas", "mdl"),
            P("mdl", "pas"),
            P("pas", "mdl"),
            P("mdl", "pas"),
            P("pas", None),
        ),
        out_specs=(
            P("pas", None),
            P("pas", None),
            P("pas", None, "mdl"),
            P(),
            P("pas", "mdl"),
            P("pas", "mdl"),
            P("pas", "mdl"),
            P("mdl", "pas"),
            P(None, "mdl"),
            P("pas", "mdl"),
            P("pas", "mdl"),
            P("pas", "mdl"),
            P("mdl", "pas"),
            P("pas", "mdl"),
            P("mdl", "pas"),
        ),
        check_vma=False,
    )
```

```python
from functools import partial
import math

import jax
import jax.numpy as jnp
import numpy as np
from jax import lax
from jax.experimental import pallas as pl
from jax.experimental.pallas import tpu as pltpu
from jax.sharding import PartitionSpec as P

HEAD_DIM = 64
MAXDIST = 128
TLEN = 256
PQ = 40


EPSILON = 1e-06
MASKED = -1e30


def bucket_table(length, buckets, distance):
    later = np.arange(length)[:, None]
    earlier = np.arange(length)[None, :]
    behind = np.maximum(later - earlier, 0)
    exact = buckets // 2
    spread = np.log(np.maximum(behind, 1) / exact) / math.log(distance / exact) * (buckets - exact)
    far_bucket = np.minimum(exact + np.floor(spread).astype(np.int32), buckets - 1)
    return np.where(behind < exact, behind, far_bucket).astype(np.int32)


def rms_forward(values, gain):
    factor = lax.rsqrt(jnp.mean(values * values, axis=-1, keepdims=True) + EPSILON)
    unit_rows = values * factor
    return (unit_rows, factor, (unit_rows * gain).astype(jnp.bfloat16))


def rms_backward(normed_grad, unit_rows, factor, gain):
    scaled_grad = normed_grad * gain
    input_grad = factor * (
        scaled_grad - unit_rows * jnp.mean(scaled_grad * unit_rows, axis=-1, keepdims=True)
    )
    return (input_grad, jnp.sum(normed_grad * unit_rows, axis=0))


def over_heads(partial_rows):
    return lax.psum(partial_rows, "mdl")


def score_block(queries, key_rows, allowed, bias):
    scores = jnp.einsum("sihe,sjhe->shij", queries, key_rows, preferred_element_type=jnp.float32)
    if bias is not None:
        scores = scores + bias
    return jnp.where(allowed, scores, MASKED)


def attend(queries, key_rows, values, allowed, bias):
    scores = score_block(queries, key_rows, allowed, bias)
    highest = jnp.max(scores, axis=-1, keepdims=True)
    totals = highest + jnp.log(jnp.sum(jnp.exp(scores - highest), axis=-1, keepdims=True))
    probability = jnp.exp(scores - totals)
    mixed = jnp.einsum(
        "shij,sjhe->sihe",
        probability.astype(jnp.bfloat16),
        values,
        preferred_element_type=jnp.float32,
    )
    return (mixed.astype(jnp.bfloat16), totals)


def attend_back(queries, key_rows, values, allowed, bias, totals, out_grad):
    scores = score_block(queries, key_rows, allowed, bias)
    probability = jnp.exp(scores - totals)
    prob_grad = jnp.einsum("sihe,sjhe->shij", out_grad, values, preferred_element_type=jnp.float32)
    centered = jnp.sum(probability * prob_grad, axis=-1, keepdims=True)
    score_grad = (probability * (prob_grad - centered)).astype(jnp.bfloat16)
    query_grad = jnp.einsum(
        "shij,sjhe->sihe", score_grad, key_rows, preferred_element_type=jnp.float32
    )
    key_grad = jnp.einsum(
        "shij,sihe->sjhe", score_grad, queries, preferred_element_type=jnp.float32
    )
    value_grad = jnp.einsum(
        "shij,sihe->sjhe",
        probability.astype(jnp.bfloat16),
        out_grad,
        preferred_element_type=jnp.float32,
    )
    return (query_grad, key_grad, value_grad, score_grad)


def send_plan(slot_query, slot_live, per_device, capacity):
    target_device = slot_query // per_device
    matching = target_device[:, None] == target_device[None, :]
    lower_part = jnp.tril(jnp.ones(matching.shape, jnp.bool_), -1)
    ranking = jnp.sum(jnp.logical_and(matching, lower_part), axis=1)
    position = target_device * capacity + ranking
    codes = jnp.where(slot_live > 0, slot_query % per_device + 1, 0).astype(jnp.bfloat16)
    return (position, codes)


def arrange_plan(got_codes, per_device, slots_each):
    local_query = got_codes.astype(jnp.int32) - 1
    matches = (local_query[:, None] == jnp.arange(per_device, dtype=jnp.int32)[None, :]).astype(
        jnp.int32
    )
    ranking = jnp.sum((jnp.cumsum(matches, axis=0) - 1) * matches, axis=1)
    spare_place = per_device * slots_each
    places = jnp.where(local_query >= 0, local_query * slots_each + ranking, spare_place)
    arrivals = got_codes.shape[0]
    gather_index = (
        jnp.zeros((spare_place + 1,), jnp.int32)
        .at[places]
        .set(jnp.arange(arrivals, dtype=jnp.int32))
    )
    valid_slot = jnp.zeros((spare_place + 1,), jnp.int32).at[places].set(1)
    return (gather_index[:spare_place], valid_slot[:spare_place] > 0)


def place_rows(rows, position, total_rows):
    return jnp.zeros((total_rows,) + rows.shape[1:], rows.dtype).at[position].set(rows)


def return_rows(rows, gather_index, total_rows):
    return jnp.zeros((total_rows,) + rows.shape[1:], rows.dtype).at[gather_index].add(rows)


def body_any(
    target_states,
    passage_states,
    slot_query,
    slot_live,
    norm_gains,
    self_query,
    self_key,
    self_value,
    self_output,
    position_bias,
    cross_query,
    cross_key,
    cross_value,
    cross_output,
    expand_weight,
    reduce_weight,
    output_cotangent,
):
    (
        query_full,
        key_full,
        value_full,
        cross_query_full,
        cross_key_full,
        cross_value_full,
        expand_full,
    ) = (
        lax.all_gather(self_query, "pas", axis=0, tiled=True),
        lax.all_gather(self_key, "pas", axis=0, tiled=True),
        lax.all_gather(self_value, "pas", axis=0, tiled=True),
        lax.all_gather(cross_query, "pas", axis=0, tiled=True),
        lax.all_gather(cross_key, "pas", axis=0, tiled=True),
        lax.all_gather(cross_value, "pas", axis=0, tiled=True),
        lax.all_gather(expand_weight, "pas", axis=0, tiled=True),
    )
    output_full, cross_output_full, reduce_full = (
        lax.all_gather(self_output, "pas", axis=1, tiled=True),
        lax.all_gather(cross_output, "pas", axis=1, tiled=True),
        lax.all_gather(reduce_weight, "pas", axis=1, tiled=True),
    )
    width_here = query_full.shape[1]
    heads_here = width_here // HEAD_DIM
    sequences = target_states.shape[0] // TLEN
    passage_len = passage_states.shape[1]
    bucket_count = position_bias.shape[0]
    devices = lax.axis_size("pas")
    slots_here = slot_query.shape[0]
    capacity = -(-slots_here // devices)
    buffer_rows = devices * capacity
    residual = target_states.astype(jnp.float32)
    unit_one, factor_one, normed_one = rms_forward(residual, norm_gains[0])
    self_weights = jnp.concatenate([query_full, key_full, value_full], axis=1)
    projected = jnp.dot(normed_one, self_weights, preferred_element_type=jnp.float32).astype(
        jnp.bfloat16
    )
    projected = projected.reshape(sequences, TLEN, 3, heads_here, HEAD_DIM)
    queries_self = projected[:, :, 0]
    keys_self = projected[:, :, 1]
    values_self = projected[:, :, 2]
    buckets = jnp.asarray(bucket_table(TLEN, bucket_count, MAXDIST))
    one_hot = (jnp.arange(bucket_count, dtype=jnp.int32)[:, None, None] == buckets[None]).astype(
        jnp.float32
    )
    bias_full = jnp.einsum("bij,bh->hij", one_hot, position_bias, precision=lax.Precision.HIGHEST)[
        None
    ]
    causal = jnp.asarray(np.tril(np.ones((TLEN, TLEN), dtype=bool)))
    attended_self, total_self = attend(queries_self, keys_self, values_self, causal, bias_full)
    merged_self = attended_self.reshape(sequences * TLEN, width_here)
    residual_two = residual + over_heads(
        jnp.dot(merged_self, output_full, preferred_element_type=jnp.float32)
    )
    unit_two, factor_two, normed_two = rms_forward(residual_two, norm_gains[1])
    cross_queries = jnp.dot(
        normed_two, cross_query_full, preferred_element_type=jnp.float32
    ).astype(jnp.bfloat16)
    cross_queries = cross_queries.reshape(sequences, TLEN, heads_here, HEAD_DIM)
    kv_weights = jnp.concatenate([cross_key_full, cross_value_full], axis=1)
    position, codes = send_plan(slot_query, slot_live, sequences, capacity)
    sent_codes = place_rows(codes, position, buffer_rows)
    states_full = lax.all_gather(passage_states, "mdl", axis=2, tiled=True)
    key_values = jnp.einsum(
        "tpd,dc->tpc", states_full, kv_weights, preferred_element_type=jnp.float32
    ).astype(jnp.bfloat16)
    received, got_codes = (
        lax.all_to_all(
            place_rows(key_values, position, buffer_rows),
            "pas",
            split_axis=0,
            concat_axis=0,
            tiled=True,
        ),
        lax.all_to_all(sent_codes, "pas", split_axis=0, concat_axis=0, tiled=True),
    )
    gather_index, valid_slot = arrange_plan(got_codes, sequences, PQ)
    arranged = jnp.take(received, gather_index, axis=0)
    arranged = arranged.reshape(sequences, PQ * passage_len, 2, heads_here, HEAD_DIM)
    key_rows = arranged[:, :, 0]
    value_rows = arranged[:, :, 1]
    allowed = jnp.repeat(valid_slot.reshape(sequences, PQ), passage_len, axis=1)[:, None, None, :]
    head_block = 2
    head_ranges = [
        slice(start_head, start_head + head_block)
        for start_head in range(0, heads_here, head_block)
    ]
    cross_parts = []
    cross_totals = []
    for head_range in head_ranges:
        mixed_part, total_part = attend(
            cross_queries[:, :, head_range],
            key_rows[:, :, head_range],
            value_rows[:, :, head_range],
            allowed,
            None,
        )
        cross_parts.append(mixed_part)
        cross_totals.append(total_part)
    merged_cross = jnp.concatenate(cross_parts, axis=2).reshape(sequences * TLEN, width_here)
    residual_three = residual_two + over_heads(
        jnp.dot(merged_cross, cross_output_full, preferred_element_type=jnp.float32)
    )
    unit_three, factor_three, normed_three = rms_forward(residual_three, norm_gains[2])
    before = jnp.dot(normed_three, expand_full, preferred_element_type=jnp.float32)
    hidden = jax.nn.gelu(before, approximate=True).astype(jnp.bfloat16)
    block_out = residual_three + over_heads(
        jnp.dot(hidden, reduce_full, preferred_element_type=jnp.float32)
    )
    grad_out = output_cotangent.astype(jnp.float32)
    reduce_grad = jnp.dot(hidden.T, output_cotangent, preferred_element_type=jnp.float32)
    hidden_grad = jnp.dot(output_cotangent, reduce_full.T, preferred_element_type=jnp.float32)
    unused_value, gelu_pullback = jax.vjp(partial(jax.nn.gelu, approximate=True), before)
    before_grad = gelu_pullback(hidden_grad)[0].astype(jnp.bfloat16)
    expand_grad = jnp.dot(normed_three.T, before_grad, preferred_element_type=jnp.float32)
    normed_grad = over_heads(
        jnp.dot(before_grad, expand_full.T, preferred_element_type=jnp.float32)
    )
    back_three, gain_three = rms_backward(normed_grad, unit_three, factor_three, norm_gains[2])
    grad_three = grad_out + back_three
    grad_low = grad_three.astype(jnp.bfloat16)
    cross_output_grad = jnp.dot(merged_cross.T, grad_low, preferred_element_type=jnp.float32)
    mixed_grad = jnp.dot(grad_low, cross_output_full.T, preferred_element_type=jnp.float32).astype(
        jnp.bfloat16
    )
    mixed_grad = mixed_grad.reshape(sequences, TLEN, heads_here, HEAD_DIM)
    query_parts = []
    key_parts = []
    value_parts = []
    for number, head_range in enumerate(head_ranges):
        query_part, key_part, value_part, unused_scores = attend_back(
            cross_queries[:, :, head_range],
            key_rows[:, :, head_range],
            value_rows[:, :, head_range],
            allowed,
            None,
            cross_totals[number],
            mixed_grad[:, :, head_range],
        )
        query_parts.append(query_part)
        key_parts.append(key_part)
        value_parts.append(value_part)
    cross_query_rows = (
        jnp.concatenate(query_parts, axis=2)
        .astype(jnp.bfloat16)
        .reshape(sequences * TLEN, width_here)
    )
    kv_grad = jnp.stack(
        [jnp.concatenate(key_parts, axis=2), jnp.concatenate(value_parts, axis=2)], axis=2
    )
    kv_grad = kv_grad.astype(jnp.bfloat16).reshape(sequences * PQ, passage_len, 2 * width_here)
    returned = lax.all_to_all(
        return_rows(kv_grad, gather_index, buffer_rows),
        "pas",
        split_axis=0,
        concat_axis=0,
        tiled=True,
    )
    kv_grad_here = jnp.take(returned, position, axis=0)
    kv_weight_grad = jnp.einsum(
        "tpd,tpc->dc", states_full, kv_grad_here, preferred_element_type=jnp.float32
    )
    states_grad = jnp.einsum(
        "tpc,dc->tpd", kv_grad_here, kv_weights, preferred_element_type=jnp.float32
    )
    passage_grad = lax.psum_scatter(
        states_grad.astype(jnp.bfloat16), "mdl", scatter_dimension=2, tiled=True
    )
    cross_query_grad = jnp.dot(normed_two.T, cross_query_rows, preferred_element_type=jnp.float32)
    normed_grad = over_heads(
        jnp.dot(cross_query_rows, cross_query_full.T, preferred_element_type=jnp.float32)
    )
    back_two, gain_two = rms_backward(normed_grad, unit_two, factor_two, norm_gains[1])
    grad_two = grad_three + back_two
    grad_low = grad_two.astype(jnp.bfloat16)
    self_output_grad = jnp.dot(merged_self.T, grad_low, preferred_element_type=jnp.float32)
    attended_grad = jnp.dot(grad_low, output_full.T, preferred_element_type=jnp.float32).astype(
        jnp.bfloat16
    )
    attended_grad = attended_grad.reshape(sequences, TLEN, heads_here, HEAD_DIM)
    query_grad, key_grad, value_grad, score_grad = attend_back(
        queries_self, keys_self, values_self, causal, bias_full, total_self, attended_grad
    )
    bias_grad = jnp.einsum(
        "hij,bij->bh",
        jnp.sum(score_grad.astype(jnp.float32), axis=0),
        one_hot,
        precision=lax.Precision.HIGHEST,
    )
    projected_grad = jnp.stack([query_grad, key_grad, value_grad], axis=2).astype(jnp.bfloat16)
    projected_grad = projected_grad.reshape(sequences * TLEN, 3 * width_here)
    self_weight_grad = jnp.dot(normed_one.T, projected_grad, preferred_element_type=jnp.float32)
    normed_grad = over_heads(
        jnp.dot(projected_grad, self_weights.T, preferred_element_type=jnp.float32)
    )
    back_one, gain_one = rms_backward(normed_grad, unit_one, factor_one, norm_gains[0])
    target_grad = (grad_two + back_one).astype(jnp.bfloat16)
    row_grads = (
        lax.psum_scatter(self_weight_grad[:, :width_here], "pas", scatter_dimension=0, tiled=True),
        lax.psum_scatter(
            self_weight_grad[:, width_here : 2 * width_here], "pas", scatter_dimension=0, tiled=True
        ),
        lax.psum_scatter(
            self_weight_grad[:, 2 * width_here :], "pas", scatter_dimension=0, tiled=True
        ),
        lax.psum_scatter(cross_query_grad, "pas", scatter_dimension=0, tiled=True),
        lax.psum_scatter(kv_weight_grad[:, :width_here], "pas", scatter_dimension=0, tiled=True),
        lax.psum_scatter(kv_weight_grad[:, width_here:], "pas", scatter_dimension=0, tiled=True),
        lax.psum_scatter(expand_grad, "pas", scatter_dimension=0, tiled=True),
    )
    col_grads = (
        lax.psum_scatter(self_output_grad, "pas", scatter_dimension=1, tiled=True),
        lax.psum_scatter(cross_output_grad, "pas", scatter_dimension=1, tiled=True),
        lax.psum_scatter(reduce_grad, "pas", scatter_dimension=1, tiled=True),
    )
    gains_total, bias_total = lax.psum(
        (jnp.stack([gain_one, gain_two, gain_three]), bias_grad), "pas"
    )
    return (
        block_out.astype(jnp.bfloat16),
        target_grad,
        passage_grad,
        gains_total,
        row_grads[0],
        row_grads[1],
        row_grads[2],
        col_grads[0],
        bias_total,
        row_grads[3],
        row_grads[4],
        row_grads[5],
        col_grads[1],
        row_grads[6],
        col_grads[2],
    )


CHIPS = 16
RANKS = 3
FLAG_ROWS = 16
MESH_ID = pl.DeviceIdType.MESH
VMEM_LIMIT = 56 * 2**20


def fits(mesh):
    return mesh.shape["pas"] == CHIPS and mesh.shape["mdl"] == 2


def places():
    me, core = lax.axis_index("pas"), lax.axis_index("mdl")
    x, y, z = me % 2, (me // 2) % 2, me // 4
    across_x, across_y = me + 1 - 2 * x, me + 2 - 4 * y
    near = across_y + (across_x - across_y) * core
    far = across_x + (across_y - across_x) * core
    return me, core, x, y, z, near, far


def remote(src, dst, send_sem, recv_sem, device):
    return pltpu.make_async_remote_copy(
        src_ref=src,
        dst_ref=dst,
        send_sem=send_sem,
        recv_sem=recv_sem,
        device_id=device,
        device_id_type=MESH_ID,
    )


def greet_all(me, core):
    barrier = pltpu.get_barrier_semaphore()
    for k in range(1, CHIPS):
        pl.semaphore_signal(
            barrier, inc=1, device_id=((me + k) % CHIPS, core), device_id_type=MESH_ID
        )
    pl.semaphore_signal(barrier, inc=1, device_id=(me, 1 - core), device_id_type=MESH_ID)
    pl.semaphore_wait(barrier, CHIPS)


ANY = pl.BlockSpec(memory_space=pl.ANY)
IN_VMEM = pl.BlockSpec(memory_space=pltpu.VMEM)
IN_SMEM = pl.BlockSpec(memory_space=pltpu.SMEM)
DMA = pltpu.SemaphoreType.DMA


def rows_nt(left, right):
    return lax.dot_general(
        left, right, (((1,), (1,)), ((), ())), preferred_element_type=jnp.float32
    )


def rows_tn(left, right):
    return lax.dot_general(
        left, right, (((0,), (0,)), ((), ())), preferred_element_type=jnp.float32
    )


TILE = 2


def mm(left, right):
    return jnp.dot(left, right, preferred_element_type=jnp.float32)


def halves_of_pair(rows, head):
    lane = lax.broadcasted_iota(jnp.int32, (rows.shape[0], 2 * HEAD_DIM), 1)
    at = head // 2 * 2 * HEAD_DIM
    return jnp.where(lane // HEAD_DIM == head % 2, rows[:, at : at + 2 * HEAD_DIM], 0.0).astype(
        jnp.bfloat16
    )


def halves_of_rows(rows, head):
    row = lax.broadcasted_iota(jnp.int32, (2 * HEAD_DIM, rows.shape[1]), 0)
    at = head // 2 * 2 * HEAD_DIM
    return jnp.where(row // HEAD_DIM == head % 2, rows[at : at + 2 * HEAD_DIM], 0.0).astype(
        jnp.bfloat16
    )


def unit_of(values):
    factor = lax.rsqrt(jnp.mean(values * values, axis=-1, keepdims=True) + EPSILON)
    return values * factor, factor


def prepare_heads(heads, query_ref, grad, mixed, q_pair, o_pair, o_rows, centre):
    grad = grad.astype(jnp.float32)
    grad_t = grad.T
    product = (grad * mixed.astype(jnp.float32)).T
    queries = query_ref[...].astype(jnp.float32)
    for h in range(heads):
        q_pair[h] = halves_of_pair(queries, h)
        o_pair[h] = halves_of_pair(grad, h)
        o_rows[h] = halves_of_rows(grad_t, h)
        centre[h : h + 1, :] = jnp.sum(
            product[h * HEAD_DIM : (h + 1) * HEAD_DIM], axis=0, keepdims=True
        )


def head_pair_back(p, keys, values, prob, q_pair, o_pair, o_rows, centre, keep_scores):
    low = jnp.bfloat16
    keys_t = keys.T
    query_parts = []
    for a in range(2):
        h = 2 * p + a
        prob_grad = mm(values, o_rows[h])
        weights = prob(h)
        score_grad = (weights * (prob_grad - centre[h : h + 1, :])).astype(low)
        if keep_scores is not None:
            keep_scores(h, score_grad)
        key_part = mm(score_grad, q_pair[h])
        value_part = mm(weights.astype(low), o_pair[h])
        key_grad = key_part if a == 0 else key_grad + key_part
        value_grad = value_part if a == 0 else value_grad + value_part
        query_parts.append(mm(keys_t[a * HEAD_DIM : (a + 1) * HEAD_DIM], score_grad))
    return key_grad.astype(low), value_grad.astype(low), query_parts


def z_turned(z, k):
    high, low = z // 2, z % 2
    if k % 2:
        high = 1 - high
    if k // 2:
        low = 1 - low
    return 2 * high + low


def exp_rows(scores):
    highest = jnp.max(scores, axis=0, keepdims=True)
    exps = jnp.exp(scores - highest)
    return exps, highest, jnp.sum(exps, axis=0, keepdims=True)


def gelu_both(values):
    first = math.sqrt(2 / math.pi)
    square = values * values
    curve = jnp.tanh(first * values * (1.0 + 0.044715 * square))
    half = 0.5 * (1.0 + curve)
    slope = half + 0.5 * values * (1.0 - curve * curve) * first * (1.0 + 3 * 0.044715 * square)
    return values * half, slope


ROW_BUFFER = (0, 1, 0, 2, 1, 0)
ROW_BEFORE = {2: 0, 4: 1, 5: 2}


def block_kernel(
    index_ref,
    position_ref,
    shard_ref,
    passage_ref,
    flag_ref,
    target_ref,
    cotangent_ref,
    gains_ref,
    table_ref,
    bucket_ref,
    count_ref,
    shard_out,
    slots_ref,
    small_ref,
    target_grad_ref,
    block_ref,
    exps_out,
    kv_out,
    full,
    states,
    flags,
    kept,
    slot_got,
    exps,
    keys,
    bias,
    q_rows,
    q_pair,
    o_pair,
    o_rows,
    centre,
    out_t,
    highest,
    total,
    tile_highest,
    scale_ref,
    query_ref,
    mixed_ref,
    residual_ref,
    qkv_ref,
    self_mixed_ref,
    self_exps_ref,
    self_scale_ref,
    upper_grad,
    row_sent,
    row_got,
    far_got,
    near_got,
    next_got,
    skip_got,
    dkv,
    outgoing,
    pair_got,
    small,
    small_got,
    skip_send,
    skip_recv,
    next_send,
    next_recv,
    near_send,
    near_recv,
    first_send,
    first_recv,
    second_send,
    second_recv,
    fold_far_send,
    fold_far_recv,
    fold_near_send,
    fold_near_recv,
    fold_next_send,
    fold_next_recv,
    fold_skip_send,
    fold_skip_recv,
    slot_send,
    slot_recv,
    flag_send,
    flag_recv,
    core_send,
    core_recv,
    return_send,
    return_recv,
    pair_send,
    pair_recv,
    row_send,
    row_recv,
    small_send,
    small_recv,
    own_sem,
    exps_sem,
    keys_sem,
    out_sem,
):
    low, wide = jnp.bfloat16, jnp.float32
    me, core, x, y, z, near, far = places()
    groups = shard_ref.shape[0]
    partner = (me, 1 - core)
    pair = me // TILE
    tiles = CHIPS // TILE
    passage_len = states.shape[2]
    block_rows = RANKS * passage_len
    tile_rows = TILE * block_rows
    tokens = target_ref.shape[0]
    width = query_ref.shape[1]
    kept_side = (1 - core) * y + core * x
    own_side = (1 - core) * x + core * y
    across_x, across_y = me + 1 - 2 * x, me + 2 - 4 * y
    pairs = width // (2 * HEAD_DIM)
    heads = 2 * pairs
    half = states.shape[3]
    other_y = y + (1 - core) * (1 - 2 * y)
    other_x = x + core * (1 - 2 * x)

    def slots_of(ref, source):
        return ref.at[pl.ds(source * RANKS, RANKS)]

    def own_copy(g):
        return pltpu.make_async_copy(shard_ref.at[g], full.at[g, z, y, x], own_sem.at[g])

    def z_at(k):
        return z_turned(z, k)

    def skip_copy(g):
        dst = full.at[g, z, y, x]
        return remote(
            shard_ref.at[g], dst, skip_send.at[g], skip_recv.at[g], (me - 4 * z + 4 * z_at(1), core)
        )

    def next_copy(g, k):
        dst = full.at[g, z_at(k), y, x]
        to = (me - 4 * z + 4 * z_at(2), core)
        return remote(held(g, k), dst, next_send.at[g, k], next_recv.at[g, k], to)

    def held(g, k):
        return shard_ref.at[g] if k == 0 else full.at[g, z_at(k), y, x]

    def near_copy(g, k):
        dst = full.at[g, z_at(k), y, x]
        return remote(held(g, k), dst, near_send.at[g, k], near_recv.at[g, k], (near, core))

    def first_copy(g, k):
        dst = full.at[g, z_at(k), y, x]
        return remote(held(g, k), dst, first_send.at[g, k], first_recv.at[g, k], (far, core))

    def second_copy(g, k):
        block = full.at[g, z_at(k), other_y, other_x]
        return remote(block, block, second_send.at[g, k], second_recv.at[g, k], (far, core))

    def slot_copy(to):
        return remote(
            slots_of(kept, to), slots_of(states.at[core], me), slot_send.at[to], slot_recv.at[me], (to, core)
        )

    def slot_arrival(came):
        block = slots_of(states.at[core], came)
        return remote(block, block, slot_send.at[came], slot_recv.at[came], (came, core))

    def flag_copy(to):
        return remote(flag_ref.at[to], flags.at[me], flag_send.at[to], flag_recv.at[me], (to, core))

    def flag_arrival(came):
        block = flags.at[came]
        return remote(block, block, flag_send.at[came], flag_recv.at[came], (came, core))

    def core_copy(came):
        block = slots_of(states.at[core], came)
        return remote(block, block, core_send.at[came], core_recv.at[came], partner)

    def row_copy(i):
        b = ROW_BUFFER[i]
        return remote(row_sent.at[b], row_got.at[b], row_send.at[i], row_recv.at[i], partner)

    def give(i, value):
        if i in ROW_BEFORE:
            row_copy(ROW_BEFORE[i]).wait_send()
        row_sent[ROW_BUFFER[i]] = value
        row_copy(i).start()

    def pair_sum(i):
        row_copy(i).wait_recv()
        return row_sent[ROW_BUFFER[i]] + row_got[ROW_BUFFER[i]]

    def launch(g):
        skip_copy(g).start()
        next_copy(g, 0).start()
        near_copy(g, 0).start()
        first_copy(g, 0).start()
        own_copy(g).start()

    def relay_skip(g):
        skip_copy(g).wait_recv()
        next_copy(g, 1).start()
        near_copy(g, 1).start()
        first_copy(g, 1).start()

    def relay_next(g):
        for k in range(2):
            next_copy(g, k).wait_recv()
            near_copy(g, k + 2).start()
            first_copy(g, k + 2).start()

    def relay_near(g):
        for k in range(4):
            near_copy(g, k).wait_recv()
            second_copy(g, k).start()

    def arrived(g):
        own_copy(g).wait()
        for k in range(4):
            first_copy(g, k).wait_recv()
            second_copy(g, k).wait_recv()

    def weight(g):
        return full[g].reshape(full.shape[1] * 4 * full.shape[4], full.shape[5])

    staging = pltpu.make_async_copy(
        passage_ref, slot_got.at[pl.ds(0, passage_ref.shape[0])], out_sem.at[0]
    )
    staging.start()
    def block_at(k, o, side):
        return z_turned(z, k), (1 - core) * o + core * side, (1 - core) * side + core * o

    def fold_far(g, i, k):
        a, b, c = block_at(k, kept_side + (1 - i) * (1 - 2 * kept_side), 1 - own_side)
        return remote(
            full.at[g, a, b, c],
            far_got.at[g, i, k],
            fold_far_send.at[g, i, k],
            fold_far_recv.at[g, i, k],
            (far, core),
        )

    def far_start(g):
        for i in range(2):
            for k in range(3, -1, -1):
                fold_far(g, i, k).start()

    def fold_near(g, k):
        return remote(
            far_got.at[g, 0, k], near_got.at[g, k], fold_near_send.at[g, k], fold_near_recv.at[g, k], (near, core)
        )

    def fold_next(g, k):
        to = (me - 4 * z + 4 * z_turned(z, 2), core)
        return remote(
            near_got.at[g, 2 + k], next_got.at[g, k], fold_next_send.at[g, k], fold_next_recv.at[g, k], to
        )

    def fold_skip(g):
        to = (me - 4 * z + 4 * z_turned(z, 1), core)
        return remote(near_got.at[g, 1], skip_got.at[g], fold_skip_send.at[g], fold_skip_recv.at[g], to)

    def far_add(g):
        for k in range(3, -1, -1):
            fold_far(g, 0, k).wait_recv()
            a, b, c = block_at(k, 1 - kept_side, own_side)
            far_got[g, 0, k] = (
                full[g, a, b, c].astype(wide) + far_got[g, 0, k].astype(wide)
            ).astype(low)
            fold_near(g, k).start()

    def near_add(g):
        for k in range(3, -1, -1):
            fold_far(g, 1, k).wait_recv()
            fold_near(g, k).wait_recv()
            a, b, c = block_at(k, kept_side, own_side)
            near_got[g, k] = (
                full[g, a, b, c].astype(wide)
                + far_got[g, 1, k].astype(wide)
                + near_got[g, k].astype(wide)
            ).astype(low)
            if k >= 2:
                fold_next(g, k - 2).start()

    def next_add(g):
        fold_next(g, 1).wait_recv()
        near_got[g, 1] = (near_got[g, 1].astype(wide) + next_got[g, 1].astype(wide)).astype(low)
        fold_skip(g).start()

    def skip_add(g):
        fold_next(g, 0).wait_recv()
        fold_skip(g).wait_recv()
        shard_out[g] = (
            near_got[g, 0].astype(wide) + next_got[g, 0].astype(wide) + skip_got[g].astype(wide)
        )

    greet_all(me, core)
    def send_pair(j):
        for i in range(TILE):
            to = (pair + j) % tiles * TILE + i

            @pl.when(to != me)
            def _():
                flag_copy(to).start()
                slot_copy(to).start()

    launch(0)

    def fill(to, carry):
        for rank in range(RANKS):
            kept[to * RANKS + rank] = slot_got[index_ref[to * RANKS + rank]]
        return carry

    staging.wait()
    lax.fori_loop(0, CHIPS, fill, 0)
    send_pair(0)
    launch(1)
    send_pair(1)
    send_pair(2)
    states[core, pl.ds(me * RANKS, RANKS)] = kept[pl.ds(me * RANKS, RANKS)]
    flags[me] = flag_ref[me]
    core_copy(me).start()

    line = jnp.dot(
        table_ref[...], bucket_ref[...], precision=lax.Precision.HIGHEST, preferred_element_type=wide
    )
    for h in range(heads):
        for s in range(8):
            row = line[h : h + 1]
            bias[h, s : s + 1, :] = row if s == 0 else pltpu.roll(row, s, 1)
    base = bias[:, 0:8, :].reshape(heads * 8, tokens)

    def bias_step(i, carry):
        rows = pltpu.roll(base, 8 * i, 1).reshape(heads, 8, tokens)
        bias[:, pl.ds(pl.multiple_of(8 * i, 8), 8), :] = rows
        return carry

    lax.fori_loop(1, tokens // 8, bias_step, 0)
    residual = target_ref[...].astype(wide)
    normed = (unit_of(residual)[0] * gains_ref[0:1, :]).astype(low)

    relay_skip(0)
    send_pair(3)
    launch(2)
    relay_next(0)
    relay_near(0)
    relay_skip(1)
    send_pair(4)
    relay_next(1)
    arrived(0)

    qkv_ref[...] = mm(normed, weight(0)[:, : 3 * width]).astype(low)
    relay_near(1)
    relay_skip(2)
    queries_t = qkv_ref[:, :width].astype(wide).T
    for h in range(heads):
        q_rows[h] = halves_of_rows(queries_t, h)
    key_at = lax.broadcasted_iota(jnp.int32, (tokens, tokens), 0)
    query_at = lax.broadcasted_iota(jnp.int32, (tokens, tokens), 1)
    self_scale_ref[...] = jnp.zeros_like(self_scale_ref)
    for p in range(pairs):
        at = 2 * HEAD_DIM * p
        head_keys = qkv_ref[:, width + at : width + at + 2 * HEAD_DIM]
        values_t = qkv_ref[:, 2 * width + at : 2 * width + at + 2 * HEAD_DIM].T
        for a in range(2):
            h = 2 * p + a
            scores = mm(head_keys, q_rows[h]) + bias[h]
            scores = jnp.where(key_at <= query_at, scores, MASKED)
            head_exps, unused, sums = exp_rows(scores)
            head_exps = head_exps.astype(low)
            self_exps_ref[h] = head_exps
            inverse = 1.0 / sums
            self_scale_ref[h : h + 1, :] = inverse
            first = at + a * HEAD_DIM
            out_t[first : first + HEAD_DIM, :] = (
                mm(values_t[a * HEAD_DIM : (a + 1) * HEAD_DIM], head_exps) * inverse
            )
    self_mixed_ref[...] = out_t[...].T.astype(low)
    give(0, rows_nt(self_mixed_ref[...], weight(0)[:, 3 * width :]))
    launch(3)
    send_pair(5)
    arrived(1)
    residual_ref[...] = residual + pair_sum(0)

    normed = (unit_of(residual_ref[...])[0] * gains_ref[1:2, :]).astype(low)
    query_ref[...] = mm(normed, weight(1)[:, :width]).astype(low)
    queries_t = query_ref[...].astype(wide).T
    for h in range(heads):
        q_rows[h] = halves_of_rows(queries_t, h)
    out_t[...] = jnp.zeros_like(out_t)
    highest[...] = jnp.full_like(highest, MASKED)
    total[...] = jnp.zeros_like(total)
    tile_highest[...] = jnp.zeros_like(tile_highest)

    def take_in(t):
        for i in range(TILE):
            came = (pair - t + tiles) % tiles * TILE + i

            @pl.when(came != me)
            def _():
                flag_arrival(came).wait_recv()
                slot_arrival(came).wait_recv()
                core_copy(came).start()

    def exps_copy(t):
        rows = pl.ds((pair - t + tiles) % tiles * tile_rows, tile_rows)
        return pltpu.make_async_copy(exps.at[t % 2], exps_out.at[:, rows], exps_sem.at[t % 2])

    def keys_copy(t):
        rows = pl.ds((pair - t + tiles) % tiles * tile_rows, tile_rows)
        return pltpu.make_async_copy(keys.at[t % 2], kv_out.at[rows], keys_sem.at[t % 2])

    send_pair(6)
    send_pair(7)
    take_in(0)

    def tile_step(t, carry):
        tile = (pair - t + tiles) % tiles

        @pl.when(t == 5)
        def _():
            relay_skip(3)

        @pl.when(t == 6)
        def _():
            relay_next(3)

        @pl.when(t + 1 < tiles)
        def _():
            take_in(t + 1)

        @pl.when(t == 2)
        def _():
            relay_next(2)

        @pl.when(t == 3)
        def _():
            relay_near(2)

        @pl.when(t >= 2)
        def _():
            exps_copy(t - 2).wait()
            keys_copy(t - 2).wait()

        for i in range(TILE):
            core_copy(tile * TILE + i).wait_recv()
        kv_parts = []
        for c in range(2):
            rows = states[c, pl.ds(tile * TILE * RANKS, TILE * RANKS)].reshape(tile_rows, half)
            w = full[1, 2 * c : 2 * c + 2, :, :, :, width : 3 * width]
            kv_parts.append(mm(rows, w.reshape(half, 2 * width)))
        keys[t % 2] = (kv_parts[0] + kv_parts[1]).astype(low)
        keys_copy(t).start()
        masks = []
        for i in range(TILE):
            for rank in range(RANKS):
                masks.append(flags[tile * TILE + i, rank : rank + 1, :].astype(wide)[None])
        masks = jnp.concatenate(masks, axis=0)
        for p in range(pairs):
            at = 2 * HEAD_DIM * p
            head_keys = keys[t % 2, :, at : at + 2 * HEAD_DIM]
            values_t = keys[t % 2, :, width + at : width + at + 2 * HEAD_DIM].T
            for a in range(2):
                h = 2 * p + a
                scores = mm(head_keys, q_rows[h]).reshape(TILE * RANKS, passage_len, tokens) + masks
                head_exps, top, sums = exp_rows(scores.reshape(tile_rows, tokens))
                head_exps = head_exps.astype(low)
                exps[t % 2, h] = head_exps
                before = highest[h : h + 1, :]
                now = jnp.maximum(before, top)
                keep, add = jnp.exp(before - now), jnp.exp(top - now)
                highest[h : h + 1, :] = now
                tile_highest[tile, h : h + 1, :] = top
                total[h : h + 1, :] = total[h : h + 1, :] * keep + sums * add
                first = at + a * HEAD_DIM
                out_t[first : first + HEAD_DIM, :] = (
                    out_t[first : first + HEAD_DIM, :] * keep
                    + mm(values_t[a * HEAD_DIM : (a + 1) * HEAD_DIM], head_exps) * add
                )
        exps_copy(t).start()

        return carry

    lax.fori_loop(0, tiles, tile_step, 0)
    relay_near(3)
    for h in range(heads):
        inverse = 1.0 / total[h : h + 1, :]
        out_t[h * HEAD_DIM : (h + 1) * HEAD_DIM, :] *= inverse
        scale_ref[:, h, :] = jnp.exp(tile_highest[:, h, :] - highest[h : h + 1, :]) * inverse
    mixed_ref[...] = out_t[...].T.astype(low)
    give(1, rows_nt(mixed_ref[...], weight(1)[:, 3 * width :]))
    residual_three = residual_ref[...] + pair_sum(1)
    unit, factor = unit_of(residual_three)
    normed = (unit * gains_ref[2:3, :]).astype(low)

    for g in range(groups):
        skip_copy(g).wait_send()
        for k in range(2):
            next_copy(g, k).wait_send()
        for k in range(4):
            near_copy(g, k).wait_send()
            first_copy(g, k).wait_send()

    def second_done(g):
        for k in range(4):
            second_copy(g, k).wait_send()

    def store_grad(g, first, value):
        blocks = value.astype(low).reshape(full.shape[1:5] + (value.shape[1],))
        full[g, :, :, :, :, first : first + value.shape[1]] = blocks

    arrived(2)
    hidden, slope = gelu_both(mm(normed, weight(2)))
    hidden = hidden.astype(low)
    arrived(3)
    hidden_grad = mm(cotangent_ref[...], weight(3))
    before_grad = (hidden_grad * slope).astype(low)
    give(2, rows_nt(before_grad, weight(2)))
    give(3, rows_nt(hidden, weight(3)))
    second_done(2)
    store_grad(2, 0, rows_tn(normed, before_grad))
    far_start(2)
    second_done(3)
    store_grad(3, 0, rows_tn(cotangent_ref[...], hidden))
    far_start(3)
    back, gain_three = rms_backward(pair_sum(2), unit, factor, gains_ref[2:3, :])
    upper_grad[...] = cotangent_ref[...].astype(wide) + back
    block_ref[...] = (residual_three + pair_sum(3)).astype(low)
    second_done(0)
    second_done(1)
    for k in range(1, CHIPS):
        to = (me + k) % CHIPS
        slot_copy(to).wait_send()
        flag_copy(to).wait_send()
    for k in range(CHIPS):
        core_copy(k).wait_send()
    for t in range(tiles - 2, tiles):
        exps_copy(t).wait()
        keys_copy(t).wait()

    def back_tile(t):
        return (t + pair) % tiles

    def exps_load(t):
        rows = pl.ds(back_tile(t) * tile_rows, tile_rows)
        return pltpu.make_async_copy(exps_out.at[:, rows], exps.at[t % 2], exps_sem.at[t % 2])

    def keys_load(t):
        rows = pl.ds(back_tile(t) * tile_rows, tile_rows)
        return pltpu.make_async_copy(kv_out.at[rows], keys.at[t % 2], keys_sem.at[t % 2])

    def loads_start(t):
        exps_load(t).start()
        keys_load(t).start()

    def kv_weights(c):
        w = full[1, pl.ds(2 * c, 2), :, :, :, width : 3 * width]
        return w.reshape(half, 2 * width)

    def pair_copy(t):
        return remote(
            outgoing.at[t % 2],
            pair_got.at[pl.ds(back_tile(t) * TILE * RANKS, TILE * RANKS)],
            pair_send.at[t % 2],
            pair_recv.at[t],
            partner,
        )

    def return_copy(to):
        return remote(
            slots_of(kept, to), slots_of(slot_got, me), return_send.at[to], return_recv.at[me], (to, core)
        )

    def return_arrival(came):
        block = slots_of(slot_got, came)
        return remote(block, block, return_send.at[came], return_recv.at[came], (came, core))

    def finish_tile(t):
        tile = back_tile(t)
        pair_copy(t).wait_recv()
        rows = pl.ds(tile * TILE * RANKS, TILE * RANKS)
        kept[rows] = (kept[rows].astype(wide) + pair_got[rows].astype(wide)).astype(low)
        for j in range(TILE):
            to = tile * TILE + j

            @pl.when(to != me)
            def _():
                return_copy(to).start()

            @pl.when(to == me)
            def _():
                own = pl.ds(me * RANKS, RANKS)
                slot_got[own] = kept[own]

    grad_low = upper_grad[...].astype(low)
    mixed_grad = mm(grad_low, weight(1)[:, 3 * width :]).astype(low)
    prepare_heads(heads, query_ref, mixed_grad, mixed_ref[...], q_pair, o_pair, o_rows, centre)
    out_t[...] = jnp.zeros_like(out_t)
    loads_start(0)

    def back_step(t, carry):
        tile = back_tile(t)
        rows = pl.ds(pl.multiple_of(tile * tile_rows, tile_rows), tile_rows)

        @pl.when(t + 1 < tiles)
        def _():
            loads_start(t + 1)

        exps_load(t).wait()
        keys_load(t).wait()

        def prob(h):
            return exps[t % 2, h].astype(wide) * scale_ref[tile, h : h + 1, :]

        for p in range(pairs):
            at = 2 * HEAD_DIM * p
            key_grad, value_grad, query_parts = head_pair_back(
                p,
                keys[t % 2, :, at : at + 2 * HEAD_DIM],
                keys[t % 2, :, width + at : width + at + 2 * HEAD_DIM],
                prob,
                q_pair,
                o_pair,
                o_rows,
                centre,
                None,
            )
            dkv[rows, at : at + 2 * HEAD_DIM] = key_grad
            dkv[rows, width + at : width + at + 2 * HEAD_DIM] = value_grad
            for a in range(2):
                first = at + a * HEAD_DIM
                out_t[first : first + HEAD_DIM, :] += query_parts[a]
        here = dkv[rows, :]

        @pl.when(t >= 2)
        def _():
            pair_copy(t - 2).wait_send()

        weights = kv_weights(1 - core)
        outgoing[t % 2] = rows_nt(here, weights).astype(low).reshape(outgoing.shape[1:])
        pair_copy(t).start()
        weights = kv_weights(core)
        mine = rows_nt(here, weights).astype(low).reshape(outgoing.shape[1:])
        kept[pl.ds(tile * TILE * RANKS, TILE * RANKS)] = mine

        @pl.when(t >= 1)
        def _():
            finish_tile(t - 1)

        @pl.when(t == 3)
        def _():
            far_add(2)

        @pl.when(t == 6)
        def _():
            far_add(3)

        return carry

    lax.fori_loop(0, tiles, back_step, 0)
    dq = out_t[...].T.astype(low)
    give(4, rows_nt(dq, weight(1)[:, :width]))
    store_grad(1, 3 * width, rows_tn(upper_grad[...].astype(low), mixed_ref[...]))
    finish_tile(tiles - 1)
    near_add(2)
    unit_two, factor_two = unit_of(residual_ref[...])
    normed_two = (unit_two * gains_ref[1:2, :]).astype(low)
    store_grad(1, 0, rows_tn(normed_two, dq))

    for n in range(2 * width // 256):
        columns = slice(n * 256, (n + 1) * 256)
        parts = [rows_tn(states[i].reshape(-1, half), dkv[:, columns]) for i in range(2)]
        store_grad(1, width + n * 256, jnp.concatenate(parts))
    far_start(1)
    next_add(2)
    near_add(3)

    back, gain_two = rms_backward(pair_sum(4), unit_two, factor_two, gains_ref[1:2, :])
    upper_grad[...] += back

    grad_low = upper_grad[...].astype(low)
    mixed_grad = mm(grad_low, weight(0)[:, 3 * width :]).astype(low)
    prepare_heads(
        heads,
        qkv_ref.at[:, :width],
        mixed_grad,
        self_mixed_ref[...],
        q_pair,
        o_pair,
        o_rows,
        centre,
    )

    def self_prob(h):
        return self_exps_ref[h].astype(wide) * self_scale_ref[h : h + 1, :]

    def keep_scores(h, score_grad):
        self_exps_ref[h] = score_grad

    query_rows, key_columns, value_columns = [], [], []
    for p in range(pairs):
        at = 2 * HEAD_DIM * p
        key_grad, value_grad, query_parts = head_pair_back(
            p,
            qkv_ref[:, width + at : width + at + 2 * HEAD_DIM],
            qkv_ref[:, 2 * width + at : 2 * width + at + 2 * HEAD_DIM],
            self_prob,
            q_pair,
            o_pair,
            o_rows,
            centre,
            keep_scores,
        )
        key_columns.append(key_grad)
        value_columns.append(value_grad)
        query_rows.extend(query_parts)
    dq = jnp.concatenate(query_rows, axis=0).T.astype(low)
    dqkv = jnp.concatenate([dq] + key_columns + value_columns, axis=1)
    give(5, rows_nt(dqkv, weight(0)[:, : 3 * width]))
    store_grad(0, 3 * width, rows_tn(upper_grad[...].astype(low), self_mixed_ref[...]))
    unit_one, factor_one = unit_of(target_ref[...].astype(wide))
    normed_one = (unit_one * gains_ref[0:1, :]).astype(low)
    store_grad(0, 0, rows_tn(normed_one, dqkv))
    far_start(0)
    far_add(1)
    next_add(3)

    length = self_exps_ref.shape[1]

    def diagonal_step(i, total):
        rows = self_exps_ref[:, pl.ds(pl.multiple_of(16 * i, 16), 16), :].astype(wide)
        rows = rows.reshape(heads * 16, length)
        return total + pltpu.roll(rows, (length - 16 * i) % length, 1)

    total = lax.fori_loop(
        0, length // 16, diagonal_step, jnp.zeros((heads * 16, length), wide)
    ).reshape(heads, 16, length)
    small[...] = jnp.zeros_like(small)
    for h in range(heads):
        line = total[h, 0:1]
        for s in range(1, 16):
            line = line + pltpu.roll(total[h, s : s + 1], length - s, 1)
        small[8 + h : 9 + h, :length] = line
    by_bucket = jnp.dot(
        small[8:16, :length], count_ref[...], precision=lax.Precision.HIGHEST,
        preferred_element_type=wide,
    )
    small[8:16, :length] = jnp.zeros((8, length), wide)
    small[8:16, : count_ref.shape[1]] = by_bucket

    back, gain_one = rms_backward(pair_sum(5), unit_one, factor_one, gains_ref[0:1, :])
    target_grad_ref[...] = (upper_grad[...] + back).astype(low)
    small[0:1, :] = gain_one[None, :]
    small[1:2, :] = gain_two[None, :]
    small[2:3, :] = gain_three[None, :]

    def small_copy(step):
        if step == 0:
            return remote(small, small_got.at[0], small_send.at[0], small_recv.at[0], (across_x, core))
        if step == 1:
            return remote(
                small_got.at[6], small_got.at[1], small_send.at[1], small_recv.at[1], (across_y, core)
            )
        return remote(
            small_got.at[7],
            small_got.at[2 + z],
            small_send.at[step],
            small_recv.at[step],
            ((me + 4 * (step - 1)) % CHIPS, core),
        )

    small_copy(0).start()
    skip_add(2)
    near_add(1)
    small_copy(0).wait_recv()
    small_got[6] = small[...] + small_got[0]
    small_copy(1).start()
    far_add(0)
    skip_add(3)
    next_add(1)
    small_copy(1).wait_recv()
    small_got[7] = small_got[6] + small_got[1]
    for step in range(2, 5):
        small_copy(step).start()
    small_got[2 + z] = small_got[7]
    near_add(0)
    skip_add(1)
    next_add(0)
    for step in range(2, 5):
        small_copy(step).wait_recv()
    small_ref[...] = small_got[2] + small_got[3] + small_got[4] + small_got[5]
    for k in range(1, CHIPS):
        return_arrival((me + k) % CHIPS).wait_recv()
    for k in range(1, CHIPS):
        return_copy((me + k) % CHIPS).wait_send()
    slots = slots_ref.shape[0]

    def pick(slot, carry):
        kept[slot] = slot_got[position_ref[slot]]
        return carry

    lax.fori_loop(0, slots, pick, 0)
    picked = pltpu.make_async_copy(kept.at[pl.ds(0, slots)], slots_ref, out_sem.at[1])
    picked.start()
    skip_add(0)
    for g in range(groups):
        for k in range(4):
            fold_far(g, 0, k).wait_send()
            fold_far(g, 1, k).wait_send()
            fold_near(g, k).wait_send()
        for k in range(2):
            fold_next(g, k).wait_send()
        fold_skip(g).wait_send()
    for t in range(tiles - 2, tiles):
        pair_copy(t).wait_send()
    for step in range(5):
        small_copy(step).wait_send()
    for i in range(3, 6):
        row_copy(i).wait_send()
    picked.wait()


def run_block(index, position, shards, passages, flags, target, cotangent, gains, table, buckets, counts):
    low, wide = jnp.bfloat16, jnp.float32
    groups, rows, columns = shards.shape
    slots, passage_len, half = passages.shape
    tokens, model = target.shape
    width = columns // 4
    heads = width // HEAD_DIM
    key_count = CHIPS * RANKS * passage_len
    tile_rows = TILE * RANKS * passage_len
    tiles = CHIPS // TILE
    small_shape = (16, model)
    shape = jax.ShapeDtypeStruct
    vmem = pltpu.VMEM
    pair_heads = vmem((heads, tokens, 2 * HEAD_DIM), low)
    pair_rows = vmem((heads, 2 * HEAD_DIM, tokens), low)
    all_slots = (CHIPS * RANKS, passage_len, half)

    def both(*dims):
        return [DMA(dims), DMA(dims)]

    return pl.pallas_call(
        block_kernel,
        out_shape=(
            shape((groups, rows, columns), wide),
            shape((slots, passage_len, half), low),
            shape(small_shape, wide),
            shape((tokens, model), low),
            shape((tokens, model), low),
            shape((heads, key_count, tokens), low),
            shape((key_count, 2 * width), low),
        ),
        in_specs=[IN_SMEM, IN_SMEM, IN_VMEM, ANY] + [IN_VMEM] * 7,
        out_specs=(IN_VMEM, ANY, IN_VMEM, IN_VMEM, IN_VMEM, ANY, ANY),
        scratch_shapes=[
            vmem((groups, 4, 2, 2, rows, columns), low),
            vmem((2,) + all_slots, low),
            vmem((CHIPS, FLAG_ROWS, tokens), low),
            vmem(all_slots, low),
            vmem(all_slots, low),
            vmem((2, heads, tile_rows, tokens), low),
            vmem((2, tile_rows, 2 * width), low),
            vmem((heads, tokens, tokens), wide),
            pair_rows,
            pair_heads,
            pair_heads,
            pair_rows,
            vmem((8, tokens), wide),
            vmem((width, tokens), wide),
            vmem((8, tokens), wide),
            vmem((8, tokens), wide),
            vmem((tiles, 8, tokens), wide),
            vmem((tiles, 8, tokens), wide),
            vmem((tokens, width), low),
            vmem((tokens, width), low),
            vmem((tokens, model), wide),
            vmem((tokens, 3 * width), low),
            vmem((tokens, width), low),
            vmem((heads, tokens, tokens), low),
            vmem((8, tokens), wide),
            vmem((tokens, model), wide),
            vmem((3, tokens, model), wide),
            vmem((3, tokens, model), wide),
            vmem((groups, 2, 4, rows, columns), low),
            vmem((groups, 4, rows, columns), low),
            vmem((groups, 2, rows, columns), low),
            vmem((groups, rows, columns), low),
            vmem((key_count, 2 * width), low),
            vmem((2, TILE * RANKS, passage_len, half), low),
            vmem(all_slots, low),
            vmem(small_shape, wide),
            vmem((8,) + small_shape, wide),
        ]
        + both(groups)
        + both(groups, 2)
        + both(groups, 4)
        + both(groups, 4)
        + both(groups, 4)
        + both(groups, 2, 4)
        + both(groups, 4)
        + both(groups, 2)
        + both(groups)
        + both(CHIPS)
        + both(CHIPS)
        + both(CHIPS)
        + both(CHIPS)
        + [DMA((2,)), DMA((tiles,))]
        + both(6)
        + both(5)
        + [DMA((groups,)), DMA((2,)), DMA((2,)), DMA((2,))],
        compiler_params=pltpu.CompilerParams(
            collective_id=0, has_side_effects=True, vmem_limit_bytes=62 * 2**20
        ),
    )(index, position, shards, passages, flags, target, cotangent, gains, table, buckets, counts)


def route(slot_query, slot_live):
    matching = slot_query[:, None] == slot_query[None, :]
    earlier = jnp.tril(jnp.ones(matching.shape, jnp.bool_), -1)
    position = slot_query * RANKS + jnp.sum(jnp.logical_and(matching, earlier), axis=1).astype(
        jnp.int32
    )
    here = position[None, :] == jnp.arange(CHIPS * RANKS, dtype=jnp.int32)[:, None]
    slots = slot_query.shape[0]
    index = jnp.sum(jnp.where(here, jnp.arange(slots, dtype=jnp.int32)[None, :], 0), axis=1)
    live = jnp.sum(jnp.where(here, slot_live[None, :], 0), axis=1)
    return position, index, live


def body(
    target_states,
    passage_states,
    slot_query,
    slot_live,
    norm_gains,
    self_query,
    self_key,
    self_value,
    self_output,
    position_bias,
    cross_query,
    cross_key,
    cross_value,
    cross_output,
    expand_weight,
    reduce_weight,
    output_cotangent,
):
    low = jnp.bfloat16
    width_here = self_query.shape[1]
    heads_here = width_here // HEAD_DIM
    passage_len, half = passage_states.shape[1:]
    bucket_count = position_bias.shape[0]
    shards = jnp.stack(
        [
            jnp.concatenate([self_query, self_key, self_value, self_output.T], axis=1),
            jnp.concatenate([cross_query, cross_key, cross_value, cross_output.T], axis=1),
            expand_weight,
            reduce_weight.T,
        ]
    )
    position, index, live = route(slot_query, slot_live)
    flags = jnp.where(live > 0, 0.0, MASKED).astype(low).reshape(CHIPS, RANKS, 1)
    flags = jnp.pad(flags, ((0, 0), (0, FLAG_ROWS - RANKS), (0, 0)))
    flags = jnp.broadcast_to(flags, (CHIPS, FLAG_ROWS, TLEN))
    distance = np.zeros((TLEN, 128), np.float32)
    distance[np.arange(TLEN), bucket_table(TLEN, bucket_count, MAXDIST)[:, 0]] = 1.0
    table = jnp.pad(position_bias.T, ((0, 8 - heads_here), (0, 0)))
    shard_grads, passage_grad, small_total, target_grad, block_out = run_block(
        index,
        position,
        shards,
        passage_states,
        flags,
        target_states,
        output_cotangent,
        norm_gains,
        table,
        jnp.asarray(distance[:, :bucket_count].T),
        jnp.asarray(distance),
    )[:5]
    w = width_here
    first, second = shard_grads[0], shard_grads[1]
    return (
        block_out,
        target_grad,
        passage_grad,
        small_total[:3],
        first[:, :w],
        first[:, w : 2 * w],
        first[:, 2 * w : 3 * w],
        first[:, 3 * w :].T,
        small_total[8 : 8 + heads_here, :bucket_count].T,
        second[:, :w],
        second[:, w : 2 * w],
        second[:, 2 * w : 3 * w],
        second[:, 3 * w :].T,
        shard_grads[2],
        shard_grads[3].T,
    )


def solution(mesh):
    return jax.shard_map(
        body if fits(mesh) else body_any,
        mesh=mesh,
        in_specs=(
            P("pas", None),
            P("pas", None, "mdl"),
            P("pas"),
            P("pas"),
            P(),
            P("pas", "mdl"),
            P("pas", "mdl"),
            P("pas", "mdl"),
            P("mdl", "pas"),
            P(None, "mdl"),
            P("pas", "mdl"),
            P("pas", "mdl"),
            P("pas", "mdl"),
            P("mdl", "pas"),
            P("pas", "mdl"),
            P("mdl", "pas"),
            P("pas", None),
        ),
        out_specs=(
            P("pas", None),
            P("pas", None),
            P("pas", None, "mdl"),
            P(),
            P("pas", "mdl"),
            P("pas", "mdl"),
            P("pas", "mdl"),
            P("mdl", "pas"),
            P(None, "mdl"),
            P("pas", "mdl"),
            P("pas", "mdl"),
            P("pas", "mdl"),
            P("mdl", "pas"),
            P("pas", "mdl"),
            P("mdl", "pas"),
        ),
        check_vma=False,
    )
```

```python
from functools import partial
import math

import jax
import jax.numpy as jnp
import numpy as np
from jax import lax
from jax.experimental import pallas as pl
from jax.experimental.pallas import tpu as pltpu
from jax.sharding import PartitionSpec as P

HEAD_DIM = 64
MAXDIST = 128
TLEN = 256
PQ = 40


EPSILON = 1e-06
MASKED = -1e30


def bucket_table(length, buckets, distance):
    later = np.arange(length)[:, None]
    earlier = np.arange(length)[None, :]
    behind = np.maximum(later - earlier, 0)
    exact = buckets // 2
    spread = np.log(np.maximum(behind, 1) / exact) / math.log(distance / exact) * (buckets - exact)
    far_bucket = np.minimum(exact + np.floor(spread).astype(np.int32), buckets - 1)
    return np.where(behind < exact, behind, far_bucket).astype(np.int32)


def rms_forward(values, gain):
    factor = lax.rsqrt(jnp.mean(values * values, axis=-1, keepdims=True) + EPSILON)
    unit_rows = values * factor
    return (unit_rows, factor, (unit_rows * gain).astype(jnp.bfloat16))


def rms_backward(normed_grad, unit_rows, factor, gain):
    scaled_grad = normed_grad * gain
    input_grad = factor * (
        scaled_grad - unit_rows * jnp.mean(scaled_grad * unit_rows, axis=-1, keepdims=True)
    )
    return (input_grad, jnp.sum(normed_grad * unit_rows, axis=0))


def over_heads(partial_rows):
    return lax.psum(partial_rows, "mdl")


def score_block(queries, key_rows, allowed, bias):
    scores = jnp.einsum("sihe,sjhe->shij", queries, key_rows, preferred_element_type=jnp.float32)
    if bias is not None:
        scores = scores + bias
    return jnp.where(allowed, scores, MASKED)


def attend(queries, key_rows, values, allowed, bias):
    scores = score_block(queries, key_rows, allowed, bias)
    highest = jnp.max(scores, axis=-1, keepdims=True)
    totals = highest + jnp.log(jnp.sum(jnp.exp(scores - highest), axis=-1, keepdims=True))
    probability = jnp.exp(scores - totals)
    mixed = jnp.einsum(
        "shij,sjhe->sihe",
        probability.astype(jnp.bfloat16),
        values,
        preferred_element_type=jnp.float32,
    )
    return (mixed.astype(jnp.bfloat16), totals)


def attend_back(queries, key_rows, values, allowed, bias, totals, out_grad):
    scores = score_block(queries, key_rows, allowed, bias)
    probability = jnp.exp(scores - totals)
    prob_grad = jnp.einsum("sihe,sjhe->shij", out_grad, values, preferred_element_type=jnp.float32)
    centered = jnp.sum(probability * prob_grad, axis=-1, keepdims=True)
    score_grad = (probability * (prob_grad - centered)).astype(jnp.bfloat16)
    query_grad = jnp.einsum(
        "shij,sjhe->sihe", score_grad, key_rows, preferred_element_type=jnp.float32
    )
    key_grad = jnp.einsum(
        "shij,sihe->sjhe", score_grad, queries, preferred_element_type=jnp.float32
    )
    value_grad = jnp.einsum(
        "shij,sihe->sjhe",
        probability.astype(jnp.bfloat16),
        out_grad,
        preferred_element_type=jnp.float32,
    )
    return (query_grad, key_grad, value_grad, score_grad)


def send_plan(slot_query, slot_live, per_device, capacity):
    target_device = slot_query // per_device
    matching = target_device[:, None] == target_device[None, :]
    lower_part = jnp.tril(jnp.ones(matching.shape, jnp.bool_), -1)
    ranking = jnp.sum(jnp.logical_and(matching, lower_part), axis=1)
    position = target_device * capacity + ranking
    codes = jnp.where(slot_live > 0, slot_query % per_device + 1, 0).astype(jnp.bfloat16)
    return (position, codes)


def arrange_plan(got_codes, per_device, slots_each):
    local_query = got_codes.astype(jnp.int32) - 1
    matches = (local_query[:, None] == jnp.arange(per_device, dtype=jnp.int32)[None, :]).astype(
        jnp.int32
    )
    ranking = jnp.sum((jnp.cumsum(matches, axis=0) - 1) * matches, axis=1)
    spare_place = per_device * slots_each
    places = jnp.where(local_query >= 0, local_query * slots_each + ranking, spare_place)
    arrivals = got_codes.shape[0]
    gather_index = (
        jnp.zeros((spare_place + 1,), jnp.int32)
        .at[places]
        .set(jnp.arange(arrivals, dtype=jnp.int32))
    )
    valid_slot = jnp.zeros((spare_place + 1,), jnp.int32).at[places].set(1)
    return (gather_index[:spare_place], valid_slot[:spare_place] > 0)


def place_rows(rows, position, total_rows):
    return jnp.zeros((total_rows,) + rows.shape[1:], rows.dtype).at[position].set(rows)


def return_rows(rows, gather_index, total_rows):
    return jnp.zeros((total_rows,) + rows.shape[1:], rows.dtype).at[gather_index].add(rows)


def body_any(
    target_states,
    passage_states,
    slot_query,
    slot_live,
    norm_gains,
    self_query,
    self_key,
    self_value,
    self_output,
    position_bias,
    cross_query,
    cross_key,
    cross_value,
    cross_output,
    expand_weight,
    reduce_weight,
    output_cotangent,
):
    (
        query_full,
        key_full,
        value_full,
        cross_query_full,
        cross_key_full,
        cross_value_full,
        expand_full,
    ) = (
        lax.all_gather(self_query, "pas", axis=0, tiled=True),
        lax.all_gather(self_key, "pas", axis=0, tiled=True),
        lax.all_gather(self_value, "pas", axis=0, tiled=True),
        lax.all_gather(cross_query, "pas", axis=0, tiled=True),
        lax.all_gather(cross_key, "pas", axis=0, tiled=True),
        lax.all_gather(cross_value, "pas", axis=0, tiled=True),
        lax.all_gather(expand_weight, "pas", axis=0, tiled=True),
    )
    output_full, cross_output_full, reduce_full = (
        lax.all_gather(self_output, "pas", axis=1, tiled=True),
        lax.all_gather(cross_output, "pas", axis=1, tiled=True),
        lax.all_gather(reduce_weight, "pas", axis=1, tiled=True),
    )
    width_here = query_full.shape[1]
    heads_here = width_here // HEAD_DIM
    sequences = target_states.shape[0] // TLEN
    passage_len = passage_states.shape[1]
    bucket_count = position_bias.shape[0]
    devices = lax.axis_size("pas")
    slots_here = slot_query.shape[0]
    capacity = -(-slots_here // devices)
    buffer_rows = devices * capacity
    residual = target_states.astype(jnp.float32)
    unit_one, factor_one, normed_one = rms_forward(residual, norm_gains[0])
    self_weights = jnp.concatenate([query_full, key_full, value_full], axis=1)
    projected = jnp.dot(normed_one, self_weights, preferred_element_type=jnp.float32).astype(
        jnp.bfloat16
    )
    projected = projected.reshape(sequences, TLEN, 3, heads_here, HEAD_DIM)
    queries_self = projected[:, :, 0]
    keys_self = projected[:, :, 1]
    values_self = projected[:, :, 2]
    buckets = jnp.asarray(bucket_table(TLEN, bucket_count, MAXDIST))
    one_hot = (jnp.arange(bucket_count, dtype=jnp.int32)[:, None, None] == buckets[None]).astype(
        jnp.float32
    )
    bias_full = jnp.einsum("bij,bh->hij", one_hot, position_bias, precision=lax.Precision.HIGHEST)[
        None
    ]
    causal = jnp.asarray(np.tril(np.ones((TLEN, TLEN), dtype=bool)))
    attended_self, total_self = attend(queries_self, keys_self, values_self, causal, bias_full)
    merged_self = attended_self.reshape(sequences * TLEN, width_here)
    residual_two = residual + over_heads(
        jnp.dot(merged_self, output_full, preferred_element_type=jnp.float32)
    )
    unit_two, factor_two, normed_two = rms_forward(residual_two, norm_gains[1])
    cross_queries = jnp.dot(
        normed_two, cross_query_full, preferred_element_type=jnp.float32
    ).astype(jnp.bfloat16)
    cross_queries = cross_queries.reshape(sequences, TLEN, heads_here, HEAD_DIM)
    kv_weights = jnp.concatenate([cross_key_full, cross_value_full], axis=1)
    position, codes = send_plan(slot_query, slot_live, sequences, capacity)
    sent_codes = place_rows(codes, position, buffer_rows)
    states_full = lax.all_gather(passage_states, "mdl", axis=2, tiled=True)
    key_values = jnp.einsum(
        "tpd,dc->tpc", states_full, kv_weights, preferred_element_type=jnp.float32
    ).astype(jnp.bfloat16)
    received, got_codes = (
        lax.all_to_all(
            place_rows(key_values, position, buffer_rows),
            "pas",
            split_axis=0,
            concat_axis=0,
            tiled=True,
        ),
        lax.all_to_all(sent_codes, "pas", split_axis=0, concat_axis=0, tiled=True),
    )
    gather_index, valid_slot = arrange_plan(got_codes, sequences, PQ)
    arranged = jnp.take(received, gather_index, axis=0)
    arranged = arranged.reshape(sequences, PQ * passage_len, 2, heads_here, HEAD_DIM)
    key_rows = arranged[:, :, 0]
    value_rows = arranged[:, :, 1]
    allowed = jnp.repeat(valid_slot.reshape(sequences, PQ), passage_len, axis=1)[:, None, None, :]
    head_block = 2
    head_ranges = [
        slice(start_head, start_head + head_block)
        for start_head in range(0, heads_here, head_block)
    ]
    cross_parts = []
    cross_totals = []
    for head_range in head_ranges:
        mixed_part, total_part = attend(
            cross_queries[:, :, head_range],
            key_rows[:, :, head_range],
            value_rows[:, :, head_range],
            allowed,
            None,
        )
        cross_parts.append(mixed_part)
        cross_totals.append(total_part)
    merged_cross = jnp.concatenate(cross_parts, axis=2).reshape(sequences * TLEN, width_here)
    residual_three = residual_two + over_heads(
        jnp.dot(merged_cross, cross_output_full, preferred_element_type=jnp.float32)
    )
    unit_three, factor_three, normed_three = rms_forward(residual_three, norm_gains[2])
    before = jnp.dot(normed_three, expand_full, preferred_element_type=jnp.float32)
    hidden = jax.nn.gelu(before, approximate=True).astype(jnp.bfloat16)
    block_out = residual_three + over_heads(
        jnp.dot(hidden, reduce_full, preferred_element_type=jnp.float32)
    )
    grad_out = output_cotangent.astype(jnp.float32)
    reduce_grad = jnp.dot(hidden.T, output_cotangent, preferred_element_type=jnp.float32)
    hidden_grad = jnp.dot(output_cotangent, reduce_full.T, preferred_element_type=jnp.float32)
    unused_value, gelu_pullback = jax.vjp(partial(jax.nn.gelu, approximate=True), before)
    before_grad = gelu_pullback(hidden_grad)[0].astype(jnp.bfloat16)
    expand_grad = jnp.dot(normed_three.T, before_grad, preferred_element_type=jnp.float32)
    normed_grad = over_heads(
        jnp.dot(before_grad, expand_full.T, preferred_element_type=jnp.float32)
    )
    back_three, gain_three = rms_backward(normed_grad, unit_three, factor_three, norm_gains[2])
    grad_three = grad_out + back_three
    grad_low = grad_three.astype(jnp.bfloat16)
    cross_output_grad = jnp.dot(merged_cross.T, grad_low, preferred_element_type=jnp.float32)
    mixed_grad = jnp.dot(grad_low, cross_output_full.T, preferred_element_type=jnp.float32).astype(
        jnp.bfloat16
    )
    mixed_grad = mixed_grad.reshape(sequences, TLEN, heads_here, HEAD_DIM)
    query_parts = []
    key_parts = []
    value_parts = []
    for number, head_range in enumerate(head_ranges):
        query_part, key_part, value_part, unused_scores = attend_back(
            cross_queries[:, :, head_range],
            key_rows[:, :, head_range],
            value_rows[:, :, head_range],
            allowed,
            None,
            cross_totals[number],
            mixed_grad[:, :, head_range],
        )
        query_parts.append(query_part)
        key_parts.append(key_part)
        value_parts.append(value_part)
    cross_query_rows = (
        jnp.concatenate(query_parts, axis=2)
        .astype(jnp.bfloat16)
        .reshape(sequences * TLEN, width_here)
    )
    kv_grad = jnp.stack(
        [jnp.concatenate(key_parts, axis=2), jnp.concatenate(value_parts, axis=2)], axis=2
    )
    kv_grad = kv_grad.astype(jnp.bfloat16).reshape(sequences * PQ, passage_len, 2 * width_here)
    returned = lax.all_to_all(
        return_rows(kv_grad, gather_index, buffer_rows),
        "pas",
        split_axis=0,
        concat_axis=0,
        tiled=True,
    )
    kv_grad_here = jnp.take(returned, position, axis=0)
    kv_weight_grad = jnp.einsum(
        "tpd,tpc->dc", states_full, kv_grad_here, preferred_element_type=jnp.float32
    )
    states_grad = jnp.einsum(
        "tpc,dc->tpd", kv_grad_here, kv_weights, preferred_element_type=jnp.float32
    )
    passage_grad = lax.psum_scatter(
        states_grad.astype(jnp.bfloat16), "mdl", scatter_dimension=2, tiled=True
    )
    cross_query_grad = jnp.dot(normed_two.T, cross_query_rows, preferred_element_type=jnp.float32)
    normed_grad = over_heads(
        jnp.dot(cross_query_rows, cross_query_full.T, preferred_element_type=jnp.float32)
    )
    back_two, gain_two = rms_backward(normed_grad, unit_two, factor_two, norm_gains[1])
    grad_two = grad_three + back_two
    grad_low = grad_two.astype(jnp.bfloat16)
    self_output_grad = jnp.dot(merged_self.T, grad_low, preferred_element_type=jnp.float32)
    attended_grad = jnp.dot(grad_low, output_full.T, preferred_element_type=jnp.float32).astype(
        jnp.bfloat16
    )
    attended_grad = attended_grad.reshape(sequences, TLEN, heads_here, HEAD_DIM)
    query_grad, key_grad, value_grad, score_grad = attend_back(
        queries_self, keys_self, values_self, causal, bias_full, total_self, attended_grad
    )
    bias_grad = jnp.einsum(
        "hij,bij->bh",
        jnp.sum(score_grad.astype(jnp.float32), axis=0),
        one_hot,
        precision=lax.Precision.HIGHEST,
    )
    projected_grad = jnp.stack([query_grad, key_grad, value_grad], axis=2).astype(jnp.bfloat16)
    projected_grad = projected_grad.reshape(sequences * TLEN, 3 * width_here)
    self_weight_grad = jnp.dot(normed_one.T, projected_grad, preferred_element_type=jnp.float32)
    normed_grad = over_heads(
        jnp.dot(projected_grad, self_weights.T, preferred_element_type=jnp.float32)
    )
    back_one, gain_one = rms_backward(normed_grad, unit_one, factor_one, norm_gains[0])
    target_grad = (grad_two + back_one).astype(jnp.bfloat16)
    row_grads = (
        lax.psum_scatter(self_weight_grad[:, :width_here], "pas", scatter_dimension=0, tiled=True),
        lax.psum_scatter(
            self_weight_grad[:, width_here : 2 * width_here], "pas", scatter_dimension=0, tiled=True
        ),
        lax.psum_scatter(
            self_weight_grad[:, 2 * width_here :], "pas", scatter_dimension=0, tiled=True
        ),
        lax.psum_scatter(cross_query_grad, "pas", scatter_dimension=0, tiled=True),
        lax.psum_scatter(kv_weight_grad[:, :width_here], "pas", scatter_dimension=0, tiled=True),
        lax.psum_scatter(kv_weight_grad[:, width_here:], "pas", scatter_dimension=0, tiled=True),
        lax.psum_scatter(expand_grad, "pas", scatter_dimension=0, tiled=True),
    )
    col_grads = (
        lax.psum_scatter(self_output_grad, "pas", scatter_dimension=1, tiled=True),
        lax.psum_scatter(cross_output_grad, "pas", scatter_dimension=1, tiled=True),
        lax.psum_scatter(reduce_grad, "pas", scatter_dimension=1, tiled=True),
    )
    gains_total, bias_total = lax.psum(
        (jnp.stack([gain_one, gain_two, gain_three]), bias_grad), "pas"
    )
    return (
        block_out.astype(jnp.bfloat16),
        target_grad,
        passage_grad,
        gains_total,
        row_grads[0],
        row_grads[1],
        row_grads[2],
        col_grads[0],
        bias_total,
        row_grads[3],
        row_grads[4],
        row_grads[5],
        col_grads[1],
        row_grads[6],
        col_grads[2],
    )


CHIPS = 16
RANKS = 3
FLAG_ROWS = 16
MESH_ID = pl.DeviceIdType.MESH
VMEM_LIMIT = 56 * 2**20


def fits(mesh):
    return mesh.shape["pas"] == CHIPS and mesh.shape["mdl"] == 2


def places():
    me, core = lax.axis_index("pas"), lax.axis_index("mdl")
    x, y, z = me % 2, (me // 2) % 2, me // 4
    across_x, across_y = me + 1 - 2 * x, me + 2 - 4 * y
    near = across_y + (across_x - across_y) * core
    far = across_x + (across_y - across_x) * core
    return me, core, x, y, z, near, far


def remote(src, dst, send_sem, recv_sem, device):
    return pltpu.make_async_remote_copy(
        src_ref=src,
        dst_ref=dst,
        send_sem=send_sem,
        recv_sem=recv_sem,
        device_id=device,
        device_id_type=MESH_ID,
    )


def greet_signal(me, core):
    barrier = pltpu.get_barrier_semaphore()
    for k in range(1, CHIPS):
        pl.semaphore_signal(
            barrier, inc=1, device_id=((me + k) % CHIPS, core), device_id_type=MESH_ID
        )
    pl.semaphore_signal(barrier, inc=1, device_id=(me, 1 - core), device_id_type=MESH_ID)


def greet_wait():
    pl.semaphore_wait(pltpu.get_barrier_semaphore(), CHIPS)


ANY = pl.BlockSpec(memory_space=pl.ANY)
IN_VMEM = pl.BlockSpec(memory_space=pltpu.VMEM)
IN_SMEM = pl.BlockSpec(memory_space=pltpu.SMEM)
DMA = pltpu.SemaphoreType.DMA


def rows_nt(left, right):
    return lax.dot_general(
        left, right, (((1,), (1,)), ((), ())), preferred_element_type=jnp.float32
    )


def rows_tn(left, right):
    return lax.dot_general(
        left, right, (((0,), (0,)), ((), ())), preferred_element_type=jnp.float32
    )


TILE = 2


def mm(left, right):
    return jnp.dot(left, right, preferred_element_type=jnp.float32)


def halves_of_pair(rows, head):
    lane = lax.broadcasted_iota(jnp.int32, (rows.shape[0], 2 * HEAD_DIM), 1)
    at = head // 2 * 2 * HEAD_DIM
    return jnp.where(lane // HEAD_DIM == head % 2, rows[:, at : at + 2 * HEAD_DIM], 0.0).astype(
        jnp.bfloat16
    )


def halves_of_rows(rows, head):
    row = lax.broadcasted_iota(jnp.int32, (2 * HEAD_DIM, rows.shape[1]), 0)
    at = head // 2 * 2 * HEAD_DIM
    return jnp.where(row // HEAD_DIM == head % 2, rows[at : at + 2 * HEAD_DIM], 0.0).astype(
        jnp.bfloat16
    )


def unit_of(values):
    factor = lax.rsqrt(jnp.mean(values * values, axis=-1, keepdims=True) + EPSILON)
    return values * factor, factor


def prepare_heads(heads, query_ref, grad, mixed, q_pair, o_pair, o_rows, centre):
    grad = grad.astype(jnp.float32)
    grad_t = grad.T
    product = (grad * mixed.astype(jnp.float32)).T
    queries = query_ref[...].astype(jnp.float32)
    for h in range(heads):
        q_pair[h] = halves_of_pair(queries, h)
        o_pair[h] = halves_of_pair(grad, h)
        o_rows[h] = halves_of_rows(grad_t, h)
        centre[h : h + 1, :] = jnp.sum(
            product[h * HEAD_DIM : (h + 1) * HEAD_DIM], axis=0, keepdims=True
        )


def head_pair_back(p, keys, values, prob, q_pair, o_pair, o_rows, centre, keep_scores):
    low = jnp.bfloat16
    keys_t = keys.T
    query_parts = []
    for a in range(2):
        h = 2 * p + a
        prob_grad = mm(values, o_rows[h])
        weights = prob(h)
        score_grad = (weights * (prob_grad - centre[h : h + 1, :])).astype(low)
        if keep_scores is not None:
            keep_scores(h, score_grad)
        key_part = mm(score_grad, q_pair[h])
        value_part = mm(weights.astype(low), o_pair[h])
        key_grad = key_part if a == 0 else key_grad + key_part
        value_grad = value_part if a == 0 else value_grad + value_part
        query_parts.append(mm(keys_t[a * HEAD_DIM : (a + 1) * HEAD_DIM], score_grad))
    return key_grad.astype(low), value_grad.astype(low), query_parts


def z_turned(z, k):
    high, low = z // 2, z % 2
    if k % 2:
        high = 1 - high
    if k // 2:
        low = 1 - low
    return 2 * high + low


def exp_rows(scores):
    highest = jnp.max(scores, axis=0, keepdims=True)
    exps = jnp.exp(scores - highest)
    return exps, highest, jnp.sum(exps, axis=0, keepdims=True)


def gelu_both(values):
    first = math.sqrt(2 / math.pi)
    square = values * values
    curve = jnp.tanh(first * values * (1.0 + 0.044715 * square))
    half = 0.5 * (1.0 + curve)
    slope = half + 0.5 * values * (1.0 - curve * curve) * first * (1.0 + 3 * 0.044715 * square)
    return values * half, slope


GATHER_MIDDLE = ()
FOLD_MIDDLE = ()
def block_kernel(
    index_ref,
    live_ref,
    query_of_ref,
    rank_ref,
    passage_ref,
    read_self_refs,
    write_self_ref,
    read_cross_refs,
    write_cross_ref,
    expand_ref,
    reduce_ref,
    target_ref,
    cotangent_ref,
    gains_ref,
    table_ref,
    bucket_ref,
    count_ref,
    shard_out,
    slots_ref,
    gains_out,
    bias_out,
    target_grad_ref,
    block_ref,
    exps_out,
    kv_out,
    shard_ref,
    flag_ref,
    full,
    states,
    flags,
    kept,
    slot_got,
    exps,
    keys,
    q_rows,
    q_pair,
    o_pair,
    o_rows,
    centre,
    out_t,
    highest,
    total,
    tile_highest,
    scale_ref,
    query_ref,
    mixed_ref,
    residual_ref,
    qkv_ref,
    self_mixed_ref,
    self_exps_ref,
    self_scale_ref,
    upper_grad,
    row_sent,
    row_got,
    far_got,
    near_got,
    next_got,
    skip_got,
    dkv,
    kv_sum,
    early,
    outgoing,
    pair_got,
    small,
    small_got,
    skip_send,
    skip_recv,
    next_send,
    next_recv,
    near_send,
    near_recv,
    far_send,
    far_recv,
    fold_far_send,
    fold_far_recv,
    fold_near_send,
    fold_near_recv,
    fold_next_send,
    fold_next_recv,
    fold_skip_send,
    fold_skip_recv,
    slot_send,
    slot_recv,
    flag_send,
    flag_recv,
    core_send,
    core_recv,
    return_send,
    return_recv,
    pair_send,
    pair_recv,
    row_send,
    row_recv,
    small_send,
    small_recv,
    own_sem,
    exps_sem,
    keys_sem,
    out_sem,
):
    low, wide = jnp.bfloat16, jnp.float32
    me, core, x, y, z, near, far = places()
    groups = shard_ref.shape[0]
    partner = (me, 1 - core)
    pair = me // TILE
    tiles = CHIPS // TILE
    passage_len = states.shape[2]
    block_rows = RANKS * passage_len
    tile_rows = TILE * block_rows
    tokens = target_ref.shape[0]
    width = query_ref.shape[1]
    turn = 1 - core
    across_x, across_y = me + 1 - 2 * x, me + 2 - 4 * y
    skip_to = (me - 4 * z + 4 * z_turned(z, 1), core)
    next_to = (me - 4 * z + 4 * z_turned(z, 2), core)
    pairs = width // (2 * HEAD_DIM)
    heads = 2 * pairs
    half = states.shape[3]
    other_y = y + (1 - core) * (1 - 2 * y)
    other_x = x + core * (1 - 2 * x)

    def slots_of(ref, source):
        return ref.at[pl.ds(source * RANKS, RANKS)]

    def own_copy(g):
        return pltpu.make_async_copy(shard_ref.at[g], full.at[g, z, y, x], own_sem.at[g])

    def z_at(k):
        return z_turned(z, k)

    def spot(g, k, m):
        if m == 0:
            return full.at[g, z_at(k), y, x]
        return full.at[g, z_at(k), other_y, other_x]

    def block_of(g, k, m):
        return shard_ref.at[g] if k == m == 0 else spot(g, k, m)

    def skip_copy(g, m):
        src, dst = block_of(g, 0, m), spot(g, 0, m)
        return remote(src, dst, skip_send.at[g, m], skip_recv.at[g, m], skip_to)

    def next_copy(g, k, m):
        src, dst = block_of(g, k, m), spot(g, k, m)
        return remote(src, dst, next_send.at[g, k, m], next_recv.at[g, k, m], next_to)

    def near_copy(g, k):
        src, dst = block_of(g, k, 0), spot(g, k, 0)
        return remote(src, dst, near_send.at[g, k], near_recv.at[g, k], (near, core))

    def far_copy(g, k, m):
        src, dst = block_of(g, k, m), spot(g, k, m)
        return remote(src, dst, far_send.at[g, k, m], far_recv.at[g, k, m], (far, core))

    def before_far(g):
        if g in GATHER_MIDDLE:
            copies = [near_copy(g, 0)] + [skip_copy(g, m) for m in range(2)]
            return copies + [next_copy(g, k, m) for k in range(2) for m in range(2)]
        copies = [skip_copy(g, 0)] + [next_copy(g, k, 0) for k in range(2)]
        return copies + [near_copy(g, k) for k in range(4)]

    def slot_copy(to):
        return remote(
            slots_of(kept, to), slots_of(states.at[core], me), slot_send.at[to], slot_recv.at[me], (to, core)
        )

    def slot_arrival(came):
        block = slots_of(states.at[core], came)
        return remote(block, block, slot_send.at[came], slot_recv.at[came], (came, core))

    def flag_copy(to):
        return remote(flag_ref.at[to], flags.at[me], flag_send.at[to], flag_recv.at[me], (to, core))

    def flag_arrival(came):
        block = flags.at[came]
        return remote(block, block, flag_send.at[came], flag_recv.at[came], (came, core))

    def core_copy(came):
        block = slots_of(states.at[core], came)
        return remote(block, block, core_send.at[came], core_recv.at[came], partner)

    def row_copy(i):
        b = i % 2
        return remote(row_sent.at[b], row_got.at[b], row_send.at[i], row_recv.at[i], partner)

    def give(i, value):
        if i >= 2:
            row_copy(i - 2).wait_send()
        row_sent[i % 2] = value
        row_copy(i).start()

    def pair_sum(i):
        row_copy(i).wait_recv()
        return row_sent[i % 2] + row_got[i % 2]

    def launch(g):
        if g in GATHER_MIDDLE:
            near_copy(g, 0).start()
        skip_copy(g, 0).start()
        next_copy(g, 0, 0).start()
        if g not in GATHER_MIDDLE:
            near_copy(g, 0).start()
        far_copy(g, 0, 0).start()
        own_copy(g).start()

    def relay_one(g):
        if g in GATHER_MIDDLE:
            near_copy(g, 0).wait_recv()
            skip_copy(g, 1).start()
            next_copy(g, 0, 1).start()
            far_copy(g, 0, 1).start()
        else:
            skip_copy(g, 0).wait_recv()
            next_copy(g, 1, 0).start()
            near_copy(g, 1).start()
            far_copy(g, 1, 0).start()

    def relay_two(g):
        for i in range(2):
            if g in GATHER_MIDDLE:
                skip_copy(g, i).wait_recv()
                next_copy(g, 1, i).start()
                far_copy(g, 1, i).start()
            else:
                next_copy(g, i, 0).wait_recv()
                near_copy(g, i + 2).start()
                far_copy(g, i + 2, 0).start()

    def relay_three(g):
        for i in range(4):
            if g in GATHER_MIDDLE:
                k, m = i % 2, i // 2
                next_copy(g, k, m).wait_recv()
                far_copy(g, k + 2, m).start()
            else:
                near_copy(g, i).wait_recv()
                far_copy(g, i, 1).start()

    def arrived(g):
        own_copy(g).wait()
        for k in range(4):
            for m in range(2):
                far_copy(g, k, m).wait_recv()

    def weight(g):
        return full[g].reshape(full.shape[1] * 4 * full.shape[4], full.shape[5])

    staging = pltpu.make_async_copy(
        passage_ref, slot_got.at[pl.ds(0, passage_ref.shape[0])], out_sem.at[0]
    )
    staging.start()

    def mine(g, k, m, here):
        near_at, far_at = (1 - turn) * y + turn * x, (1 - turn) * x + turn * y
        near_at = near_at if m == 0 else 1 - near_at
        far_at = far_at if here else 1 - far_at
        grads = early if g == 3 else full.at[g]
        return grads.at[
            z_at(k),
            (1 - turn) * near_at + turn * far_at,
            (1 - turn) * far_at + turn * near_at,
        ]

    def next_place(g, k, m):
        return next_got.at[g, k] if m == 0 else near_got.at[g, 1 + k]

    def skip_place(g, m):
        return skip_got.at[g] if m == 0 else near_got.at[g, 3]

    def fold_far(g, k, m):
        src, dst = mine(g, k, m, False), far_got.at[g, m, k]
        sems = fold_far_send.at[g, k, m], fold_far_recv.at[g, k, m]
        return remote(src, dst, *sems, (near, core))

    def fold_near(g, k):
        src, dst = far_got.at[g, 1, k], near_got.at[g, k]
        return remote(src, dst, fold_near_send.at[g, k], fold_near_recv.at[g, k], (far, core))

    def fold_next(g, k, m):
        src = far_got.at[g, m, 2 + k] if g in FOLD_MIDDLE else near_got.at[g, 2 + k]
        sems = fold_next_send.at[g, k, m], fold_next_recv.at[g, k, m]
        return remote(src, next_place(g, k, m), *sems, next_to)

    def fold_skip(g, m):
        src = far_got.at[g, m, 1] if g in FOLD_MIDDLE else near_got.at[g, 1]
        sems = fold_skip_send.at[g, m], fold_skip_recv.at[g, m]
        return remote(src, skip_place(g, m), *sems, skip_to)

    def fold_copies(g):
        copies = [fold_far(g, k, m) for k in range(4) for m in range(2)]
        if g in FOLD_MIDDLE:
            copies += [fold_next(g, k, m) for k in range(2) for m in range(2)]
            return copies + [fold_skip(g, m) for m in range(2)] + [fold_near(g, 0)]
        copies += [fold_next(g, k, 0) for k in range(2)]
        return copies + [fold_skip(g, 0)] + [fold_near(g, k) for k in range(4)]

    def add_up(ref, *others):
        total = ref[...].astype(wide)
        for other in others:
            total = total + other[...].astype(wide)
        ref[...] = total.astype(low)

    def far_start(g):
        order = [(k, m) for m in (1, 0) for k in (3, 2, 1, 0)]
        if g in FOLD_MIDDLE:
            order = [(k, m) for k in (3, 2, 1, 0) for m in (1, 0)]
        for k, m in order:
            fold_far(g, k, m).start()

    def far_add(g):
        if g in FOLD_MIDDLE:
            for k, m in ((3, 1), (3, 0), (2, 1), (2, 0)):
                fold_far(g, k, m).wait_recv()
                add_up(far_got.at[g, m, k], mine(g, k, m, True))
                fold_next(g, k - 2, m).start()
        else:
            for k in (3, 2, 1, 0):
                fold_far(g, k, 1).wait_recv()
                add_up(far_got.at[g, 1, k], mine(g, k, 1, True))
                fold_near(g, k).start()

    def near_add(g):
        if g in FOLD_MIDDLE:
            for m in (1, 0):
                fold_far(g, 1, m).wait_recv()
                fold_next(g, 1, m).wait_recv()
                add_up(far_got.at[g, m, 1], mine(g, 1, m, True), next_place(g, 1, m))
                fold_skip(g, m).start()
        else:
            for k in (3, 2, 1, 0):
                fold_far(g, k, 0).wait_recv()
                fold_near(g, k).wait_recv()
                add_up(near_got.at[g, k], mine(g, k, 0, True), far_got.at[g, 0, k])
                if k >= 2:
                    fold_next(g, k - 2, 0).start()

    def next_add(g):
        if g in FOLD_MIDDLE:
            fold_far(g, 0, 1).wait_recv()
            fold_next(g, 0, 1).wait_recv()
            fold_skip(g, 1).wait_recv()
            add_up(
                far_got.at[g, 1, 0], mine(g, 0, 1, True), next_place(g, 0, 1), skip_place(g, 1)
            )
            fold_near(g, 0).start()
        else:
            fold_next(g, 1, 0).wait_recv()
            add_up(near_got.at[g, 1], next_place(g, 1, 0))
            fold_skip(g, 0).start()

    def skip_add(g):
        fold_next(g, 0, 0).wait_recv()
        fold_skip(g, 0).wait_recv()
        if g in FOLD_MIDDLE:
            fold_far(g, 0, 0).wait_recv()
            fold_near(g, 0).wait_recv()
        parts = [near_got[g, 0], next_got[g, 0], skip_got[g]]
        if g in FOLD_MIDDLE:
            parts += [mine(g, 0, 0, True)[...], far_got[g, 0, 0]]
        total = parts[0].astype(wide)
        for part in parts[1:]:
            total = total + part.astype(wide)
        shard_out[g] = total

    def send_pair(j):
        for i in range(TILE):
            to = (pair + j) % tiles * TILE + i

            @pl.when(to != me)
            def _():
                flag_copy(to).start()
                slot_copy(to).start()

    def fill(to, carry):
        for rank in range(RANKS):
            kept[to * RANKS + rank] = slot_got[index_ref[to * RANKS + rank]]
        row = lax.broadcasted_iota(jnp.int32, flag_ref.shape[1:], 0)
        marks = jnp.zeros(flag_ref.shape[1:], wide)
        for rank in range(RANKS):
            mark = jnp.where(live_ref[to * RANKS + rank] > 0, 0.0, MASKED)
            marks = jnp.where(row == rank, mark, marks)
        flag_ref[to] = marks.astype(low)
        return carry

    greet_signal(me, core)
    for g, reads, writes in ((0, read_self_refs, write_self_ref), (1, read_cross_refs, write_cross_ref)):
        for i, read in enumerate(reads):
            shard_ref[g, :, i * width : (i + 1) * width] = read[...]
        shard_ref[g, :, 3 * width :] = writes[...]
    shard_ref[2] = expand_ref[...]
    shard_ref[3] = reduce_ref[...]
    greet_wait()
    launch(0)
    staging.wait()
    lax.fori_loop(0, CHIPS, fill, 0)
    send_pair(0)
    launch(1)
    send_pair(1)
    send_pair(2)
    states[core, pl.ds(me * RANKS, RANKS)] = kept[pl.ds(me * RANKS, RANKS)]
    flags[me] = flag_ref[me]
    core_copy(me).start()

    line = lax.dot_general(
        table_ref[...],
        bucket_ref[...],
        (((1,), (0,)), ((), ())),
        precision=lax.Precision.HIGHEST,
        preferred_element_type=wide,
    )
    def bias_of(h):
        return kv_sum.at[h // 3, pl.ds(0, tokens), pl.ds(h % 3 * tokens, tokens)]

    turns = []
    for h in range(heads):
        for s in range(8):
            row = line[h : h + 1]
            turns.append(row if s == 0 else pltpu.roll(row, s, 1))
    base = jnp.concatenate(turns, axis=0)

    def bias_step(i, carry):
        rows = pltpu.roll(base, 8 * i, 1)
        for h in range(heads):
            bias_of(h)[pl.ds(pl.multiple_of(8 * i, 8), 8), :] = rows[8 * h : 8 * h + 8]
        return carry

    lax.fori_loop(0, tokens // 8, bias_step, 0)
    residual = target_ref[...].astype(wide)
    normed = (unit_of(residual)[0] * gains_ref[0:1, :]).astype(low)

    relay_one(0)
    send_pair(3)
    launch(2)
    relay_two(0)
    relay_three(0)
    relay_one(1)
    send_pair(4)
    relay_two(1)
    arrived(0)

    qkv_ref[...] = mm(normed, weight(0)[:, : 3 * width]).astype(low)
    relay_three(1)
    relay_one(2)
    queries_t = qkv_ref[:, :width].astype(wide).T
    for h in range(heads):
        q_rows[h] = halves_of_rows(queries_t, h)
    key_at = lax.broadcasted_iota(jnp.int32, (tokens, tokens), 0)
    query_at = lax.broadcasted_iota(jnp.int32, (tokens, tokens), 1)
    self_scale_ref[...] = jnp.zeros_like(self_scale_ref)
    for p in range(pairs):
        at = 2 * HEAD_DIM * p
        head_keys = qkv_ref[:, width + at : width + at + 2 * HEAD_DIM]
        values_t = qkv_ref[:, 2 * width + at : 2 * width + at + 2 * HEAD_DIM].T
        for a in range(2):
            h = 2 * p + a
            scores = mm(head_keys, q_rows[h]) + bias_of(h)[...]
            scores = jnp.where(key_at <= query_at, scores, MASKED)
            head_exps, unused, sums = exp_rows(scores)
            head_exps = head_exps.astype(low)
            self_exps_ref[h] = head_exps
            inverse = 1.0 / sums
            self_scale_ref[h : h + 1, :] = inverse
            first = at + a * HEAD_DIM
            out_t[first : first + HEAD_DIM, :] = (
                mm(values_t[a * HEAD_DIM : (a + 1) * HEAD_DIM], head_exps) * inverse
            )
    self_mixed_ref[...] = out_t[...].T.astype(low)
    give(0, rows_nt(self_mixed_ref[...], weight(0)[:, 3 * width :]))
    launch(3)
    send_pair(5)
    arrived(1)
    residual_ref[...] = residual + pair_sum(0)

    normed = (unit_of(residual_ref[...])[0] * gains_ref[1:2, :]).astype(low)
    query_ref[...] = mm(normed, weight(1)[:, :width]).astype(low)
    queries_t = query_ref[...].astype(wide).T
    for h in range(heads):
        q_rows[h] = halves_of_rows(queries_t, h)
    out_t[...] = jnp.zeros_like(out_t)
    highest[...] = jnp.full_like(highest, MASKED)
    total[...] = jnp.zeros_like(total)
    tile_highest[...] = jnp.zeros_like(tile_highest)

    def take_in(t):
        for i in range(TILE):
            came = (pair - t + tiles) % tiles * TILE + i

            @pl.when(came != me)
            def _():
                flag_arrival(came).wait_recv()
                slot_arrival(came).wait_recv()
                core_copy(came).start()

    def exps_copy(t):
        rows = pl.ds((pair - t + tiles) % tiles * tile_rows, tile_rows)
        return pltpu.make_async_copy(exps.at[t % 2], exps_out.at[:, rows], exps_sem.at[t % 2])

    def keys_copy(t):
        rows = pl.ds((pair - t + tiles) % tiles * tile_rows, tile_rows)
        return pltpu.make_async_copy(keys.at[t % 2], kv_out.at[rows], keys_sem.at[t % 2])

    send_pair(6)
    send_pair(7)
    take_in(0)

    def tile_step(t, carry):
        tile = (pair - t + tiles) % tiles

        @pl.when(t == 5)
        def _():
            relay_one(3)

        @pl.when(t == 6)
        def _():
            relay_two(3)

        @pl.when(t + 1 < tiles)
        def _():
            take_in(t + 1)

        @pl.when(t == 2)
        def _():
            relay_two(2)

        @pl.when(t == 3)
        def _():
            relay_three(2)

        @pl.when(t >= 2)
        def _():
            exps_copy(t - 2).wait()
            keys_copy(t - 2).wait()

        for i in range(TILE):
            core_copy(tile * TILE + i).wait_recv()
        kv_parts = []
        for c in range(2):
            rows = states[c, pl.ds(tile * TILE * RANKS, TILE * RANKS)].reshape(tile_rows, half)
            w = full[1, 2 * c : 2 * c + 2, :, :, :, width : 3 * width]
            kv_parts.append(mm(rows, w.reshape(half, 2 * width)))
        keys[t % 2] = (kv_parts[0] + kv_parts[1]).astype(low)
        keys_copy(t).start()
        masks = []
        for i in range(TILE):
            for rank in range(RANKS):
                masks.append(flags[tile * TILE + i, rank : rank + 1, :].astype(wide)[None])
        masks = jnp.concatenate(masks, axis=0)
        for p in range(pairs):
            at = 2 * HEAD_DIM * p
            head_keys = keys[t % 2, :, at : at + 2 * HEAD_DIM]
            values_t = keys[t % 2, :, width + at : width + at + 2 * HEAD_DIM].T
            for a in range(2):
                h = 2 * p + a
                scores = mm(head_keys, q_rows[h]).reshape(TILE * RANKS, passage_len, tokens) + masks
                head_exps, top, sums = exp_rows(scores.reshape(tile_rows, tokens))
                head_exps = head_exps.astype(low)
                exps[t % 2, h] = head_exps
                before = highest[h : h + 1, :]
                now = jnp.maximum(before, top)
                keep, add = jnp.exp(before - now), jnp.exp(top - now)
                highest[h : h + 1, :] = now
                tile_highest[tile, h : h + 1, :] = top
                total[h : h + 1, :] = total[h : h + 1, :] * keep + sums * add
                first = at + a * HEAD_DIM
                out_t[first : first + HEAD_DIM, :] = (
                    out_t[first : first + HEAD_DIM, :] * keep
                    + mm(values_t[a * HEAD_DIM : (a + 1) * HEAD_DIM], head_exps) * add
                )
        exps_copy(t).start()

        return carry

    lax.fori_loop(0, tiles, tile_step, 0)
    relay_three(3)
    for h in range(heads):
        inverse = 1.0 / total[h : h + 1, :]
        out_t[h * HEAD_DIM : (h + 1) * HEAD_DIM, :] *= inverse
        scale_ref[:, h, :] = jnp.exp(tile_highest[:, h, :] - highest[h : h + 1, :]) * inverse
    mixed_ref[...] = out_t[...].T.astype(low)
    give(1, rows_nt(mixed_ref[...], weight(1)[:, 3 * width :]))
    residual_three = residual_ref[...] + pair_sum(1)
    unit, factor = unit_of(residual_three)
    normed = (unit * gains_ref[2:3, :]).astype(low)


    def sends_done(g):
        for copy in before_far(g) + [far_copy(g, k, m) for k in range(4) for m in range(2)]:
            copy.wait_send()

    def store_grad(g, first, value):
        blocks = value.astype(low).reshape(full.shape[1:5] + (value.shape[1],))
        full[g, :, :, :, :, first : first + value.shape[1]] = blocks

    arrived(2)
    hidden, slope = gelu_both(mm(normed, weight(2)))
    hidden = hidden.astype(low)
    early[...] = rows_tn(cotangent_ref[...], hidden).astype(low).reshape(early.shape)
    far_start(3)
    arrived(3)
    hidden_grad = mm(cotangent_ref[...], weight(3))
    before_grad = (hidden_grad * slope).astype(low)
    give(2, rows_nt(before_grad, weight(2)))
    sends_done(2)
    store_grad(2, 0, rows_tn(normed, before_grad))
    far_start(2)
    back, gain_three = rms_backward(pair_sum(2), unit, factor, gains_ref[2:3, :])
    upper_grad[...] = cotangent_ref[...].astype(wide) + back
    give(3, rows_nt(hidden, weight(3)))
    sends_done(0)
    sends_done(1)
    sends_done(3)
    for k in range(1, CHIPS):
        to = (me + k) % CHIPS
        slot_copy(to).wait_send()
        flag_copy(to).wait_send()
    for k in range(CHIPS):
        core_copy(k).wait_send()
    for t in range(tiles - 2, tiles):
        exps_copy(t).wait()
        keys_copy(t).wait()

    def back_tile(t):
        return (t + pair) % tiles

    def exps_load(t):
        rows = pl.ds(back_tile(t) * tile_rows, tile_rows)
        return pltpu.make_async_copy(exps_out.at[:, rows], exps.at[t % 2], exps_sem.at[t % 2])

    def keys_load(t):
        rows = pl.ds(back_tile(t) * tile_rows, tile_rows)
        return pltpu.make_async_copy(kv_out.at[rows], keys.at[t % 2], keys_sem.at[t % 2])

    def loads_start(t):
        exps_load(t).start()
        keys_load(t).start()

    def kv_weights(c):
        w = full[1, pl.ds(2 * c, 2), :, :, :, width : 3 * width]
        return w.reshape(half, 2 * width)

    def pair_copy(t):
        return remote(
            outgoing.at[t % 2],
            pair_got.at[pl.ds(back_tile(t) * TILE * RANKS, TILE * RANKS)],
            pair_send.at[t % 2],
            pair_recv.at[t],
            partner,
        )

    def return_copy(to):
        return remote(
            slots_of(kept, to), slots_of(slot_got, me), return_send.at[to], return_recv.at[me], (to, core)
        )

    def return_arrival(came):
        block = slots_of(slot_got, came)
        return remote(block, block, return_send.at[came], return_recv.at[came], (came, core))

    def finish_tile(t):
        tile = back_tile(t)
        pair_copy(t).wait_recv()
        rows = pl.ds(tile * TILE * RANKS, TILE * RANKS)
        kept[rows] = (kept[rows].astype(wide) + pair_got[rows].astype(wide)).astype(low)
        for j in range(TILE):
            to = tile * TILE + j

            @pl.when(to != me)
            def _():
                return_copy(to).start()

            @pl.when(to == me)
            def _():
                own = pl.ds(me * RANKS, RANKS)
                slot_got[own] = kept[own]

    grad_low = upper_grad[...].astype(low)
    mixed_grad = mm(grad_low, weight(1)[:, 3 * width :]).astype(low)
    prepare_heads(heads, query_ref, mixed_grad, mixed_ref[...], q_pair, o_pair, o_rows, centre)
    out_t[...] = jnp.zeros_like(out_t)
    kv_sum[...] = jnp.zeros_like(kv_sum)
    loads_start(0)
    block_ref[...] = (residual_three + pair_sum(3)).astype(low)

    def back_step(t, carry):
        tile = back_tile(t)
        @pl.when(t + 1 < tiles)
        def _():
            loads_start(t + 1)

        exps_load(t).wait()
        keys_load(t).wait()

        def prob(h):
            return exps[t % 2, h].astype(wide) * scale_ref[tile, h : h + 1, :]

        for p in range(pairs):
            at = 2 * HEAD_DIM * p
            key_grad, value_grad, query_parts = head_pair_back(
                p,
                keys[t % 2, :, at : at + 2 * HEAD_DIM],
                keys[t % 2, :, width + at : width + at + 2 * HEAD_DIM],
                prob,
                q_pair,
                o_pair,
                o_rows,
                centre,
                None,
            )
            dkv[:, at : at + 2 * HEAD_DIM] = key_grad
            dkv[:, width + at : width + at + 2 * HEAD_DIM] = value_grad
            for a in range(2):
                first = at + a * HEAD_DIM
                out_t[first : first + HEAD_DIM, :] += query_parts[a]
        here = dkv[...]

        @pl.when(t >= 2)
        def _():
            pair_copy(t - 2).wait_send()

        weights = kv_weights(1 - core)
        outgoing[t % 2] = rows_nt(here, weights).astype(low).reshape(outgoing.shape[1:])
        pair_copy(t).start()
        weights = kv_weights(core)
        mine = rows_nt(here, weights).astype(low).reshape(outgoing.shape[1:])
        kept[pl.ds(tile * TILE * RANKS, TILE * RANKS)] = mine

        rows = pl.ds(tile * TILE * RANKS, TILE * RANKS)
        for i in range(2):
            kv_sum[i] += rows_tn(states[i, rows].reshape(tile_rows, half), here)

        @pl.when(t >= 1)
        def _():
            finish_tile(t - 1)

        @pl.when(t == 3)
        def _():
            far_add(2)

        @pl.when(t == 6)
        def _():
            far_add(3)

        return carry

    lax.fori_loop(0, tiles, back_step, 0)
    dq = out_t[...].T.astype(low)
    give(4, rows_nt(dq, weight(1)[:, :width]))
    store_grad(1, 3 * width, rows_tn(upper_grad[...].astype(low), mixed_ref[...]))
    finish_tile(tiles - 1)
    near_add(2)
    unit_two, factor_two = unit_of(residual_ref[...])
    normed_two = (unit_two * gains_ref[1:2, :]).astype(low)
    store_grad(1, 0, rows_tn(normed_two, dq))

    store_grad(1, width, kv_sum[...].reshape(2 * half, 2 * width))
    far_start(1)
    next_add(2)

    back, gain_two = rms_backward(pair_sum(4), unit_two, factor_two, gains_ref[1:2, :])
    upper_grad[...] += back

    grad_low = upper_grad[...].astype(low)
    mixed_grad = mm(grad_low, weight(0)[:, 3 * width :]).astype(low)
    prepare_heads(
        heads,
        qkv_ref.at[:, :width],
        mixed_grad,
        self_mixed_ref[...],
        q_pair,
        o_pair,
        o_rows,
        centre,
    )

    def self_prob(h):
        return self_exps_ref[h].astype(wide) * self_scale_ref[h : h + 1, :]

    def keep_scores(h, score_grad):
        self_exps_ref[h] = score_grad

    query_rows, key_columns, value_columns = [], [], []
    for p in range(pairs):
        at = 2 * HEAD_DIM * p
        key_grad, value_grad, query_parts = head_pair_back(
            p,
            qkv_ref[:, width + at : width + at + 2 * HEAD_DIM],
            qkv_ref[:, 2 * width + at : 2 * width + at + 2 * HEAD_DIM],
            self_prob,
            q_pair,
            o_pair,
            o_rows,
            centre,
            keep_scores,
        )
        key_columns.append(key_grad)
        value_columns.append(value_grad)
        query_rows.extend(query_parts)
    dq = jnp.concatenate(query_rows, axis=0).T.astype(low)
    dqkv = jnp.concatenate([dq] + key_columns + value_columns, axis=1)
    near_add(3)
    give(5, rows_nt(dqkv, weight(0)[:, : 3 * width]))
    store_grad(0, 3 * width, rows_tn(upper_grad[...].astype(low), self_mixed_ref[...]))
    unit_one, factor_one = unit_of(target_ref[...].astype(wide))
    normed_one = (unit_one * gains_ref[0:1, :]).astype(low)
    store_grad(0, 0, rows_tn(normed_one, dqkv))
    far_start(0)
    far_add(1)
    next_add(3)

    length = self_exps_ref.shape[1]

    def diagonal_step(i, total):
        rows = self_exps_ref[:, pl.ds(pl.multiple_of(16 * i, 16), 16), :].astype(wide)
        rows = rows.reshape(heads * 16, length)
        return total + pltpu.roll(rows, (length - 16 * i) % length, 1)

    total = lax.fori_loop(
        0, length // 16, diagonal_step, jnp.zeros((heads * 16, length), wide)
    ).reshape(heads, 16, length)
    small[...] = jnp.zeros_like(small)
    for h in range(heads):
        line = total[h, 0:1]
        for s in range(1, 16):
            line = line + pltpu.roll(total[h, s : s + 1], length - s, 1)
        small[8 + h : 9 + h, :length] = line
    by_bucket = jnp.dot(
        small[8:16, :length], count_ref[...], precision=lax.Precision.HIGHEST,
        preferred_element_type=wide,
    )
    small[8:16, :length] = jnp.zeros((8, length), wide)
    small[8:16, : count_ref.shape[1]] = by_bucket

    back, gain_one = rms_backward(pair_sum(5), unit_one, factor_one, gains_ref[0:1, :])
    target_grad_ref[...] = (upper_grad[...] + back).astype(low)
    small[0:1, :] = gain_one[None, :]
    small[1:2, :] = gain_two[None, :]
    small[2:3, :] = gain_three[None, :]

    def small_copy(step):
        if step == 0:
            return remote(small, small_got.at[0], small_send.at[0], small_recv.at[0], (across_x, core))
        if step == 1:
            return remote(
                small_got.at[6], small_got.at[1], small_send.at[1], small_recv.at[1], (across_y, core)
            )
        return remote(
            small_got.at[7],
            small_got.at[2 + z],
            small_send.at[step],
            small_recv.at[step],
            ((me + 4 * (step - 1)) % CHIPS, core),
        )

    small_copy(0).start()
    skip_add(2)
    near_add(1)
    far_add(0)
    skip_add(3)
    next_add(1)
    near_add(0)
    next_add(0)
    skip_add(1)
    small_copy(0).wait_recv()
    small_got[6] = small[...] + small_got[0]
    small_copy(1).start()
    for k in range(1, CHIPS):
        return_arrival((me + k) % CHIPS).wait_recv()
    small_copy(1).wait_recv()
    small_got[7] = small_got[6] + small_got[1]
    for step in range(2, 5):
        small_copy(step).start()
    small_got[2 + z] = small_got[7]
    for k in range(1, CHIPS):
        return_copy((me + k) % CHIPS).wait_send()
    slots = slots_ref.shape[0]

    def pick(slot, carry):
        kept[slot] = slot_got[query_of_ref[slot] * RANKS + rank_ref[slot]]
        return carry

    lax.fori_loop(0, slots, pick, 0)
    picked = pltpu.make_async_copy(kept.at[pl.ds(0, slots)], slots_ref, out_sem.at[1])
    picked.start()
    skip_add(0)
    for step in range(2, 5):
        small_copy(step).wait_recv()
    whole = small_got[2] + small_got[3] + small_got[4] + small_got[5]
    gains_out[...] = whole[: gains_out.shape[0]]
    bias_out[...] = whole[8 : 8 + heads, : bias_out.shape[1]]
    for g in range(groups):
        for copy in fold_copies(g):
            copy.wait_send()
    for t in range(tiles - 2, tiles):
        pair_copy(t).wait_send()
    for step in range(5):
        small_copy(step).wait_send()
    for i in range(4, 6):
        row_copy(i).wait_send()
    picked.wait()


def run_block(
    index, live, query_of, rank, passages, weights, target, cotangent, gains, table, buckets, counts
):
    low, wide = jnp.bfloat16, jnp.float32
    groups = 4
    rows, columns = weights[4].shape
    slots, passage_len, half = passages.shape
    tokens, model = target.shape
    width = columns // 4
    heads = width // HEAD_DIM
    key_count = CHIPS * RANKS * passage_len
    tile_rows = TILE * RANKS * passage_len
    tiles = CHIPS // TILE
    small_shape = (16, model)
    shape = jax.ShapeDtypeStruct
    vmem = pltpu.VMEM
    pair_heads = vmem((heads, tokens, 2 * HEAD_DIM), low)
    pair_rows = vmem((heads, 2 * HEAD_DIM, tokens), low)
    all_slots = (CHIPS * RANKS, passage_len, half)

    def both(*dims):
        return [DMA(dims), DMA(dims)]

    return pl.pallas_call(
        block_kernel,
        out_shape=(
            shape((groups, rows, columns), wide),
            shape((slots, passage_len, half), low),
            shape(gains.shape, wide),
            shape(table.shape, wide),
            shape((tokens, model), low),
            shape((tokens, model), low),
            shape((heads, key_count, tokens), low),
            shape((key_count, 2 * width), low),
        ),
        in_specs=[IN_SMEM] * 4
        + [ANY, (IN_VMEM,) * 3, IN_VMEM, (IN_VMEM,) * 3, IN_VMEM, IN_VMEM, IN_VMEM]
        + [IN_VMEM] * 6,
        out_specs=(IN_VMEM, ANY) + (IN_VMEM,) * 4 + (ANY, ANY),
        scratch_shapes=[
            vmem((groups, rows, columns), low),
            vmem((CHIPS, FLAG_ROWS, tokens), low),
            vmem((groups, 4, 2, 2, rows, columns), low),
            vmem((2,) + all_slots, low),
            vmem((CHIPS, FLAG_ROWS, tokens), low),
            vmem(all_slots, low),
            vmem(all_slots, low),
            vmem((2, heads, tile_rows, tokens), low),
            vmem((2, tile_rows, 2 * width), low),
            pair_rows,
            pair_heads,
            pair_heads,
            pair_rows,
            vmem((8, tokens), wide),
            vmem((width, tokens), wide),
            vmem((8, tokens), wide),
            vmem((8, tokens), wide),
            vmem((tiles, 8, tokens), wide),
            vmem((tiles, 8, tokens), wide),
            vmem((tokens, width), low),
            vmem((tokens, width), low),
            vmem((tokens, model), wide),
            vmem((tokens, 3 * width), low),
            vmem((tokens, width), low),
            vmem((heads, tokens, tokens), low),
            vmem((8, tokens), wide),
            vmem((tokens, model), wide),
            vmem((2, tokens, model), wide),
            vmem((2, tokens, model), wide),
            vmem((groups, 2, 4, rows, columns), low),
            vmem((groups, 4, rows, columns), low),
            vmem((groups, 2, rows, columns), low),
            vmem((groups, rows, columns), low),
            vmem((tile_rows, 2 * width), low),
            vmem((2, half, 2 * width), wide),
            vmem((4, 2, 2, rows, columns), low),
            vmem((2, TILE * RANKS, passage_len, half), low),
            vmem(all_slots, low),
            vmem(small_shape, wide),
            vmem((8,) + small_shape, wide),
        ]
        + both(groups, 2)
        + both(groups, 2, 2)
        + both(groups, 4)
        + both(groups, 4, 2)
        + both(groups, 4, 2)
        + both(groups, 4)
        + both(groups, 2, 2)
        + both(groups, 2)
        + both(CHIPS)
        + both(CHIPS)
        + both(CHIPS)
        + both(CHIPS)
        + [DMA((2,)), DMA((tiles,))]
        + both(6)
        + both(5)
        + [DMA((groups,)), DMA((2,)), DMA((2,)), DMA((2,))],
        compiler_params=pltpu.CompilerParams(
            collective_id=0, has_side_effects=True, vmem_limit_bytes=62 * 2**20
        ),
    )(index, live, query_of, rank, passages, *weights, target, cotangent, gains, table, buckets, counts)


def route(slot_query, slot_live):
    matching = slot_query[:, None] == slot_query[None, :]
    earlier = jnp.tril(jnp.ones(matching.shape, jnp.bool_), -1)
    rank = jnp.sum(jnp.logical_and(matching, earlier), axis=1).astype(jnp.int32)
    position = slot_query * RANKS + rank
    here = position[None, :] == jnp.arange(CHIPS * RANKS, dtype=jnp.int32)[:, None]
    slots = slot_query.shape[0]
    index = jnp.sum(jnp.where(here, jnp.arange(slots, dtype=jnp.int32)[None, :], 0), axis=1)
    live = jnp.sum(jnp.where(here, slot_live[None, :], 0), axis=1)
    return rank, index, live


def body(
    target_states,
    passage_states,
    slot_query,
    slot_live,
    norm_gains,
    self_query,
    self_key,
    self_value,
    self_output,
    position_bias,
    cross_query,
    cross_key,
    cross_value,
    cross_output,
    expand_weight,
    reduce_weight,
    output_cotangent,
):
    low = jnp.bfloat16
    width_here = self_query.shape[1]
    heads_here = width_here // HEAD_DIM
    passage_len, half = passage_states.shape[1:]
    bucket_count = position_bias.shape[0]
    rank, index, live = route(slot_query, slot_live)
    distance = np.zeros((TLEN, 128), np.float32)
    distance[np.arange(TLEN), bucket_table(TLEN, bucket_count, MAXDIST)[:, 0]] = 1.0
    shard_grads, passage_grad, gains_grad, bias_grad, target_grad, block_out = run_block(
        index,
        live,
        slot_query,
        rank,
        passage_states,
        (
            (self_query, self_key, self_value),
            self_output.T,
            (cross_query, cross_key, cross_value),
            cross_output.T,
            expand_weight,
            reduce_weight.T,
        ),
        target_states,
        output_cotangent,
        norm_gains,
        position_bias.T,
        jnp.asarray(distance[:, :bucket_count].T),
        jnp.asarray(distance),
    )[:6]
    w = width_here
    first, second = shard_grads[0], shard_grads[1]
    return (
        block_out,
        target_grad,
        passage_grad,
        gains_grad,
        first[:, :w],
        first[:, w : 2 * w],
        first[:, 2 * w : 3 * w],
        first[:, 3 * w :].T,
        bias_grad.T,
        second[:, :w],
        second[:, w : 2 * w],
        second[:, 2 * w : 3 * w],
        second[:, 3 * w :].T,
        shard_grads[2],
        shard_grads[3].T,
    )


def solution(mesh):
    return jax.shard_map(
        body if fits(mesh) else body_any,
        mesh=mesh,
        in_specs=(
            P("pas", None),
            P("pas", None, "mdl"),
            P("pas"),
            P("pas"),
            P(),
            P("pas", "mdl"),
            P("pas", "mdl"),
            P("pas", "mdl"),
            P("mdl", "pas"),
            P(None, "mdl"),
            P("pas", "mdl"),
            P("pas", "mdl"),
            P("pas", "mdl"),
            P("mdl", "pas"),
            P("pas", "mdl"),
            P("mdl", "pas"),
            P("pas", None),
        ),
        out_specs=(
            P("pas", None),
            P("pas", None),
            P("pas", None, "mdl"),
            P(),
            P("pas", "mdl"),
            P("pas", "mdl"),
            P("pas", "mdl"),
            P("mdl", "pas"),
            P(None, "mdl"),
            P("pas", "mdl"),
            P("pas", "mdl"),
            P("pas", "mdl"),
            P("mdl", "pas"),
            P("pas", "mdl"),
            P("mdl", "pas"),
        ),
        check_vma=False,
    )
```

```python
from functools import partial
import math

import jax
import jax.numpy as jnp
import numpy as np
from jax import lax
from jax.experimental import pallas as pl
from jax.experimental.pallas import tpu as pltpu
from jax.sharding import PartitionSpec as P

HEAD_DIM = 64
MAXDIST = 128
TLEN = 256
PQ = 40


EPSILON = 1e-06
MASKED = -1e30


def bucket_table(length, buckets, distance):
    later = np.arange(length)[:, None]
    earlier = np.arange(length)[None, :]
    behind = np.maximum(later - earlier, 0)
    exact = buckets // 2
    spread = np.log(np.maximum(behind, 1) / exact) / math.log(distance / exact) * (buckets - exact)
    far_bucket = np.minimum(exact + np.floor(spread).astype(np.int32), buckets - 1)
    return np.where(behind < exact, behind, far_bucket).astype(np.int32)


def rms_forward(values, gain):
    factor = lax.rsqrt(jnp.mean(values * values, axis=-1, keepdims=True) + EPSILON)
    unit_rows = values * factor
    return (unit_rows, factor, (unit_rows * gain).astype(jnp.bfloat16))


def rms_backward(normed_grad, unit_rows, factor, gain):
    scaled_grad = normed_grad * gain
    input_grad = factor * (
        scaled_grad - unit_rows * jnp.mean(scaled_grad * unit_rows, axis=-1, keepdims=True)
    )
    return (input_grad, jnp.sum(normed_grad * unit_rows, axis=0))


def over_heads(partial_rows):
    return lax.psum(partial_rows, "mdl")


def score_block(queries, key_rows, allowed, bias):
    scores = jnp.einsum("sihe,sjhe->shij", queries, key_rows, preferred_element_type=jnp.float32)
    if bias is not None:
        scores = scores + bias
    return jnp.where(allowed, scores, MASKED)


def attend(queries, key_rows, values, allowed, bias):
    scores = score_block(queries, key_rows, allowed, bias)
    highest = jnp.max(scores, axis=-1, keepdims=True)
    totals = highest + jnp.log(jnp.sum(jnp.exp(scores - highest), axis=-1, keepdims=True))
    probability = jnp.exp(scores - totals)
    mixed = jnp.einsum(
        "shij,sjhe->sihe",
        probability.astype(jnp.bfloat16),
        values,
        preferred_element_type=jnp.float32,
    )
    return (mixed.astype(jnp.bfloat16), totals)


def attend_back(queries, key_rows, values, allowed, bias, totals, out_grad):
    scores = score_block(queries, key_rows, allowed, bias)
    probability = jnp.exp(scores - totals)
    prob_grad = jnp.einsum("sihe,sjhe->shij", out_grad, values, preferred_element_type=jnp.float32)
    centered = jnp.sum(probability * prob_grad, axis=-1, keepdims=True)
    score_grad = (probability * (prob_grad - centered)).astype(jnp.bfloat16)
    query_grad = jnp.einsum(
        "shij,sjhe->sihe", score_grad, key_rows, preferred_element_type=jnp.float32
    )
    key_grad = jnp.einsum(
        "shij,sihe->sjhe", score_grad, queries, preferred_element_type=jnp.float32
    )
    value_grad = jnp.einsum(
        "shij,sihe->sjhe",
        probability.astype(jnp.bfloat16),
        out_grad,
        preferred_element_type=jnp.float32,
    )
    return (query_grad, key_grad, value_grad, score_grad)


def send_plan(slot_query, slot_live, per_device, capacity):
    target_device = slot_query // per_device
    matching = target_device[:, None] == target_device[None, :]
    lower_part = jnp.tril(jnp.ones(matching.shape, jnp.bool_), -1)
    ranking = jnp.sum(jnp.logical_and(matching, lower_part), axis=1)
    position = target_device * capacity + ranking
    codes = jnp.where(slot_live > 0, slot_query % per_device + 1, 0).astype(jnp.bfloat16)
    return (position, codes)


def arrange_plan(got_codes, per_device, slots_each):
    local_query = got_codes.astype(jnp.int32) - 1
    matches = (local_query[:, None] == jnp.arange(per_device, dtype=jnp.int32)[None, :]).astype(
        jnp.int32
    )
    ranking = jnp.sum((jnp.cumsum(matches, axis=0) - 1) * matches, axis=1)
    spare_place = per_device * slots_each
    places = jnp.where(local_query >= 0, local_query * slots_each + ranking, spare_place)
    arrivals = got_codes.shape[0]
    gather_index = (
        jnp.zeros((spare_place + 1,), jnp.int32)
        .at[places]
        .set(jnp.arange(arrivals, dtype=jnp.int32))
    )
    valid_slot = jnp.zeros((spare_place + 1,), jnp.int32).at[places].set(1)
    return (gather_index[:spare_place], valid_slot[:spare_place] > 0)


def place_rows(rows, position, total_rows):
    return jnp.zeros((total_rows,) + rows.shape[1:], rows.dtype).at[position].set(rows)


def return_rows(rows, gather_index, total_rows):
    return jnp.zeros((total_rows,) + rows.shape[1:], rows.dtype).at[gather_index].add(rows)


def body_any(
    target_states,
    passage_states,
    slot_query,
    slot_live,
    norm_gains,
    self_query,
    self_key,
    self_value,
    self_output,
    position_bias,
    cross_query,
    cross_key,
    cross_value,
    cross_output,
    expand_weight,
    reduce_weight,
    output_cotangent,
):
    (
        query_full,
        key_full,
        value_full,
        cross_query_full,
        cross_key_full,
        cross_value_full,
        expand_full,
    ) = (
        lax.all_gather(self_query, "pas", axis=0, tiled=True),
        lax.all_gather(self_key, "pas", axis=0, tiled=True),
        lax.all_gather(self_value, "pas", axis=0, tiled=True),
        lax.all_gather(cross_query, "pas", axis=0, tiled=True),
        lax.all_gather(cross_key, "pas", axis=0, tiled=True),
        lax.all_gather(cross_value, "pas", axis=0, tiled=True),
        lax.all_gather(expand_weight, "pas", axis=0, tiled=True),
    )
    output_full, cross_output_full, reduce_full = (
        lax.all_gather(self_output, "pas", axis=1, tiled=True),
        lax.all_gather(cross_output, "pas", axis=1, tiled=True),
        lax.all_gather(reduce_weight, "pas", axis=1, tiled=True),
    )
    width_here = query_full.shape[1]
    heads_here = width_here // HEAD_DIM
    sequences = target_states.shape[0] // TLEN
    passage_len = passage_states.shape[1]
    bucket_count = position_bias.shape[0]
    devices = lax.axis_size("pas")
    slots_here = slot_query.shape[0]
    capacity = -(-slots_here // devices)
    buffer_rows = devices * capacity
    residual = target_states.astype(jnp.float32)
    unit_one, factor_one, normed_one = rms_forward(residual, norm_gains[0])
    self_weights = jnp.concatenate([query_full, key_full, value_full], axis=1)
    projected = jnp.dot(normed_one, self_weights, preferred_element_type=jnp.float32).astype(
        jnp.bfloat16
    )
    projected = projected.reshape(sequences, TLEN, 3, heads_here, HEAD_DIM)
    queries_self = projected[:, :, 0]
    keys_self = projected[:, :, 1]
    values_self = projected[:, :, 2]
    buckets = jnp.asarray(bucket_table(TLEN, bucket_count, MAXDIST))
    one_hot = (jnp.arange(bucket_count, dtype=jnp.int32)[:, None, None] == buckets[None]).astype(
        jnp.float32
    )
    bias_full = jnp.einsum("bij,bh->hij", one_hot, position_bias, precision=lax.Precision.HIGHEST)[
        None
    ]
    causal = jnp.asarray(np.tril(np.ones((TLEN, TLEN), dtype=bool)))
    attended_self, total_self = attend(queries_self, keys_self, values_self, causal, bias_full)
    merged_self = attended_self.reshape(sequences * TLEN, width_here)
    residual_two = residual + over_heads(
        jnp.dot(merged_self, output_full, preferred_element_type=jnp.float32)
    )
    unit_two, factor_two, normed_two = rms_forward(residual_two, norm_gains[1])
    cross_queries = jnp.dot(
        normed_two, cross_query_full, preferred_element_type=jnp.float32
    ).astype(jnp.bfloat16)
    cross_queries = cross_queries.reshape(sequences, TLEN, heads_here, HEAD_DIM)
    kv_weights = jnp.concatenate([cross_key_full, cross_value_full], axis=1)
    position, codes = send_plan(slot_query, slot_live, sequences, capacity)
    sent_codes = place_rows(codes, position, buffer_rows)
    states_full = lax.all_gather(passage_states, "mdl", axis=2, tiled=True)
    key_values = jnp.einsum(
        "tpd,dc->tpc", states_full, kv_weights, preferred_element_type=jnp.float32
    ).astype(jnp.bfloat16)
    received, got_codes = (
        lax.all_to_all(
            place_rows(key_values, position, buffer_rows),
            "pas",
            split_axis=0,
            concat_axis=0,
            tiled=True,
        ),
        lax.all_to_all(sent_codes, "pas", split_axis=0, concat_axis=0, tiled=True),
    )
    gather_index, valid_slot = arrange_plan(got_codes, sequences, PQ)
    arranged = jnp.take(received, gather_index, axis=0)
    arranged = arranged.reshape(sequences, PQ * passage_len, 2, heads_here, HEAD_DIM)
    key_rows = arranged[:, :, 0]
    value_rows = arranged[:, :, 1]
    allowed = jnp.repeat(valid_slot.reshape(sequences, PQ), passage_len, axis=1)[:, None, None, :]
    head_block = 2
    head_ranges = [
        slice(start_head, start_head + head_block)
        for start_head in range(0, heads_here, head_block)
    ]
    cross_parts = []
    cross_totals = []
    for head_range in head_ranges:
        mixed_part, total_part = attend(
            cross_queries[:, :, head_range],
            key_rows[:, :, head_range],
            value_rows[:, :, head_range],
            allowed,
            None,
        )
        cross_parts.append(mixed_part)
        cross_totals.append(total_part)
    merged_cross = jnp.concatenate(cross_parts, axis=2).reshape(sequences * TLEN, width_here)
    residual_three = residual_two + over_heads(
        jnp.dot(merged_cross, cross_output_full, preferred_element_type=jnp.float32)
    )
    unit_three, factor_three, normed_three = rms_forward(residual_three, norm_gains[2])
    before = jnp.dot(normed_three, expand_full, preferred_element_type=jnp.float32)
    hidden = jax.nn.gelu(before, approximate=True).astype(jnp.bfloat16)
    block_out = residual_three + over_heads(
        jnp.dot(hidden, reduce_full, preferred_element_type=jnp.float32)
    )
    grad_out = output_cotangent.astype(jnp.float32)
    reduce_grad = jnp.dot(hidden.T, output_cotangent, preferred_element_type=jnp.float32)
    hidden_grad = jnp.dot(output_cotangent, reduce_full.T, preferred_element_type=jnp.float32)
    unused_value, gelu_pullback = jax.vjp(partial(jax.nn.gelu, approximate=True), before)
    before_grad = gelu_pullback(hidden_grad)[0].astype(jnp.bfloat16)
    expand_grad = jnp.dot(normed_three.T, before_grad, preferred_element_type=jnp.float32)
    normed_grad = over_heads(
        jnp.dot(before_grad, expand_full.T, preferred_element_type=jnp.float32)
    )
    back_three, gain_three = rms_backward(normed_grad, unit_three, factor_three, norm_gains[2])
    grad_three = grad_out + back_three
    grad_low = grad_three.astype(jnp.bfloat16)
    cross_output_grad = jnp.dot(merged_cross.T, grad_low, preferred_element_type=jnp.float32)
    mixed_grad = jnp.dot(grad_low, cross_output_full.T, preferred_element_type=jnp.float32).astype(
        jnp.bfloat16
    )
    mixed_grad = mixed_grad.reshape(sequences, TLEN, heads_here, HEAD_DIM)
    query_parts = []
    key_parts = []
    value_parts = []
    for number, head_range in enumerate(head_ranges):
        query_part, key_part, value_part, unused_scores = attend_back(
            cross_queries[:, :, head_range],
            key_rows[:, :, head_range],
            value_rows[:, :, head_range],
            allowed,
            None,
            cross_totals[number],
            mixed_grad[:, :, head_range],
        )
        query_parts.append(query_part)
        key_parts.append(key_part)
        value_parts.append(value_part)
    cross_query_rows = (
        jnp.concatenate(query_parts, axis=2)
        .astype(jnp.bfloat16)
        .reshape(sequences * TLEN, width_here)
    )
    kv_grad = jnp.stack(
        [jnp.concatenate(key_parts, axis=2), jnp.concatenate(value_parts, axis=2)], axis=2
    )
    kv_grad = kv_grad.astype(jnp.bfloat16).reshape(sequences * PQ, passage_len, 2 * width_here)
    returned = lax.all_to_all(
        return_rows(kv_grad, gather_index, buffer_rows),
        "pas",
        split_axis=0,
        concat_axis=0,
        tiled=True,
    )
    kv_grad_here = jnp.take(returned, position, axis=0)
    kv_weight_grad = jnp.einsum(
        "tpd,tpc->dc", states_full, kv_grad_here, preferred_element_type=jnp.float32
    )
    states_grad = jnp.einsum(
        "tpc,dc->tpd", kv_grad_here, kv_weights, preferred_element_type=jnp.float32
    )
    passage_grad = lax.psum_scatter(
        states_grad.astype(jnp.bfloat16), "mdl", scatter_dimension=2, tiled=True
    )
    cross_query_grad = jnp.dot(normed_two.T, cross_query_rows, preferred_element_type=jnp.float32)
    normed_grad = over_heads(
        jnp.dot(cross_query_rows, cross_query_full.T, preferred_element_type=jnp.float32)
    )
    back_two, gain_two = rms_backward(normed_grad, unit_two, factor_two, norm_gains[1])
    grad_two = grad_three + back_two
    grad_low = grad_two.astype(jnp.bfloat16)
    self_output_grad = jnp.dot(merged_self.T, grad_low, preferred_element_type=jnp.float32)
    attended_grad = jnp.dot(grad_low, output_full.T, preferred_element_type=jnp.float32).astype(
        jnp.bfloat16
    )
    attended_grad = attended_grad.reshape(sequences, TLEN, heads_here, HEAD_DIM)
    query_grad, key_grad, value_grad, score_grad = attend_back(
        queries_self, keys_self, values_self, causal, bias_full, total_self, attended_grad
    )
    bias_grad = jnp.einsum(
        "hij,bij->bh",
        jnp.sum(score_grad.astype(jnp.float32), axis=0),
        one_hot,
        precision=lax.Precision.HIGHEST,
    )
    projected_grad = jnp.stack([query_grad, key_grad, value_grad], axis=2).astype(jnp.bfloat16)
    projected_grad = projected_grad.reshape(sequences * TLEN, 3 * width_here)
    self_weight_grad = jnp.dot(normed_one.T, projected_grad, preferred_element_type=jnp.float32)
    normed_grad = over_heads(
        jnp.dot(projected_grad, self_weights.T, preferred_element_type=jnp.float32)
    )
    back_one, gain_one = rms_backward(normed_grad, unit_one, factor_one, norm_gains[0])
    target_grad = (grad_two + back_one).astype(jnp.bfloat16)
    row_grads = (
        lax.psum_scatter(self_weight_grad[:, :width_here], "pas", scatter_dimension=0, tiled=True),
        lax.psum_scatter(
            self_weight_grad[:, width_here : 2 * width_here], "pas", scatter_dimension=0, tiled=True
        ),
        lax.psum_scatter(
            self_weight_grad[:, 2 * width_here :], "pas", scatter_dimension=0, tiled=True
        ),
        lax.psum_scatter(cross_query_grad, "pas", scatter_dimension=0, tiled=True),
        lax.psum_scatter(kv_weight_grad[:, :width_here], "pas", scatter_dimension=0, tiled=True),
        lax.psum_scatter(kv_weight_grad[:, width_here:], "pas", scatter_dimension=0, tiled=True),
        lax.psum_scatter(expand_grad, "pas", scatter_dimension=0, tiled=True),
    )
    col_grads = (
        lax.psum_scatter(self_output_grad, "pas", scatter_dimension=1, tiled=True),
        lax.psum_scatter(cross_output_grad, "pas", scatter_dimension=1, tiled=True),
        lax.psum_scatter(reduce_grad, "pas", scatter_dimension=1, tiled=True),
    )
    gains_total, bias_total = lax.psum(
        (jnp.stack([gain_one, gain_two, gain_three]), bias_grad), "pas"
    )
    return (
        block_out.astype(jnp.bfloat16),
        target_grad,
        passage_grad,
        gains_total,
        row_grads[0],
        row_grads[1],
        row_grads[2],
        col_grads[0],
        bias_total,
        row_grads[3],
        row_grads[4],
        row_grads[5],
        col_grads[1],
        row_grads[6],
        col_grads[2],
    )


CHIPS = 16
RANKS = 3
FLAG_ROWS = 16
MESH_ID = pl.DeviceIdType.MESH
VMEM_LIMIT = 56 * 2**20


def fits(mesh):
    return mesh.shape["pas"] == CHIPS and mesh.shape["mdl"] == 2


def places():
    me, core = lax.axis_index("pas"), lax.axis_index("mdl")
    x, y, z = me % 2, (me // 2) % 2, me // 4
    across_x, across_y = me + 1 - 2 * x, me + 2 - 4 * y
    near = across_y + (across_x - across_y) * core
    far = across_x + (across_y - across_x) * core
    return me, core, x, y, z, near, far


def remote(src, dst, send_sem, recv_sem, device):
    return pltpu.make_async_remote_copy(
        src_ref=src,
        dst_ref=dst,
        send_sem=send_sem,
        recv_sem=recv_sem,
        device_id=device,
        device_id_type=MESH_ID,
    )


def greet_signal(me, core):
    barrier = pltpu.get_barrier_semaphore()
    for k in range(1, CHIPS):
        pl.semaphore_signal(
            barrier, inc=1, device_id=((me + k) % CHIPS, core), device_id_type=MESH_ID
        )
    pl.semaphore_signal(barrier, inc=1, device_id=(me, 1 - core), device_id_type=MESH_ID)


def greet_wait():
    pl.semaphore_wait(pltpu.get_barrier_semaphore(), CHIPS)


ANY = pl.BlockSpec(memory_space=pl.ANY)
IN_VMEM = pl.BlockSpec(memory_space=pltpu.VMEM)
IN_SMEM = pl.BlockSpec(memory_space=pltpu.SMEM)
DMA = pltpu.SemaphoreType.DMA


def rows_nt(left, right):
    return lax.dot_general(
        left, right, (((1,), (1,)), ((), ())), preferred_element_type=jnp.float32
    )


def rows_tn(left, right):
    return lax.dot_general(
        left, right, (((0,), (0,)), ((), ())), preferred_element_type=jnp.float32
    )


TILE = 2


def mm(left, right):
    return jnp.dot(left, right, preferred_element_type=jnp.float32)


def halves_of_pair(rows, head):
    lane = lax.broadcasted_iota(jnp.int32, (rows.shape[0], 2 * HEAD_DIM), 1)
    at = head // 2 * 2 * HEAD_DIM
    return jnp.where(lane // HEAD_DIM == head % 2, rows[:, at : at + 2 * HEAD_DIM], 0.0).astype(
        jnp.bfloat16
    )


def halves_of_rows(rows, head):
    row = lax.broadcasted_iota(jnp.int32, (2 * HEAD_DIM, rows.shape[1]), 0)
    at = head // 2 * 2 * HEAD_DIM
    return jnp.where(row // HEAD_DIM == head % 2, rows[at : at + 2 * HEAD_DIM], 0.0).astype(
        jnp.bfloat16
    )


def unit_of(values):
    factor = lax.rsqrt(jnp.mean(values * values, axis=-1, keepdims=True) + EPSILON)
    return values * factor, factor


def prepare_heads(heads, query_ref, grad, mixed, q_pair, o_pair, o_rows, centre):
    grad = grad.astype(jnp.float32)
    grad_t = grad.T
    product = (grad * mixed.astype(jnp.float32)).T
    queries = query_ref[...].astype(jnp.float32)
    for h in range(heads):
        q_pair[h] = halves_of_pair(queries, h)
        o_pair[h] = halves_of_pair(grad, h)
        o_rows[h] = halves_of_rows(grad_t, h)
        centre[h : h + 1, :] = jnp.sum(
            product[h * HEAD_DIM : (h + 1) * HEAD_DIM], axis=0, keepdims=True
        )


def head_pair_back(p, keys, values, prob, q_pair, o_pair, o_rows, centre, keep_scores):
    low = jnp.bfloat16
    keys_t = keys.T
    query_parts = []
    for a in range(2):
        h = 2 * p + a
        prob_grad = mm(values, o_rows[h])
        weights = prob(h)
        score_grad = (weights * (prob_grad - centre[h : h + 1, :])).astype(low)
        if keep_scores is not None:
            keep_scores(h, score_grad)
        key_part = mm(score_grad, q_pair[h])
        value_part = mm(weights.astype(low), o_pair[h])
        key_grad = key_part if a == 0 else key_grad + key_part
        value_grad = value_part if a == 0 else value_grad + value_part
        query_parts.append(mm(keys_t[a * HEAD_DIM : (a + 1) * HEAD_DIM], score_grad))
    return key_grad.astype(low), value_grad.astype(low), query_parts


def z_turned(z, k):
    high, low = z // 2, z % 2
    if k % 2:
        high = 1 - high
    if k // 2:
        low = 1 - low
    return 2 * high + low


def exp_rows(scores):
    highest = jnp.max(scores, axis=0, keepdims=True)
    exps = jnp.exp(scores - highest)
    return exps, highest, jnp.sum(exps, axis=0, keepdims=True)


def gelu_both(values):
    first = math.sqrt(2 / math.pi)
    square = values * values
    curve = jnp.tanh(first * values * (1.0 + 0.044715 * square))
    half = 0.5 * (1.0 + curve)
    slope = half + 0.5 * values * (1.0 - curve * curve) * first * (1.0 + 3 * 0.044715 * square)
    return values * half, slope


GATHER_MIDDLE = (3, )
FOLD_MIDDLE = ()
def block_kernel(
    query_of_ref,
    live_ref,
    passage_ref,
    read_self_refs,
    write_self_ref,
    read_cross_refs,
    write_cross_ref,
    expand_ref,
    reduce_ref,
    target_ref,
    cotangent_ref,
    gains_ref,
    table_ref,
    bucket_ref,
    count_ref,
    shard_out,
    expand_out,
    reduce_out,
    slots_ref,
    gains_out,
    bias_out,
    target_grad_ref,
    block_ref,
    exps_out,
    kv_out,
    place_ref,
    shard_ref,
    flag_ref,
    full,
    states,
    flags,
    kept,
    slot_got,
    exps,
    keys,
    q_rows,
    q_pair,
    o_pair,
    o_rows,
    centre,
    out_t,
    highest,
    total,
    tile_highest,
    scale_ref,
    query_ref,
    mixed_ref,
    residual_ref,
    qkv_ref,
    self_mixed_ref,
    self_exps_ref,
    self_scale_ref,
    upper_grad,
    row_sent,
    row_got,
    far_got,
    near_got,
    next_got,
    skip_got,
    dkv,
    kv_sum,
    early,
    outgoing,
    pair_got,
    small,
    small_got,
    skip_send,
    skip_recv,
    next_send,
    next_recv,
    near_send,
    near_recv,
    far_send,
    far_recv,
    fold_far_send,
    fold_far_recv,
    fold_near_send,
    fold_near_recv,
    fold_next_send,
    fold_next_recv,
    fold_skip_send,
    fold_skip_recv,
    slot_send,
    slot_recv,
    flag_send,
    flag_recv,
    core_send,
    core_recv,
    return_send,
    return_recv,
    pair_send,
    pair_recv,
    row_send,
    row_recv,
    small_send,
    small_recv,
    own_sem,
    exps_sem,
    keys_sem,
    out_sem,
):
    low, wide = jnp.bfloat16, jnp.float32
    me, core, x, y, z, near, far = places()
    groups = shard_ref.shape[0]
    partner = (me, 1 - core)
    pair = me // TILE
    tiles = CHIPS // TILE
    passage_len = states.shape[2]
    block_rows = RANKS * passage_len
    tile_rows = TILE * block_rows
    tokens = target_ref.shape[0]
    width = query_ref.shape[1]
    turn = 1 - core
    across_x, across_y = me + 1 - 2 * x, me + 2 - 4 * y
    skip_to = (me - 4 * z + 4 * z_turned(z, 1), core)
    next_to = (me - 4 * z + 4 * z_turned(z, 2), core)
    pairs = width // (2 * HEAD_DIM)
    heads = 2 * pairs
    half = states.shape[3]
    other_y = y + (1 - core) * (1 - 2 * y)
    other_x = x + core * (1 - 2 * x)

    def slots_of(ref, source):
        return ref.at[pl.ds(source * RANKS, RANKS)]

    def own_copy(g):
        return pltpu.make_async_copy(shard_ref.at[g], full.at[g, z, y, x], own_sem.at[g])

    def z_at(k):
        return z_turned(z, k)

    def spot(g, k, m):
        if m == 0:
            return full.at[g, z_at(k), y, x]
        return full.at[g, z_at(k), other_y, other_x]

    def block_of(g, k, m):
        return shard_ref.at[g] if k == m == 0 else spot(g, k, m)

    def skip_copy(g, m):
        src, dst = block_of(g, 0, m), spot(g, 0, m)
        return remote(src, dst, skip_send.at[g, m], skip_recv.at[g, m], skip_to)

    def next_copy(g, k, m):
        src, dst = block_of(g, k, m), spot(g, k, m)
        return remote(src, dst, next_send.at[g, k, m], next_recv.at[g, k, m], next_to)

    def near_copy(g, k):
        src, dst = block_of(g, k, 0), spot(g, k, 0)
        return remote(src, dst, near_send.at[g, k], near_recv.at[g, k], (near, core))

    def far_copy(g, k, m):
        src, dst = block_of(g, k, m), spot(g, k, m)
        return remote(src, dst, far_send.at[g, k, m], far_recv.at[g, k, m], (far, core))

    def before_far(g):
        if g in GATHER_MIDDLE:
            copies = [near_copy(g, 0)] + [skip_copy(g, m) for m in range(2)]
            return copies + [next_copy(g, k, m) for k in range(2) for m in range(2)]
        copies = [skip_copy(g, 0)] + [next_copy(g, k, 0) for k in range(2)]
        return copies + [near_copy(g, k) for k in range(4)]

    def slot_copy(to):
        return remote(
            slots_of(kept, to), slots_of(states.at[core], me), slot_send.at[to], slot_recv.at[me], (to, core)
        )

    def slot_arrival(came):
        block = slots_of(states.at[core], came)
        return remote(block, block, slot_send.at[came], slot_recv.at[came], (came, core))

    def flag_copy(to):
        return remote(flag_ref.at[to], flags.at[me], flag_send.at[to], flag_recv.at[me], (to, core))

    def flag_arrival(came):
        block = flags.at[came]
        return remote(block, block, flag_send.at[came], flag_recv.at[came], (came, core))

    def core_copy(came):
        block = slots_of(states.at[core], came)
        return remote(block, block, core_send.at[came], core_recv.at[came], partner)

    def row_copy(i):
        b = i % 2
        return remote(row_sent.at[b], row_got.at[b], row_send.at[i], row_recv.at[i], partner)

    def give(i, value):
        if i >= 2:
            row_copy(i - 2).wait_send()
        row_sent[i % 2] = value
        row_copy(i).start()

    def pair_sum(i):
        row_copy(i).wait_recv()
        return row_sent[i % 2] + row_got[i % 2]

    def launch(g):
        if g in GATHER_MIDDLE:
            near_copy(g, 0).start()
        skip_copy(g, 0).start()
        next_copy(g, 0, 0).start()
        if g not in GATHER_MIDDLE:
            near_copy(g, 0).start()
        far_copy(g, 0, 0).start()
        own_copy(g).start()

    def relay_one(g):
        if g in GATHER_MIDDLE:
            near_copy(g, 0).wait_recv()
            skip_copy(g, 1).start()
            next_copy(g, 0, 1).start()
            far_copy(g, 0, 1).start()
        else:
            skip_copy(g, 0).wait_recv()
            next_copy(g, 1, 0).start()
            near_copy(g, 1).start()
            far_copy(g, 1, 0).start()

    def relay_two(g):
        for i in range(2):
            if g in GATHER_MIDDLE:
                skip_copy(g, i).wait_recv()
                next_copy(g, 1, i).start()
                far_copy(g, 1, i).start()
            else:
                next_copy(g, i, 0).wait_recv()
                near_copy(g, i + 2).start()
                far_copy(g, i + 2, 0).start()

    def relay_three(g):
        for i in range(4):
            if g in GATHER_MIDDLE:
                k, m = i % 2, i // 2
                next_copy(g, k, m).wait_recv()
                far_copy(g, k + 2, m).start()
            else:
                near_copy(g, i).wait_recv()
                far_copy(g, i, 1).start()

    def arrived(g):
        own_copy(g).wait()
        for k in range(4):
            for m in range(2):
                far_copy(g, k, m).wait_recv()

    def weight(g):
        return full[g].reshape(full.shape[1] * 4 * full.shape[4], full.shape[5])

    staging = pltpu.make_async_copy(
        passage_ref, slot_got.at[pl.ds(0, passage_ref.shape[0])], out_sem.at[0]
    )
    staging.start()

    def mine(g, k, m, here):
        near_at, far_at = (1 - turn) * y + turn * x, (1 - turn) * x + turn * y
        near_at = near_at if m == 0 else 1 - near_at
        far_at = far_at if here else 1 - far_at
        grads = early if g == 3 else full.at[g]
        return grads.at[
            z_at(k),
            (1 - turn) * near_at + turn * far_at,
            (1 - turn) * far_at + turn * near_at,
        ]

    def next_place(g, k, m):
        return next_got.at[g, k] if m == 0 else near_got.at[g, 1 + k]

    def skip_place(g, m):
        return skip_got.at[g] if m == 0 else near_got.at[g, 3]

    def fold_far(g, k, m):
        src, dst = mine(g, k, m, False), far_got.at[g, m, k]
        sems = fold_far_send.at[g, k, m], fold_far_recv.at[g, k, m]
        return remote(src, dst, *sems, (near, core))

    def fold_near(g, k):
        src, dst = far_got.at[g, 1, k], near_got.at[g, k]
        return remote(src, dst, fold_near_send.at[g, k], fold_near_recv.at[g, k], (far, core))

    def fold_next(g, k, m):
        src = far_got.at[g, m, 2 + k] if g in FOLD_MIDDLE else near_got.at[g, 2 + k]
        sems = fold_next_send.at[g, k, m], fold_next_recv.at[g, k, m]
        return remote(src, next_place(g, k, m), *sems, next_to)

    def fold_skip(g, m):
        src = far_got.at[g, m, 1] if g in FOLD_MIDDLE else near_got.at[g, 1]
        sems = fold_skip_send.at[g, m], fold_skip_recv.at[g, m]
        return remote(src, skip_place(g, m), *sems, skip_to)

    def fold_copies(g):
        copies = [fold_far(g, k, m) for k in range(4) for m in range(2)]
        if g in FOLD_MIDDLE:
            copies += [fold_next(g, k, m) for k in range(2) for m in range(2)]
            return copies + [fold_skip(g, m) for m in range(2)] + [fold_near(g, 0)]
        copies += [fold_next(g, k, 0) for k in range(2)]
        return copies + [fold_skip(g, 0)] + [fold_near(g, k) for k in range(4)]

    def add_up(ref, *others):
        total = ref[...].astype(wide)
        for other in others:
            total = total + other[...].astype(wide)
        ref[...] = total.astype(low)

    def far_start(g):
        order = [(k, m) for m in (1, 0) for k in (3, 2, 1, 0)]
        if g in FOLD_MIDDLE:
            order = [(k, m) for k in (3, 2, 1, 0) for m in (1, 0)]
        for k, m in order:
            fold_far(g, k, m).start()

    def far_add(g):
        if g in FOLD_MIDDLE:
            for k, m in ((3, 1), (3, 0), (2, 1), (2, 0)):
                fold_far(g, k, m).wait_recv()
                add_up(far_got.at[g, m, k], mine(g, k, m, True))
                fold_next(g, k - 2, m).start()
        else:
            for k in (3, 2, 1, 0):
                fold_far(g, k, 1).wait_recv()
                add_up(far_got.at[g, 1, k], mine(g, k, 1, True))
                fold_near(g, k).start()

    def near_add(g):
        if g in FOLD_MIDDLE:
            for m in (1, 0):
                fold_far(g, 1, m).wait_recv()
                fold_next(g, 1, m).wait_recv()
                add_up(far_got.at[g, m, 1], mine(g, 1, m, True), next_place(g, 1, m))
                fold_skip(g, m).start()
        else:
            for k in (3, 2, 1, 0):
                fold_far(g, k, 0).wait_recv()
                fold_near(g, k).wait_recv()
                add_up(near_got.at[g, k], mine(g, k, 0, True), far_got.at[g, 0, k])
                if k >= 2:
                    fold_next(g, k - 2, 0).start()

    def next_add(g):
        if g in FOLD_MIDDLE:
            fold_far(g, 0, 1).wait_recv()
            fold_next(g, 0, 1).wait_recv()
            fold_skip(g, 1).wait_recv()
            add_up(
                far_got.at[g, 1, 0], mine(g, 0, 1, True), next_place(g, 0, 1), skip_place(g, 1)
            )
            fold_near(g, 0).start()
        else:
            fold_next(g, 1, 0).wait_recv()
            add_up(near_got.at[g, 1], next_place(g, 1, 0))
            fold_skip(g, 0).start()

    def skip_add(g):
        fold_next(g, 0, 0).wait_recv()
        fold_skip(g, 0).wait_recv()
        if g in FOLD_MIDDLE:
            fold_far(g, 0, 0).wait_recv()
            fold_near(g, 0).wait_recv()
        parts = [near_got[g, 0], next_got[g, 0], skip_got[g]]
        if g in FOLD_MIDDLE:
            parts += [mine(g, 0, 0, True)[...], far_got[g, 0, 0]]
        total = parts[0].astype(wide)
        for part in parts[1:]:
            total = total + part.astype(wide)
        if g < 2:
            shard_out[g] = total
        else:
            (expand_out, reduce_out)[g - 2][...] = total

    def send_pair(j):
        for i in range(TILE):
            to = (pair + j) % tiles * TILE + i

            @pl.when(to != me)
            def _():
                flag_copy(to).start()
                slot_copy(to).start()

    lane = lax.broadcasted_iota(jnp.int32, (1, 2 * HEAD_DIM), 1)
    nobody = jnp.zeros_like(lane)

    def at_place(row, place):
        return jnp.sum(jnp.where(lane == place, row, 0))

    def route_step(slot, carry):
        met, found, alive, queries = carry
        query = query_of_ref[slot]
        hit = lane == query
        found = tuple(jnp.where(hit & (met == r), slot, found[r]) for r in range(RANKS))
        alive = tuple(jnp.where(hit & (met == r), live_ref[slot], alive[r]) for r in range(RANKS))
        queries = jnp.where(lane == slot, query, queries)
        return met + hit.astype(jnp.int32), found, alive, queries

    def rank_step(slot, ranks):
        later = (lane > slot) & (queries_here == query_of_ref[slot])
        return ranks + later.astype(jnp.int32)

    def fill(to, carry):
        for rank in range(RANKS):
            kept[to * RANKS + rank] = slot_got[at_place(slot_at[rank], to)]
        row = lax.broadcasted_iota(jnp.int32, flag_ref.shape[1:], 0)
        marks = jnp.zeros(flag_ref.shape[1:], wide)
        for rank in range(RANKS):
            mark = jnp.where(at_place(live_at[rank], to) > 0, 0.0, MASKED)
            marks = jnp.where(row == rank, mark, marks)
        flag_ref[to] = marks.astype(low)
        return carry

    greet_signal(me, core)
    for g, reads, writes in ((0, read_self_refs, write_self_ref), (1, read_cross_refs, write_cross_ref)):
        for i, read in enumerate(reads):
            shard_ref[g, :, i * width : (i + 1) * width] = read[...]
        shard_ref[g, :, 3 * width :] = writes[...]
    shard_ref[2] = expand_ref[...]
    shard_ref[3] = reduce_ref[...]
    greet_wait()
    launch(0)
    launch(1)
    slots_here = query_of_ref.shape[0]
    unused, slot_at, live_at, queries_here = lax.fori_loop(
        0,
        slots_here,
        route_step,
        (nobody, (nobody,) * RANKS, (nobody,) * RANKS, nobody),
        unroll=8,
    )
    staging.wait()
    lax.fori_loop(0, CHIPS, fill, 0, unroll=4)
    send_pair(0)
    send_pair(1)
    states[core, pl.ds(me * RANKS, RANKS)] = kept[pl.ds(me * RANKS, RANKS)]
    flags[me] = flag_ref[me]
    core_copy(me).start()

    line = lax.dot_general(
        table_ref[...],
        bucket_ref[...],
        (((1,), (0,)), ((), ())),
        precision=lax.Precision.HIGHEST,
        preferred_element_type=wide,
    )
    def bias_of(h):
        return kv_sum.at[h // 3, pl.ds(0, tokens), pl.ds(h % 3 * tokens, tokens)]

    turns = []
    for h in range(heads):
        for s in range(8):
            row = line[h : h + 1]
            turns.append(row if s == 0 else pltpu.roll(row, s, 1))
    base = jnp.concatenate(turns, axis=0)

    def bias_step(i, carry):
        rows = pltpu.roll(base, 8 * i, 1)
        for h in range(heads):
            bias_of(h)[pl.ds(pl.multiple_of(8 * i, 8), 8), :] = rows[8 * h : 8 * h + 8]
        return carry

    lax.fori_loop(0, tokens // 8, bias_step, 0)
    ranks = lax.fori_loop(0, slots_here, rank_step, nobody, unroll=8)

    def place_step(slot, carry):
        place_ref[slot] = query_of_ref[slot] * RANKS + at_place(ranks, slot)
        return carry

    lax.fori_loop(0, slots_here, place_step, 0, unroll=8)
    residual = target_ref[...].astype(wide)
    normed = (unit_of(residual)[0] * gains_ref[0:1, :]).astype(low)

    relay_one(0)
    launch(3)
    launch(2)
    relay_one(1)
    send_pair(2)
    relay_two(0)
    send_pair(3)
    send_pair(4)
    relay_three(0)
    relay_two(1)
    arrived(0)

    qkv_ref[...] = mm(normed, weight(0)[:, : 3 * width]).astype(low)
    relay_three(1)
    send_pair(5)
    queries_t = qkv_ref[:, :width].astype(wide).T
    for h in range(heads):
        q_rows[h] = halves_of_rows(queries_t, h)
    key_at = lax.broadcasted_iota(jnp.int32, (tokens, tokens), 0)
    query_at = lax.broadcasted_iota(jnp.int32, (tokens, tokens), 1)
    self_scale_ref[...] = jnp.zeros_like(self_scale_ref)
    for p in range(pairs):
        at = 2 * HEAD_DIM * p
        head_keys = qkv_ref[:, width + at : width + at + 2 * HEAD_DIM]
        values_t = qkv_ref[:, 2 * width + at : 2 * width + at + 2 * HEAD_DIM].T
        for a in range(2):
            h = 2 * p + a
            scores = mm(head_keys, q_rows[h]) + bias_of(h)[...]
            scores = jnp.where(key_at <= query_at, scores, MASKED)
            head_exps, unused, sums = exp_rows(scores)
            head_exps = head_exps.astype(low)
            self_exps_ref[h] = head_exps
            inverse = 1.0 / sums
            self_scale_ref[h : h + 1, :] = inverse
            first = at + a * HEAD_DIM
            out_t[first : first + HEAD_DIM, :] = (
                mm(values_t[a * HEAD_DIM : (a + 1) * HEAD_DIM], head_exps) * inverse
            )
        if p == 1:
            send_pair(6)
            send_pair(7)
    self_mixed_ref[...] = out_t[...].T.astype(low)
    give(0, rows_nt(self_mixed_ref[...], weight(0)[:, 3 * width :]))
    relay_one(2)
    arrived(1)
    residual_ref[...] = residual + pair_sum(0)

    normed = (unit_of(residual_ref[...])[0] * gains_ref[1:2, :]).astype(low)
    query_ref[...] = mm(normed, weight(1)[:, :width]).astype(low)
    queries_t = query_ref[...].astype(wide).T
    for h in range(heads):
        q_rows[h] = halves_of_rows(queries_t, h)
    out_t[...] = jnp.zeros_like(out_t)
    highest[...] = jnp.full_like(highest, MASKED)
    total[...] = jnp.zeros_like(total)
    tile_highest[...] = jnp.zeros_like(tile_highest)

    def take_in(t):
        for i in range(TILE):
            came = (pair - t + tiles) % tiles * TILE + i

            @pl.when(came != me)
            def _():
                flag_arrival(came).wait_recv()
                slot_arrival(came).wait_recv()
                core_copy(came).start()

    def exps_copy(t):
        rows = pl.ds((pair - t + tiles) % tiles * tile_rows, tile_rows)
        return pltpu.make_async_copy(exps.at[t % 2], exps_out.at[:, rows], exps_sem.at[t % 2])

    def keys_copy(t):
        rows = pl.ds((pair - t + tiles) % tiles * tile_rows, tile_rows)
        return pltpu.make_async_copy(keys.at[t % 2], kv_out.at[rows], keys_sem.at[t % 2])

    take_in(0)

    def tile_step(t, carry):
        tile = (pair - t + tiles) % tiles

        @pl.when(t == 1)
        def _():
            relay_two(2)

        @pl.when(t == 5)
        def _():
            relay_three(2)

        @pl.when(t == 7)
        def _():
            relay_two(3)

        @pl.when(t + 1 < tiles)
        def _():
            take_in(t + 1)

        @pl.when(t == 4)
        def _():
            relay_one(3)

        @pl.when(t >= 2)
        def _():
            exps_copy(t - 2).wait()
            keys_copy(t - 2).wait()

        for i in range(TILE):
            core_copy(tile * TILE + i).wait_recv()
        kv_parts = []
        for c in range(2):
            rows = states[c, pl.ds(tile * TILE * RANKS, TILE * RANKS)].reshape(tile_rows, half)
            w = full[1, 2 * c : 2 * c + 2, :, :, :, width : 3 * width]
            kv_parts.append(mm(rows, w.reshape(half, 2 * width)))
        keys[t % 2] = (kv_parts[0] + kv_parts[1]).astype(low)
        keys_copy(t).start()
        masks = []
        for i in range(TILE):
            for rank in range(RANKS):
                masks.append(flags[tile * TILE + i, rank : rank + 1, :].astype(wide)[None])
        masks = jnp.concatenate(masks, axis=0)
        for p in range(pairs):
            at = 2 * HEAD_DIM * p
            head_keys = keys[t % 2, :, at : at + 2 * HEAD_DIM]
            values_t = keys[t % 2, :, width + at : width + at + 2 * HEAD_DIM].T
            for a in range(2):
                h = 2 * p + a
                scores = mm(head_keys, q_rows[h]).reshape(TILE * RANKS, passage_len, tokens) + masks
                head_exps, top, sums = exp_rows(scores.reshape(tile_rows, tokens))
                head_exps = head_exps.astype(low)
                exps[t % 2, h] = head_exps
                before = highest[h : h + 1, :]
                now = jnp.maximum(before, top)
                keep, add = jnp.exp(before - now), jnp.exp(top - now)
                highest[h : h + 1, :] = now
                tile_highest[tile, h : h + 1, :] = top
                total[h : h + 1, :] = total[h : h + 1, :] * keep + sums * add
                first = at + a * HEAD_DIM
                out_t[first : first + HEAD_DIM, :] = (
                    out_t[first : first + HEAD_DIM, :] * keep
                    + mm(values_t[a * HEAD_DIM : (a + 1) * HEAD_DIM], head_exps) * add
                )
        exps_copy(t).start()

        return carry

    lax.fori_loop(0, tiles, tile_step, 0)
    for h in range(heads):
        inverse = 1.0 / total[h : h + 1, :]
        out_t[h * HEAD_DIM : (h + 1) * HEAD_DIM, :] *= inverse
        scale_ref[:, h, :] = jnp.exp(tile_highest[:, h, :] - highest[h : h + 1, :]) * inverse
    mixed_ref[...] = out_t[...].T.astype(low)
    give(1, rows_nt(mixed_ref[...], weight(1)[:, 3 * width :]))
    relay_three(3)
    residual_three = residual_ref[...] + pair_sum(1)
    unit, factor = unit_of(residual_three)
    normed = (unit * gains_ref[2:3, :]).astype(low)


    def sends_done(g):
        for copy in before_far(g) + [far_copy(g, k, m) for k in range(4) for m in range(2)]:
            copy.wait_send()

    def store_grad(g, first, value):
        blocks = value.astype(low).reshape(full.shape[1:5] + (value.shape[1],))
        full[g, :, :, :, :, first : first + value.shape[1]] = blocks

    arrived(2)
    hidden, slope = gelu_both(mm(normed, weight(2)))
    hidden = hidden.astype(low)
    early[...] = rows_tn(cotangent_ref[...], hidden).astype(low).reshape(early.shape)
    far_start(3)
    arrived(3)
    hidden_grad = mm(cotangent_ref[...], weight(3))
    before_grad = (hidden_grad * slope).astype(low)
    give(2, rows_nt(before_grad, weight(2)))
    sends_done(2)
    store_grad(2, 0, rows_tn(normed, before_grad))
    far_start(2)
    back, gain_three = rms_backward(pair_sum(2), unit, factor, gains_ref[2:3, :])
    upper_grad[...] = cotangent_ref[...].astype(wide) + back
    give(3, rows_nt(hidden, weight(3)))
    sends_done(0)
    sends_done(1)
    sends_done(3)
    for k in range(1, CHIPS):
        to = (me + k) % CHIPS
        slot_copy(to).wait_send()
        flag_copy(to).wait_send()
    for k in range(CHIPS):
        core_copy(k).wait_send()
    for t in range(tiles - 2, tiles):
        exps_copy(t).wait()
        keys_copy(t).wait()

    def back_tile(t):
        return (t + pair) % tiles

    def exps_load(t):
        rows = pl.ds(back_tile(t) * tile_rows, tile_rows)
        return pltpu.make_async_copy(exps_out.at[:, rows], exps.at[t % 2], exps_sem.at[t % 2])

    def keys_load(t):
        rows = pl.ds(back_tile(t) * tile_rows, tile_rows)
        return pltpu.make_async_copy(kv_out.at[rows], keys.at[t % 2], keys_sem.at[t % 2])

    def loads_start(t):
        exps_load(t).start()
        keys_load(t).start()

    def kv_weights(c):
        w = full[1, pl.ds(2 * c, 2), :, :, :, width : 3 * width]
        return w.reshape(half, 2 * width)

    def pair_copy(t):
        return remote(
            outgoing.at[t % 2],
            pair_got.at[pl.ds(back_tile(t) * TILE * RANKS, TILE * RANKS)],
            pair_send.at[t % 2],
            pair_recv.at[t],
            partner,
        )

    def return_copy(to):
        return remote(
            slots_of(kept, to), slots_of(slot_got, me), return_send.at[to], return_recv.at[me], (to, core)
        )

    def return_arrival(came):
        block = slots_of(slot_got, came)
        return remote(block, block, return_send.at[came], return_recv.at[came], (came, core))

    def finish_tile(t):
        tile = back_tile(t)
        pair_copy(t).wait_recv()
        rows = pl.ds(tile * TILE * RANKS, TILE * RANKS)
        kept[rows] = (kept[rows].astype(wide) + pair_got[rows].astype(wide)).astype(low)
        for j in range(TILE):
            to = tile * TILE + j

            @pl.when(to != me)
            def _():
                return_copy(to).start()

            @pl.when(to == me)
            def _():
                own = pl.ds(me * RANKS, RANKS)
                slot_got[own] = kept[own]

    grad_low = upper_grad[...].astype(low)
    mixed_grad = mm(grad_low, weight(1)[:, 3 * width :]).astype(low)
    prepare_heads(heads, query_ref, mixed_grad, mixed_ref[...], q_pair, o_pair, o_rows, centre)
    out_t[...] = jnp.zeros_like(out_t)
    kv_sum[...] = jnp.zeros_like(kv_sum)
    loads_start(0)
    block_ref[...] = (residual_three + pair_sum(3)).astype(low)

    def back_step(t, carry):
        tile = back_tile(t)
        @pl.when(t + 1 < tiles)
        def _():
            loads_start(t + 1)

        exps_load(t).wait()
        keys_load(t).wait()

        def prob(h):
            return exps[t % 2, h].astype(wide) * scale_ref[tile, h : h + 1, :]

        for p in range(pairs):
            at = 2 * HEAD_DIM * p
            key_grad, value_grad, query_parts = head_pair_back(
                p,
                keys[t % 2, :, at : at + 2 * HEAD_DIM],
                keys[t % 2, :, width + at : width + at + 2 * HEAD_DIM],
                prob,
                q_pair,
                o_pair,
                o_rows,
                centre,
                None,
            )
            dkv[:, at : at + 2 * HEAD_DIM] = key_grad
            dkv[:, width + at : width + at + 2 * HEAD_DIM] = value_grad
            for a in range(2):
                first = at + a * HEAD_DIM
                out_t[first : first + HEAD_DIM, :] += query_parts[a]
        here = dkv[...]

        @pl.when(t >= 2)
        def _():
            pair_copy(t - 2).wait_send()

        weights = kv_weights(1 - core)
        outgoing[t % 2] = rows_nt(here, weights).astype(low).reshape(outgoing.shape[1:])
        pair_copy(t).start()
        weights = kv_weights(core)
        mine = rows_nt(here, weights).astype(low).reshape(outgoing.shape[1:])
        kept[pl.ds(tile * TILE * RANKS, TILE * RANKS)] = mine

        rows = pl.ds(tile * TILE * RANKS, TILE * RANKS)
        for i in range(2):
            kv_sum[i] += rows_tn(states[i, rows].reshape(tile_rows, half), here)

        @pl.when(t >= 1)
        def _():
            finish_tile(t - 1)

        @pl.when(t == 3)
        def _():
            far_add(2)

        @pl.when(t == 6)
        def _():
            far_add(3)

        return carry

    lax.fori_loop(0, tiles, back_step, 0)
    dq = out_t[...].T.astype(low)
    give(4, rows_nt(dq, weight(1)[:, :width]))
    store_grad(1, 3 * width, rows_tn(upper_grad[...].astype(low), mixed_ref[...]))
    finish_tile(tiles - 1)
    near_add(2)
    unit_two, factor_two = unit_of(residual_ref[...])
    normed_two = (unit_two * gains_ref[1:2, :]).astype(low)
    store_grad(1, 0, rows_tn(normed_two, dq))

    store_grad(1, width, kv_sum[...].reshape(2 * half, 2 * width))
    far_start(1)
    next_add(2)

    back, gain_two = rms_backward(pair_sum(4), unit_two, factor_two, gains_ref[1:2, :])
    upper_grad[...] += back

    grad_low = upper_grad[...].astype(low)
    mixed_grad = mm(grad_low, weight(0)[:, 3 * width :]).astype(low)
    prepare_heads(
        heads,
        qkv_ref.at[:, :width],
        mixed_grad,
        self_mixed_ref[...],
        q_pair,
        o_pair,
        o_rows,
        centre,
    )

    def self_prob(h):
        return self_exps_ref[h].astype(wide) * self_scale_ref[h : h + 1, :]

    def keep_scores(h, score_grad):
        self_exps_ref[h] = score_grad

    query_rows, key_columns, value_columns = [], [], []
    for p in range(pairs):
        at = 2 * HEAD_DIM * p
        key_grad, value_grad, query_parts = head_pair_back(
            p,
            qkv_ref[:, width + at : width + at + 2 * HEAD_DIM],
            qkv_ref[:, 2 * width + at : 2 * width + at + 2 * HEAD_DIM],
            self_prob,
            q_pair,
            o_pair,
            o_rows,
            centre,
            keep_scores,
        )
        key_columns.append(key_grad)
        value_columns.append(value_grad)
        query_rows.extend(query_parts)
    dq = jnp.concatenate(query_rows, axis=0).T.astype(low)
    dqkv = jnp.concatenate([dq] + key_columns + value_columns, axis=1)
    near_add(3)
    give(5, rows_nt(dqkv, weight(0)[:, : 3 * width]))
    store_grad(0, 3 * width, rows_tn(upper_grad[...].astype(low), self_mixed_ref[...]))
    unit_one, factor_one = unit_of(target_ref[...].astype(wide))
    normed_one = (unit_one * gains_ref[0:1, :]).astype(low)
    store_grad(0, 0, rows_tn(normed_one, dqkv))
    far_start(0)
    far_add(1)
    next_add(3)

    length = self_exps_ref.shape[1]

    def diagonal_step(i, total):
        rows = self_exps_ref[:, pl.ds(pl.multiple_of(16 * i, 16), 16), :].astype(wide)
        rows = rows.reshape(heads * 16, length)
        return total + pltpu.roll(rows, (length - 16 * i) % length, 1)

    total = lax.fori_loop(
        0, length // 16, diagonal_step, jnp.zeros((heads * 16, length), wide)
    ).reshape(heads, 16, length)
    small[...] = jnp.zeros_like(small)
    for h in range(heads):
        line = total[h, 0:1]
        for s in range(1, 16):
            line = line + pltpu.roll(total[h, s : s + 1], length - s, 1)
        small[8 + h : 9 + h, :length] = line
    by_bucket = jnp.dot(
        small[8:16, :length], count_ref[...], precision=lax.Precision.HIGHEST,
        preferred_element_type=wide,
    )
    small[8:16, :length] = jnp.zeros((8, length), wide)
    small[8:16, : count_ref.shape[1]] = by_bucket

    back, gain_one = rms_backward(pair_sum(5), unit_one, factor_one, gains_ref[0:1, :])
    target_grad_ref[...] = (upper_grad[...] + back).astype(low)
    small[0:1, :] = gain_one[None, :]
    small[1:2, :] = gain_two[None, :]
    small[2:3, :] = gain_three[None, :]

    def small_copy(step):
        if step == 0:
            return remote(small, small_got.at[0], small_send.at[0], small_recv.at[0], (across_x, core))
        if step == 1:
            return remote(
                small_got.at[6], small_got.at[1], small_send.at[1], small_recv.at[1], (across_y, core)
            )
        return remote(
            small_got.at[7],
            small_got.at[2 + z],
            small_send.at[step],
            small_recv.at[step],
            ((me + 4 * (step - 1)) % CHIPS, core),
        )

    small_copy(0).start()
    skip_add(2)
    near_add(1)
    far_add(0)
    skip_add(3)
    next_add(1)
    near_add(0)
    next_add(0)
    skip_add(1)
    small_copy(0).wait_recv()
    small_got[6] = small[...] + small_got[0]
    small_copy(1).start()
    for k in range(1, CHIPS):
        return_arrival((me + k) % CHIPS).wait_recv()
    small_copy(1).wait_recv()
    small_got[7] = small_got[6] + small_got[1]
    for step in range(2, 5):
        small_copy(step).start()
    small_got[2 + z] = small_got[7]
    for k in range(1, CHIPS):
        return_copy((me + k) % CHIPS).wait_send()
    slots = slots_ref.shape[0]

    def pick(slot, carry):
        kept[slot] = slot_got[place_ref[slot]]
        return carry

    lax.fori_loop(0, slots, pick, 0, unroll=4)
    picked = pltpu.make_async_copy(kept.at[pl.ds(0, slots)], slots_ref, out_sem.at[1])
    picked.start()
    skip_add(0)
    for step in range(2, 5):
        small_copy(step).wait_recv()
    whole = small_got[2] + small_got[3] + small_got[4] + small_got[5]
    gains_out[...] = whole[: gains_out.shape[0]]
    bias_out[...] = whole[8 : 8 + heads, : bias_out.shape[1]]
    for g in range(groups):
        for copy in fold_copies(g):
            copy.wait_send()
    for t in range(tiles - 2, tiles):
        pair_copy(t).wait_send()
    for step in range(5):
        small_copy(step).wait_send()
    for i in range(4, 6):
        row_copy(i).wait_send()
    picked.wait()


def run_block(
    query_of, live, passages, weights, target, cotangent, gains, table, buckets, counts
):
    low, wide = jnp.bfloat16, jnp.float32
    groups = 4
    rows, columns = weights[4].shape
    slots, passage_len, half = passages.shape
    tokens, model = target.shape
    width = columns // 4
    heads = width // HEAD_DIM
    key_count = CHIPS * RANKS * passage_len
    tile_rows = TILE * RANKS * passage_len
    tiles = CHIPS // TILE
    small_shape = (16, model)
    shape = jax.ShapeDtypeStruct
    vmem = pltpu.VMEM
    pair_heads = vmem((heads, tokens, 2 * HEAD_DIM), low)
    pair_rows = vmem((heads, 2 * HEAD_DIM, tokens), low)
    all_slots = (CHIPS * RANKS, passage_len, half)

    def both(*dims):
        return [DMA(dims), DMA(dims)]

    return pl.pallas_call(
        block_kernel,
        out_shape=(
            shape((2, rows, columns), wide),
            shape((rows, columns), wide),
            shape((rows, columns), wide),
            shape((slots, passage_len, half), low),
            shape(gains.shape, wide),
            shape(table.shape, wide),
            shape((tokens, model), low),
            shape((tokens, model), low),
            shape((heads, key_count, tokens), low),
            shape((key_count, 2 * width), low),
        ),
        in_specs=[IN_SMEM] * 2
        + [ANY, (IN_VMEM,) * 3, IN_VMEM, (IN_VMEM,) * 3, IN_VMEM, IN_VMEM, IN_VMEM]
        + [IN_VMEM] * 6,
        out_specs=(IN_VMEM,) * 3 + (ANY,) + (IN_VMEM,) * 4 + (ANY, ANY),
        scratch_shapes=[
            pltpu.SMEM((slots,), jnp.int32),
            vmem((groups, rows, columns), low),
            vmem((CHIPS, FLAG_ROWS, tokens), low),
            vmem((groups, 4, 2, 2, rows, columns), low),
            vmem((2,) + all_slots, low),
            vmem((CHIPS, FLAG_ROWS, tokens), low),
            vmem(all_slots, low),
            vmem(all_slots, low),
            vmem((2, heads, tile_rows, tokens), low),
            vmem((2, tile_rows, 2 * width), low),
            pair_rows,
            pair_heads,
            pair_heads,
            pair_rows,
            vmem((8, tokens), wide),
            vmem((width, tokens), wide),
            vmem((8, tokens), wide),
            vmem((8, tokens), wide),
            vmem((tiles, 8, tokens), wide),
            vmem((tiles, 8, tokens), wide),
            vmem((tokens, width), low),
            vmem((tokens, width), low),
            vmem((tokens, model), wide),
            vmem((tokens, 3 * width), low),
            vmem((tokens, width), low),
            vmem((heads, tokens, tokens), low),
            vmem((8, tokens), wide),
            vmem((tokens, model), wide),
            vmem((2, tokens, model), wide),
            vmem((2, tokens, model), wide),
            vmem((groups, 2, 4, rows, columns), low),
            vmem((groups, 4, rows, columns), low),
            vmem((groups, 2, rows, columns), low),
            vmem((groups, rows, columns), low),
            vmem((tile_rows, 2 * width), low),
            vmem((2, half, 2 * width), wide),
            vmem((4, 2, 2, rows, columns), low),
            vmem((2, TILE * RANKS, passage_len, half), low),
            vmem(all_slots, low),
            vmem(small_shape, wide),
            vmem((8,) + small_shape, wide),
        ]
        + both(groups, 2)
        + both(groups, 2, 2)
        + both(groups, 4)
        + both(groups, 4, 2)
        + both(groups, 4, 2)
        + both(groups, 4)
        + both(groups, 2, 2)
        + both(groups, 2)
        + both(CHIPS)
        + both(CHIPS)
        + both(CHIPS)
        + both(CHIPS)
        + [DMA((2,)), DMA((tiles,))]
        + both(6)
        + both(5)
        + [DMA((groups,)), DMA((2,)), DMA((2,)), DMA((2,))],
        compiler_params=pltpu.CompilerParams(
            collective_id=0, has_side_effects=True, vmem_limit_bytes=62 * 2**20
        ),
    )(query_of, live, passages, *weights, target, cotangent, gains, table, buckets, counts)


def body(
    target_states,
    passage_states,
    slot_query,
    slot_live,
    norm_gains,
    self_query,
    self_key,
    self_value,
    self_output,
    position_bias,
    cross_query,
    cross_key,
    cross_value,
    cross_output,
    expand_weight,
    reduce_weight,
    output_cotangent,
):
    low = jnp.bfloat16
    width_here = self_query.shape[1]
    heads_here = width_here // HEAD_DIM
    passage_len, half = passage_states.shape[1:]
    bucket_count = position_bias.shape[0]
    distance = np.zeros((TLEN, 128), np.float32)
    distance[np.arange(TLEN), bucket_table(TLEN, bucket_count, MAXDIST)[:, 0]] = 1.0
    shard_grads, expand_grad, reduce_grad, passage_grad, gains_grad, bias_grad, target_grad, block_out = run_block(
        slot_query,
        slot_live,
        passage_states,
        (
            (self_query, self_key, self_value),
            self_output.T,
            (cross_query, cross_key, cross_value),
            cross_output.T,
            expand_weight,
            reduce_weight.T,
        ),
        target_states,
        output_cotangent,
        norm_gains,
        position_bias.T,
        jnp.asarray(distance[:, :bucket_count].T),
        jnp.asarray(distance),
    )[:8]
    w = width_here
    first, second = shard_grads[0], shard_grads[1]
    return (
        block_out,
        target_grad,
        passage_grad,
        gains_grad,
        first[:, :w],
        first[:, w : 2 * w],
        first[:, 2 * w : 3 * w],
        first[:, 3 * w :].T,
        bias_grad.T,
        second[:, :w],
        second[:, w : 2 * w],
        second[:, 2 * w : 3 * w],
        second[:, 3 * w :].T,
        expand_grad,
        reduce_grad.T,
    )


def solution(mesh):
    return jax.shard_map(
        body if fits(mesh) else body_any,
        mesh=mesh,
        in_specs=(
            P("pas", None),
            P("pas", None, "mdl"),
            P("pas"),
            P("pas"),
            P(),
            P("pas", "mdl"),
            P("pas", "mdl"),
            P("pas", "mdl"),
            P("mdl", "pas"),
            P(None, "mdl"),
            P("pas", "mdl"),
            P("pas", "mdl"),
            P("pas", "mdl"),
            P("mdl", "pas"),
            P("pas", "mdl"),
            P("mdl", "pas"),
            P("pas", None),
        ),
        out_specs=(
            P("pas", None),
            P("pas", None),
            P("pas", None, "mdl"),
            P(),
            P("pas", "mdl"),
            P("pas", "mdl"),
            P("pas", "mdl"),
            P("mdl", "pas"),
            P(None, "mdl"),
            P("pas", "mdl"),
            P("pas", "mdl"),
            P("pas", "mdl"),
            P("mdl", "pas"),
            P("pas", "mdl"),
            P("mdl", "pas"),
        ),
        check_vma=False,
    )
```

```python
from functools import partial
import math

import jax
import jax.numpy as jnp
import numpy as np
from jax import lax
from jax.experimental import pallas as pl
from jax.experimental.pallas import tpu as pltpu
from jax.sharding import PartitionSpec as P

HEAD_DIM = 64
MAXDIST = 128
TLEN = 256
PQ = 40


EPSILON = 1e-06
MASKED = -1e30


def bucket_table(length, buckets, distance):
    later = np.arange(length)[:, None]
    earlier = np.arange(length)[None, :]
    behind = np.maximum(later - earlier, 0)
    exact = buckets // 2
    spread = np.log(np.maximum(behind, 1) / exact) / math.log(distance / exact) * (buckets - exact)
    far_bucket = np.minimum(exact + np.floor(spread).astype(np.int32), buckets - 1)
    return np.where(behind < exact, behind, far_bucket).astype(np.int32)


def rms_forward(values, gain):
    factor = lax.rsqrt(jnp.mean(values * values, axis=-1, keepdims=True) + EPSILON)
    unit_rows = values * factor
    return (unit_rows, factor, (unit_rows * gain).astype(jnp.bfloat16))


def rms_backward(normed_grad, unit_rows, factor, gain):
    scaled_grad = normed_grad * gain
    input_grad = factor * (
        scaled_grad - unit_rows * jnp.mean(scaled_grad * unit_rows, axis=-1, keepdims=True)
    )
    return (input_grad, jnp.sum(normed_grad * unit_rows, axis=0))


def over_heads(partial_rows):
    return lax.psum(partial_rows, "mdl")


def score_block(queries, key_rows, allowed, bias):
    scores = jnp.einsum("sihe,sjhe->shij", queries, key_rows, preferred_element_type=jnp.float32)
    if bias is not None:
        scores = scores + bias
    return jnp.where(allowed, scores, MASKED)


def attend(queries, key_rows, values, allowed, bias):
    scores = score_block(queries, key_rows, allowed, bias)
    highest = jnp.max(scores, axis=-1, keepdims=True)
    totals = highest + jnp.log(jnp.sum(jnp.exp(scores - highest), axis=-1, keepdims=True))
    probability = jnp.exp(scores - totals)
    mixed = jnp.einsum(
        "shij,sjhe->sihe",
        probability.astype(jnp.bfloat16),
        values,
        preferred_element_type=jnp.float32,
    )
    return (mixed.astype(jnp.bfloat16), totals)


def attend_back(queries, key_rows, values, allowed, bias, totals, out_grad):
    scores = score_block(queries, key_rows, allowed, bias)
    probability = jnp.exp(scores - totals)
    prob_grad = jnp.einsum("sihe,sjhe->shij", out_grad, values, preferred_element_type=jnp.float32)
    centered = jnp.sum(probability * prob_grad, axis=-1, keepdims=True)
    score_grad = (probability * (prob_grad - centered)).astype(jnp.bfloat16)
    query_grad = jnp.einsum(
        "shij,sjhe->sihe", score_grad, key_rows, preferred_element_type=jnp.float32
    )
    key_grad = jnp.einsum(
        "shij,sihe->sjhe", score_grad, queries, preferred_element_type=jnp.float32
    )
    value_grad = jnp.einsum(
        "shij,sihe->sjhe",
        probability.astype(jnp.bfloat16),
        out_grad,
        preferred_element_type=jnp.float32,
    )
    return (query_grad, key_grad, value_grad, score_grad)


def send_plan(slot_query, slot_live, per_device, capacity):
    target_device = slot_query // per_device
    matching = target_device[:, None] == target_device[None, :]
    lower_part = jnp.tril(jnp.ones(matching.shape, jnp.bool_), -1)
    ranking = jnp.sum(jnp.logical_and(matching, lower_part), axis=1)
    position = target_device * capacity + ranking
    codes = jnp.where(slot_live > 0, slot_query % per_device + 1, 0).astype(jnp.bfloat16)
    return (position, codes)


def arrange_plan(got_codes, per_device, slots_each):
    local_query = got_codes.astype(jnp.int32) - 1
    matches = (local_query[:, None] == jnp.arange(per_device, dtype=jnp.int32)[None, :]).astype(
        jnp.int32
    )
    ranking = jnp.sum((jnp.cumsum(matches, axis=0) - 1) * matches, axis=1)
    spare_place = per_device * slots_each
    places = jnp.where(local_query >= 0, local_query * slots_each + ranking, spare_place)
    arrivals = got_codes.shape[0]
    gather_index = (
        jnp.zeros((spare_place + 1,), jnp.int32)
        .at[places]
        .set(jnp.arange(arrivals, dtype=jnp.int32))
    )
    valid_slot = jnp.zeros((spare_place + 1,), jnp.int32).at[places].set(1)
    return (gather_index[:spare_place], valid_slot[:spare_place] > 0)


def place_rows(rows, position, total_rows):
    return jnp.zeros((total_rows,) + rows.shape[1:], rows.dtype).at[position].set(rows)


def return_rows(rows, gather_index, total_rows):
    return jnp.zeros((total_rows,) + rows.shape[1:], rows.dtype).at[gather_index].add(rows)


def body_any(
    target_states,
    passage_states,
    slot_query,
    slot_live,
    norm_gains,
    self_query,
    self_key,
    self_value,
    self_output,
    position_bias,
    cross_query,
    cross_key,
    cross_value,
    cross_output,
    expand_weight,
    reduce_weight,
    output_cotangent,
):
    (
        query_full,
        key_full,
        value_full,
        cross_query_full,
        cross_key_full,
        cross_value_full,
        expand_full,
    ) = (
        lax.all_gather(self_query, "pas", axis=0, tiled=True),
        lax.all_gather(self_key, "pas", axis=0, tiled=True),
        lax.all_gather(self_value, "pas", axis=0, tiled=True),
        lax.all_gather(cross_query, "pas", axis=0, tiled=True),
        lax.all_gather(cross_key, "pas", axis=0, tiled=True),
        lax.all_gather(cross_value, "pas", axis=0, tiled=True),
        lax.all_gather(expand_weight, "pas", axis=0, tiled=True),
    )
    output_full, cross_output_full, reduce_full = (
        lax.all_gather(self_output, "pas", axis=1, tiled=True),
        lax.all_gather(cross_output, "pas", axis=1, tiled=True),
        lax.all_gather(reduce_weight, "pas", axis=1, tiled=True),
    )
    width_here = query_full.shape[1]
    heads_here = width_here // HEAD_DIM
    sequences = target_states.shape[0] // TLEN
    passage_len = passage_states.shape[1]
    bucket_count = position_bias.shape[0]
    devices = lax.axis_size("pas")
    slots_here = slot_query.shape[0]
    capacity = -(-slots_here // devices)
    buffer_rows = devices * capacity
    residual = target_states.astype(jnp.float32)
    unit_one, factor_one, normed_one = rms_forward(residual, norm_gains[0])
    self_weights = jnp.concatenate([query_full, key_full, value_full], axis=1)
    projected = jnp.dot(normed_one, self_weights, preferred_element_type=jnp.float32).astype(
        jnp.bfloat16
    )
    projected = projected.reshape(sequences, TLEN, 3, heads_here, HEAD_DIM)
    queries_self = projected[:, :, 0]
    keys_self = projected[:, :, 1]
    values_self = projected[:, :, 2]
    buckets = jnp.asarray(bucket_table(TLEN, bucket_count, MAXDIST))
    one_hot = (jnp.arange(bucket_count, dtype=jnp.int32)[:, None, None] == buckets[None]).astype(
        jnp.float32
    )
    bias_full = jnp.einsum("bij,bh->hij", one_hot, position_bias, precision=lax.Precision.HIGHEST)[
        None
    ]
    causal = jnp.asarray(np.tril(np.ones((TLEN, TLEN), dtype=bool)))
    attended_self, total_self = attend(queries_self, keys_self, values_self, causal, bias_full)
    merged_self = attended_self.reshape(sequences * TLEN, width_here)
    residual_two = residual + over_heads(
        jnp.dot(merged_self, output_full, preferred_element_type=jnp.float32)
    )
    unit_two, factor_two, normed_two = rms_forward(residual_two, norm_gains[1])
    cross_queries = jnp.dot(
        normed_two, cross_query_full, preferred_element_type=jnp.float32
    ).astype(jnp.bfloat16)
    cross_queries = cross_queries.reshape(sequences, TLEN, heads_here, HEAD_DIM)
    kv_weights = jnp.concatenate([cross_key_full, cross_value_full], axis=1)
    position, codes = send_plan(slot_query, slot_live, sequences, capacity)
    sent_codes = place_rows(codes, position, buffer_rows)
    states_full = lax.all_gather(passage_states, "mdl", axis=2, tiled=True)
    key_values = jnp.einsum(
        "tpd,dc->tpc", states_full, kv_weights, preferred_element_type=jnp.float32
    ).astype(jnp.bfloat16)
    received, got_codes = (
        lax.all_to_all(
            place_rows(key_values, position, buffer_rows),
            "pas",
            split_axis=0,
            concat_axis=0,
            tiled=True,
        ),
        lax.all_to_all(sent_codes, "pas", split_axis=0, concat_axis=0, tiled=True),
    )
    gather_index, valid_slot = arrange_plan(got_codes, sequences, PQ)
    arranged = jnp.take(received, gather_index, axis=0)
    arranged = arranged.reshape(sequences, PQ * passage_len, 2, heads_here, HEAD_DIM)
    key_rows = arranged[:, :, 0]
    value_rows = arranged[:, :, 1]
    allowed = jnp.repeat(valid_slot.reshape(sequences, PQ), passage_len, axis=1)[:, None, None, :]
    head_block = 2
    head_ranges = [
        slice(start_head, start_head + head_block)
        for start_head in range(0, heads_here, head_block)
    ]
    cross_parts = []
    cross_totals = []
    for head_range in head_ranges:
        mixed_part, total_part = attend(
            cross_queries[:, :, head_range],
            key_rows[:, :, head_range],
            value_rows[:, :, head_range],
            allowed,
            None,
        )
        cross_parts.append(mixed_part)
        cross_totals.append(total_part)
    merged_cross = jnp.concatenate(cross_parts, axis=2).reshape(sequences * TLEN, width_here)
    residual_three = residual_two + over_heads(
        jnp.dot(merged_cross, cross_output_full, preferred_element_type=jnp.float32)
    )
    unit_three, factor_three, normed_three = rms_forward(residual_three, norm_gains[2])
    before = jnp.dot(normed_three, expand_full, preferred_element_type=jnp.float32)
    hidden = jax.nn.gelu(before, approximate=True).astype(jnp.bfloat16)
    block_out = residual_three + over_heads(
        jnp.dot(hidden, reduce_full, preferred_element_type=jnp.float32)
    )
    grad_out = output_cotangent.astype(jnp.float32)
    reduce_grad = jnp.dot(hidden.T, output_cotangent, preferred_element_type=jnp.float32)
    hidden_grad = jnp.dot(output_cotangent, reduce_full.T, preferred_element_type=jnp.float32)
    unused_value, gelu_pullback = jax.vjp(partial(jax.nn.gelu, approximate=True), before)
    before_grad = gelu_pullback(hidden_grad)[0].astype(jnp.bfloat16)
    expand_grad = jnp.dot(normed_three.T, before_grad, preferred_element_type=jnp.float32)
    normed_grad = over_heads(
        jnp.dot(before_grad, expand_full.T, preferred_element_type=jnp.float32)
    )
    back_three, gain_three = rms_backward(normed_grad, unit_three, factor_three, norm_gains[2])
    grad_three = grad_out + back_three
    grad_low = grad_three.astype(jnp.bfloat16)
    cross_output_grad = jnp.dot(merged_cross.T, grad_low, preferred_element_type=jnp.float32)
    mixed_grad = jnp.dot(grad_low, cross_output_full.T, preferred_element_type=jnp.float32).astype(
        jnp.bfloat16
    )
    mixed_grad = mixed_grad.reshape(sequences, TLEN, heads_here, HEAD_DIM)
    query_parts = []
    key_parts = []
    value_parts = []
    for number, head_range in enumerate(head_ranges):
        query_part, key_part, value_part, unused_scores = attend_back(
            cross_queries[:, :, head_range],
            key_rows[:, :, head_range],
            value_rows[:, :, head_range],
            allowed,
            None,
            cross_totals[number],
            mixed_grad[:, :, head_range],
        )
        query_parts.append(query_part)
        key_parts.append(key_part)
        value_parts.append(value_part)
    cross_query_rows = (
        jnp.concatenate(query_parts, axis=2)
        .astype(jnp.bfloat16)
        .reshape(sequences * TLEN, width_here)
    )
    kv_grad = jnp.stack(
        [jnp.concatenate(key_parts, axis=2), jnp.concatenate(value_parts, axis=2)], axis=2
    )
    kv_grad = kv_grad.astype(jnp.bfloat16).reshape(sequences * PQ, passage_len, 2 * width_here)
    returned = lax.all_to_all(
        return_rows(kv_grad, gather_index, buffer_rows),
        "pas",
        split_axis=0,
        concat_axis=0,
        tiled=True,
    )
    kv_grad_here = jnp.take(returned, position, axis=0)
    kv_weight_grad = jnp.einsum(
        "tpd,tpc->dc", states_full, kv_grad_here, preferred_element_type=jnp.float32
    )
    states_grad = jnp.einsum(
        "tpc,dc->tpd", kv_grad_here, kv_weights, preferred_element_type=jnp.float32
    )
    passage_grad = lax.psum_scatter(
        states_grad.astype(jnp.bfloat16), "mdl", scatter_dimension=2, tiled=True
    )
    cross_query_grad = jnp.dot(normed_two.T, cross_query_rows, preferred_element_type=jnp.float32)
    normed_grad = over_heads(
        jnp.dot(cross_query_rows, cross_query_full.T, preferred_element_type=jnp.float32)
    )
    back_two, gain_two = rms_backward(normed_grad, unit_two, factor_two, norm_gains[1])
    grad_two = grad_three + back_two
    grad_low = grad_two.astype(jnp.bfloat16)
    self_output_grad = jnp.dot(merged_self.T, grad_low, preferred_element_type=jnp.float32)
    attended_grad = jnp.dot(grad_low, output_full.T, preferred_element_type=jnp.float32).astype(
        jnp.bfloat16
    )
    attended_grad = attended_grad.reshape(sequences, TLEN, heads_here, HEAD_DIM)
    query_grad, key_grad, value_grad, score_grad = attend_back(
        queries_self, keys_self, values_self, causal, bias_full, total_self, attended_grad
    )
    bias_grad = jnp.einsum(
        "hij,bij->bh",
        jnp.sum(score_grad.astype(jnp.float32), axis=0),
        one_hot,
        precision=lax.Precision.HIGHEST,
    )
    projected_grad = jnp.stack([query_grad, key_grad, value_grad], axis=2).astype(jnp.bfloat16)
    projected_grad = projected_grad.reshape(sequences * TLEN, 3 * width_here)
    self_weight_grad = jnp.dot(normed_one.T, projected_grad, preferred_element_type=jnp.float32)
    normed_grad = over_heads(
        jnp.dot(projected_grad, self_weights.T, preferred_element_type=jnp.float32)
    )
    back_one, gain_one = rms_backward(normed_grad, unit_one, factor_one, norm_gains[0])
    target_grad = (grad_two + back_one).astype(jnp.bfloat16)
    row_grads = (
        lax.psum_scatter(self_weight_grad[:, :width_here], "pas", scatter_dimension=0, tiled=True),
        lax.psum_scatter(
            self_weight_grad[:, width_here : 2 * width_here], "pas", scatter_dimension=0, tiled=True
        ),
        lax.psum_scatter(
            self_weight_grad[:, 2 * width_here :], "pas", scatter_dimension=0, tiled=True
        ),
        lax.psum_scatter(cross_query_grad, "pas", scatter_dimension=0, tiled=True),
        lax.psum_scatter(kv_weight_grad[:, :width_here], "pas", scatter_dimension=0, tiled=True),
        lax.psum_scatter(kv_weight_grad[:, width_here:], "pas", scatter_dimension=0, tiled=True),
        lax.psum_scatter(expand_grad, "pas", scatter_dimension=0, tiled=True),
    )
    col_grads = (
        lax.psum_scatter(self_output_grad, "pas", scatter_dimension=1, tiled=True),
        lax.psum_scatter(cross_output_grad, "pas", scatter_dimension=1, tiled=True),
        lax.psum_scatter(reduce_grad, "pas", scatter_dimension=1, tiled=True),
    )
    gains_total, bias_total = lax.psum(
        (jnp.stack([gain_one, gain_two, gain_three]), bias_grad), "pas"
    )
    return (
        block_out.astype(jnp.bfloat16),
        target_grad,
        passage_grad,
        gains_total,
        row_grads[0],
        row_grads[1],
        row_grads[2],
        col_grads[0],
        bias_total,
        row_grads[3],
        row_grads[4],
        row_grads[5],
        col_grads[1],
        row_grads[6],
        col_grads[2],
    )


CHIPS = 16
RANKS = 3
FLAG_ROWS = 16
MESH_ID = pl.DeviceIdType.MESH
VMEM_LIMIT = 56 * 2**20


def fits(mesh):
    return mesh.shape["pas"] == CHIPS and mesh.shape["mdl"] == 2


def places():
    me, core = lax.axis_index("pas"), lax.axis_index("mdl")
    x, y, z = me % 2, (me // 2) % 2, me // 4
    across_x, across_y = me + 1 - 2 * x, me + 2 - 4 * y
    near = across_y + (across_x - across_y) * core
    far = across_x + (across_y - across_x) * core
    return me, core, x, y, z, near, far


def remote(src, dst, send_sem, recv_sem, device):
    return pltpu.make_async_remote_copy(
        src_ref=src,
        dst_ref=dst,
        send_sem=send_sem,
        recv_sem=recv_sem,
        device_id=device,
        device_id_type=MESH_ID,
    )


def greet_signal(me, core):
    barrier = pltpu.get_barrier_semaphore()
    for k in range(1, CHIPS):
        pl.semaphore_signal(
            barrier, inc=1, device_id=((me + k) % CHIPS, core), device_id_type=MESH_ID
        )
    pl.semaphore_signal(barrier, inc=1, device_id=(me, 1 - core), device_id_type=MESH_ID)


def greet_wait():
    pl.semaphore_wait(pltpu.get_barrier_semaphore(), CHIPS)


ANY = pl.BlockSpec(memory_space=pl.ANY)
IN_VMEM = pl.BlockSpec(memory_space=pltpu.VMEM)
IN_SMEM = pl.BlockSpec(memory_space=pltpu.SMEM)
DMA = pltpu.SemaphoreType.DMA


def rows_nt(left, right):
    return lax.dot_general(
        left, right, (((1,), (1,)), ((), ())), preferred_element_type=jnp.float32
    )


def rows_tn(left, right):
    return lax.dot_general(
        left, right, (((0,), (0,)), ((), ())), preferred_element_type=jnp.float32
    )


TILE = 2


def mm(left, right):
    return jnp.dot(left, right, preferred_element_type=jnp.float32)


def halves_of_pair(rows, head):
    lane = lax.broadcasted_iota(jnp.int32, (rows.shape[0], 2 * HEAD_DIM), 1)
    at = head // 2 * 2 * HEAD_DIM
    return jnp.where(lane // HEAD_DIM == head % 2, rows[:, at : at + 2 * HEAD_DIM], 0.0).astype(
        jnp.bfloat16
    )


def halves_of_rows(rows, head):
    row = lax.broadcasted_iota(jnp.int32, (2 * HEAD_DIM, rows.shape[1]), 0)
    at = head // 2 * 2 * HEAD_DIM
    return jnp.where(row // HEAD_DIM == head % 2, rows[at : at + 2 * HEAD_DIM], 0.0).astype(
        jnp.bfloat16
    )


def unit_of(values):
    factor = lax.rsqrt(jnp.mean(values * values, axis=-1, keepdims=True) + EPSILON)
    return values * factor, factor


def prepare_heads(heads, query_ref, grad, mixed, q_pair, o_pair, o_rows, centre):
    grad = grad.astype(jnp.float32)
    grad_t = grad.T
    product = (grad * mixed.astype(jnp.float32)).T
    queries = query_ref[...].astype(jnp.float32)
    for h in range(heads):
        q_pair[h] = halves_of_pair(queries, h)
        o_pair[h] = halves_of_pair(grad, h)
        o_rows[h] = halves_of_rows(grad_t, h)
        centre[h : h + 1, :] = jnp.sum(
            product[h * HEAD_DIM : (h + 1) * HEAD_DIM], axis=0, keepdims=True
        )


def head_pair_back(p, keys, values, prob, q_pair, o_pair, o_rows, centre, keep_scores):
    low = jnp.bfloat16
    keys_t = keys.T
    query_parts = []
    for a in range(2):
        h = 2 * p + a
        prob_grad = mm(values, o_rows[h])
        weights = prob(h)
        score_grad = (weights * (prob_grad - centre[h : h + 1, :])).astype(low)
        if keep_scores is not None:
            keep_scores(h, score_grad)
        key_part = mm(score_grad, q_pair[h])
        value_part = mm(weights.astype(low), o_pair[h])
        key_grad = key_part if a == 0 else key_grad + key_part
        value_grad = value_part if a == 0 else value_grad + value_part
        query_parts.append(mm(keys_t[a * HEAD_DIM : (a + 1) * HEAD_DIM], score_grad))
    return key_grad.astype(low), value_grad.astype(low), query_parts


def z_turned(z, k):
    high, low = z // 2, z % 2
    if k % 2:
        high = 1 - high
    if k // 2:
        low = 1 - low
    return 2 * high + low


def exp_rows(scores):
    highest = jnp.max(scores, axis=0, keepdims=True)
    exps = jnp.exp(scores - highest)
    return exps, highest, jnp.sum(exps, axis=0, keepdims=True)


def gelu_both(values):
    first = math.sqrt(2 / math.pi)
    square = values * values
    curve = jnp.tanh(first * values * (1.0 + 0.044715 * square))
    half = 0.5 * (1.0 + curve)
    slope = half + 0.5 * values * (1.0 - curve * curve) * first * (1.0 + 3 * 0.044715 * square)
    return values * half, slope


GATHER_MIDDLE = (3, )
FOLD_MIDDLE = ()
def block_kernel(
    query_of_ref,
    live_ref,
    passage_ref,
    read_self_refs,
    write_self_ref,
    read_cross_refs,
    write_cross_ref,
    expand_ref,
    reduce_ref,
    target_ref,
    cotangent_ref,
    gains_ref,
    table_ref,
    bucket_ref,
    count_ref,
    shard_out,
    expand_out,
    reduce_out,
    slots_ref,
    gains_out,
    bias_out,
    target_grad_ref,
    block_ref,
    exps_out,
    kv_out,
    place_ref,
    shard_ref,
    flag_ref,
    full,
    states,
    flags,
    kept,
    slot_got,
    exps,
    keys,
    q_rows,
    q_pair,
    o_pair,
    o_rows,
    centre,
    out_t,
    highest,
    total,
    tile_highest,
    scale_ref,
    query_ref,
    mixed_ref,
    residual_ref,
    qkv_ref,
    self_mixed_ref,
    self_exps_ref,
    self_scale_ref,
    upper_grad,
    row_sent,
    row_got,
    far_got,
    near_got,
    next_got,
    skip_got,
    dkv,
    kv_sum,
    early,
    outgoing,
    pair_got,
    small,
    small_got,
    skip_send,
    skip_recv,
    next_send,
    next_recv,
    near_send,
    near_recv,
    far_send,
    far_recv,
    fold_far_send,
    fold_far_recv,
    fold_near_send,
    fold_near_recv,
    fold_next_send,
    fold_next_recv,
    fold_skip_send,
    fold_skip_recv,
    slot_send,
    slot_recv,
    flag_send,
    flag_recv,
    core_send,
    core_recv,
    return_send,
    return_recv,
    pair_send,
    pair_recv,
    row_send,
    row_recv,
    small_send,
    small_recv,
    own_sem,
    exps_sem,
    keys_sem,
    out_sem,
):
    low, wide = jnp.bfloat16, jnp.float32
    me, core, x, y, z, near, far = places()
    groups = shard_ref.shape[0]
    partner = (me, 1 - core)
    pair = me // TILE
    tiles = CHIPS // TILE
    passage_len = states.shape[2]
    block_rows = RANKS * passage_len
    tile_rows = TILE * block_rows
    tokens = target_ref.shape[0]
    width = query_ref.shape[1]
    turn = 1 - core
    across_x, across_y = me + 1 - 2 * x, me + 2 - 4 * y
    skip_to = (me - 4 * z + 4 * z_turned(z, 1), core)
    next_to = (me - 4 * z + 4 * z_turned(z, 2), core)
    pairs = width // (2 * HEAD_DIM)
    heads = 2 * pairs
    half = states.shape[3]
    other_y = y + (1 - core) * (1 - 2 * y)
    other_x = x + core * (1 - 2 * x)

    def slots_of(ref, source):
        return ref.at[pl.ds(source * RANKS, RANKS)]

    def own_copy(g):
        return pltpu.make_async_copy(shard_ref.at[g], full.at[g, z, y, x], own_sem.at[g])

    def z_at(k):
        return z_turned(z, k)

    def spot(g, k, m):
        if m == 0:
            return full.at[g, z_at(k), y, x]
        return full.at[g, z_at(k), other_y, other_x]

    def block_of(g, k, m):
        return shard_ref.at[g] if k == m == 0 else spot(g, k, m)

    def skip_copy(g, m):
        src, dst = block_of(g, 0, m), spot(g, 0, m)
        return remote(src, dst, skip_send.at[g, m], skip_recv.at[g, m], skip_to)

    def next_copy(g, k, m):
        src, dst = block_of(g, k, m), spot(g, k, m)
        return remote(src, dst, next_send.at[g, k, m], next_recv.at[g, k, m], next_to)

    def near_copy(g, k):
        src, dst = block_of(g, k, 0), spot(g, k, 0)
        return remote(src, dst, near_send.at[g, k], near_recv.at[g, k], (near, core))

    def far_copy(g, k, m):
        src, dst = block_of(g, k, m), spot(g, k, m)
        return remote(src, dst, far_send.at[g, k, m], far_recv.at[g, k, m], (far, core))

    def before_far(g):
        if g in GATHER_MIDDLE:
            copies = [near_copy(g, 0)] + [skip_copy(g, m) for m in range(2)]
            return copies + [next_copy(g, k, m) for k in range(2) for m in range(2)]
        copies = [skip_copy(g, 0)] + [next_copy(g, k, 0) for k in range(2)]
        return copies + [near_copy(g, k) for k in range(4)]

    def slot_copy(to):
        return remote(
            slots_of(kept, to), slots_of(states.at[core], me), slot_send.at[to], slot_recv.at[me], (to, core)
        )

    def slot_arrival(came):
        block = slots_of(states.at[core], came)
        return remote(block, block, slot_send.at[came], slot_recv.at[came], (came, core))

    def flag_copy(to):
        return remote(flag_ref.at[to], flags.at[me], flag_send.at[to], flag_recv.at[me], (to, core))

    def flag_arrival(came):
        block = flags.at[came]
        return remote(block, block, flag_send.at[came], flag_recv.at[came], (came, core))

    def core_copy(came):
        block = slots_of(states.at[core], came)
        return remote(block, block, core_send.at[came], core_recv.at[came], partner)

    def row_copy(i):
        b = i % 2
        return remote(row_sent.at[b], row_got.at[b], row_send.at[i], row_recv.at[i], partner)

    def give(i, value):
        if i >= 2:
            row_copy(i - 2).wait_send()
        row_sent[i % 2] = value
        row_copy(i).start()

    def pair_sum(i):
        row_copy(i).wait_recv()
        return row_sent[i % 2] + row_got[i % 2]

    def launch(g):
        if g in GATHER_MIDDLE:
            near_copy(g, 0).start()
        skip_copy(g, 0).start()
        next_copy(g, 0, 0).start()
        if g not in GATHER_MIDDLE:
            near_copy(g, 0).start()
        far_copy(g, 0, 0).start()
        own_copy(g).start()

    def relay_one(g):
        if g in GATHER_MIDDLE:
            near_copy(g, 0).wait_recv()
            skip_copy(g, 1).start()
            next_copy(g, 0, 1).start()
            far_copy(g, 0, 1).start()
        else:
            skip_copy(g, 0).wait_recv()
            next_copy(g, 1, 0).start()
            near_copy(g, 1).start()
            far_copy(g, 1, 0).start()

    def relay_two(g):
        for i in range(2):
            if g in GATHER_MIDDLE:
                skip_copy(g, i).wait_recv()
                next_copy(g, 1, i).start()
                far_copy(g, 1, i).start()
            else:
                next_copy(g, i, 0).wait_recv()
                near_copy(g, i + 2).start()
                far_copy(g, i + 2, 0).start()

    def relay_three(g):
        for i in range(4):
            if g in GATHER_MIDDLE:
                k, m = i % 2, i // 2
                next_copy(g, k, m).wait_recv()
                far_copy(g, k + 2, m).start()
            else:
                near_copy(g, i).wait_recv()
                far_copy(g, i, 1).start()

    def arrived(g):
        own_copy(g).wait()
        for k in range(4):
            for m in range(2):
                far_copy(g, k, m).wait_recv()

    def weight(g):
        return full[g].reshape(full.shape[1] * 4 * full.shape[4], full.shape[5])

    staging = pltpu.make_async_copy(
        passage_ref, slot_got.at[pl.ds(0, passage_ref.shape[0])], out_sem.at[0]
    )
    staging.start()

    def mine(g, k, m, here):
        near_at, far_at = (1 - turn) * y + turn * x, (1 - turn) * x + turn * y
        near_at = near_at if m == 0 else 1 - near_at
        far_at = far_at if here else 1 - far_at
        grads = early if g == 3 else full.at[g]
        return grads.at[
            z_at(k),
            (1 - turn) * near_at + turn * far_at,
            (1 - turn) * far_at + turn * near_at,
        ]

    def next_place(g, k, m):
        return next_got.at[g, k] if m == 0 else near_got.at[g, 1 + k]

    def skip_place(g, m):
        return skip_got.at[g] if m == 0 else near_got.at[g, 3]

    def fold_far(g, k, m):
        src, dst = mine(g, k, m, False), far_got.at[g, m, k]
        sems = fold_far_send.at[g, k, m], fold_far_recv.at[g, k, m]
        return remote(src, dst, *sems, (near, core))

    def fold_near(g, k):
        src, dst = far_got.at[g, 1, k], near_got.at[g, k]
        return remote(src, dst, fold_near_send.at[g, k], fold_near_recv.at[g, k], (far, core))

    def fold_next(g, k, m):
        src = far_got.at[g, m, 2 + k] if g in FOLD_MIDDLE else near_got.at[g, 2 + k]
        sems = fold_next_send.at[g, k, m], fold_next_recv.at[g, k, m]
        return remote(src, next_place(g, k, m), *sems, next_to)

    def fold_skip(g, m):
        src = far_got.at[g, m, 1] if g in FOLD_MIDDLE else near_got.at[g, 1]
        sems = fold_skip_send.at[g, m], fold_skip_recv.at[g, m]
        return remote(src, skip_place(g, m), *sems, skip_to)

    def fold_copies(g):
        copies = [fold_far(g, k, m) for k in range(4) for m in range(2)]
        if g in FOLD_MIDDLE:
            copies += [fold_next(g, k, m) for k in range(2) for m in range(2)]
            return copies + [fold_skip(g, m) for m in range(2)] + [fold_near(g, 0)]
        copies += [fold_next(g, k, 0) for k in range(2)]
        return copies + [fold_skip(g, 0)] + [fold_near(g, k) for k in range(4)]

    def add_up(ref, *others):
        total = ref[...].astype(wide)
        for other in others:
            total = total + other[...].astype(wide)
        ref[...] = total.astype(low)

    def far_start(g):
        order = [(k, m) for m in (1, 0) for k in (3, 2, 1, 0)]
        if g in FOLD_MIDDLE:
            order = [(k, m) for k in (3, 2, 1, 0) for m in (1, 0)]
        for k, m in order:
            fold_far(g, k, m).start()

    def far_add(g):
        if g in FOLD_MIDDLE:
            for k, m in ((3, 1), (3, 0), (2, 1), (2, 0)):
                fold_far(g, k, m).wait_recv()
                add_up(far_got.at[g, m, k], mine(g, k, m, True))
                fold_next(g, k - 2, m).start()
        else:
            for k in (3, 2, 1, 0):
                fold_far(g, k, 1).wait_recv()
                add_up(far_got.at[g, 1, k], mine(g, k, 1, True))
                fold_near(g, k).start()

    def near_add(g):
        if g in FOLD_MIDDLE:
            for m in (1, 0):
                fold_far(g, 1, m).wait_recv()
                fold_next(g, 1, m).wait_recv()
                add_up(far_got.at[g, m, 1], mine(g, 1, m, True), next_place(g, 1, m))
                fold_skip(g, m).start()
        else:
            for k in (3, 2, 1, 0):
                fold_far(g, k, 0).wait_recv()
                fold_near(g, k).wait_recv()
                add_up(near_got.at[g, k], mine(g, k, 0, True), far_got.at[g, 0, k])
                if k >= 2:
                    fold_next(g, k - 2, 0).start()

    def next_add(g):
        if g in FOLD_MIDDLE:
            fold_far(g, 0, 1).wait_recv()
            fold_next(g, 0, 1).wait_recv()
            fold_skip(g, 1).wait_recv()
            add_up(
                far_got.at[g, 1, 0], mine(g, 0, 1, True), next_place(g, 0, 1), skip_place(g, 1)
            )
            fold_near(g, 0).start()
        else:
            fold_next(g, 1, 0).wait_recv()
            add_up(near_got.at[g, 1], next_place(g, 1, 0))
            fold_skip(g, 0).start()

    def skip_add(g):
        fold_next(g, 0, 0).wait_recv()
        fold_skip(g, 0).wait_recv()
        if g in FOLD_MIDDLE:
            fold_far(g, 0, 0).wait_recv()
            fold_near(g, 0).wait_recv()
        parts = [near_got[g, 0], next_got[g, 0], skip_got[g]]
        if g in FOLD_MIDDLE:
            parts += [mine(g, 0, 0, True)[...], far_got[g, 0, 0]]
        total = parts[0].astype(wide)
        for part in parts[1:]:
            total = total + part.astype(wide)
        if g < 2:
            shard_out[g] = total
        else:
            (expand_out, reduce_out)[g - 2][...] = total

    def send_pair(j):
        for i in range(TILE):
            to = (pair + j) % tiles * TILE + i

            @pl.when(to != me)
            def _():
                flag_copy(to).start()
                slot_copy(to).start()

    lane = lax.broadcasted_iota(jnp.int32, (1, 2 * HEAD_DIM), 1)
    nobody = jnp.zeros_like(lane)

    def at_place(row, place):
        return jnp.sum(jnp.where(lane == place, row, 0))

    def route_step(slot, carry):
        met, found, alive, queries = carry
        query = query_of_ref[slot]
        hit = lane == query
        found = tuple(jnp.where(hit & (met == r), slot, found[r]) for r in range(RANKS))
        alive = tuple(jnp.where(hit & (met == r), live_ref[slot], alive[r]) for r in range(RANKS))
        queries = jnp.where(lane == slot, query, queries)
        return met + hit.astype(jnp.int32), found, alive, queries

    def rank_step(slot, ranks):
        later = (lane > slot) & (queries_here == query_of_ref[slot])
        return ranks + later.astype(jnp.int32)

    def fill(to, carry):
        for rank in range(RANKS):
            kept[to * RANKS + rank] = slot_got[at_place(slot_at[rank], to)]
        row = lax.broadcasted_iota(jnp.int32, flag_ref.shape[1:], 0)
        marks = jnp.zeros(flag_ref.shape[1:], wide)
        for rank in range(RANKS):
            mark = jnp.where(at_place(live_at[rank], to) > 0, 0.0, MASKED)
            marks = jnp.where(row == rank, mark, marks)
        flag_ref[to] = marks.astype(low)
        return carry

    greet_signal(me, core)
    for g, reads, writes in ((0, read_self_refs, write_self_ref), (1, read_cross_refs, write_cross_ref)):
        for i, read in enumerate(reads):
            shard_ref[g, :, i * width : (i + 1) * width] = read[...]
        shard_ref[g, :, 3 * width :] = writes[...]
    shard_ref[2] = expand_ref[...]
    shard_ref[3] = reduce_ref[...]
    greet_wait()
    launch(0)
    launch(1)
    slots_here = query_of_ref.shape[0]
    unused, slot_at, live_at, queries_here = lax.fori_loop(
        0,
        slots_here,
        route_step,
        (nobody, (nobody,) * RANKS, (nobody,) * RANKS, nobody),
        unroll=8,
    )
    staging.wait()
    lax.fori_loop(0, CHIPS, fill, 0, unroll=4)
    send_pair(0)
    send_pair(1)
    states[core, pl.ds(me * RANKS, RANKS)] = kept[pl.ds(me * RANKS, RANKS)]
    flags[me] = flag_ref[me]
    core_copy(me).start()

    line = lax.dot_general(
        table_ref[...],
        bucket_ref[...],
        (((1,), (0,)), ((), ())),
        precision=lax.Precision.HIGHEST,
        preferred_element_type=wide,
    )
    def bias_of(h):
        return kv_sum.at[h // 3, pl.ds(0, tokens), pl.ds(h % 3 * tokens, tokens)]

    turns = []
    for h in range(heads):
        for s in range(8):
            row = line[h : h + 1]
            turns.append(row if s == 0 else pltpu.roll(row, s, 1))
    base = jnp.concatenate(turns, axis=0)

    def bias_step(i, carry):
        rows = pltpu.roll(base, 8 * i, 1)
        for h in range(heads):
            bias_of(h)[pl.ds(pl.multiple_of(8 * i, 8), 8), :] = rows[8 * h : 8 * h + 8]
        return carry

    lax.fori_loop(0, tokens // 8, bias_step, 0)
    ranks = lax.fori_loop(0, slots_here, rank_step, nobody, unroll=8)

    def place_step(slot, carry):
        place_ref[slot] = query_of_ref[slot] * RANKS + at_place(ranks, slot)
        return carry

    lax.fori_loop(0, slots_here, place_step, 0, unroll=8)
    residual = target_ref[...].astype(wide)
    normed = (unit_of(residual)[0] * gains_ref[0:1, :]).astype(low)

    relay_one(0)
    launch(3)
    launch(2)
    relay_one(1)
    send_pair(2)
    relay_two(0)
    send_pair(3)
    send_pair(4)
    relay_three(0)
    relay_two(1)
    arrived(0)

    qkv_ref[...] = mm(normed, weight(0)[:, : 3 * width]).astype(low)
    relay_three(1)
    send_pair(5)
    queries_t = qkv_ref[:, :width].astype(wide).T
    for h in range(heads):
        q_rows[h] = halves_of_rows(queries_t, h)
    key_at = lax.broadcasted_iota(jnp.int32, (tokens, tokens), 0)
    query_at = lax.broadcasted_iota(jnp.int32, (tokens, tokens), 1)
    self_scale_ref[...] = jnp.zeros_like(self_scale_ref)
    for p in range(pairs):
        at = 2 * HEAD_DIM * p
        head_keys = qkv_ref[:, width + at : width + at + 2 * HEAD_DIM]
        values_t = qkv_ref[:, 2 * width + at : 2 * width + at + 2 * HEAD_DIM].T
        for a in range(2):
            h = 2 * p + a
            scores = mm(head_keys, q_rows[h]) + bias_of(h)[...]
            scores = jnp.where(key_at <= query_at, scores, MASKED)
            head_exps, unused, sums = exp_rows(scores)
            head_exps = head_exps.astype(low)
            self_exps_ref[h] = head_exps
            inverse = 1.0 / sums
            self_scale_ref[h : h + 1, :] = inverse
            first = at + a * HEAD_DIM
            out_t[first : first + HEAD_DIM, :] = (
                mm(values_t[a * HEAD_DIM : (a + 1) * HEAD_DIM], head_exps) * inverse
            )
        if p == 1:
            send_pair(6)
            send_pair(7)
    self_mixed_ref[...] = out_t[...].T.astype(low)
    give(0, rows_nt(self_mixed_ref[...], weight(0)[:, 3 * width :]))
    relay_one(2)
    arrived(1)
    residual_ref[...] = residual + pair_sum(0)

    normed = (unit_of(residual_ref[...])[0] * gains_ref[1:2, :]).astype(low)
    query_ref[...] = mm(normed, weight(1)[:, :width]).astype(low)
    queries_t = query_ref[...].astype(wide).T
    for h in range(heads):
        q_rows[h] = halves_of_rows(queries_t, h)
    out_t[...] = jnp.zeros_like(out_t)
    highest[...] = jnp.full_like(highest, MASKED)
    total[...] = jnp.zeros_like(total)
    tile_highest[...] = jnp.zeros_like(tile_highest)

    def take_in(t):
        for i in range(TILE):
            came = (pair - t + tiles) % tiles * TILE + i

            @pl.when(came != me)
            def _():
                flag_arrival(came).wait_recv()
                slot_arrival(came).wait_recv()
                core_copy(came).start()

    def exps_copy(t):
        rows = pl.ds((pair - t + tiles) % tiles * tile_rows, tile_rows)
        return pltpu.make_async_copy(exps.at[t % 2], exps_out.at[:, rows], exps_sem.at[t % 2])

    def keys_copy(t):
        rows = pl.ds((pair - t + tiles) % tiles * tile_rows, tile_rows)
        return pltpu.make_async_copy(keys.at[t % 2], kv_out.at[rows], keys_sem.at[t % 2])

    take_in(0)

    def tile_step(t, carry):
        tile = (pair - t + tiles) % tiles

        @pl.when(t == 1)
        def _():
            relay_two(2)

        @pl.when(t == 4)
        def _():
            relay_three(2)

        @pl.when(t == 6)
        def _():
            relay_two(3)

        @pl.when(t + 1 < tiles)
        def _():
            take_in(t + 1)

        @pl.when(t == 3)
        def _():
            relay_one(3)

        @pl.when(t >= 2)
        def _():
            exps_copy(t - 2).wait()
            keys_copy(t - 2).wait()

        for i in range(TILE):
            core_copy(tile * TILE + i).wait_recv()
        kv_parts = []
        for c in range(2):
            rows = states[c, pl.ds(tile * TILE * RANKS, TILE * RANKS)].reshape(tile_rows, half)
            w = full[1, 2 * c : 2 * c + 2, :, :, :, width : 3 * width]
            kv_parts.append(mm(rows, w.reshape(half, 2 * width)))
        keys[t % 2] = (kv_parts[0] + kv_parts[1]).astype(low)
        keys_copy(t).start()
        masks = []
        for i in range(TILE):
            for rank in range(RANKS):
                masks.append(flags[tile * TILE + i, rank : rank + 1, :].astype(wide)[None])
        masks = jnp.concatenate(masks, axis=0)
        for p in range(pairs):
            at = 2 * HEAD_DIM * p
            head_keys = keys[t % 2, :, at : at + 2 * HEAD_DIM]
            values_t = keys[t % 2, :, width + at : width + at + 2 * HEAD_DIM].T
            for a in range(2):
                h = 2 * p + a
                scores = mm(head_keys, q_rows[h]).reshape(TILE * RANKS, passage_len, tokens) + masks
                head_exps, top, sums = exp_rows(scores.reshape(tile_rows, tokens))
                head_exps = head_exps.astype(low)
                exps[t % 2, h] = head_exps
                before = highest[h : h + 1, :]
                now = jnp.maximum(before, top)
                keep, add = jnp.exp(before - now), jnp.exp(top - now)
                highest[h : h + 1, :] = now
                tile_highest[tile, h : h + 1, :] = top
                total[h : h + 1, :] = total[h : h + 1, :] * keep + sums * add
                first = at + a * HEAD_DIM
                out_t[first : first + HEAD_DIM, :] = (
                    out_t[first : first + HEAD_DIM, :] * keep
                    + mm(values_t[a * HEAD_DIM : (a + 1) * HEAD_DIM], head_exps) * add
                )
        exps_copy(t).start()

        return carry

    lax.fori_loop(0, tiles, tile_step, 0)
    for h in range(heads):
        inverse = 1.0 / total[h : h + 1, :]
        out_t[h * HEAD_DIM : (h + 1) * HEAD_DIM, :] *= inverse
        scale_ref[:, h, :] = jnp.exp(tile_highest[:, h, :] - highest[h : h + 1, :]) * inverse
    mixed_ref[...] = out_t[...].T.astype(low)
    give(1, rows_nt(mixed_ref[...], weight(1)[:, 3 * width :]))
    relay_three(3)
    residual_three = residual_ref[...] + pair_sum(1)
    unit, factor = unit_of(residual_three)
    normed = (unit * gains_ref[2:3, :]).astype(low)


    def sends_done(g):
        for copy in before_far(g) + [far_copy(g, k, m) for k in range(4) for m in range(2)]:
            copy.wait_send()

    def store_grad(g, first, value):
        blocks = value.astype(low).reshape(full.shape[1:5] + (value.shape[1],))
        full[g, :, :, :, :, first : first + value.shape[1]] = blocks

    arrived(2)
    hidden, slope = gelu_both(mm(normed, weight(2)))
    hidden = hidden.astype(low)
    early[...] = rows_tn(cotangent_ref[...], hidden).astype(low).reshape(early.shape)
    far_start(3)
    arrived(3)
    hidden_grad = mm(cotangent_ref[...], weight(3))
    before_grad = (hidden_grad * slope).astype(low)
    give(2, rows_nt(before_grad, weight(2)))
    sends_done(2)
    store_grad(2, 0, rows_tn(normed, before_grad))
    far_start(2)
    back, gain_three = rms_backward(pair_sum(2), unit, factor, gains_ref[2:3, :])
    upper_grad[...] = cotangent_ref[...].astype(wide) + back
    give(3, rows_nt(hidden, weight(3)))
    sends_done(0)
    sends_done(1)
    sends_done(3)
    for k in range(1, CHIPS):
        to = (me + k) % CHIPS
        slot_copy(to).wait_send()
        flag_copy(to).wait_send()
    for k in range(CHIPS):
        core_copy(k).wait_send()
    for t in range(tiles - 2, tiles):
        exps_copy(t).wait()
        keys_copy(t).wait()

    def back_tile(t):
        return (t + pair) % tiles

    def exps_load(t):
        rows = pl.ds(back_tile(t) * tile_rows, tile_rows)
        return pltpu.make_async_copy(exps_out.at[:, rows], exps.at[t % 2], exps_sem.at[t % 2])

    def keys_load(t):
        rows = pl.ds(back_tile(t) * tile_rows, tile_rows)
        return pltpu.make_async_copy(kv_out.at[rows], keys.at[t % 2], keys_sem.at[t % 2])

    def loads_start(t):
        exps_load(t).start()
        keys_load(t).start()

    def kv_weights(c):
        w = full[1, pl.ds(2 * c, 2), :, :, :, width : 3 * width]
        return w.reshape(half, 2 * width)

    def pair_copy(t):
        return remote(
            outgoing.at[t % 2],
            pair_got.at[pl.ds(back_tile(t) * TILE * RANKS, TILE * RANKS)],
            pair_send.at[t % 2],
            pair_recv.at[t],
            partner,
        )

    def return_copy(to):
        return remote(
            slots_of(kept, to), slots_of(slot_got, me), return_send.at[to], return_recv.at[me], (to, core)
        )

    def return_arrival(came):
        block = slots_of(slot_got, came)
        return remote(block, block, return_send.at[came], return_recv.at[came], (came, core))

    def finish_tile(t):
        tile = back_tile(t)
        pair_copy(t).wait_recv()
        rows = pl.ds(tile * TILE * RANKS, TILE * RANKS)
        kept[rows] = (kept[rows].astype(wide) + pair_got[rows].astype(wide)).astype(low)
        for j in range(TILE):
            to = tile * TILE + j

            @pl.when(to != me)
            def _():
                return_copy(to).start()

            @pl.when(to == me)
            def _():
                own = pl.ds(me * RANKS, RANKS)
                slot_got[own] = kept[own]

    grad_low = upper_grad[...].astype(low)
    mixed_grad = mm(grad_low, weight(1)[:, 3 * width :]).astype(low)
    prepare_heads(heads, query_ref, mixed_grad, mixed_ref[...], q_pair, o_pair, o_rows, centre)
    out_t[...] = jnp.zeros_like(out_t)
    kv_sum[...] = jnp.zeros_like(kv_sum)
    loads_start(0)
    block_ref[...] = (residual_three + pair_sum(3)).astype(low)

    def back_step(t, carry):
        tile = back_tile(t)
        @pl.when(t + 1 < tiles)
        def _():
            loads_start(t + 1)

        exps_load(t).wait()
        keys_load(t).wait()

        def prob(h):
            return exps[t % 2, h].astype(wide) * scale_ref[tile, h : h + 1, :]

        for p in range(pairs):
            at = 2 * HEAD_DIM * p
            key_grad, value_grad, query_parts = head_pair_back(
                p,
                keys[t % 2, :, at : at + 2 * HEAD_DIM],
                keys[t % 2, :, width + at : width + at + 2 * HEAD_DIM],
                prob,
                q_pair,
                o_pair,
                o_rows,
                centre,
                None,
            )
            dkv[:, at : at + 2 * HEAD_DIM] = key_grad
            dkv[:, width + at : width + at + 2 * HEAD_DIM] = value_grad
            for a in range(2):
                first = at + a * HEAD_DIM
                out_t[first : first + HEAD_DIM, :] += query_parts[a]
        here = dkv[...]

        @pl.when(t >= 2)
        def _():
            pair_copy(t - 2).wait_send()

        weights = kv_weights(1 - core)
        outgoing[t % 2] = rows_nt(here, weights).astype(low).reshape(outgoing.shape[1:])
        pair_copy(t).start()
        weights = kv_weights(core)
        mine = rows_nt(here, weights).astype(low).reshape(outgoing.shape[1:])
        kept[pl.ds(tile * TILE * RANKS, TILE * RANKS)] = mine

        rows = pl.ds(tile * TILE * RANKS, TILE * RANKS)
        for i in range(2):
            kv_sum[i] += rows_tn(states[i, rows].reshape(tile_rows, half), here)

        @pl.when(t >= 1)
        def _():
            finish_tile(t - 1)

        @pl.when(t == 2)
        def _():
            far_add(2)

        @pl.when(t == 5)
        def _():
            far_add(3)

        return carry

    lax.fori_loop(0, tiles, back_step, 0)
    dq = out_t[...].T.astype(low)
    give(4, rows_nt(dq, weight(1)[:, :width]))
    store_grad(1, 3 * width, rows_tn(upper_grad[...].astype(low), mixed_ref[...]))
    finish_tile(tiles - 1)
    near_add(2)
    unit_two, factor_two = unit_of(residual_ref[...])
    normed_two = (unit_two * gains_ref[1:2, :]).astype(low)
    store_grad(1, 0, rows_tn(normed_two, dq))

    store_grad(1, width, kv_sum[...].reshape(2 * half, 2 * width))
    far_start(1)
    near_add(3)
    next_add(2)

    back, gain_two = rms_backward(pair_sum(4), unit_two, factor_two, gains_ref[1:2, :])
    upper_grad[...] += back

    grad_low = upper_grad[...].astype(low)
    mixed_grad = mm(grad_low, weight(0)[:, 3 * width :]).astype(low)
    prepare_heads(
        heads,
        qkv_ref.at[:, :width],
        mixed_grad,
        self_mixed_ref[...],
        q_pair,
        o_pair,
        o_rows,
        centre,
    )

    def self_prob(h):
        return self_exps_ref[h].astype(wide) * self_scale_ref[h : h + 1, :]

    def keep_scores(h, score_grad):
        self_exps_ref[h] = score_grad

    query_rows, key_columns, value_columns = [], [], []
    for p in range(pairs):
        at = 2 * HEAD_DIM * p
        key_grad, value_grad, query_parts = head_pair_back(
            p,
            qkv_ref[:, width + at : width + at + 2 * HEAD_DIM],
            qkv_ref[:, 2 * width + at : 2 * width + at + 2 * HEAD_DIM],
            self_prob,
            q_pair,
            o_pair,
            o_rows,
            centre,
            keep_scores,
        )
        key_columns.append(key_grad)
        value_columns.append(value_grad)
        query_rows.extend(query_parts)
    dq = jnp.concatenate(query_rows, axis=0).T.astype(low)
    dqkv = jnp.concatenate([dq] + key_columns + value_columns, axis=1)
    give(5, rows_nt(dqkv, weight(0)[:, : 3 * width]))
    store_grad(0, 3 * width, rows_tn(upper_grad[...].astype(low), self_mixed_ref[...]))
    unit_one, factor_one = unit_of(target_ref[...].astype(wide))
    normed_one = (unit_one * gains_ref[0:1, :]).astype(low)
    store_grad(0, 0, rows_tn(normed_one, dqkv))
    far_start(0)
    far_add(1)
    next_add(3)

    length = self_exps_ref.shape[1]

    def diagonal_step(i, total):
        rows = self_exps_ref[:, pl.ds(pl.multiple_of(16 * i, 16), 16), :].astype(wide)
        rows = rows.reshape(heads * 16, length)
        return total + pltpu.roll(rows, (length - 16 * i) % length, 1)

    total = lax.fori_loop(
        0, length // 16, diagonal_step, jnp.zeros((heads * 16, length), wide)
    ).reshape(heads, 16, length)
    small[...] = jnp.zeros_like(small)
    for h in range(heads):
        line = total[h, 0:1]
        for s in range(1, 16):
            line = line + pltpu.roll(total[h, s : s + 1], length - s, 1)
        small[8 + h : 9 + h, :length] = line
    by_bucket = jnp.dot(
        small[8:16, :length], count_ref[...], precision=lax.Precision.HIGHEST,
        preferred_element_type=wide,
    )
    small[8:16, :length] = jnp.zeros((8, length), wide)
    small[8:16, : count_ref.shape[1]] = by_bucket

    back, gain_one = rms_backward(pair_sum(5), unit_one, factor_one, gains_ref[0:1, :])
    target_grad_ref[...] = (upper_grad[...] + back).astype(low)
    small[0:1, :] = gain_one[None, :]
    small[1:2, :] = gain_two[None, :]
    small[2:3, :] = gain_three[None, :]

    def small_copy(step):
        if step == 0:
            return remote(small, small_got.at[0], small_send.at[0], small_recv.at[0], (across_x, core))
        if step == 1:
            return remote(
                small_got.at[6], small_got.at[1], small_send.at[1], small_recv.at[1], (across_y, core)
            )
        return remote(
            small_got.at[7],
            small_got.at[2 + z],
            small_send.at[step],
            small_recv.at[step],
            ((me + 4 * (step - 1)) % CHIPS, core),
        )

    small_copy(0).start()
    skip_add(2)
    near_add(1)
    far_add(0)
    skip_add(3)
    next_add(1)
    near_add(0)
    next_add(0)
    skip_add(1)
    small_copy(0).wait_recv()
    small_got[6] = small[...] + small_got[0]
    small_copy(1).start()
    for k in range(1, CHIPS):
        return_arrival((me + k) % CHIPS).wait_recv()
    small_copy(1).wait_recv()
    small_got[7] = small_got[6] + small_got[1]
    for step in range(2, 5):
        small_copy(step).start()
    small_got[2 + z] = small_got[7]
    for k in range(1, CHIPS):
        return_copy((me + k) % CHIPS).wait_send()
    slots = slots_ref.shape[0]

    def pick(slot, carry):
        kept[slot] = slot_got[place_ref[slot]]
        return carry

    lax.fori_loop(0, slots, pick, 0, unroll=4)
    picked = pltpu.make_async_copy(kept.at[pl.ds(0, slots)], slots_ref, out_sem.at[1])
    picked.start()
    skip_add(0)
    for step in range(2, 5):
        small_copy(step).wait_recv()
    whole = small_got[2] + small_got[3] + small_got[4] + small_got[5]
    gains_out[...] = whole[: gains_out.shape[0]]
    bias_out[...] = whole[8 : 8 + heads, : bias_out.shape[1]]
    for g in range(groups):
        for copy in fold_copies(g):
            copy.wait_send()
    for t in range(tiles - 2, tiles):
        pair_copy(t).wait_send()
    for step in range(5):
        small_copy(step).wait_send()
    for i in range(4, 6):
        row_copy(i).wait_send()
    picked.wait()


def run_block(
    query_of, live, passages, weights, target, cotangent, gains, table, buckets, counts
):
    low, wide = jnp.bfloat16, jnp.float32
    groups = 4
    rows, columns = weights[4].shape
    slots, passage_len, half = passages.shape
    tokens, model = target.shape
    width = columns // 4
    heads = width // HEAD_DIM
    key_count = CHIPS * RANKS * passage_len
    tile_rows = TILE * RANKS * passage_len
    tiles = CHIPS // TILE
    small_shape = (16, model)
    shape = jax.ShapeDtypeStruct
    vmem = pltpu.VMEM
    pair_heads = vmem((heads, tokens, 2 * HEAD_DIM), low)
    pair_rows = vmem((heads, 2 * HEAD_DIM, tokens), low)
    all_slots = (CHIPS * RANKS, passage_len, half)

    def both(*dims):
        return [DMA(dims), DMA(dims)]

    return pl.pallas_call(
        block_kernel,
        out_shape=(
            shape((2, rows, columns), wide),
            shape((rows, columns), wide),
            shape((rows, columns), wide),
            shape((slots, passage_len, half), low),
            shape(gains.shape, wide),
            shape(table.shape, wide),
            shape((tokens, model), low),
            shape((tokens, model), low),
            shape((heads, key_count, tokens), low),
            shape((key_count, 2 * width), low),
        ),
        in_specs=[IN_SMEM] * 2
        + [ANY, (IN_VMEM,) * 3, IN_VMEM, (IN_VMEM,) * 3, IN_VMEM, IN_VMEM, IN_VMEM]
        + [IN_VMEM] * 6,
        out_specs=(IN_VMEM,) * 3 + (ANY,) + (IN_VMEM,) * 4 + (ANY, ANY),
        scratch_shapes=[
            pltpu.SMEM((slots,), jnp.int32),
            vmem((groups, rows, columns), low),
            vmem((CHIPS, FLAG_ROWS, tokens), low),
            vmem((groups, 4, 2, 2, rows, columns), low),
            vmem((2,) + all_slots, low),
            vmem((CHIPS, FLAG_ROWS, tokens), low),
            vmem(all_slots, low),
            vmem(all_slots, low),
            vmem((2, heads, tile_rows, tokens), low),
            vmem((2, tile_rows, 2 * width), low),
            pair_rows,
            pair_heads,
            pair_heads,
            pair_rows,
            vmem((8, tokens), wide),
            vmem((width, tokens), wide),
            vmem((8, tokens), wide),
            vmem((8, tokens), wide),
            vmem((tiles, 8, tokens), wide),
            vmem((tiles, 8, tokens), wide),
            vmem((tokens, width), low),
            vmem((tokens, width), low),
            vmem((tokens, model), wide),
            vmem((tokens, 3 * width), low),
            vmem((tokens, width), low),
            vmem((heads, tokens, tokens), low),
            vmem((8, tokens), wide),
            vmem((tokens, model), wide),
            vmem((2, tokens, model), wide),
            vmem((2, tokens, model), wide),
            vmem((groups, 2, 4, rows, columns), low),
            vmem((groups, 4, rows, columns), low),
            vmem((groups, 2, rows, columns), low),
            vmem((groups, rows, columns), low),
            vmem((tile_rows, 2 * width), low),
            vmem((2, half, 2 * width), wide),
            vmem((4, 2, 2, rows, columns), low),
            vmem((2, TILE * RANKS, passage_len, half), low),
            vmem(all_slots, low),
            vmem(small_shape, wide),
            vmem((8,) + small_shape, wide),
        ]
        + both(groups, 2)
        + both(groups, 2, 2)
        + both(groups, 4)
        + both(groups, 4, 2)
        + both(groups, 4, 2)
        + both(groups, 4)
        + both(groups, 2, 2)
        + both(groups, 2)
        + both(CHIPS)
        + both(CHIPS)
        + both(CHIPS)
        + both(CHIPS)
        + [DMA((2,)), DMA((tiles,))]
        + both(6)
        + both(5)
        + [DMA((groups,)), DMA((2,)), DMA((2,)), DMA((2,))],
        compiler_params=pltpu.CompilerParams(
            collective_id=0, has_side_effects=True, vmem_limit_bytes=62 * 2**20
        ),
    )(query_of, live, passages, *weights, target, cotangent, gains, table, buckets, counts)


def body(
    target_states,
    passage_states,
    slot_query,
    slot_live,
    norm_gains,
    self_query,
    self_key,
    self_value,
    self_output,
    position_bias,
    cross_query,
    cross_key,
    cross_value,
    cross_output,
    expand_weight,
    reduce_weight,
    output_cotangent,
):
    low = jnp.bfloat16
    width_here = self_query.shape[1]
    heads_here = width_here // HEAD_DIM
    passage_len, half = passage_states.shape[1:]
    bucket_count = position_bias.shape[0]
    distance = np.zeros((TLEN, 128), np.float32)
    distance[np.arange(TLEN), bucket_table(TLEN, bucket_count, MAXDIST)[:, 0]] = 1.0
    shard_grads, expand_grad, reduce_grad, passage_grad, gains_grad, bias_grad, target_grad, block_out = run_block(
        slot_query,
        slot_live,
        passage_states,
        (
            (self_query, self_key, self_value),
            self_output.T,
            (cross_query, cross_key, cross_value),
            cross_output.T,
            expand_weight,
            reduce_weight.T,
        ),
        target_states,
        output_cotangent,
        norm_gains,
        position_bias.T,
        jnp.asarray(distance[:, :bucket_count].T),
        jnp.asarray(distance),
    )[:8]
    w = width_here
    first, second = shard_grads[0], shard_grads[1]
    return (
        block_out,
        target_grad,
        passage_grad,
        gains_grad,
        first[:, :w],
        first[:, w : 2 * w],
        first[:, 2 * w : 3 * w],
        first[:, 3 * w :].T,
        bias_grad.T,
        second[:, :w],
        second[:, w : 2 * w],
        second[:, 2 * w : 3 * w],
        second[:, 3 * w :].T,
        expand_grad,
        reduce_grad.T,
    )


def solution(mesh):
    return jax.shard_map(
        body if fits(mesh) else body_any,
        mesh=mesh,
        in_specs=(
            P("pas", None),
            P("pas", None, "mdl"),
            P("pas"),
            P("pas"),
            P(),
            P("pas", "mdl"),
            P("pas", "mdl"),
            P("pas", "mdl"),
            P("mdl", "pas"),
            P(None, "mdl"),
            P("pas", "mdl"),
            P("pas", "mdl"),
            P("pas", "mdl"),
            P("mdl", "pas"),
            P("pas", "mdl"),
            P("mdl", "pas"),
            P("pas", None),
        ),
        out_specs=(
            P("pas", None),
            P("pas", None),
            P("pas", None, "mdl"),
            P(),
            P("pas", "mdl"),
            P("pas", "mdl"),
            P("pas", "mdl"),
            P("mdl", "pas"),
            P(None, "mdl"),
            P("pas", "mdl"),
            P("pas", "mdl"),
            P("pas", "mdl"),
            P("mdl", "pas"),
            P("pas", "mdl"),
            P("mdl", "pas"),
        ),
        check_vma=False,
    )
```

```python
from functools import partial
import math

import jax
import jax.numpy as jnp
import numpy as np
from jax import lax
from jax.experimental import pallas as pl
from jax.experimental.pallas import tpu as pltpu
from jax.sharding import PartitionSpec as P

HEAD_DIM = 64
MAXDIST = 128
TLEN = 256
PQ = 40


EPSILON = 1e-06
MASKED = -1e30


def bucket_table(length, buckets, distance):
    later = np.arange(length)[:, None]
    earlier = np.arange(length)[None, :]
    behind = np.maximum(later - earlier, 0)
    exact = buckets // 2
    spread = np.log(np.maximum(behind, 1) / exact) / math.log(distance / exact) * (buckets - exact)
    far_bucket = np.minimum(exact + np.floor(spread).astype(np.int32), buckets - 1)
    return np.where(behind < exact, behind, far_bucket).astype(np.int32)


def rms_forward(values, gain):
    factor = lax.rsqrt(jnp.mean(values * values, axis=-1, keepdims=True) + EPSILON)
    unit_rows = values * factor
    return (unit_rows, factor, (unit_rows * gain).astype(jnp.bfloat16))


def rms_backward(normed_grad, unit_rows, factor, gain):
    scaled_grad = normed_grad * gain
    input_grad = factor * (
        scaled_grad - unit_rows * jnp.mean(scaled_grad * unit_rows, axis=-1, keepdims=True)
    )
    return (input_grad, jnp.sum(normed_grad * unit_rows, axis=0))


def over_heads(partial_rows):
    return lax.psum(partial_rows, "mdl")


def score_block(queries, key_rows, allowed, bias):
    scores = jnp.einsum("sihe,sjhe->shij", queries, key_rows, preferred_element_type=jnp.float32)
    if bias is not None:
        scores = scores + bias
    return jnp.where(allowed, scores, MASKED)


def attend(queries, key_rows, values, allowed, bias):
    scores = score_block(queries, key_rows, allowed, bias)
    highest = jnp.max(scores, axis=-1, keepdims=True)
    totals = highest + jnp.log(jnp.sum(jnp.exp(scores - highest), axis=-1, keepdims=True))
    probability = jnp.exp(scores - totals)
    mixed = jnp.einsum(
        "shij,sjhe->sihe",
        probability.astype(jnp.bfloat16),
        values,
        preferred_element_type=jnp.float32,
    )
    return (mixed.astype(jnp.bfloat16), totals)


def attend_back(queries, key_rows, values, allowed, bias, totals, out_grad):
    scores = score_block(queries, key_rows, allowed, bias)
    probability = jnp.exp(scores - totals)
    prob_grad = jnp.einsum("sihe,sjhe->shij", out_grad, values, preferred_element_type=jnp.float32)
    centered = jnp.sum(probability * prob_grad, axis=-1, keepdims=True)
    score_grad = (probability * (prob_grad - centered)).astype(jnp.bfloat16)
    query_grad = jnp.einsum(
        "shij,sjhe->sihe", score_grad, key_rows, preferred_element_type=jnp.float32
    )
    key_grad = jnp.einsum(
        "shij,sihe->sjhe", score_grad, queries, preferred_element_type=jnp.float32
    )
    value_grad = jnp.einsum(
        "shij,sihe->sjhe",
        probability.astype(jnp.bfloat16),
        out_grad,
        preferred_element_type=jnp.float32,
    )
    return (query_grad, key_grad, value_grad, score_grad)


def send_plan(slot_query, slot_live, per_device, capacity):
    target_device = slot_query // per_device
    matching = target_device[:, None] == target_device[None, :]
    lower_part = jnp.tril(jnp.ones(matching.shape, jnp.bool_), -1)
    ranking = jnp.sum(jnp.logical_and(matching, lower_part), axis=1)
    position = target_device * capacity + ranking
    codes = jnp.where(slot_live > 0, slot_query % per_device + 1, 0).astype(jnp.bfloat16)
    return (position, codes)


def arrange_plan(got_codes, per_device, slots_each):
    local_query = got_codes.astype(jnp.int32) - 1
    matches = (local_query[:, None] == jnp.arange(per_device, dtype=jnp.int32)[None, :]).astype(
        jnp.int32
    )
    ranking = jnp.sum((jnp.cumsum(matches, axis=0) - 1) * matches, axis=1)
    spare_place = per_device * slots_each
    places = jnp.where(local_query >= 0, local_query * slots_each + ranking, spare_place)
    arrivals = got_codes.shape[0]
    gather_index = (
        jnp.zeros((spare_place + 1,), jnp.int32)
        .at[places]
        .set(jnp.arange(arrivals, dtype=jnp.int32))
    )
    valid_slot = jnp.zeros((spare_place + 1,), jnp.int32).at[places].set(1)
    return (gather_index[:spare_place], valid_slot[:spare_place] > 0)


def place_rows(rows, position, total_rows):
    return jnp.zeros((total_rows,) + rows.shape[1:], rows.dtype).at[position].set(rows)


def return_rows(rows, gather_index, total_rows):
    return jnp.zeros((total_rows,) + rows.shape[1:], rows.dtype).at[gather_index].add(rows)


def body_any(
    target_states,
    passage_states,
    slot_query,
    slot_live,
    norm_gains,
    self_query,
    self_key,
    self_value,
    self_output,
    position_bias,
    cross_query,
    cross_key,
    cross_value,
    cross_output,
    expand_weight,
    reduce_weight,
    output_cotangent,
):
    (
        query_full,
        key_full,
        value_full,
        cross_query_full,
        cross_key_full,
        cross_value_full,
        expand_full,
    ) = (
        lax.all_gather(self_query, "pas", axis=0, tiled=True),
        lax.all_gather(self_key, "pas", axis=0, tiled=True),
        lax.all_gather(self_value, "pas", axis=0, tiled=True),
        lax.all_gather(cross_query, "pas", axis=0, tiled=True),
        lax.all_gather(cross_key, "pas", axis=0, tiled=True),
        lax.all_gather(cross_value, "pas", axis=0, tiled=True),
        lax.all_gather(expand_weight, "pas", axis=0, tiled=True),
    )
    output_full, cross_output_full, reduce_full = (
        lax.all_gather(self_output, "pas", axis=1, tiled=True),
        lax.all_gather(cross_output, "pas", axis=1, tiled=True),
        lax.all_gather(reduce_weight, "pas", axis=1, tiled=True),
    )
    width_here = query_full.shape[1]
    heads_here = width_here // HEAD_DIM
    sequences = target_states.shape[0] // TLEN
    passage_len = passage_states.shape[1]
    bucket_count = position_bias.shape[0]
    devices = lax.axis_size("pas")
    slots_here = slot_query.shape[0]
    capacity = -(-slots_here // devices)
    buffer_rows = devices * capacity
    residual = target_states.astype(jnp.float32)
    unit_one, factor_one, normed_one = rms_forward(residual, norm_gains[0])
    self_weights = jnp.concatenate([query_full, key_full, value_full], axis=1)
    projected = jnp.dot(normed_one, self_weights, preferred_element_type=jnp.float32).astype(
        jnp.bfloat16
    )
    projected = projected.reshape(sequences, TLEN, 3, heads_here, HEAD_DIM)
    queries_self = projected[:, :, 0]
    keys_self = projected[:, :, 1]
    values_self = projected[:, :, 2]
    buckets = jnp.asarray(bucket_table(TLEN, bucket_count, MAXDIST))
    one_hot = (jnp.arange(bucket_count, dtype=jnp.int32)[:, None, None] == buckets[None]).astype(
        jnp.float32
    )
    bias_full = jnp.einsum("bij,bh->hij", one_hot, position_bias, precision=lax.Precision.HIGHEST)[
        None
    ]
    causal = jnp.asarray(np.tril(np.ones((TLEN, TLEN), dtype=bool)))
    attended_self, total_self = attend(queries_self, keys_self, values_self, causal, bias_full)
    merged_self = attended_self.reshape(sequences * TLEN, width_here)
    residual_two = residual + over_heads(
        jnp.dot(merged_self, output_full, preferred_element_type=jnp.float32)
    )
    unit_two, factor_two, normed_two = rms_forward(residual_two, norm_gains[1])
    cross_queries = jnp.dot(
        normed_two, cross_query_full, preferred_element_type=jnp.float32
    ).astype(jnp.bfloat16)
    cross_queries = cross_queries.reshape(sequences, TLEN, heads_here, HEAD_DIM)
    kv_weights = jnp.concatenate([cross_key_full, cross_value_full], axis=1)
    position, codes = send_plan(slot_query, slot_live, sequences, capacity)
    sent_codes = place_rows(codes, position, buffer_rows)
    states_full = lax.all_gather(passage_states, "mdl", axis=2, tiled=True)
    key_values = jnp.einsum(
        "tpd,dc->tpc", states_full, kv_weights, preferred_element_type=jnp.float32
    ).astype(jnp.bfloat16)
    received, got_codes = (
        lax.all_to_all(
            place_rows(key_values, position, buffer_rows),
            "pas",
            split_axis=0,
            concat_axis=0,
            tiled=True,
        ),
        lax.all_to_all(sent_codes, "pas", split_axis=0, concat_axis=0, tiled=True),
    )
    gather_index, valid_slot = arrange_plan(got_codes, sequences, PQ)
    arranged = jnp.take(received, gather_index, axis=0)
    arranged = arranged.reshape(sequences, PQ * passage_len, 2, heads_here, HEAD_DIM)
    key_rows = arranged[:, :, 0]
    value_rows = arranged[:, :, 1]
    allowed = jnp.repeat(valid_slot.reshape(sequences, PQ), passage_len, axis=1)[:, None, None, :]
    head_block = 2
    head_ranges = [
        slice(start_head, start_head + head_block)
        for start_head in range(0, heads_here, head_block)
    ]
    cross_parts = []
    cross_totals = []
    for head_range in head_ranges:
        mixed_part, total_part = attend(
            cross_queries[:, :, head_range],
            key_rows[:, :, head_range],
            value_rows[:, :, head_range],
            allowed,
            None,
        )
        cross_parts.append(mixed_part)
        cross_totals.append(total_part)
    merged_cross = jnp.concatenate(cross_parts, axis=2).reshape(sequences * TLEN, width_here)
    residual_three = residual_two + over_heads(
        jnp.dot(merged_cross, cross_output_full, preferred_element_type=jnp.float32)
    )
    unit_three, factor_three, normed_three = rms_forward(residual_three, norm_gains[2])
    before = jnp.dot(normed_three, expand_full, preferred_element_type=jnp.float32)
    hidden = jax.nn.gelu(before, approximate=True).astype(jnp.bfloat16)
    block_out = residual_three + over_heads(
        jnp.dot(hidden, reduce_full, preferred_element_type=jnp.float32)
    )
    grad_out = output_cotangent.astype(jnp.float32)
    reduce_grad = jnp.dot(hidden.T, output_cotangent, preferred_element_type=jnp.float32)
    hidden_grad = jnp.dot(output_cotangent, reduce_full.T, preferred_element_type=jnp.float32)
    unused_value, gelu_pullback = jax.vjp(partial(jax.nn.gelu, approximate=True), before)
    before_grad = gelu_pullback(hidden_grad)[0].astype(jnp.bfloat16)
    expand_grad = jnp.dot(normed_three.T, before_grad, preferred_element_type=jnp.float32)
    normed_grad = over_heads(
        jnp.dot(before_grad, expand_full.T, preferred_element_type=jnp.float32)
    )
    back_three, gain_three = rms_backward(normed_grad, unit_three, factor_three, norm_gains[2])
    grad_three = grad_out + back_three
    grad_low = grad_three.astype(jnp.bfloat16)
    cross_output_grad = jnp.dot(merged_cross.T, grad_low, preferred_element_type=jnp.float32)
    mixed_grad = jnp.dot(grad_low, cross_output_full.T, preferred_element_type=jnp.float32).astype(
        jnp.bfloat16
    )
    mixed_grad = mixed_grad.reshape(sequences, TLEN, heads_here, HEAD_DIM)
    query_parts = []
    key_parts = []
    value_parts = []
    for number, head_range in enumerate(head_ranges):
        query_part, key_part, value_part, unused_scores = attend_back(
            cross_queries[:, :, head_range],
            key_rows[:, :, head_range],
            value_rows[:, :, head_range],
            allowed,
            None,
            cross_totals[number],
            mixed_grad[:, :, head_range],
        )
        query_parts.append(query_part)
        key_parts.append(key_part)
        value_parts.append(value_part)
    cross_query_rows = (
        jnp.concatenate(query_parts, axis=2)
        .astype(jnp.bfloat16)
        .reshape(sequences * TLEN, width_here)
    )
    kv_grad = jnp.stack(
        [jnp.concatenate(key_parts, axis=2), jnp.concatenate(value_parts, axis=2)], axis=2
    )
    kv_grad = kv_grad.astype(jnp.bfloat16).reshape(sequences * PQ, passage_len, 2 * width_here)
    returned = lax.all_to_all(
        return_rows(kv_grad, gather_index, buffer_rows),
        "pas",
        split_axis=0,
        concat_axis=0,
        tiled=True,
    )
    kv_grad_here = jnp.take(returned, position, axis=0)
    kv_weight_grad = jnp.einsum(
        "tpd,tpc->dc", states_full, kv_grad_here, preferred_element_type=jnp.float32
    )
    states_grad = jnp.einsum(
        "tpc,dc->tpd", kv_grad_here, kv_weights, preferred_element_type=jnp.float32
    )
    passage_grad = lax.psum_scatter(
        states_grad.astype(jnp.bfloat16), "mdl", scatter_dimension=2, tiled=True
    )
    cross_query_grad = jnp.dot(normed_two.T, cross_query_rows, preferred_element_type=jnp.float32)
    normed_grad = over_heads(
        jnp.dot(cross_query_rows, cross_query_full.T, preferred_element_type=jnp.float32)
    )
    back_two, gain_two = rms_backward(normed_grad, unit_two, factor_two, norm_gains[1])
    grad_two = grad_three + back_two
    grad_low = grad_two.astype(jnp.bfloat16)
    self_output_grad = jnp.dot(merged_self.T, grad_low, preferred_element_type=jnp.float32)
    attended_grad = jnp.dot(grad_low, output_full.T, preferred_element_type=jnp.float32).astype(
        jnp.bfloat16
    )
    attended_grad = attended_grad.reshape(sequences, TLEN, heads_here, HEAD_DIM)
    query_grad, key_grad, value_grad, score_grad = attend_back(
        queries_self, keys_self, values_self, causal, bias_full, total_self, attended_grad
    )
    bias_grad = jnp.einsum(
        "hij,bij->bh",
        jnp.sum(score_grad.astype(jnp.float32), axis=0),
        one_hot,
        precision=lax.Precision.HIGHEST,
    )
    projected_grad = jnp.stack([query_grad, key_grad, value_grad], axis=2).astype(jnp.bfloat16)
    projected_grad = projected_grad.reshape(sequences * TLEN, 3 * width_here)
    self_weight_grad = jnp.dot(normed_one.T, projected_grad, preferred_element_type=jnp.float32)
    normed_grad = over_heads(
        jnp.dot(projected_grad, self_weights.T, preferred_element_type=jnp.float32)
    )
    back_one, gain_one = rms_backward(normed_grad, unit_one, factor_one, norm_gains[0])
    target_grad = (grad_two + back_one).astype(jnp.bfloat16)
    row_grads = (
        lax.psum_scatter(self_weight_grad[:, :width_here], "pas", scatter_dimension=0, tiled=True),
        lax.psum_scatter(
            self_weight_grad[:, width_here : 2 * width_here], "pas", scatter_dimension=0, tiled=True
        ),
        lax.psum_scatter(
            self_weight_grad[:, 2 * width_here :], "pas", scatter_dimension=0, tiled=True
        ),
        lax.psum_scatter(cross_query_grad, "pas", scatter_dimension=0, tiled=True),
        lax.psum_scatter(kv_weight_grad[:, :width_here], "pas", scatter_dimension=0, tiled=True),
        lax.psum_scatter(kv_weight_grad[:, width_here:], "pas", scatter_dimension=0, tiled=True),
        lax.psum_scatter(expand_grad, "pas", scatter_dimension=0, tiled=True),
    )
    col_grads = (
        lax.psum_scatter(self_output_grad, "pas", scatter_dimension=1, tiled=True),
        lax.psum_scatter(cross_output_grad, "pas", scatter_dimension=1, tiled=True),
        lax.psum_scatter(reduce_grad, "pas", scatter_dimension=1, tiled=True),
    )
    gains_total, bias_total = lax.psum(
        (jnp.stack([gain_one, gain_two, gain_three]), bias_grad), "pas"
    )
    return (
        block_out.astype(jnp.bfloat16),
        target_grad,
        passage_grad,
        gains_total,
        row_grads[0],
        row_grads[1],
        row_grads[2],
        col_grads[0],
        bias_total,
        row_grads[3],
        row_grads[4],
        row_grads[5],
        col_grads[1],
        row_grads[6],
        col_grads[2],
    )


CHIPS = 16
RANKS = 3
FLAG_ROWS = 16
MESH_ID = pl.DeviceIdType.MESH
VMEM_LIMIT = 56 * 2**20


def fits(mesh):
    return mesh.shape["pas"] == CHIPS and mesh.shape["mdl"] == 2


def places():
    me, core = lax.axis_index("pas"), lax.axis_index("mdl")
    x, y, z = me % 2, (me // 2) % 2, me // 4
    across_x, across_y = me + 1 - 2 * x, me + 2 - 4 * y
    near = across_y + (across_x - across_y) * core
    far = across_x + (across_y - across_x) * core
    return me, core, x, y, z, near, far


def remote(src, dst, send_sem, recv_sem, device):
    return pltpu.make_async_remote_copy(
        src_ref=src,
        dst_ref=dst,
        send_sem=send_sem,
        recv_sem=recv_sem,
        device_id=device,
        device_id_type=MESH_ID,
    )


def greet_signal(me, core):
    barrier = pltpu.get_barrier_semaphore()
    for k in range(1, CHIPS):
        pl.semaphore_signal(
            barrier, inc=1, device_id=((me + k) % CHIPS, core), device_id_type=MESH_ID
        )
    pl.semaphore_signal(barrier, inc=1, device_id=(me, 1 - core), device_id_type=MESH_ID)


def greet_wait():
    pl.semaphore_wait(pltpu.get_barrier_semaphore(), CHIPS)


ANY = pl.BlockSpec(memory_space=pl.ANY)
IN_VMEM = pl.BlockSpec(memory_space=pltpu.VMEM)
IN_SMEM = pl.BlockSpec(memory_space=pltpu.SMEM)
DMA = pltpu.SemaphoreType.DMA


def rows_nt(left, right):
    return lax.dot_general(
        left, right, (((1,), (1,)), ((), ())), preferred_element_type=jnp.float32
    )


def rows_tn(left, right):
    return lax.dot_general(
        left, right, (((0,), (0,)), ((), ())), preferred_element_type=jnp.float32
    )


TILE = 2


def mm(left, right):
    return jnp.dot(left, right, preferred_element_type=jnp.float32)


def halves_of_pair(rows, head):
    lane = lax.broadcasted_iota(jnp.int32, (rows.shape[0], 2 * HEAD_DIM), 1)
    at = head // 2 * 2 * HEAD_DIM
    return jnp.where(lane // HEAD_DIM == head % 2, rows[:, at : at + 2 * HEAD_DIM], 0.0).astype(
        jnp.bfloat16
    )


def halves_of_rows(rows, head):
    row = lax.broadcasted_iota(jnp.int32, (2 * HEAD_DIM, rows.shape[1]), 0)
    at = head // 2 * 2 * HEAD_DIM
    return jnp.where(row // HEAD_DIM == head % 2, rows[at : at + 2 * HEAD_DIM], 0.0).astype(
        jnp.bfloat16
    )


def unit_of(values):
    factor = lax.rsqrt(jnp.mean(values * values, axis=-1, keepdims=True) + EPSILON)
    return values * factor, factor


def prepare_heads(heads, query_ref, grad, mixed, q_pair, o_pair, o_rows, centre):
    grad = grad.astype(jnp.float32)
    grad_t = grad.T
    product = (grad * mixed.astype(jnp.float32)).T
    queries = query_ref[...].astype(jnp.float32)
    for h in range(heads):
        q_pair[h] = halves_of_pair(queries, h)
        o_pair[h] = halves_of_pair(grad, h)
        o_rows[h] = halves_of_rows(grad_t, h)
        centre[h : h + 1, :] = jnp.sum(
            product[h * HEAD_DIM : (h + 1) * HEAD_DIM], axis=0, keepdims=True
        )


def head_pair_back(p, keys, values, prob, q_pair, o_pair, o_rows, centre, keep_scores):
    low = jnp.bfloat16
    keys_t = keys.T
    query_parts = []
    for a in range(2):
        h = 2 * p + a
        prob_grad = mm(values, o_rows[h])
        weights = prob(h)
        score_grad = (weights * (prob_grad - centre[h : h + 1, :])).astype(low)
        if keep_scores is not None:
            keep_scores(h, score_grad)
        key_part = mm(score_grad, q_pair[h])
        value_part = mm(weights.astype(low), o_pair[h])
        key_grad = key_part if a == 0 else key_grad + key_part
        value_grad = value_part if a == 0 else value_grad + value_part
        query_parts.append(mm(keys_t[a * HEAD_DIM : (a + 1) * HEAD_DIM], score_grad))
    return key_grad.astype(low), value_grad.astype(low), query_parts


def z_turned(z, k):
    high, low = z // 2, z % 2
    if k % 2:
        high = 1 - high
    if k // 2:
        low = 1 - low
    return 2 * high + low


def exp_rows(scores):
    highest = jnp.max(scores, axis=0, keepdims=True)
    exps = jnp.exp(scores - highest)
    return exps, highest, jnp.sum(exps, axis=0, keepdims=True)


def gelu_both(values):
    first = math.sqrt(2 / math.pi)
    square = values * values
    curve = jnp.tanh(first * values * (1.0 + 0.044715 * square))
    half = 0.5 * (1.0 + curve)
    slope = half + 0.5 * values * (1.0 - curve * curve) * first * (1.0 + 3 * 0.044715 * square)
    return values * half, slope


GATHER_MIDDLE = (3, )
FOLD_MIDDLE = ()
def block_kernel(
    query_of_ref,
    live_ref,
    passage_ref,
    read_self_refs,
    write_self_ref,
    read_cross_refs,
    write_cross_ref,
    expand_ref,
    reduce_ref,
    target_ref,
    cotangent_ref,
    gains_ref,
    table_ref,
    bucket_ref,
    count_ref,
    shard_out,
    expand_out,
    reduce_out,
    slots_ref,
    gains_out,
    bias_out,
    target_grad_ref,
    block_ref,
    exps_out,
    kv_out,
    place_ref,
    shard_ref,
    flag_ref,
    full,
    states,
    flags,
    kept,
    slot_got,
    exps,
    keys,
    q_rows,
    q_pair,
    o_pair,
    o_rows,
    centre,
    out_t,
    highest,
    total,
    tile_highest,
    scale_ref,
    query_ref,
    mixed_ref,
    residual_ref,
    qkv_ref,
    self_mixed_ref,
    self_exps_ref,
    self_scale_ref,
    upper_grad,
    row_sent,
    row_got,
    far_got,
    near_got,
    next_got,
    skip_got,
    dkv,
    kv_sum,
    early,
    outgoing,
    pair_got,
    small,
    small_got,
    skip_send,
    skip_recv,
    next_send,
    next_recv,
    near_send,
    near_recv,
    far_send,
    far_recv,
    fold_far_send,
    fold_far_recv,
    fold_near_send,
    fold_near_recv,
    fold_next_send,
    fold_next_recv,
    fold_skip_send,
    fold_skip_recv,
    slot_send,
    slot_recv,
    flag_send,
    flag_recv,
    core_send,
    core_recv,
    return_send,
    return_recv,
    pair_send,
    pair_recv,
    row_send,
    row_recv,
    small_send,
    small_recv,
    own_sem,
    exps_sem,
    keys_sem,
    out_sem,
):
    low, wide = jnp.bfloat16, jnp.float32
    me, core, x, y, z, near, far = places()
    groups = shard_ref.shape[0]
    partner = (me, 1 - core)
    pair = me // TILE
    tiles = CHIPS // TILE
    passage_len = states.shape[2]
    block_rows = RANKS * passage_len
    tile_rows = TILE * block_rows
    tokens = target_ref.shape[0]
    width = query_ref.shape[1]
    turn = 1 - core
    across_x, across_y = me + 1 - 2 * x, me + 2 - 4 * y
    skip_to = (me - 4 * z + 4 * z_turned(z, 1), core)
    next_to = (me - 4 * z + 4 * z_turned(z, 2), core)
    pairs = width // (2 * HEAD_DIM)
    heads = 2 * pairs
    half = states.shape[3]
    other_y = y + (1 - core) * (1 - 2 * y)
    other_x = x + core * (1 - 2 * x)

    def slots_of(ref, source):
        return ref.at[pl.ds(source * RANKS, RANKS)]

    def own_copy(g):
        return pltpu.make_async_copy(shard_ref.at[g], full.at[g, z, y, x], own_sem.at[g])

    def z_at(k):
        return z_turned(z, k)

    def spot(g, k, m):
        if m == 0:
            return full.at[g, z_at(k), y, x]
        return full.at[g, z_at(k), other_y, other_x]

    def block_of(g, k, m):
        return shard_ref.at[g] if k == m == 0 else spot(g, k, m)

    def skip_copy(g, m):
        src, dst = block_of(g, 0, m), spot(g, 0, m)
        return remote(src, dst, skip_send.at[g, m], skip_recv.at[g, m], skip_to)

    def next_copy(g, k, m):
        src, dst = block_of(g, k, m), spot(g, k, m)
        return remote(src, dst, next_send.at[g, k, m], next_recv.at[g, k, m], next_to)

    def near_copy(g, k):
        src, dst = block_of(g, k, 0), spot(g, k, 0)
        return remote(src, dst, near_send.at[g, k], near_recv.at[g, k], (near, core))

    def far_copy(g, k, m):
        src, dst = block_of(g, k, m), spot(g, k, m)
        return remote(src, dst, far_send.at[g, k, m], far_recv.at[g, k, m], (far, core))

    def before_far(g):
        if g in GATHER_MIDDLE:
            copies = [near_copy(g, 0)] + [skip_copy(g, m) for m in range(2)]
            return copies + [next_copy(g, k, m) for k in range(2) for m in range(2)]
        copies = [skip_copy(g, 0)] + [next_copy(g, k, 0) for k in range(2)]
        return copies + [near_copy(g, k) for k in range(4)]

    def slot_copy(to):
        return remote(
            slots_of(kept, to), slots_of(states.at[core], me), slot_send.at[to], slot_recv.at[me], (to, core)
        )

    def slot_arrival(came):
        block = slots_of(states.at[core], came)
        return remote(block, block, slot_send.at[came], slot_recv.at[came], (came, core))

    def flag_copy(to):
        return remote(flag_ref.at[to], flags.at[me], flag_send.at[to], flag_recv.at[me], (to, core))

    def flag_arrival(came):
        block = flags.at[came]
        return remote(block, block, flag_send.at[came], flag_recv.at[came], (came, core))

    def core_copy(came):
        block = slots_of(states.at[core], came)
        return remote(block, block, core_send.at[came], core_recv.at[came], partner)

    def row_copy(i):
        b = i % 2
        return remote(row_sent.at[b], row_got.at[b], row_send.at[i], row_recv.at[i], partner)

    def give(i, value):
        if i >= 2:
            row_copy(i - 2).wait_send()
        row_sent[i % 2] = value
        row_copy(i).start()

    def pair_sum(i):
        row_copy(i).wait_recv()
        return row_sent[i % 2] + row_got[i % 2]

    def launch(g):
        if g in GATHER_MIDDLE:
            near_copy(g, 0).start()
        skip_copy(g, 0).start()
        next_copy(g, 0, 0).start()
        if g not in GATHER_MIDDLE:
            near_copy(g, 0).start()
        far_copy(g, 0, 0).start()
        own_copy(g).start()

    def relay_one(g):
        if g in GATHER_MIDDLE:
            near_copy(g, 0).wait_recv()
            skip_copy(g, 1).start()
            next_copy(g, 0, 1).start()
            far_copy(g, 0, 1).start()
        else:
            skip_copy(g, 0).wait_recv()
            next_copy(g, 1, 0).start()
            near_copy(g, 1).start()
            far_copy(g, 1, 0).start()

    def relay_two(g):
        for i in range(2):
            if g in GATHER_MIDDLE:
                skip_copy(g, i).wait_recv()
                next_copy(g, 1, i).start()
                far_copy(g, 1, i).start()
            else:
                next_copy(g, i, 0).wait_recv()
                near_copy(g, i + 2).start()
                far_copy(g, i + 2, 0).start()

    def relay_three(g):
        for i in range(4):
            if g in GATHER_MIDDLE:
                k, m = i % 2, i // 2
                next_copy(g, k, m).wait_recv()
                far_copy(g, k + 2, m).start()
            else:
                near_copy(g, i).wait_recv()
                far_copy(g, i, 1).start()

    def arrived(g):
        own_copy(g).wait()
        for k in range(4):
            for m in range(2):
                far_copy(g, k, m).wait_recv()

    def weight(g):
        return full[g].reshape(full.shape[1] * 4 * full.shape[4], full.shape[5])

    staging = pltpu.make_async_copy(
        passage_ref, slot_got.at[pl.ds(0, passage_ref.shape[0])], out_sem.at[0]
    )
    staging.start()

    def mine(g, k, m, here):
        near_at, far_at = (1 - turn) * y + turn * x, (1 - turn) * x + turn * y
        near_at = near_at if m == 0 else 1 - near_at
        far_at = far_at if here else 1 - far_at
        grads = early if g == 3 else full.at[g]
        return grads.at[
            z_at(k),
            (1 - turn) * near_at + turn * far_at,
            (1 - turn) * far_at + turn * near_at,
        ]

    def next_place(g, k, m):
        return next_got.at[g, k] if m == 0 else near_got.at[g, 1 + k]

    def skip_place(g, m):
        return skip_got.at[g] if m == 0 else near_got.at[g, 3]

    def fold_far(g, k, m):
        src, dst = mine(g, k, m, False), far_got.at[g, m, k]
        sems = fold_far_send.at[g, k, m], fold_far_recv.at[g, k, m]
        return remote(src, dst, *sems, (near, core))

    def fold_near(g, k):
        src, dst = far_got.at[g, 1, k], near_got.at[g, k]
        return remote(src, dst, fold_near_send.at[g, k], fold_near_recv.at[g, k], (far, core))

    def fold_next(g, k, m):
        src = far_got.at[g, m, 2 + k] if g in FOLD_MIDDLE else near_got.at[g, 2 + k]
        sems = fold_next_send.at[g, k, m], fold_next_recv.at[g, k, m]
        return remote(src, next_place(g, k, m), *sems, next_to)

    def fold_skip(g, m):
        src = far_got.at[g, m, 1] if g in FOLD_MIDDLE else near_got.at[g, 1]
        sems = fold_skip_send.at[g, m], fold_skip_recv.at[g, m]
        return remote(src, skip_place(g, m), *sems, skip_to)

    def fold_copies(g):
        copies = [fold_far(g, k, m) for k in range(4) for m in range(2)]
        if g in FOLD_MIDDLE:
            copies += [fold_next(g, k, m) for k in range(2) for m in range(2)]
            return copies + [fold_skip(g, m) for m in range(2)] + [fold_near(g, 0)]
        copies += [fold_next(g, k, 0) for k in range(2)]
        return copies + [fold_skip(g, 0)] + [fold_near(g, k) for k in range(4)]

    def add_up(ref, *others):
        total = ref[...].astype(wide)
        for other in others:
            total = total + other[...].astype(wide)
        ref[...] = total.astype(low)

    def far_start(g):
        order = [(k, m) for m in (1, 0) for k in (3, 2, 1, 0)]
        if g in FOLD_MIDDLE:
            order = [(k, m) for k in (3, 2, 1, 0) for m in (1, 0)]
        for k, m in order:
            fold_far(g, k, m).start()

    def far_add(g):
        if g in FOLD_MIDDLE:
            for k, m in ((3, 1), (3, 0), (2, 1), (2, 0)):
                fold_far(g, k, m).wait_recv()
                add_up(far_got.at[g, m, k], mine(g, k, m, True))
                fold_next(g, k - 2, m).start()
        else:
            for k in (3, 2, 1, 0):
                fold_far(g, k, 1).wait_recv()
                add_up(far_got.at[g, 1, k], mine(g, k, 1, True))
                fold_near(g, k).start()

    def near_add(g):
        if g in FOLD_MIDDLE:
            for m in (1, 0):
                fold_far(g, 1, m).wait_recv()
                fold_next(g, 1, m).wait_recv()
                add_up(far_got.at[g, m, 1], mine(g, 1, m, True), next_place(g, 1, m))
                fold_skip(g, m).start()
        else:
            for k in (3, 2, 1, 0):
                fold_far(g, k, 0).wait_recv()
                fold_near(g, k).wait_recv()
                add_up(near_got.at[g, k], mine(g, k, 0, True), far_got.at[g, 0, k])
                if k >= 2:
                    fold_next(g, k - 2, 0).start()

    def next_add(g):
        if g in FOLD_MIDDLE:
            fold_far(g, 0, 1).wait_recv()
            fold_next(g, 0, 1).wait_recv()
            fold_skip(g, 1).wait_recv()
            add_up(
                far_got.at[g, 1, 0], mine(g, 0, 1, True), next_place(g, 0, 1), skip_place(g, 1)
            )
            fold_near(g, 0).start()
        else:
            fold_next(g, 1, 0).wait_recv()
            add_up(near_got.at[g, 1], next_place(g, 1, 0))
            fold_skip(g, 0).start()

    def skip_add(g):
        fold_next(g, 0, 0).wait_recv()
        fold_skip(g, 0).wait_recv()
        if g in FOLD_MIDDLE:
            fold_far(g, 0, 0).wait_recv()
            fold_near(g, 0).wait_recv()
        parts = [near_got[g, 0], next_got[g, 0], skip_got[g]]
        if g in FOLD_MIDDLE:
            parts += [mine(g, 0, 0, True)[...], far_got[g, 0, 0]]
        total = parts[0].astype(wide)
        for part in parts[1:]:
            total = total + part.astype(wide)
        if g < 2:
            shard_out[g] = total
        else:
            (expand_out, reduce_out)[g - 2][...] = total

    def send_pair(j):
        for i in range(TILE):
            to = (pair + j) % tiles * TILE + i

            @pl.when(to != me)
            def _():
                flag_copy(to).start()
                slot_copy(to).start()

    lane = lax.broadcasted_iota(jnp.int32, (1, 2 * HEAD_DIM), 1)
    nobody = jnp.zeros_like(lane)

    def at_place(row, place):
        return jnp.sum(jnp.where(lane == place, row, 0))

    def route_step(slot, carry):
        met, found, alive, queries = carry
        query = query_of_ref[slot]
        hit = lane == query
        found = tuple(jnp.where(hit & (met == r), slot, found[r]) for r in range(RANKS))
        alive = tuple(jnp.where(hit & (met == r), live_ref[slot], alive[r]) for r in range(RANKS))
        queries = jnp.where(lane == slot, query, queries)
        return met + hit.astype(jnp.int32), found, alive, queries

    def rank_step(slot, ranks):
        later = (lane > slot) & (queries_here == query_of_ref[slot])
        return ranks + later.astype(jnp.int32)

    def fill(to, carry):
        for rank in range(RANKS):
            kept[to * RANKS + rank] = slot_got[at_place(slot_at[rank], to)]
        row = lax.broadcasted_iota(jnp.int32, flag_ref.shape[1:], 0)
        marks = jnp.zeros(flag_ref.shape[1:], wide)
        for rank in range(RANKS):
            mark = jnp.where(at_place(live_at[rank], to) > 0, 0.0, MASKED)
            marks = jnp.where(row == rank, mark, marks)
        flag_ref[to] = marks.astype(low)
        return carry

    greet_signal(me, core)
    for g, reads, writes in ((0, read_self_refs, write_self_ref), (1, read_cross_refs, write_cross_ref)):
        for i, read in enumerate(reads):
            shard_ref[g, :, i * width : (i + 1) * width] = read[...]
        shard_ref[g, :, 3 * width :] = writes[...]
    shard_ref[2] = expand_ref[...]
    shard_ref[3] = reduce_ref[...]
    greet_wait()
    launch(0)
    launch(1)
    slots_here = query_of_ref.shape[0]
    unused, slot_at, live_at, queries_here = lax.fori_loop(
        0,
        slots_here,
        route_step,
        (nobody, (nobody,) * RANKS, (nobody,) * RANKS, nobody),
        unroll=8,
    )
    staging.wait()
    lax.fori_loop(0, CHIPS, fill, 0, unroll=4)
    send_pair(0)
    send_pair(1)
    states[core, pl.ds(me * RANKS, RANKS)] = kept[pl.ds(me * RANKS, RANKS)]
    flags[me] = flag_ref[me]
    core_copy(me).start()

    line = lax.dot_general(
        table_ref[...],
        bucket_ref[...],
        (((1,), (0,)), ((), ())),
        precision=lax.Precision.HIGHEST,
        preferred_element_type=wide,
    )
    def bias_of(h):
        return kv_sum.at[h // 3, pl.ds(0, tokens), pl.ds(h % 3 * tokens, tokens)]

    turns = []
    for h in range(heads):
        for s in range(8):
            row = line[h : h + 1]
            turns.append(row if s == 0 else pltpu.roll(row, s, 1))
    base = jnp.concatenate(turns, axis=0)

    def bias_step(i, carry):
        rows = pltpu.roll(base, 8 * i, 1)
        for h in range(heads):
            bias_of(h)[pl.ds(pl.multiple_of(8 * i, 8), 8), :] = rows[8 * h : 8 * h + 8]
        return carry

    lax.fori_loop(0, tokens // 8, bias_step, 0)
    ranks = lax.fori_loop(0, slots_here, rank_step, nobody, unroll=8)

    def place_step(slot, carry):
        place_ref[slot] = query_of_ref[slot] * RANKS + at_place(ranks, slot)
        return carry

    lax.fori_loop(0, slots_here, place_step, 0, unroll=8)
    residual = target_ref[...].astype(wide)
    normed = (unit_of(residual)[0] * gains_ref[0:1, :]).astype(low)

    relay_one(0)
    launch(3)
    launch(2)
    relay_one(1)
    send_pair(2)
    relay_two(0)
    send_pair(3)
    send_pair(4)
    relay_three(0)
    relay_two(1)
    arrived(0)

    qkv_ref[...] = mm(normed, weight(0)[:, : 3 * width]).astype(low)
    relay_three(1)
    send_pair(5)
    queries_t = qkv_ref[:, :width].astype(wide).T
    for h in range(heads):
        q_rows[h] = halves_of_rows(queries_t, h)
    key_at = lax.broadcasted_iota(jnp.int32, (tokens, tokens), 0)
    query_at = lax.broadcasted_iota(jnp.int32, (tokens, tokens), 1)
    self_scale_ref[...] = jnp.zeros_like(self_scale_ref)
    for p in range(pairs):
        at = 2 * HEAD_DIM * p
        head_keys = qkv_ref[:, width + at : width + at + 2 * HEAD_DIM]
        values_t = qkv_ref[:, 2 * width + at : 2 * width + at + 2 * HEAD_DIM].T
        for a in range(2):
            h = 2 * p + a
            scores = mm(head_keys, q_rows[h]) + bias_of(h)[...]
            scores = jnp.where(key_at <= query_at, scores, MASKED)
            head_exps, unused, sums = exp_rows(scores)
            head_exps = head_exps.astype(low)
            self_exps_ref[h] = head_exps
            inverse = 1.0 / sums
            self_scale_ref[h : h + 1, :] = inverse
            first = at + a * HEAD_DIM
            out_t[first : first + HEAD_DIM, :] = (
                mm(values_t[a * HEAD_DIM : (a + 1) * HEAD_DIM], head_exps) * inverse
            )
        if p == 1:
            send_pair(6)
            send_pair(7)
    self_mixed_ref[...] = out_t[...].T.astype(low)
    give(0, rows_nt(self_mixed_ref[...], weight(0)[:, 3 * width :]))
    relay_one(2)
    arrived(1)
    residual_ref[...] = residual + pair_sum(0)

    normed = (unit_of(residual_ref[...])[0] * gains_ref[1:2, :]).astype(low)
    query_ref[...] = mm(normed, weight(1)[:, :width]).astype(low)
    queries_t = query_ref[...].astype(wide).T
    for h in range(heads):
        q_rows[h] = halves_of_rows(queries_t, h)
    out_t[...] = jnp.zeros_like(out_t)
    highest[...] = jnp.full_like(highest, MASKED)
    total[...] = jnp.zeros_like(total)
    tile_highest[...] = jnp.zeros_like(tile_highest)

    def take_in(t):
        for i in range(TILE):
            came = (pair - t + tiles) % tiles * TILE + i

            @pl.when(came != me)
            def _():
                flag_arrival(came).wait_recv()
                slot_arrival(came).wait_recv()
                core_copy(came).start()

    def exps_copy(t):
        rows = pl.ds((pair - t + tiles) % tiles * tile_rows, tile_rows)
        return pltpu.make_async_copy(exps.at[t % 2], exps_out.at[:, rows], exps_sem.at[t % 2])

    def keys_copy(t):
        rows = pl.ds((pair - t + tiles) % tiles * tile_rows, tile_rows)
        return pltpu.make_async_copy(keys.at[t % 2], kv_out.at[rows], keys_sem.at[t % 2])

    take_in(0)

    def tile_step(t, carry):
        tile = (pair - t + tiles) % tiles

        @pl.when(t == 1)
        def _():
            relay_two(2)

        @pl.when(t == 4)
        def _():
            relay_three(2)

        @pl.when(t == 6)
        def _():
            relay_two(3)

        @pl.when(t + 1 < tiles)
        def _():
            take_in(t + 1)

        @pl.when(t == 3)
        def _():
            relay_one(3)

        @pl.when(t >= 2)
        def _():
            exps_copy(t - 2).wait()
            keys_copy(t - 2).wait()

        for i in range(TILE):
            core_copy(tile * TILE + i).wait_recv()
        kv_parts = []
        for c in range(2):
            rows = states[c, pl.ds(tile * TILE * RANKS, TILE * RANKS)].reshape(tile_rows, half)
            w = full[1, 2 * c : 2 * c + 2, :, :, :, width : 3 * width]
            kv_parts.append(mm(rows, w.reshape(half, 2 * width)))
        keys[t % 2] = (kv_parts[0] + kv_parts[1]).astype(low)
        keys_copy(t).start()
        masks = []
        for i in range(TILE):
            for rank in range(RANKS):
                masks.append(flags[tile * TILE + i, rank : rank + 1, :].astype(wide)[None])
        masks = jnp.concatenate(masks, axis=0)
        for p in range(pairs):
            at = 2 * HEAD_DIM * p
            head_keys = keys[t % 2, :, at : at + 2 * HEAD_DIM]
            values_t = keys[t % 2, :, width + at : width + at + 2 * HEAD_DIM].T
            for a in range(2):
                h = 2 * p + a
                scores = mm(head_keys, q_rows[h]).reshape(TILE * RANKS, passage_len, tokens) + masks
                head_exps, top, sums = exp_rows(scores.reshape(tile_rows, tokens))
                head_exps = head_exps.astype(low)
                exps[t % 2, h] = head_exps
                before = highest[h : h + 1, :]
                now = jnp.maximum(before, top)
                keep, add = jnp.exp(before - now), jnp.exp(top - now)
                highest[h : h + 1, :] = now
                tile_highest[tile, h : h + 1, :] = top
                total[h : h + 1, :] = total[h : h + 1, :] * keep + sums * add
                first = at + a * HEAD_DIM
                out_t[first : first + HEAD_DIM, :] = (
                    out_t[first : first + HEAD_DIM, :] * keep
                    + mm(values_t[a * HEAD_DIM : (a + 1) * HEAD_DIM], head_exps) * add
                )
        exps_copy(t).start()

        return carry

    lax.fori_loop(0, tiles, tile_step, 0)
    for h in range(heads):
        inverse = 1.0 / total[h : h + 1, :]
        out_t[h * HEAD_DIM : (h + 1) * HEAD_DIM, :] *= inverse
        scale_ref[:, h, :] = jnp.exp(tile_highest[:, h, :] - highest[h : h + 1, :]) * inverse
    mixed_ref[...] = out_t[...].T.astype(low)
    give(1, rows_nt(mixed_ref[...], weight(1)[:, 3 * width :]))
    relay_three(3)
    residual_three = residual_ref[...] + pair_sum(1)
    unit, factor = unit_of(residual_three)
    normed = (unit * gains_ref[2:3, :]).astype(low)


    def sends_done(g):
        for copy in before_far(g) + [far_copy(g, k, m) for k in range(4) for m in range(2)]:
            copy.wait_send()

    def store_grad(g, first, value):
        blocks = value.astype(low).reshape(full.shape[1:5] + (value.shape[1],))
        full[g, :, :, :, :, first : first + value.shape[1]] = blocks

    arrived(2)
    hidden, slope = gelu_both(mm(normed, weight(2)))
    hidden = hidden.astype(low)
    early[...] = rows_tn(cotangent_ref[...], hidden).astype(low).reshape(early.shape)
    far_start(3)
    arrived(3)
    hidden_grad = mm(cotangent_ref[...], weight(3))
    before_grad = (hidden_grad * slope).astype(low)
    give(2, rows_nt(before_grad, weight(2)))
    sends_done(2)
    store_grad(2, 0, rows_tn(normed, before_grad))
    far_start(2)
    back, gain_three = rms_backward(pair_sum(2), unit, factor, gains_ref[2:3, :])
    upper_grad[...] = cotangent_ref[...].astype(wide) + back
    give(3, rows_nt(hidden, weight(3)))
    sends_done(0)
    sends_done(1)
    sends_done(3)
    for k in range(1, CHIPS):
        to = (me + k) % CHIPS
        slot_copy(to).wait_send()
        flag_copy(to).wait_send()
    for k in range(CHIPS):
        core_copy(k).wait_send()
    for t in range(tiles - 2, tiles):
        exps_copy(t).wait()
        keys_copy(t).wait()

    def back_tile(t):
        return (t + pair) % tiles

    def exps_load(t):
        rows = pl.ds(back_tile(t) * tile_rows, tile_rows)
        return pltpu.make_async_copy(exps_out.at[:, rows], exps.at[t % 2], exps_sem.at[t % 2])

    def keys_load(t):
        rows = pl.ds(back_tile(t) * tile_rows, tile_rows)
        return pltpu.make_async_copy(kv_out.at[rows], keys.at[t % 2], keys_sem.at[t % 2])

    def loads_start(t):
        exps_load(t).start()
        keys_load(t).start()

    def kv_weights(c):
        w = full[1, pl.ds(2 * c, 2), :, :, :, width : 3 * width]
        return w.reshape(half, 2 * width)

    def pair_copy(t):
        return remote(
            outgoing.at[t % 2],
            pair_got.at[pl.ds(back_tile(t) * TILE * RANKS, TILE * RANKS)],
            pair_send.at[t % 2],
            pair_recv.at[t],
            partner,
        )

    def return_copy(to):
        return remote(
            slots_of(kept, to), slots_of(slot_got, me), return_send.at[to], return_recv.at[me], (to, core)
        )

    def return_arrival(came):
        block = slots_of(slot_got, came)
        return remote(block, block, return_send.at[came], return_recv.at[came], (came, core))

    def finish_tile(t):
        tile = back_tile(t)
        pair_copy(t).wait_recv()
        rows = pl.ds(tile * TILE * RANKS, TILE * RANKS)
        kept[rows] = (kept[rows].astype(wide) + pair_got[rows].astype(wide)).astype(low)
        for j in range(TILE):
            to = tile * TILE + j

            @pl.when(to != me)
            def _():
                return_copy(to).start()

            @pl.when(to == me)
            def _():
                own = pl.ds(me * RANKS, RANKS)
                slot_got[own] = kept[own]

    grad_low = upper_grad[...].astype(low)
    mixed_grad = mm(grad_low, weight(1)[:, 3 * width :]).astype(low)
    prepare_heads(heads, query_ref, mixed_grad, mixed_ref[...], q_pair, o_pair, o_rows, centre)
    out_t[...] = jnp.zeros_like(out_t)
    kv_sum[...] = jnp.zeros_like(kv_sum)
    loads_start(0)
    block_ref[...] = (residual_three + pair_sum(3)).astype(low)

    def back_step(t, carry):
        tile = back_tile(t)
        @pl.when(t + 1 < tiles)
        def _():
            loads_start(t + 1)

        exps_load(t).wait()
        keys_load(t).wait()

        def prob(h):
            return exps[t % 2, h].astype(wide) * scale_ref[tile, h : h + 1, :]

        for p in range(pairs):
            at = 2 * HEAD_DIM * p
            key_grad, value_grad, query_parts = head_pair_back(
                p,
                keys[t % 2, :, at : at + 2 * HEAD_DIM],
                keys[t % 2, :, width + at : width + at + 2 * HEAD_DIM],
                prob,
                q_pair,
                o_pair,
                o_rows,
                centre,
                None,
            )
            dkv[:, at : at + 2 * HEAD_DIM] = key_grad
            dkv[:, width + at : width + at + 2 * HEAD_DIM] = value_grad
            for a in range(2):
                first = at + a * HEAD_DIM
                out_t[first : first + HEAD_DIM, :] += query_parts[a]
        here = dkv[...]

        @pl.when(t >= 2)
        def _():
            pair_copy(t - 2).wait_send()

        weights = kv_weights(1 - core)
        outgoing[t % 2] = rows_nt(here, weights).astype(low).reshape(outgoing.shape[1:])
        pair_copy(t).start()
        weights = kv_weights(core)
        mine = rows_nt(here, weights).astype(low).reshape(outgoing.shape[1:])
        kept[pl.ds(tile * TILE * RANKS, TILE * RANKS)] = mine

        rows = pl.ds(tile * TILE * RANKS, TILE * RANKS)
        for i in range(2):
            kv_sum[i] += rows_tn(states[i, rows].reshape(tile_rows, half), here)

        @pl.when(t >= 1)
        def _():
            finish_tile(t - 1)

        @pl.when(t == 2)
        def _():
            far_add(2)

        @pl.when(t == 5)
        def _():
            far_add(3)

        return carry

    lax.fori_loop(0, tiles, back_step, 0)
    dq = out_t[...].T.astype(low)
    give(4, rows_nt(dq, weight(1)[:, :width]))
    near_add(2)
    store_grad(1, 3 * width, rows_tn(upper_grad[...].astype(low), mixed_ref[...]))
    finish_tile(tiles - 1)
    unit_two, factor_two = unit_of(residual_ref[...])
    normed_two = (unit_two * gains_ref[1:2, :]).astype(low)
    store_grad(1, 0, rows_tn(normed_two, dq))

    store_grad(1, width, kv_sum[...].reshape(2 * half, 2 * width))
    far_start(1)
    next_add(2)

    back, gain_two = rms_backward(pair_sum(4), unit_two, factor_two, gains_ref[1:2, :])
    near_add(3)
    upper_grad[...] += back

    grad_low = upper_grad[...].astype(low)
    mixed_grad = mm(grad_low, weight(0)[:, 3 * width :]).astype(low)
    prepare_heads(
        heads,
        qkv_ref.at[:, :width],
        mixed_grad,
        self_mixed_ref[...],
        q_pair,
        o_pair,
        o_rows,
        centre,
    )

    def self_prob(h):
        return self_exps_ref[h].astype(wide) * self_scale_ref[h : h + 1, :]

    def keep_scores(h, score_grad):
        self_exps_ref[h] = score_grad

    query_rows, key_columns, value_columns = [], [], []
    for p in range(pairs):
        at = 2 * HEAD_DIM * p
        key_grad, value_grad, query_parts = head_pair_back(
            p,
            qkv_ref[:, width + at : width + at + 2 * HEAD_DIM],
            qkv_ref[:, 2 * width + at : 2 * width + at + 2 * HEAD_DIM],
            self_prob,
            q_pair,
            o_pair,
            o_rows,
            centre,
            keep_scores,
        )
        key_columns.append(key_grad)
        value_columns.append(value_grad)
        query_rows.extend(query_parts)
    dq = jnp.concatenate(query_rows, axis=0).T.astype(low)
    dqkv = jnp.concatenate([dq] + key_columns + value_columns, axis=1)
    give(5, rows_nt(dqkv, weight(0)[:, : 3 * width]))
    store_grad(0, 3 * width, rows_tn(upper_grad[...].astype(low), self_mixed_ref[...]))
    unit_one, factor_one = unit_of(target_ref[...].astype(wide))
    normed_one = (unit_one * gains_ref[0:1, :]).astype(low)
    store_grad(0, 0, rows_tn(normed_one, dqkv))
    far_start(0)
    far_add(1)
    next_add(3)

    length = self_exps_ref.shape[1]

    def diagonal_step(i, total):
        rows = self_exps_ref[:, pl.ds(pl.multiple_of(16 * i, 16), 16), :].astype(wide)
        rows = rows.reshape(heads * 16, length)
        return total + pltpu.roll(rows, (length - 16 * i) % length, 1)

    total = lax.fori_loop(
        0, length // 16, diagonal_step, jnp.zeros((heads * 16, length), wide)
    ).reshape(heads, 16, length)
    small[...] = jnp.zeros_like(small)
    for h in range(heads):
        line = total[h, 0:1]
        for s in range(1, 16):
            line = line + pltpu.roll(total[h, s : s + 1], length - s, 1)
        small[8 + h : 9 + h, :length] = line
    by_bucket = jnp.dot(
        small[8:16, :length], count_ref[...], precision=lax.Precision.HIGHEST,
        preferred_element_type=wide,
    )
    small[8:16, :length] = jnp.zeros((8, length), wide)
    small[8:16, : count_ref.shape[1]] = by_bucket

    back, gain_one = rms_backward(pair_sum(5), unit_one, factor_one, gains_ref[0:1, :])
    target_grad_ref[...] = (upper_grad[...] + back).astype(low)
    small[0:1, :] = gain_one[None, :]
    small[1:2, :] = gain_two[None, :]
    small[2:3, :] = gain_three[None, :]

    def small_copy(step):
        if step == 0:
            return remote(small, small_got.at[0], small_send.at[0], small_recv.at[0], (across_x, core))
        if step == 1:
            return remote(
                small_got.at[6], small_got.at[1], small_send.at[1], small_recv.at[1], (across_y, core)
            )
        return remote(
            small_got.at[7],
            small_got.at[2 + z],
            small_send.at[step],
            small_recv.at[step],
            ((me + 4 * (step - 1)) % CHIPS, core),
        )

    small_copy(0).start()
    skip_add(2)
    near_add(1)
    far_add(0)
    skip_add(3)
    next_add(1)
    near_add(0)
    next_add(0)
    skip_add(1)
    small_copy(0).wait_recv()
    small_got[6] = small[...] + small_got[0]
    small_copy(1).start()
    for k in range(1, CHIPS):
        return_arrival((me + k) % CHIPS).wait_recv()
    small_copy(1).wait_recv()
    small_got[7] = small_got[6] + small_got[1]
    for step in range(2, 5):
        small_copy(step).start()
    small_got[2 + z] = small_got[7]
    for k in range(1, CHIPS):
        return_copy((me + k) % CHIPS).wait_send()
    slots = slots_ref.shape[0]

    def pick(slot, carry):
        kept[slot] = slot_got[place_ref[slot]]
        return carry

    lax.fori_loop(0, slots, pick, 0, unroll=4)
    picked = pltpu.make_async_copy(kept.at[pl.ds(0, slots)], slots_ref, out_sem.at[1])
    picked.start()
    skip_add(0)
    for step in range(2, 5):
        small_copy(step).wait_recv()
    whole = small_got[2] + small_got[3] + small_got[4] + small_got[5]
    gains_out[...] = whole[: gains_out.shape[0]]
    bias_out[...] = whole[8 : 8 + heads, : bias_out.shape[1]]
    for g in range(groups):
        for copy in fold_copies(g):
            copy.wait_send()
    for t in range(tiles - 2, tiles):
        pair_copy(t).wait_send()
    for step in range(5):
        small_copy(step).wait_send()
    for i in range(4, 6):
        row_copy(i).wait_send()
    picked.wait()


def run_block(
    query_of, live, passages, weights, target, cotangent, gains, table, buckets, counts
):
    low, wide = jnp.bfloat16, jnp.float32
    groups = 4
    rows, columns = weights[4].shape
    slots, passage_len, half = passages.shape
    tokens, model = target.shape
    width = columns // 4
    heads = width // HEAD_DIM
    key_count = CHIPS * RANKS * passage_len
    tile_rows = TILE * RANKS * passage_len
    tiles = CHIPS // TILE
    small_shape = (16, model)
    shape = jax.ShapeDtypeStruct
    vmem = pltpu.VMEM
    pair_heads = vmem((heads, tokens, 2 * HEAD_DIM), low)
    pair_rows = vmem((heads, 2 * HEAD_DIM, tokens), low)
    all_slots = (CHIPS * RANKS, passage_len, half)

    def both(*dims):
        return [DMA(dims), DMA(dims)]

    return pl.pallas_call(
        block_kernel,
        out_shape=(
            shape((2, rows, columns), wide),
            shape((rows, columns), wide),
            shape((rows, columns), wide),
            shape((slots, passage_len, half), low),
            shape(gains.shape, wide),
            shape(table.shape, wide),
            shape((tokens, model), low),
            shape((tokens, model), low),
            shape((heads, key_count, tokens), low),
            shape((key_count, 2 * width), low),
        ),
        in_specs=[IN_SMEM] * 2
        + [ANY, (IN_VMEM,) * 3, IN_VMEM, (IN_VMEM,) * 3, IN_VMEM, IN_VMEM, IN_VMEM]
        + [IN_VMEM] * 6,
        out_specs=(IN_VMEM,) * 3 + (ANY,) + (IN_VMEM,) * 4 + (ANY, ANY),
        scratch_shapes=[
            pltpu.SMEM((slots,), jnp.int32),
            vmem((groups, rows, columns), low),
            vmem((CHIPS, FLAG_ROWS, tokens), low),
            vmem((groups, 4, 2, 2, rows, columns), low),
            vmem((2,) + all_slots, low),
            vmem((CHIPS, FLAG_ROWS, tokens), low),
            vmem(all_slots, low),
            vmem(all_slots, low),
            vmem((2, heads, tile_rows, tokens), low),
            vmem((2, tile_rows, 2 * width), low),
            pair_rows,
            pair_heads,
            pair_heads,
            pair_rows,
            vmem((8, tokens), wide),
            vmem((width, tokens), wide),
            vmem((8, tokens), wide),
            vmem((8, tokens), wide),
            vmem((tiles, 8, tokens), wide),
            vmem((tiles, 8, tokens), wide),
            vmem((tokens, width), low),
            vmem((tokens, width), low),
            vmem((tokens, model), wide),
            vmem((tokens, 3 * width), low),
            vmem((tokens, width), low),
            vmem((heads, tokens, tokens), low),
            vmem((8, tokens), wide),
            vmem((tokens, model), wide),
            vmem((2, tokens, model), wide),
            vmem((2, tokens, model), wide),
            vmem((groups, 2, 4, rows, columns), low),
            vmem((groups, 4, rows, columns), low),
            vmem((groups, 2, rows, columns), low),
            vmem((groups, rows, columns), low),
            vmem((tile_rows, 2 * width), low),
            vmem((2, half, 2 * width), wide),
            vmem((4, 2, 2, rows, columns), low),
            vmem((2, TILE * RANKS, passage_len, half), low),
            vmem(all_slots, low),
            vmem(small_shape, wide),
            vmem((8,) + small_shape, wide),
        ]
        + both(groups, 2)
        + both(groups, 2, 2)
        + both(groups, 4)
        + both(groups, 4, 2)
        + both(groups, 4, 2)
        + both(groups, 4)
        + both(groups, 2, 2)
        + both(groups, 2)
        + both(CHIPS)
        + both(CHIPS)
        + both(CHIPS)
        + both(CHIPS)
        + [DMA((2,)), DMA((tiles,))]
        + both(6)
        + both(5)
        + [DMA((groups,)), DMA((2,)), DMA((2,)), DMA((2,))],
        compiler_params=pltpu.CompilerParams(
            collective_id=0, has_side_effects=True, vmem_limit_bytes=62 * 2**20
        ),
    )(query_of, live, passages, *weights, target, cotangent, gains, table, buckets, counts)


def body(
    target_states,
    passage_states,
    slot_query,
    slot_live,
    norm_gains,
    self_query,
    self_key,
    self_value,
    self_output,
    position_bias,
    cross_query,
    cross_key,
    cross_value,
    cross_output,
    expand_weight,
    reduce_weight,
    output_cotangent,
):
    low = jnp.bfloat16
    width_here = self_query.shape[1]
    heads_here = width_here // HEAD_DIM
    passage_len, half = passage_states.shape[1:]
    bucket_count = position_bias.shape[0]
    distance = np.zeros((TLEN, 128), np.float32)
    distance[np.arange(TLEN), bucket_table(TLEN, bucket_count, MAXDIST)[:, 0]] = 1.0
    shard_grads, expand_grad, reduce_grad, passage_grad, gains_grad, bias_grad, target_grad, block_out = run_block(
        slot_query,
        slot_live,
        passage_states,
        (
            (self_query, self_key, self_value),
            self_output.T,
            (cross_query, cross_key, cross_value),
            cross_output.T,
            expand_weight,
            reduce_weight.T,
        ),
        target_states,
        output_cotangent,
        norm_gains,
        position_bias.T,
        jnp.asarray(distance[:, :bucket_count].T),
        jnp.asarray(distance),
    )[:8]
    w = width_here
    first, second = shard_grads[0], shard_grads[1]
    return (
        block_out,
        target_grad,
        passage_grad,
        gains_grad,
        first[:, :w],
        first[:, w : 2 * w],
        first[:, 2 * w : 3 * w],
        first[:, 3 * w :].T,
        bias_grad.T,
        second[:, :w],
        second[:, w : 2 * w],
        second[:, 2 * w : 3 * w],
        second[:, 3 * w :].T,
        expand_grad,
        reduce_grad.T,
    )


def solution(mesh):
    return jax.shard_map(
        body if fits(mesh) else body_any,
        mesh=mesh,
        in_specs=(
            P("pas", None),
            P("pas", None, "mdl"),
            P("pas"),
            P("pas"),
            P(),
            P("pas", "mdl"),
            P("pas", "mdl"),
            P("pas", "mdl"),
            P("mdl", "pas"),
            P(None, "mdl"),
            P("pas", "mdl"),
            P("pas", "mdl"),
            P("pas", "mdl"),
            P("mdl", "pas"),
            P("pas", "mdl"),
            P("mdl", "pas"),
            P("pas", None),
        ),
        out_specs=(
            P("pas", None),
            P("pas", None),
            P("pas", None, "mdl"),
            P(),
            P("pas", "mdl"),
            P("pas", "mdl"),
            P("pas", "mdl"),
            P("mdl", "pas"),
            P(None, "mdl"),
            P("pas", "mdl"),
            P("pas", "mdl"),
            P("pas", "mdl"),
            P("mdl", "pas"),
            P("pas", "mdl"),
            P("mdl", "pas"),
        ),
        check_vma=False,
    )
```
